32 devices in a mesh: rows: 8 (over z, y), seq: 4 (over x, core).
Axes of the slice: x: 2, y: 2, z: 4, core: 2. Of those that a mesh axis runs over, the one named last changes fastest.
Arguments:
- block_input: bfloat16 [8, 1024, 768], P('rows', 'seq'), may hold values from -6 to 6
- output_cotangent: bfloat16 [8, 1024, 768], P('rows', 'seq'), may hold values from -6 to 6
- doc_ids: int32 [8, 1024], P('rows'), may hold values from 0 to 510, as said below
- w_qkv: bfloat16 [2, 768, 2304], P(None, 'seq'), may hold values from -0.21875 to 0.21875
- w_o: bfloat16 [2, 768, 768], P(None, 'seq'), may hold values from -0.875 to 0.875
- w_fc: bfloat16 [2, 768, 3072], P(None, 'seq'), may hold values from -0.21875 to 0.21875
- w_proj: bfloat16 [2, 3072, 768], P(None, 'seq'), may hold values from -0.21875 to 0.21875
- norm_gain: bfloat16 [2, 2, 768], P(None, None, 'seq'), may hold values from 0.5 to 1.5
- norm_bias: bfloat16 [2, 2, 768], P(None, None, 'seq'), may hold values from -4 to 4
- qv_bias: bfloat16 [2, 2, 768], P(None, None, 'seq'), may hold values from -4 to 4
- out_bias: bfloat16 [2, 2, 768], P(None, None, 'seq'), may hold values from -6 to 6
- fc_bias: bfloat16 [2, 3072], P(None, 'seq'), may hold values from -4 to 4
Outputs:
- block_output: float32 [8, 1024, 768], P('rows', 'seq')
- input_grad: float32 [8, 1024, 768], P('rows', 'seq')
- grad_w_qkv: float32 [2, 768, 2304], P(None, 'seq')
- grad_w_o: float32 [2, 768, 768], P(None, 'seq')
- grad_w_fc: float32 [2, 768, 3072], P(None, 'seq')
- grad_w_proj: float32 [2, 3072, 768], P(None, 'seq')
- grad_norm_gain: float32 [2, 2, 768], P(None, None, 'seq')
- grad_norm_bias: float32 [2, 2, 768], P(None, None, 'seq')
- grad_qv_bias: float32 [2, 2, 768], P(None, None, 'seq')
- grad_out_bias: float32 [2, 2, 768], P(None, None, 'seq')
- grad_fc_bias: float32 [2, 3072], P(None, 'seq')
The draws below stay inside these ranges and needn't reach their ends.
Inputs may be any that keep to these rules, and one draw needn't show every extreme that they name: `doc_ids`: along each row the ids start at 0 and rise by 0 or 1 from one token to the next; in every row one document has tokens in the first quarter and in the last quarter of the row; in one row every token outside that document is a document of its own.
All inputs are finite; a program needn't handle non-finite values.
Results may differ from the reference program's by a relative error of at most 0.015.
Values may be sent and summed in bfloat16 or wider, within the bound.
No kernel may reach another device: no remote copies, remote signals or barrier semaphores. Data moves between devices by JAX's collectives and lax.ppermute only.
A program may use at most 320 MiB of HBM per device.

```python
import jax
import jax.numpy as jnp
from jax import lax

D = 768
H = 12
HD = 64
FF = 3072
LAYERS = 2
LEN = 1024
BATCH = 8


def draw_doc_ids(key, part):
    key = jax.random.fold_in(key, 11)
    key_start, key_end, key_breaks, key_pick = jax.random.split(key, 4)
    positions = jnp.arange(LEN, dtype=jnp.int32)[None, :]
    picked = jax.random.randint(key_pick, (), 0, BATCH)
    special = (jnp.arange(BATCH, dtype=jnp.int32) == picked)[:, None]
    doc_start = jax.random.randint(key_start, (BATCH, 1), 0, LEN // 4)
    doc_end = jax.random.randint(key_end, (BATCH, 1), 3 * (LEN // 4) + 1, LEN + 1)
    doc_start = jnp.where(special, LEN // 4 - 1, doc_start)
    doc_end = jnp.where(special, 3 * (LEN // 4) + 1, doc_end)
    rough = (jax.random.randint(key_breaks, (BATCH, LEN), 0, max(8, LEN // 16)) == 0) | special
    inside = (positions > doc_start) & (positions < doc_end)
    breaks = jnp.where(inside, False, rough) | (positions == doc_start) | (positions == doc_end)
    breaks = breaks & (positions > 0)
    return jnp.cumsum(breaks.astype(jnp.int32), axis=1).astype(jnp.int32)


def block_scale(own_key, shape, cuts, low, high):
    def one(position, parts):
        steps = jax.random.uniform(jax.random.fold_in(jax.random.fold_in(own_key, 6), position), (parts,), jnp.float32, low / len(cuts), high / len(cuts))
        return jnp.repeat(jnp.exp(steps), shape[position] // parts).reshape((-1,) + (1,) * (len(shape) - position - 1))

    gain = one(*cuts[0])
    for cut in cuts[1:]:
        gain = gain * one(*cut)
    return gain


def noise(key, extent, deviation, bound, cuts=(), kind=jnp.bfloat16):
    array = jax.random.normal(key, extent, jnp.float32) * deviation
    if len(cuts) > 0:
        array = block_scale(key, extent, cuts, -0.22, 0.18) * array
    return jnp.clip(array, min=-bound, max=bound).astype(kind)


def setup_inputs(seed: int = 0) -> dict:
    streams_of = jax.random.split(jax.random.key(seed), 13)
    block_input = noise(streams_of[0], (BATCH, LEN, D), 1.0, 6.0, ((0, 8), (1, 4)))
    output_cotangent = noise(streams_of[1], (BATCH, LEN, D), 1.0, 6.0, ((0, 8), (1, 4)))
    doc_ids = draw_doc_ids(jax.random.fold_in(streams_of[12], 71), 0)
    w_qkv = noise(streams_of[3], (LAYERS, D, 3 * D), D ** -0.5, 0.21875, ((1, 4),))
    w_o = noise(streams_of[4], (LAYERS, D, D), (D // 16) ** -0.5, 0.875, ((1, 4),))
    w_fc = noise(streams_of[5], (LAYERS, D, FF), D ** -0.5, 0.21875, ((1, 4),))
    w_proj = noise(streams_of[6], (LAYERS, FF, D), (FF // 4) ** -0.5, 0.21875, ((1, 4),))
    norm_gain = jnp.clip(1.0 + 0.1 * jax.random.normal(streams_of[7], (LAYERS, 2, D), jnp.float32), 0.5, 1.5).astype(jnp.bfloat16)
    norm_bias = noise(streams_of[8], (LAYERS, 2, D), 0.3, 4.0, ((2, 4),))
    qv_bias = noise(streams_of[9], (LAYERS, 2, D), 0.3, 4.0, ((2, 4),))
    out_bias = noise(streams_of[10], (LAYERS, 2, D), 0.5, 6.0, ((2, 4),))
    fc_bias = noise(streams_of[11], (LAYERS, FF), 0.3, 4.0, ((1, 4),))
    return {"block_input": block_input, "output_cotangent": output_cotangent, "doc_ids": doc_ids, "w_qkv": w_qkv, "w_o": w_o, "w_fc": w_fc, "w_proj": w_proj, "norm_gain": norm_gain, "norm_bias": norm_bias, "qv_bias": qv_bias, "out_bias": out_bias, "fc_bias": fc_bias}


@jax.custom_vjp
def low(v):
    return lax.optimization_barrier(v.astype(jnp.bfloat16)).astype(jnp.float32)

@jax.custom_vjp
def low_back(v):
    return v

def low_keep(v):
    return (low(v), None)

def low_pass(kept, grad):
    return (grad,)

def back_keep(v):
    return (v, None)

def back_low(kept, grad):
    return (low(grad),)
low.defvjp(low_keep, low_pass)
low_back.defvjp(back_keep, back_low)
branch_scale = 48.0 ** (-0.5)
norm_eps = 1e-05
masked_score = -1e+30

def dense(left, right):
    return jnp.dot(left, right, precision=lax.Precision.HIGHEST)

def layer_norm(values, norm_scale, norm_shift):
    centre = values - lax.optimization_barrier(jnp.mean(values, axis=-1, keepdims=True))
    spread = lax.optimization_barrier(jnp.mean(centre * centre, axis=-1, keepdims=True))
    return centre * lax.rsqrt(spread + norm_eps) * norm_scale + norm_shift

def attention_row(head_rows, doc_row):
    length = head_rows.shape[0]
    block_rows = min(512, length)
    queries = head_rows[:, 0]
    key_rows = head_rows[:, 1]
    value_rows = head_rows[:, 2]
    score_scale = HD ** (-0.5)

    def one_block(block_index):
        first_row = (block_index * block_rows).astype(jnp.int32)
        block_q = lax.dynamic_slice_in_dim(queries, first_row, block_rows)
        scores = jnp.einsum('qhd,khd->hqk', block_q, key_rows, precision=lax.Precision.HIGHEST) * score_scale
        scores = low_back(scores)
        key_pos = lax.broadcasted_iota(jnp.int32, (block_rows, length), 1)
        query_pos = first_row + lax.broadcasted_iota(jnp.int32, (block_rows, length), 0)
        query_doc = lax.dynamic_slice_in_dim(doc_row, first_row, block_rows)
        allowed = (key_pos <= query_pos) & (doc_row[None, :] == query_doc[:, None])
        scores = jnp.where(allowed[None], scores, masked_score)
        row_max = lax.optimization_barrier(jnp.max(scores, axis=-1, keepdims=True))
        weights = jnp.exp(scores - row_max)
        attn_probs = weights / lax.optimization_barrier(jnp.sum(weights, axis=-1, keepdims=True))
        return jnp.einsum('hqk,khd->qhd', low(attn_probs), value_rows, precision=lax.Precision.HIGHEST)
    blocks = lax.map(jax.checkpoint(one_block), jnp.arange(length // block_rows, dtype=jnp.int32))
    return blocks.reshape(length, H, HD)

def row_forward(stream, doc_row, params):
    w_qkv, w_o, w_fc, w_proj, norm_gain, norm_bias, qv_bias, out_bias, fc_bias = params
    length, model_width = stream.shape
    for layer_index in range(LAYERS):
        ln_a = low(layer_norm(stream, norm_gain[layer_index, 0], norm_bias[layer_index, 0]))
        qkv_bias = jnp.concatenate([qv_bias[layer_index, 0], jnp.zeros_like(qv_bias[layer_index, 0]), qv_bias[layer_index, 1]])
        qkv_rows = low_back(low(dense(ln_a, w_qkv[layer_index]) + qkv_bias))
        mixed_heads = attention_row(qkv_rows.reshape(length, 3, H, HD), doc_row)
        attended = low_back(low(mixed_heads.reshape(length, model_width)))
        branch_out = low_back(dense(attended, w_o[layer_index]) + out_bias[layer_index, 0])
        mid_stream = stream + branch_scale * branch_out
        ln_c = low(layer_norm(mid_stream, norm_gain[layer_index, 1], norm_bias[layer_index, 1]))
        pre_act = low_back(dense(ln_c, w_fc[layer_index]) + fc_bias[layer_index])
        act_low = low(jax.nn.gelu(pre_act, approximate=True))
        mlp_out = low_back(dense(act_low, w_proj[layer_index]) + out_bias[layer_index, 1])
        stream = mid_stream + branch_scale * mlp_out
    return stream

def reference(block_input, output_cotangent, doc_ids, w_qkv, w_o, w_fc, w_proj, norm_gain, norm_bias, qv_bias, out_bias, fc_bias):
    params = (w_qkv.astype(jnp.float32), w_o.astype(jnp.float32), w_fc.astype(jnp.float32), w_proj.astype(jnp.float32), norm_gain.astype(jnp.float32), norm_bias.astype(jnp.float32), qv_bias.astype(jnp.float32), out_bias.astype(jnp.float32), fc_bias.astype(jnp.float32))

    def whole(stream_all, weights):

        def one_row(pair):
            return row_forward(pair[0], pair[1], weights)
        return lax.map(jax.checkpoint(one_row), (stream_all, doc_ids))
    outputs, pullback = jax.vjp(whole, block_input.astype(jnp.float32), params)
    grad_input, grads = pullback(output_cotangent.astype(jnp.float32))
    return (outputs, grad_input, grads[0], grads[1], grads[2], grads[3], grads[4], grads[5], grads[6], grads[7], grads[8])
```

```python
import functools
import math

import jax
import jax.numpy as jnp
from jax import lax
from jax.experimental import pallas as pl
from jax.experimental.pallas import tpu as pltpu
from jax.sharding import PartitionSpec as P

HD = 64
branch_scale = 48.0 ** (-0.5)
norm_eps = 1e-05
masked_score = -1e30
log2_e = math.log2(math.e)
MIB = 1 << 20
BLK = 256

f32 = jnp.float32
bf16 = jnp.bfloat16

SWAP_CORE = [(s, s ^ 1) for s in range(4)]
SWAP_X = [(s, s ^ 2) for s in range(4)]
SWAP_BOTH = [(s, s ^ 3) for s in range(4)]


def dot_nn(a, b):
    return lax.dot_general(a, b, (((1,), (0,)), ((), ())), preferred_element_type=f32)


def dot_nt(a, b):
    return lax.dot_general(a, b, (((1,), (1,)), ((), ())), preferred_element_type=f32)


def dot_tn(a, b):
    return lax.dot_general(a, b, (((0,), (0,)), ((), ())), preferred_element_type=f32)


def call(body, name, sidx, grid, ins, outs, scratch, flops, vmem, exps=0):
    arrays = [a for a, _, _ in ins]
    in_specs = [
        pl.BlockSpec(memory_space=pl.ANY) if b is None else pl.BlockSpec(b, m) for _, b, m in ins
    ]
    out_specs = [pl.BlockSpec(b, m) for _, b, m in outs]
    out_shape = [s for s, _, _ in outs]
    nbytes = sum(a.size * a.dtype.itemsize for a in arrays)
    nbytes += sum(math.prod(s.shape) * s.dtype.itemsize for s in out_shape)
    return pl.pallas_call(
        body,
        name=name,
        grid_spec=pltpu.PrefetchScalarGridSpec(
            num_scalar_prefetch=1,
            grid=grid,
            in_specs=in_specs,
            out_specs=out_specs,
            scratch_shapes=scratch,
        ),
        out_shape=out_shape,
        compiler_params=pltpu.CompilerParams(
            dimension_semantics=("arbitrary",) * len(grid), vmem_limit_bytes=vmem * MIB
        ),
        cost_estimate=pl.CostEstimate(
            flops=int(flops), bytes_accessed=int(nbytes), transcendentals=int(exps)
        ),
    )(sidx, *arrays)


def sds(shape, dtype):
    return jax.ShapeDtypeStruct(shape, dtype)


def whole(block):
    zeros = (0,) * len(block)
    return lambda i, m: zeros


def row_tile(i, m):
    return (i, 0)


def stack_tile(i, m):
    return (i ^ m[0], 0, 0)


def piece_copies(refs, dst, sems, first, rows):
    out = []
    for j, ref in enumerate(refs):
        where = pl.multiple_of((first ^ j) * rows, 16)
        out.append(pltpu.make_async_copy(ref, dst.at[pl.ds(where, rows)], sems.at[j]))
    return out


def normed(x):
    centre = x - jnp.mean(x, axis=-1, keepdims=True)
    spread = jnp.mean(centre * centre, axis=-1, keepdims=True)
    rstd = lax.rsqrt(spread + norm_eps)
    return centre * rstd, rstd


def norm_back(x, grad, gain):
    unit, rstd = normed(x)
    inner = grad * gain
    mean_inner = jnp.mean(inner, axis=-1, keepdims=True)
    mean_prod = jnp.mean(inner * unit, axis=-1, keepdims=True)
    return rstd * (inner - mean_inner - unit * mean_prod), unit


GAIN_A, GAIN_C, SHIFT_A, SHIFT_C, OUT_A, OUT_M = range(6)


def row_of(ref, k):
    return ref[k : k + 1, :]


def qkv_body(first, m, *refs):
    if first:
        x_ref, vec, bias, w0, w1, w2, w3, ln_ref, qkv_ref, w, sems = refs
    else:
        mid_ref, p_ref, r_ref, prev, vec, bias, w0, w1, w2, w3, x_out, ln_ref, qkv_ref, w, sems = refs
    rows = w0.shape[0]
    copies = piece_copies((w0, w1, w2, w3), w, sems, m[0], rows)

    @pl.when(pl.program_id(0) == 0)
    def _():
        for cp in copies:
            cp.start()

    if first:
        x = x_ref[0].astype(f32)
    else:
        part = p_ref[...].astype(f32) + r_ref[...].astype(f32) + row_of(prev, OUT_M)
        x = mid_ref[...] + branch_scale * part
        x_out[...] = x
    unit, _ = normed(x)
    ln = (unit * row_of(vec, GAIN_A) + row_of(vec, SHIFT_A)).astype(bf16)
    ln_ref[...] = ln

    @pl.when(pl.program_id(0) == 0)
    def _():
        for cp in copies:
            cp.wait()

    qkv_ref[...] = (dot_nn(ln, w[...]) + bias[...]).astype(bf16)


def qkv_forward(sidx, source, vec, prev_vec, bias, pieces):
    rows, cols = pieces[0].shape
    depth = 4 * rows
    first = len(source) == 1
    tokens = source[0].shape[0] * source[0].shape[1] if first else source[0].shape[0]
    ins = []
    outs = []
    if first:
        ins.append((source[0], (1, BLK, depth), stack_tile))
    else:
        for a in source:
            ins.append((a, (BLK, depth), row_tile))
        ins.append((prev_vec, prev_vec.shape, whole(prev_vec.shape)))
        outs.append((sds((tokens, depth), f32), (BLK, depth), row_tile))
    ins.append((vec, vec.shape, whole(vec.shape)))
    ins.append((bias, bias.shape, whole(bias.shape)))
    ins += [(p, None, None) for p in pieces]
    outs.append((sds((tokens, depth), bf16), (BLK, depth), row_tile))
    outs.append((sds((tokens, cols), bf16), (BLK, cols), row_tile))
    return call(
        functools.partial(qkv_body, first),
        "norm_qkv",
        sidx,
        (tokens // BLK,),
        ins,
        outs,
        [pltpu.VMEM((depth, cols), bf16), pltpu.SemaphoreType.DMA((4,))],
        2 * tokens * depth * cols,
        24,
    )


def lane_half(shape):
    return lax.broadcasted_iota(jnp.int32, shape, 1) // HD


def block_start(i):
    return BLK * (i * (i + 1) // 2)


def attn_body(m, q_ref, k_ref, v_ref, drow, dcol, wo0, wo1, att_ref, lse_ref, part_ref, bias, wo, held, sems):
    pair = pl.program_id(0)
    tokens = q_ref.shape[0]
    blocks = tokens // BLK
    rows = wo0.shape[0]
    copies = piece_copies((wo0, wo1), wo, sems, m[1], rows)

    @pl.when(pair == 0)
    def _():
        for cp in copies:
            cp.start()
        for i in range(blocks):
            width = BLK * (i + 1)
            first = i * BLK
            qpos = first + lax.broadcasted_iota(jnp.int32, (BLK, width), 0)
            kpos = lax.broadcasted_iota(jnp.int32, (BLK, width), 1)
            same = dcol[first : first + BLK, :] == drow[:, :width]
            allowed = (kpos <= qpos) & same
            bias[:, block_start(i) : block_start(i) + width] = jnp.where(allowed, 0.0, masked_score)

    half = lane_half((BLK, 2 * HD))
    scale = HD ** (-0.5) * log2_e
    for i in range(blocks):
        width = BLK * (i + 1)
        span = slice(i * BLK, (i + 1) * BLK)
        qb = q_ref[span, :]
        kk = k_ref[:width, :]
        vv = v_ref[:width, :]
        mixed = []
        logs = []
        for h in range(2):
            qh = jnp.where(half == h, qb, jnp.zeros_like(qb))
            t = dot_nt(qh, kk) * scale + bias[:, block_start(i) : block_start(i) + width]
            top = jnp.max(t, axis=-1, keepdims=True)
            p = jnp.exp2(t - top)
            total = jnp.sum(p, axis=-1, keepdims=True)
            o = dot_nn(p.astype(bf16), vv)
            mixed.append(o / total)
            logs.append(jnp.broadcast_to(top + jnp.log2(total), (BLK, 2 * HD)))
        att = jnp.where(half == 0, mixed[0], mixed[1]).astype(bf16)
        att_ref[span, :] = att
        held[pair, span, :] = att
        turned = jnp.transpose(jnp.where(half == 0, logs[0], logs[1]))
        lse_ref[0, 0:1, span] = turned[0:1, :]
        lse_ref[0, 1:2, span] = turned[HD : HD + 1, :]

    @pl.when(pair == pl.num_programs(0) - 1)
    def _():
        for cp in copies:
            cp.wait()
        for i in range(blocks):
            span = slice(i * BLK, (i + 1) * BLK)
            row = jnp.concatenate([held[p, span, :] for p in range(held.shape[0])], axis=1)
            part_ref[span, :] = dot_nn(row, wo[...]).astype(bf16)


def attention_forward(sidx, qkv, drow, dcol, wo_pieces):
    tokens = qkv.shape[0]
    width = qkv.shape[1] // 3
    pairs = width // (2 * HD)
    depth = wo_pieces[0].shape[1]
    col = lambda k: (lambda i, m: (0, k * pairs + i))
    pair_block = (tokens, 2 * HD)
    ins = [(qkv, pair_block, col(0)), (qkv, pair_block, col(1)), (qkv, pair_block, col(2))]
    ins += [(drow, drow.shape, whole(drow.shape)), (dcol, dcol.shape, whole(dcol.shape))]
    ins += [(p, None, None) for p in wo_pieces]
    outs = [
        (sds((tokens, width), bf16), pair_block, lambda i, m: (0, i)),
        (sds((pairs, 8, tokens), f32), (1, 8, tokens), lambda i, m: (i, 0, 0)),
        (sds((tokens, depth), bf16), (tokens, depth), whole((0, 0))),
    ]
    blocks = tokens // BLK
    scratch = [
        pltpu.VMEM((BLK, block_start(blocks)), f32),
        pltpu.VMEM((width, depth), bf16),
        pltpu.VMEM((pairs, tokens, 2 * HD), bf16),
        pltpu.SemaphoreType.DMA((2,)),
    ]
    return call(
        attn_body,
        "attention_forward",
        sidx,
        (pairs,),
        ins,
        outs,
        scratch,
        4 * tokens * tokens * width,
        40,
        exps=tokens * tokens * pairs,
    )


def mlp_body(first, m, x_ref, p_ref, r_ref, vec, fcb, f0, f1, f2, f3, j0, j1, mid_ref, ln_ref, act_ref, slope_ref, part_ref, wf, wp, sems):
    copies = piece_copies((f0, f1, f2, f3), wf, sems, m[0], f0.shape[0])
    copies2 = piece_copies((j0, j1), wp, sems.at[pl.ds(4, 2)], m[1], j0.shape[0])

    @pl.when(pl.program_id(0) == 0)
    def _():
        for cp in copies + copies2:
            cp.start()

    x = x_ref[0].astype(f32) if first else x_ref[...]
    part = p_ref[...].astype(f32) + r_ref[...].astype(f32) + row_of(vec, OUT_A)
    mid = x + branch_scale * part
    mid_ref[...] = mid
    unit, _ = normed(mid)
    ln = (unit * row_of(vec, GAIN_C) + row_of(vec, SHIFT_C)).astype(bf16)
    ln_ref[...] = ln

    @pl.when(pl.program_id(0) == 0)
    def _():
        for cp in copies:
            cp.wait()

    pre = dot_nn(ln, wf[...]) + fcb[...]
    root = math.sqrt(2.0 / math.pi)
    sq = pre * pre
    th = jnp.tanh(root * pre * (1.0 + 0.044715 * sq))
    gate = 0.5 * (1.0 + th)
    act = (pre * gate).astype(bf16)
    act_ref[...] = act
    inner = root * (1.0 + 3.0 * 0.044715 * sq)
    slope_ref[...] = (gate + 0.5 * pre * (1.0 - th * th) * inner).astype(bf16)

    @pl.when(pl.program_id(0) == 0)
    def _():
        for cp in copies2:
            cp.wait()

    part_ref[...] = dot_nn(act, wp[...]).astype(bf16)


def mlp_forward(sidx, x, part, recv, vec, fcb, fc_pieces, proj_pieces):
    first = x.ndim == 3
    tokens, depth = part.shape
    hidden = fc_pieces[0].shape[1]
    ins = [(x, (1, BLK, depth), stack_tile) if first else (x, (BLK, depth), row_tile)]
    ins += [(part, (BLK, depth), row_tile), (recv, (BLK, depth), row_tile)]
    ins += [(vec, vec.shape, whole(vec.shape)), (fcb, fcb.shape, whole(fcb.shape))]
    ins += [(p, None, None) for p in fc_pieces + proj_pieces]
    outs = [
        (sds((tokens, depth), f32), (BLK, depth), row_tile),
        (sds((tokens, depth), bf16), (BLK, depth), row_tile),
        (sds((tokens, hidden), bf16), (BLK, hidden), row_tile),
        (sds((tokens, hidden), bf16), (BLK, hidden), row_tile),
        (sds((tokens, depth), bf16), (BLK, depth), row_tile),
    ]
    scratch = [
        pltpu.VMEM((depth, hidden), bf16),
        pltpu.VMEM((hidden, depth), bf16),
        pltpu.SemaphoreType.DMA((6,)),
    ]
    return call(
        functools.partial(mlp_body, first),
        "mlp_forward",
        sidx,
        (tokens // BLK,),
        ins,
        outs,
        scratch,
        4 * tokens * depth * hidden,
        32,
        exps=tokens * hidden,
    )


def add_rows(ref, value, start):
    @pl.when(start)
    def _():
        ref[...] = jnp.zeros_like(ref)

    ref[...] += jnp.sum(value, axis=0, keepdims=True)


def mlp_back_body(last, m, *refs):
    if last:
        g_ref, slope_ref, f0, f1, f2, f3, j0, j1 = refs[:8]
        dmlp_ref, dpre_ref, part_ref, sum_mlp, sum_pre, wf, wp, sems = refs[8:]
    else:
        gm_ref, x_ref, p_ref, r_ref, nvec, slope_ref, f0, f1, f2, f3, j0, j1 = refs[:12]
        g_out, dmlp_ref, dpre_ref, part_ref, sum_mlp, sum_pre, sum_gain, sum_shift, wf, wp, sems = refs[12:]
    start = pl.program_id(0) == 0
    copies = piece_copies((f0, f1, f2, f3), wf, sems, m[0], f0.shape[0])
    copies2 = piece_copies((j0, j1), wp, sems.at[pl.ds(4, 2)], m[1], j0.shape[0])

    @pl.when(start)
    def _():
        for cp in copies2 + copies:
            cp.start()

    if last:
        g = g_ref[0].astype(f32)
    else:
        grad = p_ref[...].astype(f32) + r_ref[...].astype(f32)
        part, unit = norm_back(x_ref[...], grad, row_of(nvec, GAIN_A))
        add_rows(sum_gain, grad * unit, start)
        add_rows(sum_shift, grad, start)
        g = gm_ref[...] + part
        g_out[...] = g
    dmlp = (branch_scale * g).astype(bf16)
    dmlp_ref[...] = dmlp
    add_rows(sum_mlp, dmlp.astype(f32), start)

    @pl.when(start)
    def _():
        for cp in copies2:
            cp.wait()

    dact = dot_nt(dmlp, wp[...])
    dpre = (dact * slope_ref[...].astype(f32)).astype(bf16)
    dpre_ref[...] = dpre
    add_rows(sum_pre, dpre.astype(f32), start)

    @pl.when(start)
    def _():
        for cp in copies:
            cp.wait()

    part_ref[...] = dot_nt(dpre, wf[...]).astype(bf16)


def mlp_backward(sidx, source, slope, fc_pieces, proj_pieces):
    last = len(source) == 1
    tokens, hidden = slope.shape
    depth = proj_pieces[0].shape[1]
    tile = (BLK, depth)
    ins = []
    outs = []
    if last:
        ins.append((source[0], (1, BLK, depth), stack_tile))
    else:
        gm, x, part, recv, vec = source
        ins += [(a, tile, row_tile) for a in (gm, x, part, recv)]
        ins.append((vec, vec.shape, whole(vec.shape)))
        outs.append((sds((tokens, depth), f32), tile, row_tile))
    ins.append((slope, (BLK, hidden), row_tile))
    ins += [(p, None, None) for p in fc_pieces + proj_pieces]
    outs += [
        (sds((tokens, depth), bf16), tile, row_tile),
        (sds((tokens, hidden), bf16), (BLK, hidden), row_tile),
        (sds((tokens, depth), bf16), tile, row_tile),
        (sds((1, depth), f32), (1, depth), whole((0, 0))),
        (sds((1, hidden), f32), (1, hidden), whole((0, 0))),
    ]
    if not last:
        outs += [(sds((1, depth), f32), (1, depth), whole((0, 0)))] * 2
    scratch = [
        pltpu.VMEM((depth, hidden), bf16),
        pltpu.VMEM((hidden, depth), bf16),
        pltpu.SemaphoreType.DMA((6,)),
    ]
    return call(
        functools.partial(mlp_back_body, last),
        "mlp_backward",
        sidx,
        (tokens // BLK,),
        ins,
        outs,
        scratch,
        4 * tokens * depth * hidden,
        32,
    )


def out_back_body(last, m, g_ref, mid_ref, p_ref, r_ref, vec, wo0, wo1, gm_ref, dattn_ref, datt_ref, sum_attn, sum_gain, sum_shift, wo, sems):
    start = pl.program_id(0) == 0
    copies = piece_copies((wo0, wo1), wo, sems, m[1], wo0.shape[0])

    @pl.when(start)
    def _():
        for cp in copies:
            cp.start()

    g = g_ref[0].astype(f32) if last else g_ref[...]
    grad = p_ref[...].astype(f32) + r_ref[...].astype(f32)
    part, unit = norm_back(mid_ref[...], grad, row_of(vec, GAIN_C))
    add_rows(sum_gain, grad * unit, start)
    add_rows(sum_shift, grad, start)
    gm = g + part
    gm_ref[...] = gm
    dattn = (branch_scale * gm).astype(bf16)
    dattn_ref[...] = dattn
    add_rows(sum_attn, dattn.astype(f32), start)

    @pl.when(start)
    def _():
        for cp in copies:
            cp.wait()

    datt_ref[...] = dot_nt(dattn, wo[...]).astype(bf16)


def out_backward(sidx, g, mid, part, recv, vec, wo_pieces):
    last = g.ndim == 3
    tokens, depth = part.shape
    width = 2 * wo_pieces[0].shape[0]
    tile = (BLK, depth)
    ins = [(g, (1, BLK, depth), stack_tile) if last else (g, tile, row_tile)]
    ins += [(a, tile, row_tile) for a in (mid, part, recv)]
    ins.append((vec, vec.shape, whole(vec.shape)))
    ins += [(p, None, None) for p in wo_pieces]
    outs = [
        (sds((tokens, depth), f32), tile, row_tile),
        (sds((tokens, depth), bf16), tile, row_tile),
        (sds((tokens, width), bf16), (BLK, width), row_tile),
    ]
    outs += [(sds((1, depth), f32), (1, depth), whole((0, 0)))] * 3
    return call(
        functools.partial(out_back_body, last),
        "out_backward",
        sidx,
        (tokens // BLK,),
        ins,
        outs,
        [pltpu.VMEM((width, depth), bf16), pltpu.SemaphoreType.DMA((2,))],
        2 * tokens * depth * width,
        24,
    )


def attn_back_body(m, q_ref, k_ref, v_ref, do_ref, att_ref, lse_ref, drow, dcol, w0, w1, w2, w3, dqkv_ref, part_ref, sum_ref, bias, w, held, dq_acc, sems):
    pair = pl.program_id(0)
    pairs = pl.num_programs(0)
    tokens = q_ref.shape[0]
    blocks = tokens // BLK
    copies = piece_copies((w0, w1, w2, w3), w, sems, m[0], w0.shape[0])
    starts = [sum(tokens - BLK * a for a in range(j)) for j in range(blocks)]

    @pl.when(pair == 0)
    def _():
        for cp in copies:
            cp.start()
        for j in range(blocks):
            width = tokens - j * BLK
            first = j * BLK
            kpos = lax.broadcasted_iota(jnp.int32, (BLK, width), 0)
            qpos = lax.broadcasted_iota(jnp.int32, (BLK, width), 1)
            same = dcol[first : first + BLK, :] == drow[:, first:]
            allowed = (kpos <= qpos) & same
            bias[:, starts[j] : starts[j] + width] = jnp.where(allowed, 0.0, masked_score)

    half = lane_half((BLK, 2 * HD))
    score_scale = HD ** (-0.5)
    scale = score_scale * log2_e
    pick_row = lax.broadcasted_iota(jnp.int32, (8, 2 * HD), 0)
    pick = jnp.where(lane_half((8, 2 * HD)) == pick_row, 1.0, 0.0)
    prod = do_ref[...].astype(f32) * att_ref[...].astype(f32)
    delta = lax.dot_general(
        pick, prod, (((1,), (1,)), ((), ())), precision=lax.Precision.HIGHEST, preferred_element_type=f32
    )
    for j in range(blocks):
        first = j * BLK
        span = slice(first, first + BLK)
        kj = k_ref[span, :]
        vj = v_ref[span, :]
        qq = q_ref[first:, :]
        dd = do_ref[first:, :]
        width = tokens - first
        zero = jnp.zeros_like(kj)
        dks = []
        dvs = []
        dss = []
        khs = []
        for h in range(2):
            kh = jnp.where(half == h, kj, zero)
            vh = jnp.where(half == h, vj, zero)
            t = dot_nt(kh, qq) * scale + bias[:, starts[j] : starts[j] + width]
            p = jnp.exp2(t - lse_ref[0, h : h + 1, first:])
            dp = dot_nt(vh, dd)
            ds = (p * (dp - delta[h : h + 1, first:])).astype(bf16)
            dvs.append(dot_nn(p.astype(bf16), dd))
            dks.append(dot_nn(ds, qq))
            dss.append(ds)
            khs.append(kh)
        dk = jnp.where(half == 0, dks[0], dks[1]) * score_scale
        dv = jnp.where(half == 0, dvs[0], dvs[1])
        held[pair + pairs, span, :] = dk.astype(bf16)
        held[pair + 2 * pairs, span, :] = dv.astype(bf16)
        dq = dot_tn(jnp.concatenate(dss, axis=0), jnp.concatenate(khs, axis=0))
        if j == 0:
            dq_acc[...] = dq
        else:
            dq_acc[first:, :] += dq
    held[pair] = (dq_acc[...] * score_scale).astype(bf16)

    @pl.when(pair == pairs - 1)
    def _():
        for cp in copies:
            cp.wait()
        total = None
        for i in range(blocks):
            span = slice(i * BLK, (i + 1) * BLK)
            row = jnp.concatenate([held[p, span, :] for p in range(held.shape[0])], axis=1)
            dqkv_ref[span, :] = row
            part_ref[span, :] = dot_nt(row, w[...]).astype(bf16)
            here = jnp.sum(row.astype(f32), axis=0, keepdims=True)
            total = here if total is None else total + here
        sum_ref[...] = total


def attention_backward(sidx, qkv, datt, att, lse, drow, dcol, pieces):
    tokens, cols = qkv.shape
    width = cols // 3
    pairs = width // (2 * HD)
    rows = pieces[0].shape[0]
    depth = 4 * rows
    col = lambda k: (lambda i, m: (0, k * pairs + i))
    pair_block = (tokens, 2 * HD)
    ins = [(qkv, pair_block, col(0)), (qkv, pair_block, col(1)), (qkv, pair_block, col(2))]
    ins += [(datt, pair_block, col(0)), (att, pair_block, col(0))]
    ins += [(lse, (1, 8, tokens), lambda i, m: (i, 0, 0))]
    ins += [(drow, drow.shape, whole(drow.shape)), (dcol, dcol.shape, whole(dcol.shape))]
    ins += [(p, None, None) for p in pieces]
    outs = [
        (sds((tokens, cols), bf16), (tokens, cols), whole((0, 0))),
        (sds((tokens, depth), bf16), (tokens, depth), whole((0, 0))),
        (sds((1, cols), f32), (1, cols), whole((0, 0))),
    ]
    blocks = tokens // BLK
    scratch = [
        pltpu.VMEM((BLK, block_start(blocks)), f32),
        pltpu.VMEM((depth, cols), bf16),
        pltpu.VMEM((3 * pairs, tokens, 2 * HD), bf16),
        pltpu.VMEM((tokens, 2 * HD), f32),
        pltpu.SemaphoreType.DMA((4,)),
    ]
    return call(
        attn_back_body,
        "attention_backward",
        sidx,
        (pairs,),
        ins,
        outs,
        scratch,
        10 * tokens * tokens * width,
        48,
        exps=tokens * tokens * pairs,
    )


def weight_grad_body(parts, m, a_ref, b_ref, *refs):
    outs, turned = refs[:-1], refs[-1]

    @pl.when(pl.program_id(0) == 0)
    def _():
        turned[...] = jnp.transpose(a_ref[...])

    for out, (pick, rows) in zip(outs, parts):
        if rows == turned.shape[0]:
            left = turned[...]
        else:
            left = turned[pl.ds(pl.multiple_of(pick(m) * rows, 16), rows), :]
        out[...] = dot_nn(left, b_ref[...]).astype(bf16)


def weight_grad(name, sidx, a, a_width, a_pick, b, parts, tile):
    tokens, cols = b.shape
    ins = [(a, (tokens, a_width), lambda i, m: (0, a_pick(m))), (b, (tokens, tile), lambda i, m: (0, i))]
    outs = [(sds((rows, cols), bf16), (rows, tile), lambda i, m: (0, i)) for _, rows in parts]
    return call(
        functools.partial(weight_grad_body, parts),
        name,
        sidx,
        (cols // tile,),
        ins,
        outs,
        [pltpu.VMEM((a_width, tokens), bf16)],
        2 * tokens * cols * sum(rows for _, rows in parts),
        24,
    )


def input_back_body(m, gm_ref, x_ref, p_ref, r_ref, vec, out_ref, sum_gain, sum_shift):
    tile = pl.program_id(0)
    grad = p_ref[...].astype(f32) + r_ref[...].astype(f32)
    part, unit = norm_back(x_ref[0].astype(f32), grad, row_of(vec, GAIN_A))
    add_rows(sum_gain, grad * unit, tile == 0)
    add_rows(sum_shift, grad, tile == 0)

    @pl.when(tile == m[0])
    def _():
        out_ref[...] = gm_ref[...] + part


def input_backward(sidx, gm, x, part, recv, vec):
    tokens, depth = gm.shape
    tile = (BLK, depth)
    ins = [(gm, tile, row_tile), (x, (1, BLK, depth), stack_tile)]
    ins += [(a, tile, row_tile) for a in (part, recv)]
    ins.append((vec, vec.shape, whole(vec.shape)))
    outs = [(sds((BLK, depth), f32), tile, whole((0, 0)))]
    outs += [(sds((1, depth), f32), (1, depth), whole((0, 0)))] * 2
    return call(input_back_body, "input_backward", sidx, (tokens // BLK,), ins, outs, [], tokens * depth, 16)


def swap(a, perm):
    return lax.ppermute(a, "seq", perm)


def core_columns(w, parts, core):
    rows, cols = w.shape
    cut = w.reshape(rows, parts, 2, 2, cols // (4 * parts))
    one = cut[:, :, :, 0].reshape(rows, cols // 2)
    two = cut[:, :, :, 1].reshape(rows, cols // 2)
    return jnp.where(core == 0, one, two), jnp.where(core == 0, two, one)


def column_pieces(w, parts, core):
    keep, send = core_columns(w, parts, core)
    return [keep, swap(send, SWAP_CORE), swap(keep, SWAP_X), swap(send, SWAP_BOTH)]


def row_pieces(w):
    return [w, swap(w, SWAP_X)]


def gather_rows(a):
    near = swap(a, SWAP_CORE)
    far = swap(a, SWAP_X)
    return jnp.stack([a, near, far, swap(far, SWAP_CORE)])


def interleave(keep, recv, core):
    rows, cols = keep.shape
    q = cols // 2
    keep = keep.reshape(rows, 2, 1, q)
    recv = recv.reshape(rows, 2, 1, q)
    both = jnp.where(
        core == 0, jnp.concatenate([keep, recv], axis=2), jnp.concatenate([recv, keep], axis=2)
    )
    return both.reshape(rows, 2 * cols)


def interleave3(keep, recv, core):
    rows, cols = keep.shape
    q = cols // 6
    keep = keep.reshape(rows, 3, 2, 1, q)
    recv = recv.reshape(rows, 3, 2, 1, q)
    both = jnp.where(
        core == 0, jnp.concatenate([keep, recv], axis=3), jnp.concatenate([recv, keep], axis=3)
    )
    return both.reshape(rows, 2 * cols)


def vectors(norm_gain, norm_bias, qv_bias, out_bias, fc_bias, s, core):
    layers, _, q = norm_gain.shape
    mine = jnp.concatenate(
        [norm_gain, norm_bias, qv_bias, out_bias, fc_bias.reshape(layers, -1, q)], axis=1
    )
    got = jnp.stack([mine, swap(mine, SWAP_CORE), swap(mine, SWAP_X), swap(mine, SWAP_BOTH)])
    full = jnp.stack([lax.dynamic_index_in_dim(got, j ^ s, 0, keepdims=False) for j in range(4)])
    full = full.astype(f32)
    wide = jnp.concatenate([full[:, :, 0:4], full[:, :, 6:8]], axis=2)
    wide = wide.transpose(1, 2, 0, 3).reshape(layers, 6, 4 * q)
    wide = jnp.pad(wide, ((0, 0), (0, 2), (0, 0)))
    here = lax.dynamic_index_in_dim(full.reshape(2, 2, layers, -1, q), core, 1, keepdims=False)
    qv = here[:, :, 4:6].transpose(1, 2, 0, 3).reshape(layers, 2, 2 * q)
    qkv_bias = jnp.concatenate([qv[:, 0], jnp.zeros_like(qv[:, 0]), qv[:, 1]], axis=1)
    fcb = here[:, :, 8:].transpose(1, 0, 2, 3).reshape(layers, -1)
    return wide, qkv_bias, fcb


def on_device(
    block_input,
    output_cotangent,
    doc_ids,
    w_qkv,
    w_o,
    w_fc,
    w_proj,
    norm_gain,
    norm_bias,
    qv_bias,
    out_bias,
    fc_bias,
):
    s = lax.axis_index("seq").astype(jnp.int32)
    xi, core = s // 2, s % 2
    sidx = jnp.stack([s, xi, core])
    layers = w_qkv.shape[0]
    quarter = w_qkv.shape[1]
    tokens = doc_ids.shape[1]
    drow = doc_ids
    dcol = doc_ids.reshape(tokens, 1)
    xs = gather_rows(block_input[0])
    wide, qkv_bias, fcb = vectors(norm_gain, norm_bias, qv_bias, out_bias, fc_bias, s, core)
    wq, wo, wf, wp = [], [], [], []
    for l in range(layers):
        wq.append(column_pieces(w_qkv[l], 3, core))
        wo.append(row_pieces(w_o[l]))
        wf.append(column_pieces(w_fc[l], 1, core))
        wp.append(row_pieces(w_proj[l]))
    cot = gather_rows(output_cotangent[0])

    saved = []
    source = (xs,)
    for l in range(layers):
        vec = wide[l]
        outs = qkv_forward(
            sidx, source, vec, wide[l - 1] if l else None, qkv_bias[l : l + 1], wq[l]
        )
        x = xs if l == 0 else outs[0]
        ln_a, qkv = outs[-2:]
        att, lse, part = attention_forward(sidx, qkv, drow, dcol, wo[l])
        recv = swap(part, SWAP_CORE)
        mid, ln_c, act, slope, part = mlp_forward(
            sidx, x, part, recv, vec, fcb[l : l + 1], wf[l], wp[l]
        )
        recv = swap(part, SWAP_CORE)
        source = (mid, part, recv)
        saved.append((x, ln_a, qkv, att, lse, mid, ln_c, act, slope))
    mid, part, recv = source
    first = s * block_input.shape[1]
    own = lambda a: lax.dynamic_slice_in_dim(a, first, block_input.shape[1])
    result = own(mid) + branch_scale * (
        own(part).astype(f32) + own(recv).astype(f32) + wide[layers - 1][OUT_M]
    )

    quarter_of = lambda a: lax.dynamic_slice_in_dim(a[0], s * quarter, quarter)
    x_pick = lambda m: m[1]
    zero_pick = lambda m: 0
    core_pick = lambda m: m[2]
    other_pick = lambda m: 1 - m[2]
    grads = [None] * layers
    norm_a = [None] * layers
    back = (cot,)
    g = cot
    for l in reversed(range(layers)):
        x, ln_a, qkv, att, lse, mid, ln_c, act, slope = saved[l]
        outs = mlp_backward(sidx, back, slope, wf[l], wp[l])
        if len(back) > 1:
            g, dmlp, dpre, part, sum_mlp, sum_pre, gain_a, shift_a = outs
            norm_a[l + 1] = (gain_a, shift_a)
        else:
            dmlp, dpre, part, sum_mlp, sum_pre = outs
        recv = swap(part, SWAP_CORE)
        (g_proj,) = weight_grad(
            "grad_proj", sidx, act, act.shape[1] // 2, x_pick, dmlp, [(zero_pick, act.shape[1] // 2)], 256
        )
        fc_keep, fc_send = weight_grad(
            "grad_fc", sidx, ln_c, 2 * quarter, x_pick, dpre, [(core_pick, quarter), (other_pick, quarter)], 512
        )
        fc_recv = swap(fc_send, SWAP_CORE)
        gm, dattn, datt, sum_attn, gain_c, shift_c = out_backward(
            sidx, g, mid, part, recv, wide[l], wo[l]
        )
        dqkv, part, sum_qkv = attention_backward(sidx, qkv, datt, att, lse, drow, dcol, wq[l])
        recv = swap(part, SWAP_CORE)
        (g_o,) = weight_grad("grad_o", sidx, att, att.shape[1], zero_pick, dattn, [(x_pick, quarter)], 256)
        q_keep, q_send = weight_grad(
            "grad_qkv", sidx, ln_a, 2 * quarter, x_pick, dqkv, [(core_pick, quarter), (other_pick, quarter)], 384
        )
        q_recv = swap(q_send, SWAP_CORE)
        back = (gm, x, part, recv, wide[l])
        own_q = lambda a, at: lax.dynamic_slice_in_dim(a[0], at + xi * quarter, quarter)
        hidden_q = sum_pre.shape[1] // 2
        grads[l] = [
            [g_proj, fc_keep, fc_recv, g_o, q_keep, q_recv],
            [
                own_q(sum_qkv, 0),
                own_q(sum_qkv, 4 * quarter),
                quarter_of(sum_attn),
                quarter_of(sum_mlp),
                lax.dynamic_slice_in_dim(sum_pre[0], xi * hidden_q, hidden_q),
                quarter_of(gain_c),
                quarter_of(shift_c),
            ],
        ]
    gm, x, part, recv, vec = back
    grad_input, gain_a, shift_a = input_backward(sidx, gm, x, part, recv, vec)
    norm_a[0] = (gain_a, shift_a)

    big = []
    small = []
    for l in reversed(range(layers)):
        summed = lax.psum(tuple(grads[l][0]), "rows")
        big.append(summed)
    big = big[::-1]
    for l in range(layers):
        qb, vb, ob, mb, fb, gain_c, shift_c = grads[l][1]
        small.append(
            jnp.concatenate(
                [quarter_of(norm_a[l][0]), gain_c, quarter_of(norm_a[l][1]), shift_c, qb, vb, ob, mb, fb]
            )
        )
    small = lax.psum(jnp.stack(small), "rows")
    out_proj = jnp.stack([big[l][0] for l in range(layers)]).astype(f32)
    out_fc = jnp.stack([interleave(big[l][1], big[l][2], core) for l in range(layers)]).astype(f32)
    out_o = jnp.stack([big[l][3] for l in range(layers)]).astype(f32)
    out_qkv = jnp.stack([interleave3(big[l][4], big[l][5], core) for l in range(layers)]).astype(f32)
    pair = lambda k: small[:, k * quarter : (k + 2) * quarter].reshape(layers, 2, quarter)
    return (
        result[None],
        grad_input[None],
        out_qkv,
        out_o,
        out_fc,
        out_proj,
        pair(0),
        pair(2),
        pair(4),
        pair(6),
        small[:, 8 * quarter :],
    )


def solution(mesh):
    in_specs = (
        P("rows", "seq", None),
        P("rows", "seq", None),
        P("rows", None),
        P(None, "seq", None),
        P(None, "seq", None),
        P(None, "seq", None),
        P(None, "seq", None),
        P(None, None, "seq"),
        P(None, None, "seq"),
        P(None, None, "seq"),
        P(None, None, "seq"),
        P(None, "seq"),
    )
    out_specs = (
        P("rows", "seq", None),
        P("rows", "seq", None),
        P(None, "seq", None),
        P(None, "seq", None),
        P(None, "seq", None),
        P(None, "seq", None),
        P(None, None, "seq"),
        P(None, None, "seq"),
        P(None, None, "seq"),
        P(None, None, "seq"),
        P(None, "seq"),
    )
    return jax.shard_map(
        on_device, mesh=mesh, in_specs=in_specs, out_specs=out_specs, check_vma=False
    )
```

```python
import functools
import math

import jax
import jax.numpy as jnp
from jax import lax
from jax.experimental import pallas as pl
from jax.experimental.pallas import tpu as pltpu
from jax.sharding import PartitionSpec as P

HD = 64
branch_scale = 48.0 ** (-0.5)
norm_eps = 1e-05
masked_score = -1e30
log2_e = math.log2(math.e)
MIB = 1 << 20
BLK = 256

f32 = jnp.float32
bf16 = jnp.bfloat16

SWAP_CORE = [(s, s ^ 1) for s in range(4)]
SWAP_X = [(s, s ^ 2) for s in range(4)]
SWAP_BOTH = [(s, s ^ 3) for s in range(4)]


def dot_nn(a, b):
    return lax.dot_general(a, b, (((1,), (0,)), ((), ())), preferred_element_type=f32)


def dot_nt(a, b):
    return lax.dot_general(a, b, (((1,), (1,)), ((), ())), preferred_element_type=f32)


def dot_tn(a, b):
    return lax.dot_general(a, b, (((0,), (0,)), ((), ())), preferred_element_type=f32)


def call(body, name, sidx, grid, ins, outs, scratch, flops, vmem, exps=0):
    arrays = [a for a, _, _ in ins]
    in_specs = [
        pl.BlockSpec(memory_space=pl.ANY) if b is None else pl.BlockSpec(b, m) for _, b, m in ins
    ]
    out_specs = [pl.BlockSpec(b, m) for _, b, m in outs]
    out_shape = [s for s, _, _ in outs]
    nbytes = sum(a.size * a.dtype.itemsize for a in arrays)
    nbytes += sum(math.prod(s.shape) * s.dtype.itemsize for s in out_shape)
    return pl.pallas_call(
        body,
        name=name,
        grid_spec=pltpu.PrefetchScalarGridSpec(
            num_scalar_prefetch=1,
            grid=grid,
            in_specs=in_specs,
            out_specs=out_specs,
            scratch_shapes=scratch,
        ),
        out_shape=out_shape,
        compiler_params=pltpu.CompilerParams(
            dimension_semantics=("arbitrary",) * len(grid), vmem_limit_bytes=vmem * MIB
        ),
        cost_estimate=pl.CostEstimate(
            flops=int(flops), bytes_accessed=int(nbytes), transcendentals=int(exps)
        ),
    )(sidx, *arrays)


RING = [0, 2, 4, 6, 7, 5, 3, 1]
RING_NEXT = [(RING[i], RING[(i + 1) % 8]) for i in range(8)]
RING_PREV = [(b, a) for a, b in RING_NEXT]
RING_AT = [RING.index(r) for r in range(8)]
RING_STEPS = [0, -1, 1, -2, 2, -3, 3, -4]


def ring_place():
    return jnp.asarray(RING_AT, jnp.int32)[lax.axis_index("rows")]


def ring_index(s, xi, core):
    place = ring_place() if lax.axis_size("rows") == 8 else jnp.int32(0)
    return jnp.stack([s, xi, core, place])


def sds(shape, dtype):
    return jax.ShapeDtypeStruct(shape, dtype)


def whole(block):
    zeros = (0,) * len(block)
    return lambda i, m: zeros


def row_tile(i, m):
    return (i, 0)


def stack_tile(i, m):
    return (i ^ m[0], 0, 0)


def piece_copies(refs, dst, sems, first, rows):
    out = []
    for j, ref in enumerate(refs):
        where = pl.multiple_of((first ^ j) * rows, 16)
        out.append(pltpu.make_async_copy(ref, dst.at[pl.ds(where, rows)], sems.at[j]))
    return out


def mlp_copies(refs, wf, wp, sems, m):
    if len(refs) == 6:
        return (
            piece_copies(refs[:4], wf, sems, m[0], refs[0].shape[0]),
            piece_copies(refs[4:], wp, sems.at[pl.ds(4, 2)], m[1], refs[4].shape[0]),
        )
    keep, near, own = refs[:3]
    far = refs[3:]
    rows = keep.shape[0]
    deep, wide = own.shape
    first = piece_copies((keep, near), wf, sems, m[0], rows)
    second = piece_copies((own,), wp, sems.at[pl.ds(2, 1)], m[1], deep)
    n = len(far)
    part = far[0].shape[0] // 2
    k = 3
    for ref, t in zip(far, RING_STEPS):
        chunk = (m[3] + t + n) % n
        at = pl.multiple_of((1 - m[1]) * 2 * rows + chunk * part, 16)
        first.append(pltpu.make_async_copy(ref.at[pl.ds(0, part)], wf.at[pl.ds(at, part)], sems.at[k]))
        k += 1
        for side in range(2):
            at = pl.multiple_of((1 - m[1]) * deep + side * (deep // 2) + chunk * part, 16)
            src = ref.at[pl.ds(part, part), pl.ds(side * wide, wide)]
            second.append(pltpu.make_async_copy(src, wp.at[pl.ds(at, part)], sems.at[k]))
            k += 1
    return first, second


def normed(x):
    centre = x - jnp.mean(x, axis=-1, keepdims=True)
    spread = jnp.mean(centre * centre, axis=-1, keepdims=True)
    rstd = lax.rsqrt(spread + norm_eps)
    return centre * rstd, rstd


def norm_back(x, grad, gain):
    unit, rstd = normed(x)
    inner = grad * gain
    mean_inner = jnp.mean(inner, axis=-1, keepdims=True)
    mean_prod = jnp.mean(inner * unit, axis=-1, keepdims=True)
    return rstd * (inner - mean_inner - unit * mean_prod), unit


GAIN_A, GAIN_C, SHIFT_A, SHIFT_C, OUT_A, OUT_M = range(6)


def row_of(ref, k):
    return ref[k : k + 1, :]


def qkv_body(first, m, *refs):
    if first:
        x_ref, vec, bias, w0, w1, w2, w3, ln_ref, qkv_ref, w, sems = refs
    else:
        mid_ref, p_ref, r_ref, prev, vec, bias, w0, w1, w2, w3, x_out, ln_ref, qkv_ref, w, sems = refs
    rows = w0.shape[0]
    copies = piece_copies((w0, w1, w2, w3), w, sems, m[0], rows)

    @pl.when(pl.program_id(0) == 0)
    def _():
        for cp in copies:
            cp.start()

    if first:
        x = x_ref[0].astype(f32)
    else:
        part = p_ref[...].astype(f32) + r_ref[...].astype(f32) + row_of(prev, OUT_M)
        x = mid_ref[...] + branch_scale * part
        x_out[...] = x
    unit, _ = normed(x)
    ln = (unit * row_of(vec, GAIN_A) + row_of(vec, SHIFT_A)).astype(bf16)
    ln_ref[...] = ln

    @pl.when(pl.program_id(0) == 0)
    def _():
        for cp in copies:
            cp.wait()

    qkv_ref[...] = (dot_nn(ln, w[...]) + bias[...]).astype(bf16)


def qkv_forward(sidx, source, vec, prev_vec, bias, pieces):
    rows, cols = pieces[0].shape
    depth = 4 * rows
    first = len(source) == 1
    tokens = source[0].shape[0] * source[0].shape[1] if first else source[0].shape[0]
    ins = []
    outs = []
    if first:
        ins.append((source[0], (1, BLK, depth), stack_tile))
    else:
        for a in source:
            ins.append((a, (BLK, depth), row_tile))
        ins.append((prev_vec, prev_vec.shape, whole(prev_vec.shape)))
        outs.append((sds((tokens, depth), f32), (BLK, depth), row_tile))
    ins.append((vec, vec.shape, whole(vec.shape)))
    ins.append((bias, bias.shape, whole(bias.shape)))
    ins += [(p, None, None) for p in pieces]
    outs.append((sds((tokens, depth), bf16), (BLK, depth), row_tile))
    outs.append((sds((tokens, cols), bf16), (BLK, cols), row_tile))
    return call(
        functools.partial(qkv_body, first),
        "norm_qkv",
        sidx,
        (tokens // BLK,),
        ins,
        outs,
        [pltpu.VMEM((depth, cols), bf16), pltpu.SemaphoreType.DMA((4,))],
        2 * tokens * depth * cols,
        24,
    )


def lane_half(shape):
    return lax.broadcasted_iota(jnp.int32, shape, 1) // HD


def block_start(i):
    return BLK * (i * (i + 1) // 2)


def attn_body(m, q_ref, k_ref, v_ref, drow, dcol, wo0, wo1, att_ref, lse_ref, part_ref, bias, wo, held, sems):
    pair = pl.program_id(0)
    tokens = q_ref.shape[0]
    blocks = tokens // BLK
    rows = wo0.shape[0]
    copies = piece_copies((wo0, wo1), wo, sems, m[1], rows)

    @pl.when(pair == 0)
    def _():
        for cp in copies:
            cp.start()
        for i in range(blocks):
            width = BLK * (i + 1)
            first = i * BLK
            qpos = first + lax.broadcasted_iota(jnp.int32, (BLK, width), 0)
            kpos = lax.broadcasted_iota(jnp.int32, (BLK, width), 1)
            same = dcol[first : first + BLK, :] == drow[:, :width]
            allowed = (kpos <= qpos) & same
            bias[:, block_start(i) : block_start(i) + width] = jnp.where(allowed, 0.0, masked_score)

    half = lane_half((BLK, 2 * HD))
    scale = HD ** (-0.5) * log2_e
    for i in range(blocks):
        width = BLK * (i + 1)
        span = slice(i * BLK, (i + 1) * BLK)
        qb = q_ref[span, :]
        kk = k_ref[:width, :]
        vv = v_ref[:width, :]
        mixed = []
        logs = []
        for h in range(2):
            qh = jnp.where(half == h, qb, jnp.zeros_like(qb))
            t = dot_nt(qh, kk) * scale + bias[:, block_start(i) : block_start(i) + width]
            top = jnp.max(t, axis=-1, keepdims=True)
            p = jnp.exp2(t - top)
            total = jnp.sum(p, axis=-1, keepdims=True)
            o = dot_nn(p.astype(bf16), vv)
            mixed.append(o / total)
            logs.append(jnp.broadcast_to(top + jnp.log2(total), (BLK, 2 * HD)))
        att = jnp.where(half == 0, mixed[0], mixed[1]).astype(bf16)
        att_ref[span, :] = att
        held[pair, span, :] = att
        turned = jnp.transpose(jnp.where(half == 0, logs[0], logs[1]))
        lse_ref[0, 0:1, span] = turned[0:1, :]
        lse_ref[0, 1:2, span] = turned[HD : HD + 1, :]

    @pl.when(pair == pl.num_programs(0) - 1)
    def _():
        for cp in copies:
            cp.wait()
        for i in range(blocks):
            span = slice(i * BLK, (i + 1) * BLK)
            row = jnp.concatenate([held[p, span, :] for p in range(held.shape[0])], axis=1)
            part_ref[span, :] = dot_nn(row, wo[...]).astype(bf16)


def attention_forward(sidx, qkv, drow, dcol, wo_pieces):
    tokens = qkv.shape[0]
    width = qkv.shape[1] // 3
    pairs = width // (2 * HD)
    depth = wo_pieces[0].shape[1]
    col = lambda k: (lambda i, m: (0, k * pairs + i))
    pair_block = (tokens, 2 * HD)
    ins = [(qkv, pair_block, col(0)), (qkv, pair_block, col(1)), (qkv, pair_block, col(2))]
    ins += [(drow, drow.shape, whole(drow.shape)), (dcol, dcol.shape, whole(dcol.shape))]
    ins += [(p, None, None) for p in wo_pieces]
    outs = [
        (sds((tokens, width), bf16), pair_block, lambda i, m: (0, i)),
        (sds((pairs, 8, tokens), f32), (1, 8, tokens), lambda i, m: (i, 0, 0)),
        (sds((tokens, depth), bf16), (tokens, depth), whole((0, 0))),
    ]
    blocks = tokens // BLK
    scratch = [
        pltpu.VMEM((BLK, block_start(blocks)), f32),
        pltpu.VMEM((width, depth), bf16),
        pltpu.VMEM((pairs, tokens, 2 * HD), bf16),
        pltpu.SemaphoreType.DMA((2,)),
    ]
    return call(
        attn_body,
        "attention_forward",
        sidx,
        (pairs,),
        ins,
        outs,
        scratch,
        4 * tokens * tokens * width,
        40,
        exps=tokens * tokens * pairs,
    )


def mlp_body(first, m, x_ref, p_ref, r_ref, vec, fcb, *refs):
    mid_ref, ln_ref, act_ref, slope_ref, part_ref, wf, wp, sems = refs[-8:]
    copies, copies2 = mlp_copies(refs[:-8], wf, wp, sems, m)

    @pl.when(pl.program_id(0) == 0)
    def _():
        for cp in copies + copies2:
            cp.start()

    x = x_ref[0].astype(f32) if first else x_ref[...]
    part = p_ref[...].astype(f32) + r_ref[...].astype(f32) + row_of(vec, OUT_A)
    mid = x + branch_scale * part
    mid_ref[...] = mid
    unit, _ = normed(mid)
    ln = (unit * row_of(vec, GAIN_C) + row_of(vec, SHIFT_C)).astype(bf16)
    ln_ref[...] = ln

    @pl.when(pl.program_id(0) == 0)
    def _():
        for cp in copies:
            cp.wait()

    pre = dot_nn(ln, wf[...]) + fcb[...]
    root = math.sqrt(2.0 / math.pi)
    sq = pre * pre
    th = jnp.tanh(root * pre * (1.0 + 0.044715 * sq))
    gate = 0.5 * (1.0 + th)
    act = (pre * gate).astype(bf16)
    act_ref[...] = act
    inner = root * (1.0 + 3.0 * 0.044715 * sq)
    slope_ref[...] = (gate + 0.5 * pre * (1.0 - th * th) * inner).astype(bf16)

    @pl.when(pl.program_id(0) == 0)
    def _():
        for cp in copies2:
            cp.wait()

    part_ref[...] = dot_nn(act, wp[...]).astype(bf16)


def mlp_forward(sidx, x, part, recv, vec, fcb, pieces):
    first = x.ndim == 3
    tokens, depth = part.shape
    hidden = fcb.shape[1]
    ins = [(x, (1, BLK, depth), stack_tile) if first else (x, (BLK, depth), row_tile)]
    ins += [(part, (BLK, depth), row_tile), (recv, (BLK, depth), row_tile)]
    ins += [(vec, vec.shape, whole(vec.shape)), (fcb, fcb.shape, whole(fcb.shape))]
    ins += [(p, None, None) for p in pieces]
    outs = [
        (sds((tokens, depth), f32), (BLK, depth), row_tile),
        (sds((tokens, depth), bf16), (BLK, depth), row_tile),
        (sds((tokens, hidden), bf16), (BLK, hidden), row_tile),
        (sds((tokens, hidden), bf16), (BLK, hidden), row_tile),
        (sds((tokens, depth), bf16), (BLK, depth), row_tile),
    ]
    scratch = [
        pltpu.VMEM((depth, hidden), bf16),
        pltpu.VMEM((hidden, depth), bf16),
        pltpu.SemaphoreType.DMA((32,)),
    ]
    return call(
        functools.partial(mlp_body, first),
        "mlp_forward",
        sidx,
        (tokens // BLK,),
        ins,
        outs,
        scratch,
        4 * tokens * depth * hidden,
        32,
        exps=tokens * hidden,
    )


def add_rows(ref, value, start):
    @pl.when(start)
    def _():
        ref[...] = jnp.zeros_like(ref)

    ref[...] += jnp.sum(value, axis=0, keepdims=True)


def mlp_back_body(last, m, *refs):
    if last:
        g_ref, slope_ref = refs[:2]
        dmlp_ref, dpre_ref, part_ref, sum_mlp, sum_pre, wf, wp, sems = refs[-8:]
        weights = refs[2:-8]
    else:
        gm_ref, x_ref, p_ref, r_ref, nvec, slope_ref = refs[:6]
        g_out, dmlp_ref, dpre_ref, part_ref, sum_mlp, sum_pre, sum_gain, sum_shift, wf, wp, sems = refs[-11:]
        weights = refs[6:-11]
    start = pl.program_id(0) == 0
    copies, copies2 = mlp_copies(weights, wf, wp, sems, m)

    @pl.when(start)
    def _():
        for cp in copies2 + copies:
            cp.start()

    if last:
        g = g_ref[0].astype(f32)
    else:
        grad = p_ref[...].astype(f32) + r_ref[...].astype(f32)
        part, unit = norm_back(x_ref[...], grad, row_of(nvec, GAIN_A))
        add_rows(sum_gain, grad * unit, start)
        add_rows(sum_shift, grad, start)
        g = gm_ref[...] + part
        g_out[...] = g
    dmlp = (branch_scale * g).astype(bf16)
    dmlp_ref[...] = dmlp
    add_rows(sum_mlp, dmlp.astype(f32), start)

    @pl.when(start)
    def _():
        for cp in copies2:
            cp.wait()

    dact = dot_nt(dmlp, wp[...])
    dpre = (dact * slope_ref[...].astype(f32)).astype(bf16)
    dpre_ref[...] = dpre
    add_rows(sum_pre, dpre.astype(f32), start)

    @pl.when(start)
    def _():
        for cp in copies:
            cp.wait()

    part_ref[...] = dot_nt(dpre, wf[...]).astype(bf16)


def mlp_backward(sidx, source, slope, pieces):
    last = len(source) == 1
    tokens, hidden = slope.shape
    depth = source[0].shape[-1]
    tile = (BLK, depth)
    ins = []
    outs = []
    if last:
        ins.append((source[0], (1, BLK, depth), stack_tile))
    else:
        gm, x, part, recv, vec = source
        ins += [(a, tile, row_tile) for a in (gm, x, part, recv)]
        ins.append((vec, vec.shape, whole(vec.shape)))
        outs.append((sds((tokens, depth), f32), tile, row_tile))
    ins.append((slope, (BLK, hidden), row_tile))
    ins += [(p, None, None) for p in pieces]
    outs += [
        (sds((tokens, depth), bf16), tile, row_tile),
        (sds((tokens, hidden), bf16), (BLK, hidden), row_tile),
        (sds((tokens, depth), bf16), tile, row_tile),
        (sds((1, depth), f32), (1, depth), whole((0, 0))),
        (sds((1, hidden), f32), (1, hidden), whole((0, 0))),
    ]
    if not last:
        outs += [(sds((1, depth), f32), (1, depth), whole((0, 0)))] * 2
    scratch = [
        pltpu.VMEM((depth, hidden), bf16),
        pltpu.VMEM((hidden, depth), bf16),
        pltpu.SemaphoreType.DMA((32,)),
    ]
    return call(
        functools.partial(mlp_back_body, last),
        "mlp_backward",
        sidx,
        (tokens // BLK,),
        ins,
        outs,
        scratch,
        4 * tokens * depth * hidden,
        32,
    )


def out_back_body(last, m, g_ref, mid_ref, p_ref, r_ref, vec, wo0, wo1, gm_ref, dattn_ref, datt_ref, sum_attn, sum_gain, sum_shift, wo, sems):
    start = pl.program_id(0) == 0
    copies = piece_copies((wo0, wo1), wo, sems, m[1], wo0.shape[0])

    @pl.when(start)
    def _():
        for cp in copies:
            cp.start()

    g = g_ref[0].astype(f32) if last else g_ref[...]
    grad = p_ref[...].astype(f32) + r_ref[...].astype(f32)
    part, unit = norm_back(mid_ref[...], grad, row_of(vec, GAIN_C))
    add_rows(sum_gain, grad * unit, start)
    add_rows(sum_shift, grad, start)
    gm = g + part
    gm_ref[...] = gm
    dattn = (branch_scale * gm).astype(bf16)
    dattn_ref[...] = dattn
    add_rows(sum_attn, dattn.astype(f32), start)

    @pl.when(start)
    def _():
        for cp in copies:
            cp.wait()

    datt_ref[...] = dot_nt(dattn, wo[...]).astype(bf16)


def out_backward(sidx, g, mid, part, recv, vec, wo_pieces):
    last = g.ndim == 3
    tokens, depth = part.shape
    width = 2 * wo_pieces[0].shape[0]
    tile = (BLK, depth)
    ins = [(g, (1, BLK, depth), stack_tile) if last else (g, tile, row_tile)]
    ins += [(a, tile, row_tile) for a in (mid, part, recv)]
    ins.append((vec, vec.shape, whole(vec.shape)))
    ins += [(p, None, None) for p in wo_pieces]
    outs = [
        (sds((tokens, depth), f32), tile, row_tile),
        (sds((tokens, depth), bf16), tile, row_tile),
        (sds((tokens, width), bf16), (BLK, width), row_tile),
    ]
    outs += [(sds((1, depth), f32), (1, depth), whole((0, 0)))] * 3
    return call(
        functools.partial(out_back_body, last),
        "out_backward",
        sidx,
        (tokens // BLK,),
        ins,
        outs,
        [pltpu.VMEM((width, depth), bf16), pltpu.SemaphoreType.DMA((2,))],
        2 * tokens * depth * width,
        24,
    )


def attn_back_body(m, q_ref, k_ref, v_ref, do_ref, att_ref, lse_ref, drow, dcol, w0, w1, w2, w3, dqkv_ref, part_ref, sum_ref, bias, w, held, dq_acc, sems):
    pair = pl.program_id(0)
    pairs = pl.num_programs(0)
    tokens = q_ref.shape[0]
    blocks = tokens // BLK
    copies = piece_copies((w0, w1, w2, w3), w, sems, m[0], w0.shape[0])
    starts = [sum(tokens - BLK * a for a in range(j)) for j in range(blocks)]

    @pl.when(pair == 0)
    def _():
        for cp in copies:
            cp.start()
        for j in range(blocks):
            width = tokens - j * BLK
            first = j * BLK
            kpos = lax.broadcasted_iota(jnp.int32, (BLK, width), 0)
            qpos = lax.broadcasted_iota(jnp.int32, (BLK, width), 1)
            same = dcol[first : first + BLK, :] == drow[:, first:]
            allowed = (kpos <= qpos) & same
            bias[:, starts[j] : starts[j] + width] = jnp.where(allowed, 0.0, masked_score)

    half = lane_half((BLK, 2 * HD))
    score_scale = HD ** (-0.5)
    scale = score_scale * log2_e
    pick_row = lax.broadcasted_iota(jnp.int32, (8, 2 * HD), 0)
    pick = jnp.where(lane_half((8, 2 * HD)) == pick_row, 1.0, 0.0)
    prod = do_ref[...].astype(f32) * att_ref[...].astype(f32)
    delta = lax.dot_general(
        pick, prod, (((1,), (1,)), ((), ())), precision=lax.Precision.HIGHEST, preferred_element_type=f32
    )
    for j in range(blocks):
        first = j * BLK
        span = slice(first, first + BLK)
        kj = k_ref[span, :]
        vj = v_ref[span, :]
        qq = q_ref[first:, :]
        dd = do_ref[first:, :]
        width = tokens - first
        zero = jnp.zeros_like(kj)
        dks = []
        dvs = []
        dss = []
        khs = []
        for h in range(2):
            kh = jnp.where(half == h, kj, zero)
            vh = jnp.where(half == h, vj, zero)
            t = dot_nt(kh, qq) * scale + bias[:, starts[j] : starts[j] + width]
            p = jnp.exp2(t - lse_ref[0, h : h + 1, first:])
            dp = dot_nt(vh, dd)
            ds = (p * (dp - delta[h : h + 1, first:])).astype(bf16)
            dvs.append(dot_nn(p.astype(bf16), dd))
            dks.append(dot_nn(ds, qq))
            dss.append(ds)
            khs.append(kh)
        dk = jnp.where(half == 0, dks[0], dks[1]) * score_scale
        dv = jnp.where(half == 0, dvs[0], dvs[1])
        held[pair + pairs, span, :] = dk.astype(bf16)
        held[pair + 2 * pairs, span, :] = dv.astype(bf16)
        dq = dot_tn(jnp.concatenate(dss, axis=0), jnp.concatenate(khs, axis=0))
        if j == 0:
            dq_acc[...] = dq
        else:
            dq_acc[first:, :] += dq
    held[pair] = (dq_acc[...] * score_scale).astype(bf16)

    @pl.when(pair == pairs - 1)
    def _():
        for cp in copies:
            cp.wait()
        total = None
        for i in range(blocks):
            span = slice(i * BLK, (i + 1) * BLK)
            row = jnp.concatenate([held[p, span, :] for p in range(held.shape[0])], axis=1)
            dqkv_ref[span, :] = row
            part_ref[span, :] = dot_nt(row, w[...]).astype(bf16)
            here = jnp.sum(row.astype(f32), axis=0, keepdims=True)
            total = here if total is None else total + here
        sum_ref[...] = total


def attention_backward(sidx, qkv, datt, att, lse, drow, dcol, pieces):
    tokens, cols = qkv.shape
    width = cols // 3
    pairs = width // (2 * HD)
    rows = pieces[0].shape[0]
    depth = 4 * rows
    col = lambda k: (lambda i, m: (0, k * pairs + i))
    pair_block = (tokens, 2 * HD)
    ins = [(qkv, pair_block, col(0)), (qkv, pair_block, col(1)), (qkv, pair_block, col(2))]
    ins += [(datt, pair_block, col(0)), (att, pair_block, col(0))]
    ins += [(lse, (1, 8, tokens), lambda i, m: (i, 0, 0))]
    ins += [(drow, drow.shape, whole(drow.shape)), (dcol, dcol.shape, whole(dcol.shape))]
    ins += [(p, None, None) for p in pieces]
    outs = [
        (sds((tokens, cols), bf16), (tokens, cols), whole((0, 0))),
        (sds((tokens, depth), bf16), (tokens, depth), whole((0, 0))),
        (sds((1, cols), f32), (1, cols), whole((0, 0))),
    ]
    blocks = tokens // BLK
    scratch = [
        pltpu.VMEM((BLK, block_start(blocks)), f32),
        pltpu.VMEM((depth, cols), bf16),
        pltpu.VMEM((3 * pairs, tokens, 2 * HD), bf16),
        pltpu.VMEM((tokens, 2 * HD), f32),
        pltpu.SemaphoreType.DMA((4,)),
    ]
    return call(
        attn_back_body,
        "attention_backward",
        sidx,
        (pairs,),
        ins,
        outs,
        scratch,
        10 * tokens * tokens * width,
        48,
        exps=tokens * tokens * pairs,
    )


def weight_grad_body(parts, m, a_ref, b_ref, *refs):
    outs, turned = refs[:-1], refs[-1]

    @pl.when(pl.program_id(0) == 0)
    def _():
        turned[...] = jnp.transpose(a_ref[...])

    for out, (pick, rows) in zip(outs, parts):
        if rows == turned.shape[0]:
            left = turned[...]
        else:
            left = turned[pl.ds(pl.multiple_of(pick(m) * rows, 16), rows), :]
        out[...] = dot_nn(left, b_ref[...]).astype(bf16)


def weight_grad(name, sidx, a, a_width, a_pick, b, parts, tile):
    tokens, cols = b.shape
    ins = [(a, (tokens, a_width), lambda i, m: (0, a_pick(m))), (b, (tokens, tile), lambda i, m: (0, i))]
    outs = [(sds((rows, cols), bf16), (rows, tile), lambda i, m: (0, i)) for _, rows in parts]
    return call(
        functools.partial(weight_grad_body, parts),
        name,
        sidx,
        (cols // tile,),
        ins,
        outs,
        [pltpu.VMEM((a_width, tokens), bf16)],
        2 * tokens * cols * sum(rows for _, rows in parts),
        24,
    )


def input_back_body(m, gm_ref, x_ref, p_ref, r_ref, vec, out_ref, sum_gain, sum_shift):
    tile = pl.program_id(0)
    grad = p_ref[...].astype(f32) + r_ref[...].astype(f32)
    part, unit = norm_back(x_ref[0].astype(f32), grad, row_of(vec, GAIN_A))
    add_rows(sum_gain, grad * unit, tile == 0)
    add_rows(sum_shift, grad, tile == 0)

    @pl.when(tile == m[0])
    def _():
        out_ref[...] = gm_ref[...] + part


def input_backward(sidx, gm, x, part, recv, vec):
    tokens, depth = gm.shape
    tile = (BLK, depth)
    ins = [(gm, tile, row_tile), (x, (1, BLK, depth), stack_tile)]
    ins += [(a, tile, row_tile) for a in (part, recv)]
    ins.append((vec, vec.shape, whole(vec.shape)))
    outs = [(sds((BLK, depth), f32), tile, whole((0, 0)))]
    outs += [(sds((1, depth), f32), (1, depth), whole((0, 0)))] * 2
    return call(input_back_body, "input_backward", sidx, (tokens // BLK,), ins, outs, [], tokens * depth, 16)


def swap(a, perm):
    return lax.ppermute(a, "seq", perm)


def split_body(m, qkv_ref, fc_ref, qkv_keep, qkv_send, fc_keep, fc_send):
    core = m[2]
    q = qkv_ref.shape[1]
    pair = 2 * q
    for p in range(3):
        own, other = [], []
        for xside in range(2):
            col = (2 * p + xside) * pair
            both = qkv_ref[0, :, col : col + pair]
            own.append(jnp.where(core == 0, both[:, :q], both[:, q:]))
            other.append(jnp.where(core == 0, both[:, q:], both[:, :q]))
        qkv_keep[:, p * pair : (p + 1) * pair] = jnp.concatenate(own, axis=1)
        qkv_send[:, p * pair : (p + 1) * pair] = jnp.concatenate(other, axis=1)
    d = fc_ref.shape[2] // 4
    for xside in range(2):
        one = fc_ref[0, :, 2 * xside * d : (2 * xside + 1) * d]
        two = fc_ref[0, :, (2 * xside + 1) * d : (2 * xside + 2) * d]
        fc_keep[:, xside * d : (xside + 1) * d] = jnp.where(core == 0, one, two)
        fc_send[:, xside * d : (xside + 1) * d] = jnp.where(core == 0, two, one)


def split_columns(sidx, w_qkv, w_fc, l):
    _, rows, cols = w_qkv.shape
    hidden = w_fc.shape[2]
    at = lambda i, m: (l, 0, 0)
    ins = [(w_qkv, (1, rows, cols), at), (w_fc, (1, rows, hidden), at)]
    outs = []
    for width in (cols // 2, cols // 2, hidden // 2, hidden // 2):
        outs.append((sds((rows, width), bf16), (rows, width), whole((0, 0))))
    return call(split_body, "split_columns", sidx, (1,), ins, outs, [], rows * cols, 16)


def column_pieces(keep, send):
    return [keep, swap(send, SWAP_CORE), swap(keep, SWAP_X), swap(send, SWAP_BOTH)]


def row_pieces(w):
    return [w, swap(w, SWAP_X)]


def mlp_pieces(keep, send, w_proj, core):
    if lax.axis_size("rows") != 8:
        return column_pieces(keep, send) + row_pieces(w_proj), None
    n = 8
    near = swap(send, SWAP_CORE)
    place = ring_place()
    rows = keep.shape[0]
    part = 2 * rows // n
    deep = w_proj.shape[0] // 2
    at = (place % 4) * part
    cut = lambda a, first: lax.dynamic_slice_in_dim(a, first, part)
    top = jnp.where(place // 4 == core, cut(keep, at), cut(near, at))
    low = jnp.concatenate([cut(w_proj, place * part), cut(w_proj, deep + place * part)], axis=1)
    mine = swap(jnp.concatenate([top, low]), SWAP_X)
    return [keep, near, w_proj], [mine]


def ring_pass(held, t):
    if held is None:
        return []
    on = lax.ppermute(held[max(0, len(held) - 2)], "rows", RING_NEXT)
    if t == 4:
        new = [on]
    else:
        new = [on, lax.ppermute(held[-1], "rows", RING_PREV)]
    held += new
    return new


def gather_rows(a):
    near = swap(a, SWAP_CORE)
    far = swap(a, SWAP_X)
    return jnp.stack([a, near, far, swap(far, SWAP_CORE)])


def pack_mlp(g_proj, fc_keep, fc_recv):
    d = g_proj.shape[1]
    return jnp.concatenate(
        [g_proj, fc_keep[:, :d], fc_keep[:, d:], fc_recv[:, :d], fc_recv[:, d:]], axis=0
    )


def pack_attn(g_o, q_keep, q_recv):
    d = g_o.shape[1]
    h = d // 2
    both = jnp.concatenate([q_keep[:, d : d + h], q_recv[:, d : d + h]], axis=1)
    return jnp.concatenate([g_o, q_keep[:, :d], q_recv[:, :d], both], axis=0)


def ring_sum(packed):
    n = lax.axis_size("rows")
    if n != 8:
        return [lax.psum(packed, "rows")]
    place = ring_place()
    rows, cols = packed.shape
    step = rows // n
    part = step // 2
    half = cols // 2

    def chunk(k, way, side):
        first = jnp.mod(k, n) * step + way * part
        return lax.dynamic_slice(packed, (first, side * half), (part, half))

    rings = [(way, side) for side in range(2) for way in range(2)]
    perms = (RING_NEXT, RING_PREV)
    sign = (-1, 1)
    held = [chunk(place, way, side) for way, side in rings]
    for t in range(1, n):
        for i, (way, side) in enumerate(rings):
            got = lax.ppermute(held[i], "rows", perms[way])
            mine = chunk(place + sign[way] * t, way, side)
            held[i] = (got.astype(f32) + mine.astype(f32)).astype(bf16)
    pieces = [[h] for h in held]
    for t in range(1, n):
        for i, (way, side) in enumerate(rings):
            pieces[i].append(lax.ppermute(pieces[i][-1], "rows", perms[way]))
    return [p for ring in pieces for p in ring]


def double_sum(a):
    n = lax.axis_size("rows")
    if n & (n - 1):
        return lax.psum(a, "rows")
    step = 1
    while step < n:
        a = a + lax.ppermute(a, "rows", [(r, r ^ step) for r in range(n)])
        step *= 2
    return a


def write_mlp(full, first, core, q, out_fc, out_proj):
    d = 4 * q
    out_proj[0] = full[first : first + d, :].astype(f32)
    block = lambda i: full[first + d + i * q : first + d + (i + 1) * q, :].astype(f32)
    for xside in range(2):
        for c in range(2):
            col = (2 * xside + c) * d
            out_fc[0, :, col : col + d] = jnp.where(core == c, block(xside), block(2 + xside))


def write_attn(full, first, core, q, out_qkv, out_o, at):
    d = 4 * q
    h = d // 2
    block = lambda i: full[first + i * q : first + (i + 1) * q, :].astype(f32)
    out_o[at] = block(0)
    keep_qk, recv_qk, both_v = block(1), block(2), block(3)
    parts = [
        (keep_qk[:, :h], recv_qk[:, :h]),
        (keep_qk[:, h:], recv_qk[:, h:]),
        (both_v[:, :h], both_v[:, h:]),
    ]
    for p, (keep, recv) in enumerate(parts):
        for xside in range(2):
            a = keep[:, xside * q : (xside + 1) * q]
            b = recv[:, xside * q : (xside + 1) * q]
            col = p * d + xside * h
            out_qkv[at, :, col : col + h] = jnp.concatenate(
                [jnp.where(core == 0, a, b), jnp.where(core == 0, b, a)], axis=1
            )


def finish_mlp_body(q, m, proj, keep, recv, out_fc, out_proj):
    out_proj[0] = proj[...].astype(f32)
    d = 4 * q
    for xside in range(2):
        a = keep[:, xside * d : (xside + 1) * d].astype(f32)
        b = recv[:, xside * d : (xside + 1) * d].astype(f32)
        for c in range(2):
            col = (2 * xside + c) * d
            out_fc[0, :, col : col + d] = jnp.where(m[2] == c, a, b)


def finish_mlp(sidx, l, layers, sums, q):
    d = 4 * q
    size = sum(a.size for a in sums)
    shapes = [(q, 4 * d), (d, d)]
    return pl.pallas_call(
        functools.partial(finish_mlp_body, q),
        name="unpack_mlp",
        grid_spec=pltpu.PrefetchScalarGridSpec(
            num_scalar_prefetch=1,
            grid=(1,),
            in_specs=[pl.BlockSpec(a.shape, lambda i, m: (0, 0)) for a in sums],
            out_specs=[pl.BlockSpec((1,) + sh, lambda i, m: (l, 0, 0)) for sh in shapes],
        ),
        out_shape=[sds((layers,) + sh, f32) for sh in shapes],
        compiler_params=pltpu.CompilerParams(vmem_limit_bytes=48 * MIB),
        cost_estimate=pl.CostEstimate(flops=size, bytes_accessed=6 * size, transcendentals=0),
    )(sidx, *sums)


def finish_body(count, layers, q, m, *refs):
    pieces = refs[:count]
    out_fc, out_proj, out_qkv, out_o, full = refs[-5:]
    rows, d = full.shape
    if count == 1:
        full[...] = pieces[0][...].astype(f32)
    else:
        n = 8
        step = rows // n
        part = step // 2
        half = d // 2
        k = 0
        for side in range(2):
            for way in range(2):
                for t in range(n):
                    chunk = (m[3] + (1 - t if way == 0 else t - 1) + 2 * n) % n
                    first = pl.multiple_of(chunk * step + way * part, 8)
                    full[pl.ds(first, part), side * half : (side + 1) * half] = pieces[k][...].astype(f32)
                    k += 1
    write_mlp(full, 0, m[2], q, out_fc, out_proj)
    for l in range(layers):
        write_attn(full, 2 * d + l * d, m[2], q, out_qkv, out_o, l)


def finish(sidx, layers, pieces, before, q):
    count = len(pieces)
    d = 4 * q
    rows = 2 * d + layers * d
    shapes = [(1, q, 4 * d), (1, d, d), (layers, q, 3 * d), (layers, q, d)]
    in_specs = [pl.BlockSpec(p.shape, lambda i, m: (0, 0)) for p in pieces]
    in_specs += [pl.BlockSpec(memory_space=pl.ANY)] * len(before)
    aliases = {1 + count + k: k for k in range(len(before))}
    return pl.pallas_call(
        functools.partial(finish_body, count, layers, q),
        name="unpack_grads",
        grid_spec=pltpu.PrefetchScalarGridSpec(
            num_scalar_prefetch=1,
            grid=(1,),
            in_specs=in_specs,
            out_specs=[pl.BlockSpec(sh, lambda i, m: (0, 0, 0)) for sh in shapes],
            scratch_shapes=[pltpu.VMEM((rows, d), f32)],
        ),
        out_shape=[sds((layers,) + sh[1:], f32) for sh in shapes],
        input_output_aliases=aliases,
        compiler_params=pltpu.CompilerParams(vmem_limit_bytes=56 * MIB),
        cost_estimate=pl.CostEstimate(flops=rows * d, bytes_accessed=6 * rows * d, transcendentals=0),
    )(sidx, *pieces, *before)


def vectors(norm_gain, norm_bias, qv_bias, out_bias, fc_bias, s, core):
    layers, _, q = norm_gain.shape
    mine = jnp.concatenate(
        [norm_gain, norm_bias, qv_bias, out_bias, fc_bias.reshape(layers, -1, q)], axis=1
    )
    got = jnp.stack([mine, swap(mine, SWAP_CORE), swap(mine, SWAP_X), swap(mine, SWAP_BOTH)])
    full = jnp.stack([lax.dynamic_index_in_dim(got, j ^ s, 0, keepdims=False) for j in range(4)])
    full = full.astype(f32)
    wide = jnp.concatenate([full[:, :, 0:4], full[:, :, 6:8]], axis=2)
    wide = wide.transpose(1, 2, 0, 3).reshape(layers, 6, 4 * q)
    wide = jnp.pad(wide, ((0, 0), (0, 2), (0, 0)))
    here = lax.dynamic_index_in_dim(full.reshape(2, 2, layers, -1, q), core, 1, keepdims=False)
    qv = here[:, :, 4:6].transpose(1, 2, 0, 3).reshape(layers, 2, 2 * q)
    qkv_bias = jnp.concatenate([qv[:, 0], jnp.zeros_like(qv[:, 0]), qv[:, 1]], axis=1)
    fcb = here[:, :, 8:].transpose(1, 0, 2, 3).reshape(layers, -1)
    return wide, qkv_bias, fcb


def on_device(
    block_input,
    output_cotangent,
    doc_ids,
    w_qkv,
    w_o,
    w_fc,
    w_proj,
    norm_gain,
    norm_bias,
    qv_bias,
    out_bias,
    fc_bias,
):
    s = lax.axis_index("seq").astype(jnp.int32)
    xi, core = s // 2, s % 2
    sidx = ring_index(s, xi, core)
    layers = w_qkv.shape[0]
    quarter = w_qkv.shape[1]
    tokens = doc_ids.shape[1]
    drow = doc_ids
    dcol = doc_ids.reshape(tokens, 1)
    xs = gather_rows(block_input[0])
    wide, qkv_bias, fcb = vectors(norm_gain, norm_bias, qv_bias, out_bias, fc_bias, s, core)
    wq, wo, near, far = [], [], [], []
    for l in range(layers):
        keep, send, fc_keep, fc_send = split_columns(sidx, w_qkv, w_fc, l)
        fixed, moved = mlp_pieces(fc_keep, fc_send, w_proj[l], core)
        near.append(fixed)
        far.append(moved)
        wq.append(column_pieces(keep, send))
        wo.append(row_pieces(w_o[l]))
    cot = gather_rows(output_cotangent[0])

    def pin(outs, *groups):
        flat, tree = jax.tree.flatten((outs, groups))
        outs, groups = jax.tree.unflatten(tree, lax.optimization_barrier(flat))
        return (outs,) + tuple(groups)

    ring_pass(far[0], 1)
    ring_pass(far[0], 2)
    xs, far[0] = pin(xs, far[0])
    saved = []
    source = (xs,)
    for l in range(layers):
        vec = wide[l]
        more = l + 1 < layers
        outs = qkv_forward(
            sidx, source, vec, wide[l - 1] if l else None, qkv_bias[l : l + 1], wq[l]
        )
        ring_pass(far[l], 3)
        outs, far[l] = pin(outs, far[l])
        if more:
            outs, far[l + 1] = pin(outs, far[l + 1])
        else:
            outs, cot = pin(outs, cot)
        x = xs if l == 0 else outs[0]
        ln_a, qkv = outs[-2:]
        att, lse, part = attention_forward(sidx, qkv, drow, dcol, wo[l])
        ring_pass(far[l], 4)
        part, far[l] = pin(part, far[l])
        if more:
            ring_pass(far[l + 1], 1)
            part, far[l + 1], wq[l + 1][2] = pin(part, far[l + 1], wq[l + 1][2])
        recv = swap(part, SWAP_CORE)
        mid, ln_c, act, slope, part = mlp_forward(
            sidx, x, part, recv, vec, fcb[l : l + 1], near[l] + (far[l] or [])
        )
        if more:
            ring_pass(far[l + 1], 2)
            part, far[l + 1], wq[l + 1][3], wo[l + 1][1] = pin(
                part, far[l + 1], wq[l + 1][3], wo[l + 1][1]
            )
        recv = swap(part, SWAP_CORE)
        source = (mid, part, recv)
        saved.append((x, ln_a, qkv, att, lse, mid, ln_c, act, slope))
    wm = [a + (b or []) for a, b in zip(near, far)]
    mid, part, recv = source
    first = s * block_input.shape[1]
    own = lambda a: lax.dynamic_slice_in_dim(a, first, block_input.shape[1])
    result = own(mid) + branch_scale * (
        own(part).astype(f32) + own(recv).astype(f32) + wide[layers - 1][OUT_M]
    )

    quarter_of = lambda a: lax.dynamic_slice_in_dim(a[0], s * quarter, quarter)
    x_pick = lambda m: m[1]
    zero_pick = lambda m: 0
    core_pick = lambda m: m[2]
    other_pick = lambda m: 1 - m[2]
    grads = [None] * layers
    norm_a = [None] * layers
    back = (cot,)
    g = cot
    for l in reversed(range(layers)):
        x, ln_a, qkv, att, lse, mid, ln_c, act, slope = saved[l]
        outs = mlp_backward(sidx, back, slope, wm[l])
        if len(back) > 1:
            g, dmlp, dpre, part, sum_mlp, sum_pre, gain_a, shift_a = outs
            norm_a[l + 1] = (gain_a, shift_a)
        else:
            dmlp, dpre, part, sum_mlp, sum_pre = outs
        recv = swap(part, SWAP_CORE)
        (g_proj,) = weight_grad(
            "grad_proj", sidx, act, act.shape[1] // 2, x_pick, dmlp, [(zero_pick, act.shape[1] // 2)], 256
        )
        fc_keep, fc_send = weight_grad(
            "grad_fc", sidx, ln_c, 2 * quarter, x_pick, dpre, [(core_pick, quarter), (other_pick, quarter)], 512
        )
        fc_recv = swap(fc_send, SWAP_CORE)
        recv, g_proj, fc_keep, fc_recv = lax.optimization_barrier((recv, g_proj, fc_keep, fc_recv))
        gm, dattn, datt, sum_attn, gain_c, shift_c = out_backward(
            sidx, g, mid, part, recv, wide[l], wo[l]
        )
        dqkv, part, sum_qkv = attention_backward(sidx, qkv, datt, att, lse, drow, dcol, wq[l])
        recv = swap(part, SWAP_CORE)
        (g_o,) = weight_grad("grad_o", sidx, att, att.shape[1], zero_pick, dattn, [(x_pick, quarter)], 256)
        q_keep, q_send = weight_grad(
            "grad_qkv", sidx, ln_a, 2 * quarter, x_pick, dqkv, [(core_pick, quarter), (other_pick, quarter)], 384
        )
        q_recv = swap(q_send, SWAP_CORE)
        back = (gm, x, part, recv, wide[l])
        own_q = lambda a, at: lax.dynamic_slice_in_dim(a[0], at + xi * quarter, quarter)
        hidden_q = sum_pre.shape[1] // 2
        grads[l] = [
            ((g_proj, fc_keep, fc_recv), pack_attn(g_o, q_keep, q_recv)),
            [
                own_q(sum_qkv, 0),
                own_q(sum_qkv, 4 * quarter),
                quarter_of(sum_attn),
                quarter_of(sum_mlp),
                lax.dynamic_slice_in_dim(sum_pre[0], xi * hidden_q, hidden_q),
                quarter_of(gain_c),
                quarter_of(shift_c),
            ],
        ]
    gm, x, part, recv, vec = back
    grad_input, gain_a, shift_a = input_backward(sidx, gm, x, part, recv, vec)
    norm_a[0] = (gain_a, shift_a)

    small = []
    for l in range(layers):
        qb, vb, ob, mb, fb, gain_c, shift_c = grads[l][1]
        small.append(
            jnp.concatenate(
                [quarter_of(norm_a[l][0]), gain_c, quarter_of(norm_a[l][1]), shift_c, qb, vb, ob, mb, fb]
            )
        )
    small = double_sum(jnp.stack(small))
    before = finish_mlp(sidx, 1, layers, lax.psum(grads[1][0][0], "rows"), quarter)
    packed = jnp.concatenate([pack_mlp(*grads[0][0][0])] + [grads[l][0][1] for l in range(layers)])
    out_fc, out_proj, out_qkv, out_o = finish(sidx, layers, ring_sum(packed), before, quarter)
    pair = lambda k: small[:, k * quarter : (k + 2) * quarter].reshape(layers, 2, quarter)
    return (
        result[None],
        grad_input[None],
        out_qkv,
        out_o,
        out_fc,
        out_proj,
        pair(0),
        pair(2),
        pair(4),
        pair(6),
        small[:, 8 * quarter :],
    )


def solution(mesh):
    in_specs = (
        P("rows", "seq", None),
        P("rows", "seq", None),
        P("rows", None),
        P(None, "seq", None),
        P(None, "seq", None),
        P(None, "seq", None),
        P(None, "seq", None),
        P(None, None, "seq"),
        P(None, None, "seq"),
        P(None, None, "seq"),
        P(None, None, "seq"),
        P(None, "seq"),
    )
    out_specs = (
        P("rows", "seq", None),
        P("rows", "seq", None),
        P(None, "seq", None),
        P(None, "seq", None),
        P(None, "seq", None),
        P(None, "seq", None),
        P(None, None, "seq"),
        P(None, None, "seq"),
        P(None, None, "seq"),
        P(None, None, "seq"),
        P(None, "seq"),
    )
    return jax.shard_map(
        on_device, mesh=mesh, in_specs=in_specs, out_specs=out_specs, check_vma=False
    )
```

```python
import functools
import math

import jax
import jax.numpy as jnp
from jax import lax
from jax.experimental import pallas as pl
from jax.experimental.pallas import tpu as pltpu
from jax.sharding import PartitionSpec as P

HD = 64
branch_scale = 48.0 ** (-0.5)
norm_eps = 1e-05
masked_score = -1e30
log2_e = math.log2(math.e)
MIB = 1 << 20
VMEM = 62
BLK = 256

f32 = jnp.float32
bf16 = jnp.bfloat16
STREAM = bf16

SWAP_CORE = [(s, s ^ 1) for s in range(4)]
SWAP_X = [(s, s ^ 2) for s in range(4)]
SWAP_BOTH = [(s, s ^ 3) for s in range(4)]


def dot_nn(a, b):
    return lax.dot_general(a, b, (((1,), (0,)), ((), ())), preferred_element_type=f32)


def dot_nt(a, b):
    return lax.dot_general(a, b, (((1,), (1,)), ((), ())), preferred_element_type=f32)


def dot_tn(a, b):
    return lax.dot_general(a, b, (((0,), (0,)), ((), ())), preferred_element_type=f32)


def call(body, name, sidx, grid, ins, outs, scratch, flops, vmem, exps=0):
    arrays = [a for a, _, _ in ins]
    in_specs = [
        pl.BlockSpec(memory_space=pl.ANY) if b is None else pl.BlockSpec(b, m) for _, b, m in ins
    ]
    out_specs = [
        pl.BlockSpec(memory_space=pl.ANY) if b is None else pl.BlockSpec(b, m) for _, b, m in outs
    ]
    out_shape = [s for s, _, _ in outs]
    nbytes = sum(a.size * a.dtype.itemsize for a in arrays)
    nbytes += sum(math.prod(s.shape) * s.dtype.itemsize for s in out_shape)
    return pl.pallas_call(
        body,
        name=name,
        grid_spec=pltpu.PrefetchScalarGridSpec(
            num_scalar_prefetch=1,
            grid=grid,
            in_specs=in_specs,
            out_specs=out_specs,
            scratch_shapes=scratch,
        ),
        out_shape=out_shape,
        compiler_params=pltpu.CompilerParams(
            dimension_semantics=("arbitrary",) * len(grid), vmem_limit_bytes=VMEM * MIB
        ),
        cost_estimate=pl.CostEstimate(
            flops=int(flops), bytes_accessed=int(nbytes), transcendentals=int(exps)
        ),
    )(sidx, *arrays)


RING = [0, 2, 4, 6, 7, 5, 3, 1]
RING_NEXT = [(RING[i], RING[(i + 1) % 8]) for i in range(8)]
RING_PREV = [(b, a) for a, b in RING_NEXT]
RING_STEPS = [0, -1, 1, -2, 2, -3, 3, -4]


def ring_place():
    row = lax.axis_index("rows").astype(jnp.int32)
    return jnp.where(row % 2 == 0, row // 2, 7 - row // 2)


def place_index():
    s = lax.axis_index("seq").astype(jnp.int32)
    zero = jnp.int32(0)
    row = lax.axis_index("rows").astype(jnp.int32) if lax.axis_size("rows") == 8 else zero
    place = ring_place() if lax.axis_size("rows") == 8 else zero
    return jnp.stack([s, s // 2, s % 2, place, row % 2, row // 2])


def sds(shape, dtype):
    return jax.ShapeDtypeStruct(shape, dtype)


def whole(block):
    zeros = (0,) * len(block)
    return lambda i, m: zeros


def row_tile(i, m):
    return (i, 0)


def stack_tile(i, m):
    return (i ^ m[0], 0, 0)


def normed(x):
    centre = x - jnp.mean(x, axis=-1, keepdims=True)
    spread = jnp.mean(centre * centre, axis=-1, keepdims=True)
    rstd = lax.rsqrt(spread + norm_eps)
    return centre * rstd, rstd


def norm_back(x, grad, gain):
    unit, rstd = normed(x)
    inner = grad * gain
    mean_inner = jnp.mean(inner, axis=-1, keepdims=True)
    mean_prod = jnp.mean(inner * unit, axis=-1, keepdims=True)
    return rstd * (inner - mean_inner - unit * mean_prod), unit


GAIN_A, GAIN_C, SHIFT_A, SHIFT_C, OUT_A, OUT_M = range(6)


def row_of(ref, k):
    return ref[k : k + 1, :]


def lane_half(shape):
    return lax.broadcasted_iota(jnp.int32, shape, 1) // HD


def block_start(i):
    return BLK * (i * (i + 1) // 2)


class Mover:
    def __init__(self, sems):
        self.sems = sems
        self.used = 0

    def make(self, src, dst):
        cp = pltpu.make_async_copy(src, dst, self.sems.at[self.used])
        self.used += 1
        return cp

    def go(self, src, dst):
        cp = self.make(src, dst)
        cp.start()
        return cp


def wait_all(copies):
    for cp in copies:
        cp.wait()


def tile_of(i):
    return pl.ds(i * BLK, BLK)


def pieces_in(mover, refs, dst, first, rows):
    out = []
    for j, ref in enumerate(refs):
        where = pl.multiple_of((first ^ j) * rows, 16)
        out.append(mover.go(ref, dst.at[pl.ds(where, rows)]))
    return out


def add_up(ref, value, start):
    here = jnp.sum(value, axis=0, keepdims=True)
    if start:
        ref[...] = here
    else:
        ref[...] += here


def back_pair(pair, pairs, tokens, qkv, att, datt, lse, bias, starts, dqkv, dq_acc):
    blocks = tokens // BLK
    half = lane_half((BLK, 2 * HD))
    score_scale = HD ** (-0.5)
    scale = score_scale * log2_e
    pick_row = lax.broadcasted_iota(jnp.int32, (8, 2 * HD), 0)
    pick = jnp.where(lane_half((8, 2 * HD)) == pick_row, 1.0, 0.0)
    prod = datt[pair].astype(f32) * att[pair].astype(f32)
    delta = lax.dot_general(
        pick, prod, (((1,), (1,)), ((), ())), precision=lax.Precision.HIGHEST, preferred_element_type=f32
    )
    for j in range(blocks):
        first = j * BLK
        span = slice(first, first + BLK)
        rest = pl.ds(first, tokens - first)
        kj = qkv[pair + pairs, span, :]
        vj = qkv[pair + 2 * pairs, span, :]
        qq = qkv[pair, rest, :]
        dd = datt[pair, rest, :]
        width = tokens - first
        zero = jnp.zeros_like(kj)
        dks, dvs, dss, khs = [], [], [], []
        for h in range(2):
            kh = jnp.where(half == h, kj, zero)
            vh = jnp.where(half == h, vj, zero)
            t = dot_nt(kh, qq) * scale + bias[:, starts[j] : starts[j] + width]
            p = jnp.exp2(t - lse[pair, h : h + 1, first:])
            dp = dot_nt(vh, dd)
            ds = (p * (dp - delta[h : h + 1, first:])).astype(bf16)
            dvs.append(dot_nn(p.astype(bf16), dd))
            dks.append(dot_nn(ds, qq))
            dss.append(ds)
            khs.append(kh)
        dk = jnp.where(half == 0, dks[0], dks[1]) * score_scale
        dv = jnp.where(half == 0, dvs[0], dvs[1])
        dqkv[pair + pairs, span, :] = dk.astype(bf16)
        dqkv[pair + 2 * pairs, span, :] = dv.astype(bf16)
        dq = dot_tn(jnp.concatenate(dss, axis=0), jnp.concatenate(khs, axis=0))
        if j == 0:
            dq_acc[...] = dq
        else:
            dq_acc[first:, :] += dq
    dqkv[pair] = (dq_acc[...] * score_scale).astype(bf16)


def forward_pair(pair, pairs, blocks, qkv, bias, att, lse):
    half = lane_half((BLK, 2 * HD))
    scale = HD ** (-0.5) * log2_e
    for i in range(blocks):
        width = BLK * (i + 1)
        span = slice(i * BLK, (i + 1) * BLK)
        qb = qkv[pair, span, :]
        kk = qkv[pair + pairs, 0:width, :]
        vv = qkv[pair + 2 * pairs, 0:width, :]
        mixed, logs = [], []
        for h in range(2):
            qh = jnp.where(half == h, qb, jnp.zeros_like(qb))
            t = dot_nt(qh, kk) * scale + bias[:, block_start(i) : block_start(i) + width]
            top = jnp.max(t, axis=-1, keepdims=True)
            p = jnp.exp2(t - top)
            total = jnp.sum(p, axis=-1, keepdims=True)
            o = dot_nn(p.astype(bf16), vv)
            mixed.append(o / total)
            logs.append(jnp.broadcast_to(top + jnp.log2(total), (BLK, 2 * HD)))
        att[pair, span, :] = jnp.where(half == 0, mixed[0], mixed[1]).astype(bf16)
        turned = jnp.transpose(jnp.where(half == 0, logs[0], logs[1]))
        lse[pair, 0:1, span] = turned[0:1, :]
        lse[pair, 1:2, span] = turned[HD : HD + 1, :]


def attn_block_body(l, first, m, *refs):
    count = 1 if first else 3
    sources = refs[:count]
    wo0, wo1, w0, w1, w2, w3 = refs[count : count + 6]
    vec, prev, bias_row, drow, dcol = refs[count + 6 : count + 11]
    refs = refs[count + 11 :]
    if not first:
        x_out, refs = refs[0], refs[1:]
    ln_out, qkv_out, att_out, part_out, lse = refs[:5]
    bufs = refs[5 : 5 + count]
    (wo, w, lns, qkv, att, parts, bias, sems) = refs[5 + count :]
    tokens, d = lns.shape
    blocks = tokens // BLK
    pairs = att.shape[0]
    q = w0.shape[0]
    half = d // 2
    move = Mover(sems)
    c_w = pieces_in(move, (w0, w1, w2, w3), w, m[0], q)
    c_tiles = []
    for t in range(blocks):
        for ref, dst in zip(sources, bufs):
            src = ref.at[t ^ m[0]] if len(ref.shape) == 3 else ref.at[tile_of(t)]
            c_tiles.append(move.go(src, dst.at[tile_of(t)]))
    c_wo = pieces_in(move, (wo0.at[l], wo1), wo, m[1], q)
    for i in range(blocks):
        width = BLK * (i + 1)
        begin = i * BLK
        qpos = begin + lax.broadcasted_iota(jnp.int32, (BLK, width), 0)
        kpos = lax.broadcasted_iota(jnp.int32, (BLK, width), 1)
        same = dcol[begin : begin + BLK, :] == drow[:, :width]
        allowed = (kpos <= qpos) & same
        bias[:, block_start(i) : block_start(i) + width] = jnp.where(allowed, 0.0, masked_score)
    wait_all(c_w)
    c_out = []
    mine = pl.ds(pl.multiple_of(m[1] * half, 128), half)
    for t in range(blocks):
        wait_all(c_tiles[count * t : count * t + count])
        span = tile_of(t)
        if first:
            x = bufs[0][span, :].astype(f32)
        else:
            part = bufs[1][span, :].astype(f32) + bufs[2][span, :].astype(f32) + row_of(prev, OUT_M)
            x = bufs[0][span, :].astype(f32) + branch_scale * part
            bufs[0][span, :] = x.astype(STREAM)
            c_out.append(move.go(bufs[0].at[span], x_out.at[span]))
        unit, _ = normed(x)
        ln = (unit * row_of(vec, GAIN_A) + row_of(vec, SHIFT_A)).astype(bf16)
        lns[span, :] = ln
        c_out.append(move.go(lns.at[span, mine], ln_out.at[span]))
        row = (dot_nn(ln, w[...]) + bias_row[...]).astype(bf16)
        for k in range(3 * pairs):
            cols = slice(k * 2 * HD, (k + 1) * 2 * HD)
            qkv[k, span, :] = row[:, cols]
    for k in range(3 * pairs):
        c_out.append(move.go(qkv.at[k], qkv_out.at[k]))

    @pl.loop(0, pairs)
    def _(pair):
        forward_pair(pair, pairs, blocks, qkv, bias, att, lse)

    for k in range(pairs):
        c_out.append(move.go(att.at[k], att_out.at[k]))
    wait_all(c_wo)
    for t in range(blocks):
        span = tile_of(t)
        row = jnp.concatenate([att[k, span, :] for k in range(pairs)], axis=1)
        parts[span, :] = dot_nn(row, wo[...]).astype(bf16)
        c_out.append(move.go(parts.at[span], part_out.at[span]))
    wait_all(c_out)


def attn_block_forward(sidx, l, source, wo_pieces, pieces, vec, prev, bias, drow, dcol):
    first = len(source) == 1
    q, cols = pieces[0].shape
    d = 4 * q
    tokens = drow.shape[1]
    width = cols // 3
    pairs = width // (2 * HD)
    ins = [(a, None, None) for a in (*source, *wo_pieces, *pieces)]
    ins += [(a, a.shape, whole(a.shape)) for a in (vec, prev, bias, drow, dcol)]
    outs = [] if first else [(sds((tokens, d), STREAM), None, None)]
    outs += [
        (sds((tokens, d // 2), bf16), None, None),
        (sds((3 * pairs, tokens, 2 * HD), bf16), None, None),
        (sds((pairs, tokens, 2 * HD), bf16), None, None),
        (sds((tokens, d), bf16), None, None),
        (sds((pairs, 8, tokens), f32), (pairs, 8, tokens), whole((0, 0, 0))),
    ]
    blocks = tokens // BLK
    scratch = [pltpu.VMEM((tokens, d), a.dtype) for a in source]
    scratch += [
        pltpu.VMEM((width, d), bf16),
        pltpu.VMEM((d, cols), bf16),
        pltpu.VMEM((tokens, d), bf16),
        pltpu.VMEM((3 * pairs, tokens, 2 * HD), bf16),
        pltpu.VMEM((pairs, tokens, 2 * HD), bf16),
        pltpu.VMEM((tokens, d), bf16),
        pltpu.VMEM((BLK, block_start(blocks)), f32),
        pltpu.SemaphoreType.DMA((64,)),
    ]
    return call(
        functools.partial(attn_block_body, l, first),
        "attention_block",
        sidx,
        (1,),
        ins,
        outs,
        scratch,
        4 * tokens * tokens * width + 2 * tokens * d * (cols + width),
        40,
        exps=tokens * tokens * pairs,
    )


def mlp_weights_in(move, l, m, refs, wf, wp):
    if len(refs) == 6:
        first = pieces_in(move, refs[:4], wf, m[0], refs[0].shape[0])
        return first, pieces_in(move, refs[4:], wp, m[1], refs[4].shape[0])
    keep, near, own = refs[0], refs[1], refs[2].at[l]
    far = refs[3:]
    rows = keep.shape[0]
    deep, wide = own.shape
    first = pieces_in(move, (keep, near), wf, m[0], rows)
    second = pieces_in(move, (own,), wp, m[1], deep)
    n = len(far)
    part = far[0].shape[0] // 2
    for ref, t in zip(far, RING_STEPS):
        chunk = (m[3] + t + n) % n
        at = pl.multiple_of((1 - m[1]) * 2 * rows + chunk * part, 16)
        first.append(move.go(ref.at[pl.ds(0, part)], wf.at[pl.ds(at, part)]))
        for side in range(2):
            at = pl.multiple_of((1 - m[1]) * deep + side * (deep // 2) + chunk * part, 16)
            src = ref.at[pl.ds(part, part), pl.ds(side * wide, wide)]
            second.append(move.go(src, wp.at[pl.ds(at, part)]))
    return first, second


def gelu_and_slope(pre):
    root = math.sqrt(2.0 / math.pi)
    sq = pre * pre
    gate = 0.5 * jnp.tanh(pre * (root + root * 0.044715 * sq)) + 0.5
    rise = pre * (2.0 * root + 6.0 * root * 0.044715 * sq)
    return pre * gate, gate + gate * ((1.0 - gate) * rise)


def mlp_block_body(l, ahead, back, count, m, *refs):
    take = lambda k: (refs[:k], refs[k:])
    vec = prev = fcb = None
    sources, refs = take(3 if ahead else 0)
    (cot,), refs = take(1) if ahead and back else ((None,), refs)
    grads, refs = take(4 if back and not ahead else 0)
    (slope_in, act_in, ln_in), refs = take(3) if back and not ahead else ((None,) * 3, refs)
    weights, refs = take(count)
    if ahead:
        (vec, fcb), refs = take(2)
    else:
        (vec,), refs = take(1)
    if ahead:
        (mid_out, part_out), refs = take(2)
        if back:
            (own_out,), refs = take(1)
        else:
            (ln_out, act_out, slope_out), refs = take(3)
    if back:
        if not ahead:
            (g_out,), refs = take(1)
        (back_out, mine, other, send_mine, send_other, sum_mlp, sum_pre), refs = take(7)
        if not ahead:
            (sum_gain, sum_shift), refs = take(2)
    b0, b1, b2, b3, wf, wp, lns, act, slope, dmlp, sems = refs
    tokens, d = b1.shape
    blocks = tokens // BLK
    hidden = wf.shape[1]
    q = d // 4
    move = Mover(sems)
    c_tiles = []
    if ahead:
        loads = list(zip(sources, (b0, b1, b2))) + ([(cot, b3)] if back else [])
    else:
        loads = list(zip(grads, (b0, b1, b2, b3)))
    c_wp = []
    if ahead:
        c_wf, c_wp = mlp_weights_in(move, l, m, weights, wf, wp)
    for t in range(blocks):
        for ref, dst in loads:
            src = ref.at[t ^ m[0]] if len(ref.shape) == 3 else ref.at[tile_of(t)]
            c_tiles.append(move.go(src, dst.at[tile_of(t)]))
    if not ahead:
        c_wf, c_wp = mlp_weights_in(move, l, m, weights, wf, wp)
        c_slope = [move.go(slope_in.at[tile_of(t)], slope.at[tile_of(t)]) for t in range(blocks)]
        c_late = [move.go(act_in, act.at[:, pl.ds(0, act_in.shape[1])]), move.go(ln_in, lns.at[:, pl.ds(0, d // 2)])]
    c_out = []
    n = len(loads)
    wide = hidden // 2
    for t in range(blocks):
        wait_all(c_tiles[n * t : n * t + n])
        span = tile_of(t)
        if ahead:
            part = b1[span, :].astype(f32) + b2[span, :].astype(f32) + row_of(vec, OUT_A)
            mid = b0[span, :].astype(f32) + branch_scale * part
            b0[span, :] = mid.astype(b0.dtype)
            c_out.append(move.go(b0.at[span], mid_out.at[span]))
            if back:

                @pl.when(m[0] == t)
                def _():
                    own_out[...] = mid

            unit, _ = normed(mid)
            ln = (unit * row_of(vec, GAIN_C) + row_of(vec, SHIFT_C)).astype(bf16)
            lns[span, :] = ln
            if t == 0:
                wait_all(c_wf)
            value, rise = gelu_and_slope(dot_nn(ln, wf[...]) + fcb[...])
            low = value.astype(bf16)
            act[span, :] = low
            if not back:
                slope[span, :] = rise.astype(bf16)
                cols = pl.ds(pl.multiple_of(m[1] * (d // 2), 128), d // 2)
                c_out.append(move.go(lns.at[span, cols], ln_out.at[span]))
                cols = pl.ds(pl.multiple_of(m[1] * wide, 128), wide)
                c_out.append(move.go(act.at[span, cols], act_out.at[span]))
                c_out.append(move.go(slope.at[span], slope_out.at[span]))
            if t == 0:
                wait_all(c_wp)
            b1[span, :] = dot_nn(low, wp[...]).astype(bf16)
            c_out.append(move.go(b1.at[span], part_out.at[span]))
        if back:
            if ahead:
                g = b3[span, :].astype(f32)
            else:
                if t == 0:
                    wait_all(c_wp)
                wait_all(c_slope[t : t + 1])
                rise = slope[span, :].astype(f32)
                grad = b2[span, :].astype(f32) + b3[span, :].astype(f32)
                part, unit = norm_back(b1[span, :].astype(f32), grad, row_of(vec, GAIN_A))
                add_up(sum_gain, grad * unit, t == 0)
                add_up(sum_shift, grad, t == 0)
                g = b0[span, :].astype(f32) + part
                b0[span, :] = g.astype(b0.dtype)
                c_out.append(move.go(b0.at[span], g_out.at[span]))
            low = (branch_scale * g).astype(bf16)
            dmlp[span, :] = low
            add_up(sum_mlp, low.astype(f32), t == 0)
            dpre = (dot_nt(low, wp[...]) * rise).astype(bf16)
            slope[span, :] = dpre
            add_up(sum_pre, dpre.astype(f32), t == 0)
            if t == 0 and not ahead:
                wait_all(c_wf)
            b2[span, :] = dot_nt(dpre, wf[...]).astype(bf16)
            c_out.append(move.go(b2.at[span], back_out.at[span]))
    if back:
        y = m[4]
        if not ahead:
            wait_all(c_late)
            turned = jnp.transpose(act[:, 0:wide])
        else:
            turned = jnp.transpose(jnp.where(m[1] == 0, act[:, 0:wide], act[:, wide:]))
        grad = dot_nn(turned, dmlp[...]).astype(bf16)
        h = grad.shape[0] // 2
        mine[0:h, :] = jnp.where(y == 0, grad[:h], grad[h:])
        other[0:h, :] = jnp.where(y == 0, grad[h:], grad[:h])
        half = d // 2
        if not ahead:
            turned = jnp.transpose(lns[:, 0:half])
        else:
            turned = jnp.transpose(jnp.where(m[1] == 0, lns[:, 0:half], lns[:, half:]))
        sides = [dot_nn(turned, slope[:, i * d : (i + 1) * d]).astype(bf16) for i in range(2)]
        for here, there, i in ((mine, send_mine, 0), (other, send_other, 1)):
            side = jnp.where(y == i, sides[0], sides[1])
            here[h : h + q, :] = jnp.where(m[2] == 0, side[:q], side[q:])
            there[...] = jnp.where(m[2] == 0, side[q:], side[:q])
    wait_all(c_out)


def mlp_block(sidx, l, vec, weights, ahead=None, back=None, fcb=None):
    d = vec.shape[1]
    if ahead is not None:
        tokens = ahead[1].shape[0]
        hidden = fcb.shape[1]
        sources = list(ahead) + ([back[0]] if back else [])
        types = [STREAM if ahead[0].ndim == 2 else ahead[0].dtype, bf16, bf16, bf16]
        vectors_in = [vec, fcb]
    else:
        tokens, hidden = back[4].shape
        sources = list(back)
        types = [back[0].dtype, back[1].dtype, bf16, bf16]
        vectors_in = [vec]
    q = d // 4
    ins = [(a, None, None) for a in sources + list(weights)]
    ins += [(a, a.shape, whole(a.shape)) for a in vectors_in]
    stay = lambda shape, dtype: (sds(shape, dtype), shape, whole(shape))
    away = lambda shape, dtype: (sds(shape, dtype), None, None)
    outs = []
    if ahead is not None:
        outs += [away((tokens, d), STREAM), away((tokens, d), bf16)]
        if back:
            outs += [stay((BLK, d), f32)]
        else:
            outs += [
                away((tokens, d // 2), bf16),
                away((tokens, hidden // 2), bf16),
                away((tokens, hidden), bf16),
            ]
    if back:
        if ahead is None:
            outs += [away((tokens, d), back[0].dtype)]
        outs += [away((tokens, d), bf16)]
        outs += [stay((3 * q, d), bf16)] * 2 + [stay((q, d), bf16)] * 2
        outs += [stay((1, d), f32), stay((1, hidden), f32)]
        if ahead is None:
            outs += [stay((1, d), f32)] * 2
    scratch = [pltpu.VMEM((tokens, d), t) for t in types]
    scratch += [
        pltpu.VMEM((d, hidden), bf16),
        pltpu.VMEM((hidden, d), bf16),
        pltpu.VMEM((tokens, d), bf16),
        pltpu.VMEM((tokens, hidden), bf16),
        pltpu.VMEM((tokens, hidden), bf16),
        pltpu.VMEM((tokens, d), bf16),
        pltpu.SemaphoreType.DMA((96,)),
    ]
    return call(
        functools.partial(mlp_block_body, l, ahead is not None, bool(back), len(weights)),
        "mlp_block" + ("_forward" if ahead is not None else "") + ("_backward" if back else ""),
        sidx,
        (1,),
        ins,
        outs,
        scratch,
        (4 * bool(ahead is not None) + 8 * bool(back)) * tokens * d * hidden,
        48,
        exps=tokens * hidden,
    )


def attn_block_back_body(l, m, *refs):
    (g_in, mid_in, p_in, r_in, wo0, wo1, qkv_in, att_in, ln_in, w0, w1, w2, w3) = refs[:13]
    (vec, drow, dcol, lse) = refs[13:17]
    (gm_out, part_out, mine, other, send_mine, send_other) = refs[17:23]
    (sum_attn, sum_gain, sum_shift, sum_qkv) = refs[23:27]
    (gs, mids, ps, rs, wo, qkv, att, lns, w, dattn, datt, dqkv, bias, dq_acc, sems) = refs[27:]
    tokens, d = mids.shape
    blocks = tokens // BLK
    pairs = att.shape[0]
    q = w0.shape[0]
    move = Mover(sems)
    c_wo = pieces_in(move, (wo0.at[l], wo1), wo, m[1], q)
    c_tiles = []
    loads = [(g_in, gs), (mid_in, mids), (p_in, ps), (r_in, rs)]
    for t in range(blocks):
        for ref, dst in loads:
            src = ref.at[t ^ m[0]] if len(ref.shape) == 3 else ref.at[tile_of(t)]
            c_tiles.append(move.go(src, dst.at[tile_of(t)]))
    c_qkv = [move.go(qkv_in, qkv), move.go(att_in, att)]
    c_w = pieces_in(move, (w0, w1, w2, w3), w, m[0], q)
    half = d // 2
    c_ln = [move.go(ln_in, lns)]

    starts = [sum(tokens - BLK * a for a in range(j)) for j in range(blocks)]
    for j in range(blocks):
        width = tokens - j * BLK
        first = j * BLK
        kpos = lax.broadcasted_iota(jnp.int32, (BLK, width), 0)
        qpos = lax.broadcasted_iota(jnp.int32, (BLK, width), 1)
        same = dcol[first : first + BLK, :] == drow[:, first:]
        allowed = (kpos <= qpos) & same
        bias[:, starts[j] : starts[j] + width] = jnp.where(allowed, 0.0, masked_score)

    wait_all(c_wo)
    c_out = []
    for t in range(blocks):
        wait_all(c_tiles[4 * t : 4 * t + 4])
        span = tile_of(t)
        grad = ps[span, :].astype(f32) + rs[span, :].astype(f32)
        part, unit = norm_back(mids[span, :].astype(f32), grad, row_of(vec, GAIN_C))
        add_up(sum_gain, grad * unit, t == 0)
        add_up(sum_shift, grad, t == 0)
        gm = gs[span, :].astype(f32) + part
        gs[span, :] = gm.astype(gs.dtype)
        c_out.append(move.go(gs.at[span], gm_out.at[span]))
        low = (branch_scale * gm).astype(bf16)
        dattn[span, :] = low
        add_up(sum_attn, low.astype(f32), t == 0)
        heads = dot_nt(low, wo[...]).astype(bf16)
        for k in range(pairs):
            datt[k, span, :] = heads[:, k * 2 * HD : (k + 1) * 2 * HD]

    wait_all(c_qkv)

    @pl.loop(0, pairs)
    def _(pair):
        back_pair(pair, pairs, tokens, qkv, att, datt, lse, bias, starts, dqkv, dq_acc)

    wait_all(c_w)
    for t in range(blocks):
        span = tile_of(t)
        row = jnp.concatenate([dqkv[k, span, :] for k in range(3 * pairs)], axis=1)
        ps[span, :] = dot_nt(row, w[...]).astype(bf16)
        c_out.append(move.go(ps.at[span], part_out.at[span]))
        add_up(sum_qkv, row.astype(f32), t == 0)

    wait_all(c_ln)
    quart = q // 2
    y = m[4]
    turned = jnp.concatenate([jnp.transpose(att[k]) for k in range(pairs)], axis=0)
    left = jnp.where(m[1] == 0, turned[:q], turned[q : 2 * q])
    g_o = dot_nn(left, dattn[...]).astype(bf16)
    for i in range(2):
        cols = slice(i * half, (i + 1) * half)
        a, b = g_o[:quart, cols], g_o[quart:, cols]
        mine[i * quart : (i + 1) * quart, :] = jnp.where(y == 0, a, b)
        other[i * quart : (i + 1) * quart, :] = jnp.where(y == 0, b, a)
    turned = jnp.transpose(lns[...])
    for p in range(3):
        right = jnp.concatenate([dqkv[p * pairs + k] for k in range(pairs)], axis=1)
        grad = dot_nn(turned, right).astype(bf16)
        keep = jnp.where(m[2] == 0, grad[:q], grad[q:])
        send = jnp.where(m[2] == 0, grad[q:], grad[:q])
        at = (2 + p) * quart
        mine[at : at + quart, :] = jnp.where(y == 0, keep[:quart], keep[quart:])
        other[at : at + quart, :] = jnp.where(y == 0, keep[quart:], keep[:quart])
        at = p * quart
        send_mine[at : at + quart, :] = jnp.where(y == 0, send[:quart], send[quart:])
        send_other[at : at + quart, :] = jnp.where(y == 0, send[quart:], send[:quart])
    wait_all(c_out)


def attn_block_backward(sidx, l, g, mid, part, recv, wo_pieces, qkv, att, ln_a, pieces, vec, drow, dcol, lse):
    tokens, d = mid.shape
    q, cols = pieces[0].shape
    width = cols // 3
    pairs = width // (2 * HD)
    ins = [(a, None, None) for a in (g, mid, part, recv, *wo_pieces, qkv, att, ln_a, *pieces)]
    ins += [(a, a.shape, whole(a.shape)) for a in (vec, drow, dcol, lse)]
    stay = lambda shape, dtype: (sds(shape, dtype), shape, whole(shape))
    outs = [
        (sds((tokens, d), STREAM), None, None),
        (sds((tokens, d), bf16), None, None),
        stay((5 * q // 2, width), bf16),
        stay((5 * q // 2, width), bf16),
        stay((3 * q // 2, width), bf16),
        stay((3 * q // 2, width), bf16),
        stay((1, d), f32),
        stay((1, d), f32),
        stay((1, d), f32),
        stay((1, cols), f32),
    ]
    blocks = tokens // BLK
    wide = (tokens, 2 * HD)
    scratch = [
        pltpu.VMEM((tokens, d), g.dtype),
        pltpu.VMEM((tokens, d), mid.dtype),
        pltpu.VMEM((tokens, d), bf16),
        pltpu.VMEM((tokens, d), bf16),
        pltpu.VMEM((width, d), bf16),
        pltpu.VMEM((3 * pairs,) + wide, bf16),
        pltpu.VMEM((pairs,) + wide, bf16),
        pltpu.VMEM((tokens, d // 2), bf16),
        pltpu.VMEM((d, cols), bf16),
        pltpu.VMEM((tokens, d), bf16),
        pltpu.VMEM((pairs,) + wide, bf16),
        pltpu.VMEM((3 * pairs,) + wide, bf16),
        pltpu.VMEM((BLK, block_start(blocks)), f32),
        pltpu.VMEM(wide, f32),
        pltpu.SemaphoreType.DMA((64,)),
    ]
    return call(
        functools.partial(attn_block_back_body, l),
        "attention_block_backward",
        sidx,
        (1,),
        ins,
        outs,
        scratch,
        10 * tokens * tokens * width,
        48,
        exps=tokens * tokens * pairs,
    )


def add_rows(ref, value, start):
    @pl.when(start)
    def _():
        ref[...] = jnp.zeros_like(ref)

    ref[...] += jnp.sum(value, axis=0, keepdims=True)


def input_back_body(m, gm_ref, x_ref, p_ref, r_ref, vec, out_ref, sum_gain, sum_shift):
    tile = pl.program_id(0)
    grad = p_ref[...].astype(f32) + r_ref[...].astype(f32)
    part, unit = norm_back(x_ref[0].astype(f32), grad, row_of(vec, GAIN_A))
    add_rows(sum_gain, grad * unit, tile == 0)
    add_rows(sum_shift, grad, tile == 0)

    @pl.when(tile == m[0])
    def _():
        out_ref[...] = gm_ref[...].astype(f32) + part


def input_backward(sidx, gm, x, part, recv, vec):
    tokens, depth = gm.shape
    tile = (BLK, depth)
    ins = [(gm, tile, row_tile), (x, (1, BLK, depth), stack_tile)]
    ins += [(a, tile, row_tile) for a in (part, recv)]
    ins.append((vec, vec.shape, whole(vec.shape)))
    outs = [(sds((BLK, depth), f32), tile, whole((0, 0)))]
    outs += [(sds((1, depth), f32), (1, depth), whole((0, 0)))] * 2
    return call(input_back_body, "input_backward", sidx, (tokens // BLK,), ins, outs, [], tokens * depth, 16)


def swap(a, perm):
    return lax.ppermute(a, "seq", perm)


def split_body(m, qkv_ref, fc_ref, o_ref, qkv_keep, qkv_send, fc_keep, fc_send, o_out):
    core = m[2]
    o_out[...] = o_ref[0]
    q = qkv_ref.shape[1]
    pair = 2 * q
    for p in range(3):
        own, other = [], []
        for xside in range(2):
            col = (2 * p + xside) * pair
            both = qkv_ref[0, :, col : col + pair]
            own.append(jnp.where(core == 0, both[:, :q], both[:, q:]))
            other.append(jnp.where(core == 0, both[:, q:], both[:, :q]))
        qkv_keep[:, p * pair : (p + 1) * pair] = jnp.concatenate(own, axis=1)
        qkv_send[:, p * pair : (p + 1) * pair] = jnp.concatenate(other, axis=1)
    d = fc_ref.shape[2] // 4
    for xside in range(2):
        one = fc_ref[0, :, 2 * xside * d : (2 * xside + 1) * d]
        two = fc_ref[0, :, (2 * xside + 1) * d : (2 * xside + 2) * d]
        fc_keep[:, xside * d : (xside + 1) * d] = jnp.where(core == 0, one, two)
        fc_send[:, xside * d : (xside + 1) * d] = jnp.where(core == 0, two, one)


def split_columns(sidx, w_qkv, w_fc, w_o, l):
    _, rows, cols = w_qkv.shape
    hidden = w_fc.shape[2]
    at = lambda i, m: (l, 0, 0)
    depth = w_o.shape[2]
    ins = [(w_qkv, (1, rows, cols), at), (w_fc, (1, rows, hidden), at), (w_o, (1, rows, depth), at)]
    outs = []
    for width in (cols // 2, cols // 2, hidden // 2, hidden // 2, depth):
        outs.append((sds((rows, width), bf16), (rows, width), whole((0, 0))))
    return call(split_body, "split_columns", sidx, (1,), ins, outs, [], rows * cols, 16)


def column_pieces(keep, send):
    return [keep, swap(send, SWAP_CORE), swap(keep, SWAP_X), swap(send, SWAP_BOTH)]


def row_pieces(w):
    return [w, swap(w, SWAP_X)]


def far_piece_body(l, m, keep, near, proj, out, sems):
    part = out.shape[0] // 2
    wide = proj.shape[2]
    deep = proj.shape[1] // 2
    place = m[3]
    at = pl.multiple_of((place % 4) * part, 16)
    own = place // 4 == m[2]
    first = pltpu.make_async_copy(keep.at[pl.ds(at, part)], out.at[pl.ds(0, part)], sems.at[0])
    second = pltpu.make_async_copy(near.at[pl.ds(at, part)], out.at[pl.ds(0, part)], sems.at[0])
    lows = []
    for side in range(2):
        at = pl.multiple_of(side * deep + place * part, 16)
        dst = out.at[pl.ds(part, part), pl.ds(side * wide, wide)]
        lows.append(pltpu.make_async_copy(proj.at[l, pl.ds(at, part)], dst, sems.at[1 + side]))
    for cp in lows:
        cp.start()

    @pl.when(own)
    def _():
        first.start()
        first.wait()

    @pl.when(jnp.logical_not(own))
    def _():
        second.start()
        second.wait()

    for cp in lows:
        cp.wait()


def far_piece(sidx, keep, near, w_proj, l):
    shape = (keep.shape[0] // 2, keep.shape[1])
    ins = [(a, None, None) for a in (keep, near, w_proj)]
    outs = [(sds(shape, bf16), shape, whole(shape))]
    return call(
        functools.partial(far_piece_body, l),
        "far_piece",
        sidx,
        (1,),
        ins,
        outs,
        [pltpu.SemaphoreType.DMA((3,))],
        0,
        16,
    )[0]


def mlp_pieces(sidx, keep, send, w_proj, l, direct):
    if direct:
        return column_pieces(keep, send) + row_pieces(w_proj[l]), None
    near = swap(send, SWAP_CORE)
    mine = swap(far_piece(sidx, keep, near, w_proj, l), SWAP_X)
    return [keep, near, w_proj], [mine]


def ring_pass(held, t):
    if held is None:
        return []
    on = lax.ppermute(held[max(0, len(held) - 2)], "rows", RING_NEXT)
    if t == 4:
        new = [on]
    else:
        new = [on, lax.ppermute(held[-1], "rows", RING_PREV)]
    held += new
    return new


def gather_rows(a):
    near = swap(a, SWAP_CORE)
    far = swap(a, SWAP_X)
    return jnp.stack([a, near, far, swap(far, SWAP_CORE)])


SWAP_Y = [(r, r ^ 1) for r in range(8)]
SWAP_Z = [None] + [[(r, r ^ (2 * d)) for r in range(8)] for d in range(1, 4)]


def sum_y_body(m, mine, got, recv, got_recv, *refs):
    outs, full = refs[:-1], refs[-1]
    cut = mine.shape[0]
    full[0:cut, :] = (mine[...].astype(f32) + got[...].astype(f32)).astype(bf16)
    full[cut:, :] = (recv[...].astype(f32) + got_recv[...].astype(f32)).astype(bf16)
    rows = outs[0].shape[0]
    for d, out in enumerate(outs):
        out[...] = full[pl.ds(pl.multiple_of((m[5] ^ d) * rows, 16), rows), :]


def sum_y(sidx, mine, got, recv, got_recv):
    rows, d = mine.shape[0] + recv.shape[0], mine.shape[1]
    ins = [(a, a.shape, whole(a.shape)) for a in (mine, got, recv, got_recv)]
    outs = [(sds((rows // 4, d), bf16), (rows // 4, d), whole((0, 0)))] * 4
    scratch = [pltpu.VMEM((rows, d), bf16)]
    return call(sum_y_body, "sum_y", sidx, (1,), ins, outs, scratch, rows * d, 16)


class RowSum:
    def __init__(self, sidx, mine, other, send_mine, send_other):
        recv, recv_other = swap(send_mine, SWAP_CORE), swap(send_other, SWAP_CORE)
        self.sidx = sidx
        self.shape = (4, (mine.shape[0] + recv.shape[0]) // 4, mine.shape[1])
        self.direct = lax.axis_size("rows") != 8
        self.got = [None] * 4
        if self.direct:
            halves = [jnp.concatenate([mine, recv]), jnp.concatenate([other, recv_other])]
            self.held = [t.reshape(self.shape) for t in lax.psum(halves, "rows")]
        else:
            far = [lax.ppermute(a, "rows", SWAP_Y) for a in (other, recv_other)]
            self.held = [mine, far[0], recv, far[1]]

    def split(self):
        if not self.direct:
            self.held = list(sum_y(self.sidx, *self.held))

    def scatter(self, *steps):
        for d in steps:
            if not self.direct:
                self.got[d] = lax.ppermute(self.held[d], "rows", SWAP_Z[d])

    def total(self):
        if not self.direct:
            terms = [self.held[0]] + self.got[1:]
            self.held = [sum(a.astype(f32) for a in terms).astype(bf16)]
            self.got = [None] * 4

    def gather(self, *steps):
        for d in steps:
            if not self.direct:
                self.got[d] = lax.ppermute(self.held[0], "rows", SWAP_Z[d])

    def gather_y(self):
        if not self.direct:
            near = jnp.concatenate([self.held[0]] + self.got[1:]).reshape(self.shape)
            self.held = [near, lax.ppermute(near, "rows", SWAP_Y)]

    def state(self):
        return self.held, self.got

    def restore(self, state):
        self.held, self.got = list(state[0]), list(state[1])


def halves(m, near, far):
    def quarter(k):
        a, b = near[k ^ m[5]].astype(f32), far[k ^ m[5]].astype(f32)
        return jnp.where(m[4] == 0, a, b), jnp.where(m[4] == 0, b, a)

    return [quarter(k) for k in range(4)]


def finish_mlp_body(m, near, far, *refs):
    out_fc, out_proj = refs[-2:]
    q, d = near.shape[1:]
    parts = halves(m, near, far)
    for h in range(2):
        for k in range(2):
            at = (2 * h + k) * q
            out_proj[0, at : at + q, :] = parts[k][h]
        for c in range(2):
            col = (2 * h + c) * d
            out_fc[0, :, col : col + d] = jnp.where(m[2] == c, parts[2][h], parts[3][h])


def finish_attn_body(m, near, far, *refs):
    out_qkv, out_o = refs[-2:]
    rows, width = near.shape[1:]
    n = rows // 2
    q = width // 2
    parts = halves(m, near, far)
    for h in range(2):
        span = slice(h * n, (h + 1) * n)
        bits = [p for k in range(4) for p in (parts[k][h][:n], parts[k][h][n:])]
        out_o[0, span, 0:width] = bits[0]
        out_o[0, span, width:] = bits[1]
        for p in range(3):
            keep, recv = bits[2 + p], bits[5 + p]
            for xside in range(2):
                a = keep[:, xside * q : (xside + 1) * q]
                b = recv[:, xside * q : (xside + 1) * q]
                col = (2 * p + xside) * width
                out_qkv[0, span, col : col + width] = jnp.concatenate(
                    [jnp.where(m[2] == 0, a, b), jnp.where(m[2] == 0, b, a)], axis=1
                )


def finish(body, name, sidx, l, layers, held, before, shapes):
    args = list(held)
    in_specs = [pl.BlockSpec(a.shape, lambda i, m: (0, 0, 0)) for a in held]
    aliases = {}
    if before is not None:
        aliases = {1 + len(args) + k: k for k in range(len(before))}
        args += list(before)
        in_specs += [pl.BlockSpec(memory_space=pl.ANY)] * len(before)
    size = sum(math.prod(sh) for sh in shapes)
    return pl.pallas_call(
        body,
        name=name,
        grid_spec=pltpu.PrefetchScalarGridSpec(
            num_scalar_prefetch=1,
            grid=(1,),
            in_specs=in_specs,
            out_specs=[pl.BlockSpec((1,) + sh, lambda i, m: (l, 0, 0)) for sh in shapes],
        ),
        out_shape=[sds((layers,) + sh, f32) for sh in shapes],
        input_output_aliases=aliases,
        compiler_params=pltpu.CompilerParams(vmem_limit_bytes=VMEM * MIB),
        cost_estimate=pl.CostEstimate(flops=size, bytes_accessed=6 * size, transcendentals=0),
    )(sidx, *args)


def double_sum(a):
    n = lax.axis_size("rows")
    if n & (n - 1):
        return lax.psum(a, "rows")
    step = 1
    while step < n:
        a = a + lax.ppermute(a, "rows", [(r, r ^ step) for r in range(n)])
        step *= 2
    return a


def vectors_body(m, near, far, wide, qkv_bias, fcb):
    layers = near.shape[1]
    q = near.shape[3]
    for l in range(layers):
        full = []
        for k in range(4):
            core = (k % 2) ^ m[2]
            full.append(jnp.where(m[1] == k // 2, near[core, l], far[core, l]).astype(f32))
        every = jnp.concatenate(full, axis=1)
        wide[l, 0:4, :] = every[0:4]
        wide[l, 4:6, :] = every[6:8]
        wide[l, 6:8, :] = jnp.zeros((2, 4 * q), f32)
        here = [jnp.where(m[2] == 0, full[2 * xside], full[2 * xside + 1]) for xside in range(2)]
        pick = lambda r: [a[r : r + 1] for a in here]
        none = jnp.zeros((1, 2 * q), f32)
        qkv_bias[l] = jnp.concatenate(pick(4) + [none] + pick(5), axis=1)
        rest = [a[r : r + 1] for a in here for r in range(8, a.shape[0])]
        fcb[l] = jnp.concatenate(rest, axis=1)


def vectors(sidx, norm_gain, norm_bias, qv_bias, out_bias, fc_bias):
    layers, _, q = norm_gain.shape
    mine = jnp.concatenate(
        [norm_gain, norm_bias, qv_bias, out_bias, fc_bias.reshape(layers, -1, q)], axis=1
    )
    near = jnp.stack([mine, swap(mine, SWAP_CORE)])
    far = swap(near, SWAP_X)
    ins = [(a, a.shape, whole(a.shape)) for a in (near, far)]
    hidden = 2 * fc_bias.shape[1]
    outs = []
    for shape in ((layers, 8, 4 * q), (layers, 1, 6 * q), (layers, 1, hidden)):
        outs.append((sds(shape, f32), shape, whole(shape)))
    return call(vectors_body, "vectors", sidx, (1,), ins, outs, [], near.size, 16)


def on_device(
    block_input,
    output_cotangent,
    doc_ids,
    w_qkv,
    w_o,
    w_fc,
    w_proj,
    norm_gain,
    norm_bias,
    qv_bias,
    out_bias,
    fc_bias,
):
    sidx = place_index()
    s, xi, core = sidx[0], sidx[1], sidx[2]
    layers = w_qkv.shape[0]
    quarter = w_qkv.shape[1]
    tokens = doc_ids.shape[1]
    drow = doc_ids
    dcol = doc_ids.reshape(tokens, 1)

    def pin(outs, *groups):
        flat, tree = jax.tree.flatten((outs, groups))
        outs, groups = jax.tree.unflatten(tree, lax.optimization_barrier(flat))
        return (outs,) + tuple(groups)

    few = lax.axis_size("rows") != 8
    xs = gather_rows(block_input[0])
    wq, wo, wm, far = [], [], [], [None] * layers
    source = (w_qkv, w_fc, w_o)
    for l in range(layers):
        keep, send, fc_keep, fc_send, o = split_columns(sidx, *source, l)
        fixed, moved = mlp_pieces(sidx, fc_keep, fc_send, w_proj, l, few or l > 0)
        wm.append(fixed)
        far[l] = moved
        wq.append(column_pieces(keep, send))
        wo.append([w_o, swap(o, SWAP_X)])
        if moved is not None:
            source, far[l] = pin(source, moved)
    wide, qkv_bias, fcb = vectors(sidx, norm_gain, norm_bias, qv_bias, out_bias, fc_bias)
    cot = gather_rows(output_cotangent[0])

    ring_pass(far[0], 1)
    ring_pass(far[0], 2)
    ring_pass(far[0], 3)
    xs, far[0], wq[0] = pin(xs, far[0], wq[0])
    outs = attn_block_forward(sidx, 0, (xs,), wo[0], wq[0], wide[0], wide[0], qkv_bias[0], drow, dcol)
    ring_pass(far[0], 4)
    outs, far[0], wq[1] = pin(outs, far[0], wq[1])
    ln_a, qkv, att, part, lse = outs
    save_a = [(xs, ln_a, qkv, att, lse)]
    recv = swap(part, SWAP_CORE)
    outs = mlp_block(sidx, 0, wide[0], wm[0] + (far[0] or []), ahead=(xs, part, recv), fcb=fcb[0])
    outs, wo[1], wm[1][2], cot = pin(outs, wo[1], wm[1][2], cot)
    mid, part, ln_c, act, slope = outs
    save_m = (ln_c, act, slope)
    mids = [mid]
    recv = swap(part, SWAP_CORE)
    outs = attn_block_forward(
        sidx, 1, (mid, part, recv), wo[1], wq[1], wide[1], wide[0], qkv_bias[1], drow, dcol
    )
    outs, wm[1] = pin(outs, wm[1])
    x, ln_a, qkv, att, part, lse = outs
    save_a.append((x, ln_a, qkv, att, lse))
    recv = swap(part, SWAP_CORE)
    outs = mlp_block(sidx, 1, wide[1], wm[1], ahead=(x, part, recv), back=(cot,), fcb=fcb[1])
    mid, part, own_mid, part_b, *pack, sum_mlp, sum_pre = outs
    mids.append(mid)

    quarter_of = lambda a: lax.dynamic_slice_in_dim(a[0], s * quarter, quarter)
    own_q = lambda a, at: lax.dynamic_slice_in_dim(a[0], at + xi * quarter, quarter)
    own_h = lambda a: lax.dynamic_slice_in_dim(a[0], xi * (a.shape[1] // 2), a.shape[1] // 2)
    grads = [None] * layers
    norm_a = [None] * layers

    recv = swap(part_b, SWAP_CORE)
    up_m = RowSum(sidx, *pack)
    outs = attn_block_backward(sidx, 1, cot, mids[1], part_b, recv, wo[1], *save_a[1][2:4], save_a[1][1], wq[1], wide[1], drow, dcol, save_a[1][4])
    outs, up_m.held = pin(outs, up_m.held)
    gm, part_b, *pack, sum_attn, gain_c, shift_c, sum_qkv = outs
    grads[1] = [own_q(sum_qkv, 0), own_q(sum_qkv, 4 * quarter), quarter_of(sum_attn), quarter_of(sum_mlp), own_h(sum_pre), quarter_of(gain_c), quarter_of(shift_c)]
    up_m.split()
    up_a = RowSum(sidx, *pack)
    recv = swap(part_b, SWAP_CORE)
    recv, up_m.held = pin(recv, up_m.held)
    up_m.scatter(2, 1)

    outs = mlp_block(sidx, 0, wide[1], wm[0] + (far[0] or []), back=(gm, save_a[1][0], part_b, recv, save_m[2], save_m[1], save_m[0]))
    outs, up_m.got, up_a.held = pin(outs, up_m.got, up_a.held)
    g, part_b, *pack, sum_mlp, sum_pre, gain_a, shift_a = outs
    norm_a[1] = (gain_a, shift_a)
    up_m.scatter(3)
    up_a.split()
    up_a.scatter(2, 3, 1)
    low_m = RowSum(sidx, *pack)
    recv = swap(part_b, SWAP_CORE)
    recv, up_a.held = pin(recv, up_a.held)

    outs = attn_block_backward(sidx, 0, g, mids[0], part_b, recv, wo[0], *save_a[0][2:4], save_a[0][1], wq[0], wide[0], drow, dcol, save_a[0][4])
    outs, up_m.got, up_a.got, low_m.held = pin(outs, up_m.got, up_a.got, low_m.held)
    gm, part_b, *pack, sum_attn, gain_c, shift_c, sum_qkv = outs
    grads[0] = [own_q(sum_qkv, 0), own_q(sum_qkv, 4 * quarter), quarter_of(sum_attn), quarter_of(sum_mlp), own_h(sum_pre), quarter_of(gain_c), quarter_of(shift_c)]
    low_a = RowSum(sidx, *pack)
    up_m.total()
    up_m.gather(2, 3, 1)
    low_m.split()
    low_m.scatter(2, 3, 1)
    up_a.total()
    up_a.gather(2, 3, 1)
    recv = swap(part_b, SWAP_CORE)
    grad_input, gain_a, shift_a = input_backward(sidx, gm, xs, part_b, recv, wide[0])
    norm_a[0] = (gain_a, shift_a)
    low_a.split()
    low_a.scatter(2, 3, 1)
    up_m.gather_y()
    up_a.gather_y()
    low_m.total()
    low_m.gather(2, 3, 1)
    low_a.total()
    low_a.gather(2, 3, 1)
    low_m.gather_y()
    low_a.gather_y()

    recv = swap(part, SWAP_CORE)
    at = s * block_input.shape[1]
    own = lambda a: lax.dynamic_slice_in_dim(a, at, block_input.shape[1]).astype(f32)
    result = own_mid + branch_scale * (own(part) + own(recv) + wide[layers - 1][OUT_M])

    d = 4 * quarter
    outs_m, outs_a = None, None
    for l, sums_m, sums_a in ((1, up_m, up_a), (0, low_m, low_a)):
        outs_m = finish(
            finish_mlp_body, "unpack_mlp", sidx, l, layers, sums_m.held, outs_m, [(quarter, 4 * d), (d, d)]
        )
        outs_a = finish(
            finish_attn_body, "unpack_attn", sidx, l, layers, sums_a.held, outs_a, [(quarter, 3 * d), (quarter, d)]
        )
    out_fc, out_proj = outs_m
    out_qkv, out_o = outs_a

    small = []
    for l in range(layers):
        qb, vb, ob, mb, fb, gain_c, shift_c = grads[l]
        small.append(
            jnp.concatenate(
                [quarter_of(norm_a[l][0]), gain_c, quarter_of(norm_a[l][1]), shift_c, qb, vb, ob, mb, fb]
            )
        )
    small = double_sum(jnp.stack(small))
    pair = lambda k: small[:, k * quarter : (k + 2) * quarter].reshape(layers, 2, quarter)
    return (
        result[None],
        grad_input[None],
        out_qkv,
        out_o,
        out_fc,
        out_proj,
        pair(0),
        pair(2),
        pair(4),
        pair(6),
        small[:, 8 * quarter :],
    )


def solution(mesh):
    in_specs = (
        P("rows", "seq", None),
        P("rows", "seq", None),
        P("rows", None),
        P(None, "seq", None),
        P(None, "seq", None),
        P(None, "seq", None),
        P(None, "seq", None),
        P(None, None, "seq"),
        P(None, None, "seq"),
        P(None, None, "seq"),
        P(None, None, "seq"),
        P(None, "seq"),
    )
    out_specs = (
        P("rows", "seq", None),
        P("rows", "seq", None),
        P(None, "seq", None),
        P(None, "seq", None),
        P(None, "seq", None),
        P(None, "seq", None),
        P(None, None, "seq"),
        P(None, None, "seq"),
        P(None, None, "seq"),
        P(None, None, "seq"),
        P(None, "seq"),
    )
    return jax.shard_map(
        on_device, mesh=mesh, in_specs=in_specs, out_specs=out_specs, check_vma=False
    )
```

```python
import functools
import math

import jax
import jax.numpy as jnp
from jax import lax
from jax.experimental import pallas as pl
from jax.experimental.pallas import tpu as pltpu
from jax.sharding import PartitionSpec as P

HD = 64
branch_scale = 48.0 ** (-0.5)
norm_eps = 1e-05
masked_score = -1e30
log2_e = math.log2(math.e)
MIB = 1 << 20
VMEM = 62
BLK = 256

f32 = jnp.float32
bf16 = jnp.bfloat16
STREAM = bf16

SWAP_CORE = [(s, s ^ 1) for s in range(4)]
SWAP_X = [(s, s ^ 2) for s in range(4)]
SWAP_BOTH = [(s, s ^ 3) for s in range(4)]


def dot_nn(a, b):
    return lax.dot_general(a, b, (((1,), (0,)), ((), ())), preferred_element_type=f32)


def dot_nt(a, b):
    return lax.dot_general(a, b, (((1,), (1,)), ((), ())), preferred_element_type=f32)


def dot_tn(a, b):
    return lax.dot_general(a, b, (((0,), (0,)), ((), ())), preferred_element_type=f32)


def call(body, name, sidx, grid, ins, outs, scratch, flops, vmem, exps=0):
    arrays = [a for a, _, _ in ins]
    in_specs = [
        pl.BlockSpec(memory_space=pl.ANY) if b is None else pl.BlockSpec(b, m) for _, b, m in ins
    ]
    out_specs = [
        pl.BlockSpec(memory_space=pl.ANY) if b is None else pl.BlockSpec(b, m) for _, b, m in outs
    ]
    out_shape = [s for s, _, _ in outs]
    nbytes = sum(a.size * a.dtype.itemsize for a in arrays)
    nbytes += sum(math.prod(s.shape) * s.dtype.itemsize for s in out_shape)
    return pl.pallas_call(
        body,
        name=name,
        grid_spec=pltpu.PrefetchScalarGridSpec(
            num_scalar_prefetch=1,
            grid=grid,
            in_specs=in_specs,
            out_specs=out_specs,
            scratch_shapes=scratch,
        ),
        out_shape=out_shape,
        compiler_params=pltpu.CompilerParams(
            dimension_semantics=("arbitrary",) * len(grid), vmem_limit_bytes=vmem * MIB
        ),
        cost_estimate=pl.CostEstimate(
            flops=int(flops), bytes_accessed=int(nbytes), transcendentals=int(exps)
        ),
    )(sidx, *arrays)


RING = [0, 2, 4, 6, 7, 5, 3, 1]
RING_NEXT = [(RING[i], RING[(i + 1) % 8]) for i in range(8)]
RING_PREV = [(b, a) for a, b in RING_NEXT]
RING_STEPS = [0, -1, 1, -2, 2, -3, 3, -4]


def ring_place():
    row = lax.axis_index("rows").astype(jnp.int32)
    return jnp.where(row % 2 == 0, row // 2, 7 - row // 2)


def place_index():
    s = lax.axis_index("seq").astype(jnp.int32)
    zero = jnp.int32(0)
    row = lax.axis_index("rows").astype(jnp.int32) if lax.axis_size("rows") == 8 else zero
    place = ring_place() if lax.axis_size("rows") == 8 else zero
    return jnp.stack([s, s // 2, s % 2, place, row % 2, row // 2])


def sds(shape, dtype):
    return jax.ShapeDtypeStruct(shape, dtype)


def whole(block):
    zeros = (0,) * len(block)
    return lambda i, m: zeros


def row_tile(i, m):
    return (i, 0)


def stack_tile(i, m):
    return (i ^ m[0], 0, 0)


def normed(x):
    centre = x - jnp.mean(x, axis=-1, keepdims=True)
    spread = jnp.mean(centre * centre, axis=-1, keepdims=True)
    rstd = lax.rsqrt(spread + norm_eps)
    return centre * rstd, rstd


def norm_back(x, grad, gain):
    unit, rstd = normed(x)
    inner = grad * gain
    mean_inner = jnp.mean(inner, axis=-1, keepdims=True)
    mean_prod = jnp.mean(inner * unit, axis=-1, keepdims=True)
    return rstd * (inner - mean_inner - unit * mean_prod), unit


GAIN_A, GAIN_C, SHIFT_A, SHIFT_C, OUT_A, OUT_M = range(6)


def row_of(ref, k):
    return ref[k : k + 1, :]


def lane_half(shape):
    return lax.broadcasted_iota(jnp.int32, shape, 1) // HD


def block_start(i):
    return BLK * (i * (i + 1) // 2)


class Mover:
    def __init__(self, sems):
        self.sems = sems
        self.used = 0

    def make(self, src, dst):
        cp = pltpu.make_async_copy(src, dst, self.sems.at[self.used])
        self.used += 1
        return cp

    def go(self, src, dst):
        cp = self.make(src, dst)
        cp.start()
        return cp


def wait_all(copies):
    for cp in copies:
        cp.wait()


def tile_of(i):
    return pl.ds(i * BLK, BLK)


def pieces_in(mover, refs, dst, first, rows):
    out = []
    for j, ref in enumerate(refs):
        where = pl.multiple_of((first ^ j) * rows, 16)
        out.append(mover.go(ref, dst.at[pl.ds(where, rows)]))
    return out


def add_up(ref, value, start):
    here = jnp.sum(value, axis=0, keepdims=True)
    if start:
        ref[...] = here
    else:
        ref[...] += here


def back_pair(pair, pairs, tokens, qkv, att, datt, lse, bias, starts, dqkv, dq_acc):
    blocks = tokens // BLK
    half = lane_half((BLK, 2 * HD))
    score_scale = HD ** (-0.5)
    scale = score_scale * log2_e
    pick_row = lax.broadcasted_iota(jnp.int32, (8, 2 * HD), 0)
    pick = jnp.where(lane_half((8, 2 * HD)) == pick_row, 1.0, 0.0)
    prod = datt[pair].astype(f32) * att[pair].astype(f32)
    delta = lax.dot_general(
        pick, prod, (((1,), (1,)), ((), ())), precision=lax.Precision.HIGHEST, preferred_element_type=f32
    )
    for j in range(blocks):
        first = j * BLK
        span = slice(first, first + BLK)
        rest = pl.ds(first, tokens - first)
        kj = qkv[pair + pairs, span, :]
        vj = qkv[pair + 2 * pairs, span, :]
        qq = qkv[pair, rest, :]
        dd = datt[pair, rest, :]
        width = tokens - first
        zero = jnp.zeros_like(kj)
        dks, dvs, dss, khs = [], [], [], []
        for h in range(2):
            kh = jnp.where(half == h, kj, zero)
            vh = jnp.where(half == h, vj, zero)
            t = dot_nt(kh, qq) * scale + bias[:, starts[j] : starts[j] + width]
            p = jnp.exp2(t - lse[pair, h : h + 1, first:])
            dp = dot_nt(vh, dd)
            ds = (p * (dp - delta[h : h + 1, first:])).astype(bf16)
            dvs.append(dot_nn(p.astype(bf16), dd))
            dks.append(dot_nn(ds, qq))
            dss.append(ds)
            khs.append(kh)
        dk = jnp.where(half == 0, dks[0], dks[1]) * score_scale
        dv = jnp.where(half == 0, dvs[0], dvs[1])
        dqkv[pair + pairs, span, :] = dk.astype(bf16)
        dqkv[pair + 2 * pairs, span, :] = dv.astype(bf16)
        dq = dot_tn(jnp.concatenate(dss, axis=0), jnp.concatenate(khs, axis=0))
        if j == 0:
            dq_acc[...] = dq
        else:
            dq_acc[first:, :] += dq
    dqkv[pair] = (dq_acc[...] * score_scale).astype(bf16)


def forward_pair(pair, pairs, blocks, qkv, bias, att, lse):
    half = lane_half((BLK, 2 * HD))
    scale = HD ** (-0.5) * log2_e
    for i in range(blocks):
        width = BLK * (i + 1)
        span = slice(i * BLK, (i + 1) * BLK)
        qb = qkv[pair, span, :]
        kk = qkv[pair + pairs, 0:width, :]
        vv = qkv[pair + 2 * pairs, 0:width, :]
        mixed, logs = [], []
        for h in range(2):
            qh = jnp.where(half == h, qb, jnp.zeros_like(qb))
            t = dot_nt(qh, kk) * scale + bias[:, block_start(i) : block_start(i) + width]
            top = jnp.max(t, axis=-1, keepdims=True)
            p = jnp.exp2(t - top)
            total = jnp.sum(p, axis=-1, keepdims=True)
            o = dot_nn(p.astype(bf16), vv)
            mixed.append(o / total)
            logs.append(jnp.broadcast_to(top + jnp.log2(total), (BLK, 2 * HD)))
        att[pair, span, :] = jnp.where(half == 0, mixed[0], mixed[1]).astype(bf16)
        turned = jnp.transpose(jnp.where(half == 0, logs[0], logs[1]))
        lse[pair, 0:1, span] = turned[0:1, :]
        lse[pair, 1:2, span] = turned[HD : HD + 1, :]


def attn_block_body(l, first, m, *refs):
    count = 1 if first else 3
    sources = refs[:count]
    wo0, wo1, w0, w1, w2, w3 = refs[count : count + 6]
    vec, prev, bias_row, drow, dcol = refs[count + 6 : count + 11]
    refs = refs[count + 11 :]
    if not first:
        x_out, refs = refs[0], refs[1:]
    ln_out, qkv_out, att_out, part_out, lse = refs[:5]
    bufs = refs[5 : 5 + count]
    (wo, w, lns, qkv, att, parts, bias, sems) = refs[5 + count :]
    tokens, d = lns.shape
    blocks = tokens // BLK
    pairs = att.shape[0]
    q = w0.shape[0]
    half = d // 2
    move = Mover(sems)
    c_w = pieces_in(move, (w0, w1, w2, w3), w, m[0], q)
    c_tiles = []
    for t in range(blocks):
        for ref, dst in zip(sources, bufs):
            src = ref.at[t ^ m[0]] if len(ref.shape) == 3 else ref.at[tile_of(t)]
            c_tiles.append(move.go(src, dst.at[tile_of(t)]))
    c_wo = pieces_in(move, (wo0.at[l], wo1), wo, m[1], q)
    for i in range(blocks):
        width = BLK * (i + 1)
        begin = i * BLK
        qpos = begin + lax.broadcasted_iota(jnp.int32, (BLK, width), 0)
        kpos = lax.broadcasted_iota(jnp.int32, (BLK, width), 1)
        same = dcol[begin : begin + BLK, :] == drow[:, :width]
        allowed = (kpos <= qpos) & same
        bias[:, block_start(i) : block_start(i) + width] = jnp.where(allowed, 0.0, masked_score)
    wait_all(c_w)
    wait_all(c_tiles)
    c_out = []
    mine = pl.ds(pl.multiple_of(m[1] * half, 128), half)
    for t in range(blocks):
        span = tile_of(t)
        if first:
            x = bufs[0][span, :].astype(f32)
        else:
            part = bufs[1][span, :].astype(f32) + bufs[2][span, :].astype(f32) + row_of(prev, OUT_M)
            x = bufs[0][span, :].astype(f32) + branch_scale * part
            bufs[0][span, :] = x.astype(STREAM)
            c_out.append(move.go(bufs[0].at[span], x_out.at[span]))
        unit, _ = normed(x)
        ln = (unit * row_of(vec, GAIN_A) + row_of(vec, SHIFT_A)).astype(bf16)
        lns[span, :] = ln
        c_out.append(move.go(lns.at[span, mine], ln_out.at[span]))
        row = (dot_nn(ln, w[...]) + bias_row[...]).astype(bf16)
        for k in range(3 * pairs):
            cols = slice(k * 2 * HD, (k + 1) * 2 * HD)
            qkv[k, span, :] = row[:, cols]
    for k in range(3 * pairs):
        c_out.append(move.go(qkv.at[k], qkv_out.at[k]))

    @pl.loop(0, pairs)
    def _(pair):
        forward_pair(pair, pairs, blocks, qkv, bias, att, lse)

    for k in range(pairs):
        c_out.append(move.go(att.at[k], att_out.at[k]))
    wait_all(c_wo)
    for t in range(blocks):
        span = tile_of(t)
        row = jnp.concatenate([att[k, span, :] for k in range(pairs)], axis=1)
        parts[span, :] = dot_nn(row, wo[...]).astype(bf16)
        c_out.append(move.go(parts.at[span], part_out.at[span]))
    wait_all(c_out)


def attn_block_forward(sidx, l, source, wo_pieces, pieces, vec, prev, bias, drow, dcol):
    first = len(source) == 1
    q, cols = pieces[0].shape
    d = 4 * q
    tokens = drow.shape[1]
    width = cols // 3
    pairs = width // (2 * HD)
    ins = [(a, None, None) for a in (*source, *wo_pieces, *pieces)]
    ins += [(a, a.shape, whole(a.shape)) for a in (vec, prev, bias, drow, dcol)]
    outs = [] if first else [(sds((tokens, d), STREAM), None, None)]
    outs += [
        (sds((tokens, d // 2), bf16), None, None),
        (sds((3 * pairs, tokens, 2 * HD), bf16), None, None),
        (sds((pairs, tokens, 2 * HD), bf16), None, None),
        (sds((tokens, d), bf16), None, None),
        (sds((pairs, 8, tokens), f32), (pairs, 8, tokens), whole((0, 0, 0))),
    ]
    blocks = tokens // BLK
    scratch = [pltpu.VMEM((tokens, d), a.dtype) for a in source]
    scratch += [
        pltpu.VMEM((width, d), bf16),
        pltpu.VMEM((d, cols), bf16),
        pltpu.VMEM((tokens, d), bf16),
        pltpu.VMEM((3 * pairs, tokens, 2 * HD), bf16),
        pltpu.VMEM((pairs, tokens, 2 * HD), bf16),
        pltpu.VMEM((tokens, d), bf16),
        pltpu.VMEM((BLK, block_start(blocks)), f32),
        pltpu.SemaphoreType.DMA((64,)),
    ]
    return call(
        functools.partial(attn_block_body, l, first),
        "attention_block",
        sidx,
        (1,),
        ins,
        outs,
        scratch,
        4 * tokens * tokens * width + 2 * tokens * d * (cols + width),
        VMEM,
        exps=tokens * tokens * pairs,
    )


def mlp_weights_in(move, l, m, refs, wf, wp):
    if len(refs) == 6:
        first = pieces_in(move, refs[:4], wf, m[0], refs[0].shape[0])
        return first, pieces_in(move, refs[4:], wp, m[1], refs[4].shape[0])
    keep, near, own = refs[0], refs[1], refs[2].at[l]
    q = keep.shape[0]
    deep, d = own.shape
    apart = len(refs) == 12
    first = pieces_in(move, (keep, near), wf, m[0], q)
    second = pieces_in(move, (own, refs[3]) if apart else (own,), wp, m[1], deep)
    far = refs[4:] if apart else refs[3:]
    n = len(far)
    part, more = q // 4, deep // 8
    for ref, t in zip(far, RING_STEPS):
        chunk = (m[3] + t + n) % n
        lanes = pl.ds(pl.multiple_of((chunk // 4) * d, 128), d)
        for src, who in ((0, 2), (ref.shape[0] - part, 3)):
            at = pl.multiple_of((m[0] ^ who) * q + (chunk % 4) * part, 16)
            first.append(move.go(ref.at[pl.ds(src, part)], wf.at[pl.ds(at, part), lanes]))
        if not apart:
            at = pl.multiple_of((1 - m[1]) * deep + chunk * more, 16)
            second.append(move.go(ref.at[pl.ds(part, more)], wp.at[pl.ds(at, more)]))
    return first, second


def gelu_and_slope(pre):
    root = math.sqrt(2.0 / math.pi)
    sq = pre * pre
    gate = 0.5 * jnp.tanh(pre * (root + root * 0.044715 * sq)) + 0.5
    rise = pre * (2.0 * root + 6.0 * root * 0.044715 * sq)
    return pre * gate, gate + gate * ((1.0 - gate) * rise)


def mlp_block_body(l, ahead, back, count, m, *refs):
    take = lambda k: (refs[:k], refs[k:])
    vec = prev = fcb = None
    sources, refs = take(3 if ahead else 0)
    (cot,), refs = take(1) if ahead and back else ((None,), refs)
    grads, refs = take(4 if back and not ahead else 0)
    (slope_in, act_in, ln_in), refs = take(3) if back and not ahead else ((None,) * 3, refs)
    weights, refs = take(count)
    if ahead:
        (vec, fcb), refs = take(2)
    else:
        (vec,), refs = take(1)
    if ahead:
        (mid_out, part_out), refs = take(2)
        if back:
            (own_out,), refs = take(1)
        else:
            (ln_out, act_out, slope_out), refs = take(3)
    if back:
        if not ahead:
            (g_out,), refs = take(1)
        (back_out, mine, other, send, sum_mlp, sum_pre), refs = take(6)
        if not ahead:
            (sum_gain, sum_shift), refs = take(2)
    b0, b1, b2, b3, wf, wp, lns, act, slope, dmlp, sems = refs
    tokens, d = b1.shape
    blocks = tokens // BLK
    hidden = wf.shape[1]
    q = d // 4
    move = Mover(sems)
    c_tiles = []
    if ahead:
        loads = list(zip(sources, (b0, b1, b2))) + ([(cot, b3)] if back else [])
    else:
        loads = list(zip(grads, (b0, b1, b2, b3)))
    c_wp = []
    if ahead:
        c_wf, c_wp = mlp_weights_in(move, l, m, weights, wf, wp)
    for t in range(blocks):
        for ref, dst in loads:
            src = ref.at[t ^ m[0]] if len(ref.shape) == 3 else ref.at[tile_of(t)]
            c_tiles.append(move.go(src, dst.at[tile_of(t)]))
    if not ahead:
        c_wf, c_wp = mlp_weights_in(move, l, m, weights, wf, wp)
        c_slope = [move.go(slope_in.at[tile_of(t)], slope.at[tile_of(t)]) for t in range(blocks)]
        c_late = [move.go(act_in, act.at[:, pl.ds(0, act_in.shape[1])]), move.go(ln_in, lns.at[:, pl.ds(0, d // 2)])]
    c_out = []
    n = len(loads)
    wide = hidden // 2
    for t in range(blocks):
        wait_all(c_tiles[n * t : n * t + n])
        span = tile_of(t)
        if ahead:
            part = b1[span, :].astype(f32) + b2[span, :].astype(f32) + row_of(vec, OUT_A)
            mid = b0[span, :].astype(f32) + branch_scale * part
            b0[span, :] = mid.astype(b0.dtype)
            c_out.append(move.go(b0.at[span], mid_out.at[span]))
            if back:

                @pl.when(m[0] == t)
                def _():
                    own_out[...] = mid

            unit, _ = normed(mid)
            ln = (unit * row_of(vec, GAIN_C) + row_of(vec, SHIFT_C)).astype(bf16)
            lns[span, :] = ln
            if t == 0:
                wait_all(c_wf)
            value, rise = gelu_and_slope(dot_nn(ln, wf[...]) + fcb[...])
            low = value.astype(bf16)
            act[span, :] = low
            if not back:
                slope[span, :] = rise.astype(bf16)
                cols = pl.ds(pl.multiple_of(m[1] * (d // 2), 128), d // 2)
                c_out.append(move.go(lns.at[span, cols], ln_out.at[span]))
                cols = pl.ds(pl.multiple_of(m[1] * wide, 128), wide)
                c_out.append(move.go(act.at[span, cols], act_out.at[span]))
                c_out.append(move.go(slope.at[span], slope_out.at[span]))
            if t == 0:
                wait_all(c_wp)
            b1[span, :] = dot_nn(low, wp[...]).astype(bf16)
            c_out.append(move.go(b1.at[span], part_out.at[span]))
        if back:
            if ahead:
                g = b3[span, :].astype(f32)
            else:
                if t == 0:
                    wait_all(c_wp)
                wait_all(c_slope[t : t + 1])
                rise = slope[span, :].astype(f32)
                grad = b2[span, :].astype(f32) + b3[span, :].astype(f32)
                part, unit = norm_back(b1[span, :].astype(f32), grad, row_of(vec, GAIN_A))
                add_up(sum_gain, grad * unit, t == 0)
                add_up(sum_shift, grad, t == 0)
                g = b0[span, :].astype(f32) + part
                b0[span, :] = g.astype(b0.dtype)
                c_out.append(move.go(b0.at[span], g_out.at[span]))
            low = (branch_scale * g).astype(bf16)
            dmlp[span, :] = low
            add_up(sum_mlp, low.astype(f32), t == 0)
            dpre = (dot_nt(low, wp[...]) * rise).astype(bf16)
            slope[span, :] = dpre
            add_up(sum_pre, dpre.astype(f32), t == 0)
            if t == 0 and not ahead:
                wait_all(c_wf)
            b2[span, :] = dot_nt(dpre, wf[...]).astype(bf16)
            c_out.append(move.go(b2.at[span], back_out.at[span]))
    if back:
        y = m[4]
        if not ahead:
            wait_all(c_late)
            turned = jnp.transpose(act[:, 0:wide])
        else:
            turned = jnp.transpose(jnp.where(m[1] == 0, act[:, 0:wide], act[:, wide:]))
        grad = dot_nn(turned, dmlp[...]).astype(bf16)
        h = grad.shape[0] // 2
        mine[0:h, :] = jnp.where(y == 0, grad[:h], grad[h:])
        other[0:h, :] = jnp.where(y == 0, grad[h:], grad[:h])
        half = d // 2
        if not ahead:
            turned = jnp.transpose(lns[:, 0:half])
        else:
            turned = jnp.transpose(jnp.where(m[1] == 0, lns[:, 0:half], lns[:, half:]))
        sides = [dot_nn(turned, slope[:, i * d : (i + 1) * d]).astype(bf16) for i in range(2)]
        for i, here in enumerate((mine, other)):
            side = jnp.where(y == i, sides[0], sides[1])
            here[h : h + q, :] = jnp.where(m[2] == 0, side[:q], side[q:])
            send[i * q : (i + 1) * q, :] = jnp.where(m[2] == 0, side[q:], side[:q])
    wait_all(c_out)


def mlp_block(sidx, l, vec, weights, ahead=None, back=None, fcb=None):
    d = vec.shape[1]
    if ahead is not None:
        tokens = ahead[1].shape[0]
        hidden = fcb.shape[1]
        sources = list(ahead) + ([back[0]] if back else [])
        types = [STREAM if ahead[0].ndim == 2 else ahead[0].dtype, bf16, bf16, bf16]
        vectors_in = [vec, fcb]
    else:
        tokens, hidden = back[4].shape
        sources = list(back)
        types = [back[0].dtype, back[1].dtype, bf16, bf16]
        vectors_in = [vec]
    q = d // 4
    ins = [(a, None, None) for a in sources + list(weights)]
    ins += [(a, a.shape, whole(a.shape)) for a in vectors_in]
    stay = lambda shape, dtype: (sds(shape, dtype), shape, whole(shape))
    away = lambda shape, dtype: (sds(shape, dtype), None, None)
    outs = []
    if ahead is not None:
        outs += [away((tokens, d), STREAM), away((tokens, d), bf16)]
        if back:
            outs += [stay((BLK, d), f32)]
        else:
            outs += [
                away((tokens, d // 2), bf16),
                away((tokens, hidden // 2), bf16),
                away((tokens, hidden), bf16),
            ]
    if back:
        if ahead is None:
            outs += [away((tokens, d), back[0].dtype)]
        outs += [away((tokens, d), bf16)]
        outs += [stay((3 * q, d), bf16)] * 2 + [stay((2 * q, d), bf16)]
        outs += [stay((1, d), f32), stay((1, hidden), f32)]
        if ahead is None:
            outs += [stay((1, d), f32)] * 2
    scratch = [pltpu.VMEM((tokens, d), t) for t in types]
    scratch += [
        pltpu.VMEM((d, hidden), bf16),
        pltpu.VMEM((hidden, d), bf16),
        pltpu.VMEM((tokens, d), bf16),
        pltpu.VMEM((tokens, hidden), bf16),
        pltpu.VMEM((tokens, hidden), bf16),
        pltpu.VMEM((tokens, d), bf16),
        pltpu.SemaphoreType.DMA((96,)),
    ]
    return call(
        functools.partial(mlp_block_body, l, ahead is not None, bool(back), len(weights)),
        "mlp_block" + ("_forward" if ahead is not None else "") + ("_backward" if back else ""),
        sidx,
        (1,),
        ins,
        outs,
        scratch,
        (4 * bool(ahead is not None) + 8 * bool(back)) * tokens * d * hidden,
        VMEM,
        exps=tokens * hidden,
    )


def attn_block_back_body(l, m, *refs):
    (g_in, mid_in, p_in, r_in, wo0, wo1, qkv_in, att_in, ln_in, w0, w1, w2, w3) = refs[:13]
    (vec, drow, dcol, lse) = refs[13:17]
    (gm_out, part_out, mine, other, to_core) = refs[17:22]
    (sum_attn, sum_gain, sum_shift, sum_qkv) = refs[22:26]
    (gs, mids, ps, rs, wo, qkv, att, lns, w, dattn, datt, dqkv, bias, dq_acc, sems) = refs[26:]
    tokens, d = mids.shape
    blocks = tokens // BLK
    pairs = att.shape[0]
    q = w0.shape[0]
    move = Mover(sems)
    c_wo = pieces_in(move, (wo0.at[l], wo1), wo, m[1], q)
    c_tiles = []
    loads = [(g_in, gs), (mid_in, mids), (p_in, ps), (r_in, rs)]
    for t in range(blocks):
        for ref, dst in loads:
            src = ref.at[t ^ m[0]] if len(ref.shape) == 3 else ref.at[tile_of(t)]
            c_tiles.append(move.go(src, dst.at[tile_of(t)]))
    c_qkv = [move.go(qkv_in, qkv), move.go(att_in, att)]
    c_w = pieces_in(move, (w0, w1, w2, w3), w, m[0], q)
    half = d // 2
    c_ln = [move.go(ln_in, lns)]

    starts = [sum(tokens - BLK * a for a in range(j)) for j in range(blocks)]
    for j in range(blocks):
        width = tokens - j * BLK
        first = j * BLK
        kpos = lax.broadcasted_iota(jnp.int32, (BLK, width), 0)
        qpos = lax.broadcasted_iota(jnp.int32, (BLK, width), 1)
        same = dcol[first : first + BLK, :] == drow[:, first:]
        allowed = (kpos <= qpos) & same
        bias[:, starts[j] : starts[j] + width] = jnp.where(allowed, 0.0, masked_score)

    wait_all(c_wo)
    c_out = []
    for t in range(blocks):
        wait_all(c_tiles[4 * t : 4 * t + 4])
        span = tile_of(t)
        grad = ps[span, :].astype(f32) + rs[span, :].astype(f32)
        part, unit = norm_back(mids[span, :].astype(f32), grad, row_of(vec, GAIN_C))
        add_up(sum_gain, grad * unit, t == 0)
        add_up(sum_shift, grad, t == 0)
        gm = gs[span, :].astype(f32) + part
        gs[span, :] = gm.astype(gs.dtype)
        c_out.append(move.go(gs.at[span], gm_out.at[span]))
        low = (branch_scale * gm).astype(bf16)
        dattn[span, :] = low
        add_up(sum_attn, low.astype(f32), t == 0)
        heads = dot_nt(low, wo[...]).astype(bf16)
        for k in range(pairs):
            datt[k, span, :] = heads[:, k * 2 * HD : (k + 1) * 2 * HD]

    wait_all(c_qkv)

    @pl.loop(0, pairs)
    def _(pair):
        back_pair(pair, pairs, tokens, qkv, att, datt, lse, bias, starts, dqkv, dq_acc)

    wait_all(c_w)
    for t in range(blocks):
        span = tile_of(t)
        row = jnp.concatenate([dqkv[k, span, :] for k in range(3 * pairs)], axis=1)
        ps[span, :] = dot_nt(row, w[...]).astype(bf16)
        c_out.append(move.go(ps.at[span], part_out.at[span]))
        add_up(sum_qkv, row.astype(f32), t == 0)

    wait_all(c_ln)
    quart = q // 2
    y = m[4]
    turned = jnp.concatenate([jnp.transpose(att[k]) for k in range(pairs)], axis=0)
    left = jnp.where(m[1] == 0, turned[:q], turned[q : 2 * q])
    g_o = dot_nn(left, dattn[...]).astype(bf16)
    for i in range(2):
        cols = slice(i * half, (i + 1) * half)
        a, b = g_o[:quart, cols], g_o[quart:, cols]
        mine[i * quart : (i + 1) * quart, :] = jnp.where(y == 0, a, b)
        other[i * quart : (i + 1) * quart, :] = jnp.where(y == 0, b, a)
    turned = jnp.transpose(lns[...])
    for p in range(3):
        right = jnp.concatenate([dqkv[p * pairs + k] for k in range(pairs)], axis=1)
        grad = dot_nn(turned, right).astype(bf16)
        keep = jnp.where(m[2] == 0, grad[:q], grad[q:])
        send = jnp.where(m[2] == 0, grad[q:], grad[:q])
        at = (2 + p) * quart
        mine[at : at + quart, :] = jnp.where(y == 0, keep[:quart], keep[quart:])
        other[at : at + quart, :] = jnp.where(y == 0, keep[quart:], keep[:quart])
        at = p * quart
        to_core[at : at + quart, :] = jnp.where(y == 0, send[:quart], send[quart:])
        at += 3 * quart
        to_core[at : at + quart, :] = jnp.where(y == 0, send[quart:], send[:quart])
    wait_all(c_out)


def attn_block_backward(sidx, l, g, mid, part, recv, wo_pieces, qkv, att, ln_a, pieces, vec, drow, dcol, lse):
    tokens, d = mid.shape
    q, cols = pieces[0].shape
    width = cols // 3
    pairs = width // (2 * HD)
    ins = [(a, None, None) for a in (g, mid, part, recv, *wo_pieces, qkv, att, ln_a, *pieces)]
    ins += [(a, a.shape, whole(a.shape)) for a in (vec, drow, dcol, lse)]
    stay = lambda shape, dtype: (sds(shape, dtype), shape, whole(shape))
    outs = [
        (sds((tokens, d), STREAM), None, None),
        (sds((tokens, d), bf16), None, None),
        stay((5 * q // 2, width), bf16),
        stay((5 * q // 2, width), bf16),
        stay((3 * q, width), bf16),
        stay((1, d), f32),
        stay((1, d), f32),
        stay((1, d), f32),
        stay((1, cols), f32),
    ]
    blocks = tokens // BLK
    wide = (tokens, 2 * HD)
    scratch = [
        pltpu.VMEM((tokens, d), g.dtype),
        pltpu.VMEM((tokens, d), mid.dtype),
        pltpu.VMEM((tokens, d), bf16),
        pltpu.VMEM((tokens, d), bf16),
        pltpu.VMEM((width, d), bf16),
        pltpu.VMEM((3 * pairs,) + wide, bf16),
        pltpu.VMEM((pairs,) + wide, bf16),
        pltpu.VMEM((tokens, d // 2), bf16),
        pltpu.VMEM((d, cols), bf16),
        pltpu.VMEM((tokens, d), bf16),
        pltpu.VMEM((pairs,) + wide, bf16),
        pltpu.VMEM((3 * pairs,) + wide, bf16),
        pltpu.VMEM((BLK, block_start(blocks)), f32),
        pltpu.VMEM(wide, f32),
        pltpu.SemaphoreType.DMA((64,)),
    ]
    return call(
        functools.partial(attn_block_back_body, l),
        "attention_block_backward",
        sidx,
        (1,),
        ins,
        outs,
        scratch,
        10 * tokens * tokens * width,
        VMEM,
        exps=tokens * tokens * pairs,
    )


def add_rows(ref, value, start):
    @pl.when(start)
    def _():
        ref[...] = jnp.zeros_like(ref)

    ref[...] += jnp.sum(value, axis=0, keepdims=True)


def input_back_body(m, gm_ref, x_ref, p_ref, r_ref, vec, out_ref, sum_gain, sum_shift):
    tile = pl.program_id(0)
    grad = p_ref[...].astype(f32) + r_ref[...].astype(f32)
    part, unit = norm_back(x_ref[0].astype(f32), grad, row_of(vec, GAIN_A))
    add_rows(sum_gain, grad * unit, tile == 0)
    add_rows(sum_shift, grad, tile == 0)

    @pl.when(tile == m[0])
    def _():
        out_ref[...] = gm_ref[...].astype(f32) + part


def input_backward(sidx, gm, x, part, recv, vec):
    tokens, depth = gm.shape
    tile = (BLK, depth)
    ins = [(gm, tile, row_tile), (x, (1, BLK, depth), stack_tile)]
    ins += [(a, tile, row_tile) for a in (part, recv)]
    ins.append((vec, vec.shape, whole(vec.shape)))
    outs = [(sds((BLK, depth), f32), tile, whole((0, 0)))]
    outs += [(sds((1, depth), f32), (1, depth), whole((0, 0)))] * 2
    return call(input_back_body, "input_backward", sidx, (tokens // BLK,), ins, outs, [], tokens * depth, 16)


def swap(a, perm):
    return lax.ppermute(a, "seq", perm)


def split_body(m, qkv_ref, fc_ref, o_ref, qkv_keep, qkv_send, fc_keep, fc_send, o_out):
    core = m[2]
    o_out[...] = o_ref[0]
    q = qkv_ref.shape[1]
    pair = 2 * q
    for p in range(3):
        own, other = [], []
        for xside in range(2):
            col = (2 * p + xside) * pair
            both = qkv_ref[0, :, col : col + pair]
            own.append(jnp.where(core == 0, both[:, :q], both[:, q:]))
            other.append(jnp.where(core == 0, both[:, q:], both[:, :q]))
        qkv_keep[:, p * pair : (p + 1) * pair] = jnp.concatenate(own, axis=1)
        qkv_send[:, p * pair : (p + 1) * pair] = jnp.concatenate(other, axis=1)
    d = fc_ref.shape[2] // 4
    for xside in range(2):
        one = fc_ref[0, :, 2 * xside * d : (2 * xside + 1) * d]
        two = fc_ref[0, :, (2 * xside + 1) * d : (2 * xside + 2) * d]
        fc_keep[:, xside * d : (xside + 1) * d] = jnp.where(core == 0, one, two)
        fc_send[:, xside * d : (xside + 1) * d] = jnp.where(core == 0, two, one)


def split_columns(sidx, w_qkv, w_fc, w_o, l):
    _, rows, cols = w_qkv.shape
    hidden = w_fc.shape[2]
    at = lambda i, m: (l, 0, 0)
    depth = w_o.shape[2]
    ins = [(w_qkv, (1, rows, cols), at), (w_fc, (1, rows, hidden), at), (w_o, (1, rows, depth), at)]
    outs = []
    for width in (cols // 2, cols // 2, hidden // 2, hidden // 2, depth):
        outs.append((sds((rows, width), bf16), (rows, width), whole((0, 0))))
    return call(split_body, "split_columns", sidx, (1,), ins, outs, [], rows * cols, VMEM)


def column_pieces(keep, send):
    return [keep, swap(send, SWAP_CORE), swap(keep, SWAP_X), swap(send, SWAP_BOTH)]


def row_pieces(w):
    return [w, swap(w, SWAP_X)]


def far_piece_body(l, m, w_fc, *refs):
    straight, across, sems = refs[-3:]
    part, d = across.shape
    group, half = m[3] % 4, m[3] // 4
    move = Mover(sems)
    rows = pl.ds(pl.multiple_of(group * part, 16), part)
    here = pl.ds(pl.multiple_of((2 * half + m[2]) * d, 128), d)
    there = pl.ds(pl.multiple_of((2 * half + 1 - m[2]) * d, 128), d)
    copies = [
        move.go(w_fc.at[l, rows, here], straight.at[pl.ds(0, part)]),
        move.go(w_fc.at[l, rows, there], across),
    ]
    if len(refs) == 4:
        more = d // 8
        rows = pl.ds(pl.multiple_of(m[3] * more, 16), more)
        copies.append(move.go(refs[0].at[l, rows], straight.at[pl.ds(part, more)]))
    wait_all(copies)


def far_piece(sidx, w_fc, l, *w_proj):
    _, q, hidden = w_fc.shape
    d, part = hidden // 4, q // 4
    first = (part + len(w_proj) * (d // 8), d)
    ins = [(a, None, None) for a in (w_fc, *w_proj)]
    outs = [(sds(sh, bf16), sh, whole(sh)) for sh in (first, (part, d))]
    straight, across = call(
        functools.partial(far_piece_body, l), "far_piece", sidx, (1,), ins, outs, [pltpu.SemaphoreType.DMA((3,))], 0, VMEM
    )
    return swap(straight, SWAP_X), swap(across, SWAP_BOTH)


def ring_pass(held, t):
    if held is None:
        return []
    on = lax.ppermute(held[max(0, len(held) - 2)], "rows", RING_NEXT)
    if t == 4:
        new = [on]
    else:
        new = [on, lax.ppermute(held[-1], "rows", RING_PREV)]
    held += new
    return new


def gather_rows(a, far):
    return jnp.stack([a, swap(a, SWAP_CORE), far, swap(far, SWAP_CORE)])


SWAP_Y = [(r, r ^ 1) for r in range(8)]
SWAP_Z = [None] + [[(r, r ^ (2 * d)) for r in range(8)] for d in range(1, 4)]


def join_attn(own, recv, at):
    n = own.shape[0] // 5
    bit = lambda k: own[k * n : (k + 1) * n, :]
    got = lambda k: recv[at + k * n : at + (k + 1) * n, :]
    pairs = [(bit(0), bit(1)), (bit(2), bit(3)), (bit(4), got(0)), (got(1), got(2))]
    return [jnp.concatenate(p, axis=1) for p in pairs]


def pack_attn_body(which, m, own, recv, out):
    n = out.shape[0] // 4
    for k, rows in enumerate(join_attn(own, recv, which * 3 * n)):
        out[k * n : (k + 1) * n, :] = rows


def pack_attn(sidx, own, recv, which):
    shape = (4 * (own.shape[0] // 5), 2 * own.shape[1])
    ins = [(a, a.shape, whole(a.shape)) for a in (own, recv)]
    outs = [(sds(shape, bf16), shape, whole(shape))]
    return call(
        functools.partial(pack_attn_body, which), "pack_attn", sidx, (1,), ins, outs, [], 0, 16
    )[0]


def pack_mlp(own, recv, which):
    q = recv.shape[0] // 2
    return jnp.concatenate([own, recv[which * q : (which + 1) * q]])


def add_low(a, b):
    return (a.astype(f32) + b.astype(f32)).astype(bf16)


def total_low(first, rest):
    return (first.astype(f32) + sum(r.astype(f32) for r in rest)).astype(bf16)


def fill_mlp(full, own, recv, got):
    cut = own.shape[0]
    full[0:cut, :] = add_low(own[...], got[0:cut, :])
    full[cut:, :] = add_low(recv[0 : full.shape[0] - cut, :], got[cut : full.shape[0], :])


def fill_attn(full, own, recv, got):
    n = full.shape[0] // 4
    for k, rows in enumerate(join_attn(own, recv, 0)):
        full[k * n : (k + 1) * n, :] = add_low(rows, got[k * n : (k + 1) * n, :])


def quarter_at(full, m, d):
    n = full.shape[0] // 4
    return full[pl.ds(pl.multiple_of((m[5] ^ d) * n, 16), n), :]


def split_mlp_body(m, own, recv, got, *refs):
    outs, full = refs[:-1], refs[-1]
    fill_mlp(full, own, recv, got)
    for d, out in enumerate(outs):
        out[...] = quarter_at(full, m, d)


def split_attn_body(m, own, recv, got, *refs):
    outs, full = refs[:-1], refs[-1]
    fill_attn(full, own, recv, got)
    for d, out in enumerate(outs):
        out[...] = quarter_at(full, m, d)


def mlp_total_attn_split_body(m, first, g1, g2, g3, own, recv, got, total, keep, s1, s2, s3, full):
    acc = total_low(first[...], [g1[...], g2[...], g3[...]])
    total[...] = acc
    n = acc.shape[0]
    fill_attn(full, own, recv, got)
    keep[...] = quarter_at(full, m, 0)
    for d, out in enumerate((s1, s2, s3)):
        out[0:n, :] = acc
        out[n:, :] = quarter_at(full, m, d + 1)


def attn_total_mlp_split_body(m, first, g1, g2, g3, own, recv, got, total, keep, s1, s2, s3, full):
    n = g1.shape[0] - first.shape[0]
    acc = total_low(first[...], [g[n:, :] for g in (g1, g2, g3)])
    total[...] = acc
    fill_mlp(full, own, recv, got)
    keep[...] = quarter_at(full, m, 0)
    for d, out in enumerate((s1, s2, s3)):
        out[0:n, :] = quarter_at(full, m, d + 1)
        out[n:, :] = acc


def sum_kernel(body, name, sidx, arrays, shapes, scratch=None):
    ins = [(a, a.shape, whole(a.shape)) for a in arrays]
    outs = [(sds(sh, bf16), sh, whole(sh)) for sh in shapes]
    extra = [] if scratch is None else [pltpu.VMEM(scratch, bf16)]
    return call(body, name, sidx, (1,), ins, outs, extra, 0, 16)


def along_y(a):
    return lax.ppermute(a, "rows", SWAP_Y)


def along_z(arrays):
    return [lax.ppermute(a, "rows", SWAP_Z[d + 1]) for d, a in enumerate(arrays)]


def halves(m, near, far, at, n):
    def quarter(k):
        rows = pl.ds(pl.multiple_of(at + (k ^ m[5]) * n, 16), n)
        a, b = near[rows, :].astype(f32), far[rows, :].astype(f32)
        return jnp.where(m[4] == 0, a, b), jnp.where(m[4] == 0, b, a)

    return [quarter(k) for k in range(4)]


def finish_mlp_body(at, m, near, far, *refs):
    out_fc, out_proj = refs[-2:]
    q, d = out_fc.shape[1], out_proj.shape[2]
    parts = halves(m, near, far, at, q)
    for h in range(2):
        for k in range(2):
            row = (2 * h + k) * q
            out_proj[0, row : row + q, :] = parts[k][h]
        for c in range(2):
            col = (2 * h + c) * d
            out_fc[0, :, col : col + d] = jnp.where(m[2] == c, parts[2][h], parts[3][h])


def finish_attn_body(at, m, near, far, *refs):
    out_qkv, out_o = refs[-2:]
    q, d = out_o.shape[1:]
    n, width = q // 2, d // 2
    parts = halves(m, near, far, at, n)
    for h in range(2):
        span = slice(h * n, (h + 1) * n)
        out_o[0, span, :] = parts[0][h]
        bits = [b for k in range(1, 4) for b in (parts[k][h][:, :width], parts[k][h][:, width:])]
        for p in range(3):
            keep, recv = bits[p], bits[3 + p]
            for xside in range(2):
                a = keep[:, xside * q : (xside + 1) * q]
                b = recv[:, xside * q : (xside + 1) * q]
                col = (2 * p + xside) * width
                out_qkv[0, span, col : col + width] = jnp.concatenate(
                    [jnp.where(m[2] == 0, a, b), jnp.where(m[2] == 0, b, a)], axis=1
                )


def finish(body, name, sidx, l, layers, held, before, shapes):
    args = list(held)
    in_specs = [pl.BlockSpec(a.shape, lambda i, m: (0, 0)) for a in held]
    aliases = {}
    if before is not None:
        aliases = {1 + len(args) + k: k for k in range(len(before))}
        args += list(before)
        in_specs += [pl.BlockSpec(memory_space=pl.ANY)] * len(before)
    size = sum(math.prod(sh) for sh in shapes)
    return pl.pallas_call(
        body,
        name=name,
        grid_spec=pltpu.PrefetchScalarGridSpec(
            num_scalar_prefetch=1,
            grid=(1,),
            in_specs=in_specs,
            out_specs=[pl.BlockSpec((1,) + sh, lambda i, m: (l, 0, 0)) for sh in shapes],
        ),
        out_shape=[sds((layers,) + sh, f32) for sh in shapes],
        input_output_aliases=aliases,
        compiler_params=pltpu.CompilerParams(vmem_limit_bytes=32 * MIB),
        cost_estimate=pl.CostEstimate(flops=size, bytes_accessed=6 * size, transcendentals=0),
    )(sidx, *args)


def pair_row(a, step):
    n = lax.axis_size("rows")
    return lax.ppermute(a, "rows", [(r, r ^ step) for r in range(n)])


def vectors_body(m, near, far, wide, qkv_bias, fcb):
    layers = near.shape[1]
    q = near.shape[3]
    for l in range(layers):
        full = []
        for k in range(4):
            core = (k % 2) ^ m[2]
            full.append(jnp.where(m[1] == k // 2, near[core, l], far[core, l]).astype(f32))
        every = jnp.concatenate(full, axis=1)
        wide[l, 0:4, :] = every[0:4]
        wide[l, 4:6, :] = every[6:8]
        wide[l, 6:8, :] = jnp.zeros((2, 4 * q), f32)
        here = [jnp.where(m[2] == 0, full[2 * xside], full[2 * xside + 1]) for xside in range(2)]
        pick = lambda r: [a[r : r + 1] for a in here]
        none = jnp.zeros((1, 2 * q), f32)
        qkv_bias[l] = jnp.concatenate(pick(4) + [none] + pick(5), axis=1)
        rest = [a[r : r + 1] for a in here for r in range(8, a.shape[0])]
        fcb[l] = jnp.concatenate(rest, axis=1)


def pack_small_body(q, m, *refs):
    out = refs[-1]
    count = len(refs[:-1]) // out.shape[0]
    for l in range(out.shape[0]):
        sum_qkv, attn, mlp, pre, gain_c, shift_c, gain_a, shift_a = refs[l * count : (l + 1) * count]

        def mine(ref):
            bits = [ref[:, k * q : (k + 1) * q] for k in range(4)]
            return jnp.where(
                m[1] == 0, jnp.where(m[2] == 0, bits[0], bits[1]), jnp.where(m[2] == 0, bits[2], bits[3])
            )

        side = lambda ref, at, n: jnp.where(m[1] == 0, ref[:, at : at + n], ref[:, at + n : at + 2 * n])
        row = [mine(gain_a), mine(gain_c), mine(shift_a), mine(shift_c)]
        row += [side(sum_qkv, 0, q), side(sum_qkv, 4 * q, q), mine(attn), mine(mlp), side(pre, 0, 4 * q)]
        out[l : l + 1, :] = jnp.concatenate(row, axis=1)


def pack_small(sidx, small, q):
    arrays = [a for row in small for a in row]
    ins = [(a, a.shape, whole(a.shape)) for a in arrays]
    shape = (len(small), 12 * q)
    outs = [(sds(shape, f32), shape, whole(shape))]
    return call(functools.partial(pack_small_body, q), "pack_small", sidx, (1,), ins, outs, [], 0, 16)[0]


def spread_small_body(q, m, all_ref, gain, shift, qv, outb, fcb):
    for l in range(all_ref.shape[0]):
        for k, ref in enumerate((gain, shift, qv, outb)):
            for i in range(2):
                at = (2 * k + i) * q
                ref[l, i : i + 1, :] = all_ref[l : l + 1, at : at + q]
    fcb[...] = all_ref[:, 8 * q :]


def spread_small(sidx, sums, q):
    layers = sums.shape[0]
    ins = [(sums, sums.shape, whole(sums.shape))]
    shapes = [(layers, 2, q)] * 4 + [(layers, 4 * q)]
    outs = [(sds(sh, f32), sh, whole(sh)) for sh in shapes]
    return call(functools.partial(spread_small_body, q), "spread_small", sidx, (1,), ins, outs, [], 0, 16)


def gather_vectors(norm_gain, norm_bias, qv_bias, out_bias, fc_bias):
    layers, _, q = norm_gain.shape
    mine = jnp.concatenate(
        [norm_gain, norm_bias, qv_bias, out_bias, fc_bias.reshape(layers, -1, q)], axis=1
    )
    near = jnp.stack([mine, swap(mine, SWAP_CORE)])
    return near, swap(near, SWAP_X)


def vectors(sidx, near, far):
    _, layers, rows, q = near.shape
    ins = [(a, a.shape, whole(a.shape)) for a in (near, far)]
    hidden = 2 * (rows - 8) * q
    outs = []
    for shape in ((layers, 8, 4 * q), (layers, 1, 6 * q), (layers, 1, hidden)):
        outs.append((sds(shape, f32), shape, whole(shape)))
    return call(vectors_body, "vectors", sidx, (1,), ins, outs, [], near.size, 16)


def on_device(
    block_input,
    output_cotangent,
    doc_ids,
    w_qkv,
    w_o,
    w_fc,
    w_proj,
    norm_gain,
    norm_bias,
    qv_bias,
    out_bias,
    fc_bias,
):
    sidx = place_index()
    s, xi, core = sidx[0], sidx[1], sidx[2]
    layers = w_qkv.shape[0]
    quarter = w_qkv.shape[1]
    tokens = doc_ids.shape[1]
    drow = doc_ids
    dcol = doc_ids.reshape(tokens, 1)

    def pin(outs, *groups):
        flat, tree = jax.tree.flatten((outs, groups))
        outs, groups = jax.tree.unflatten(tree, lax.optimization_barrier(flat))
        return (outs,) + tuple(groups)

    ringed = lax.axis_size("rows") == 8
    pieces_0 = far_piece(sidx, w_fc, 0, w_proj) if ringed else ()
    x_far = swap(block_input[0], SWAP_X)
    keep, send, fc_keep, fc_send, o = split_columns(sidx, w_qkv, w_fc, w_o, 0)
    wq = [column_pieces(keep, send), None]
    fc_near = swap(fc_send, SWAP_CORE)
    if ringed:
        near_0 = [fc_keep, fc_near, w_proj]
    else:
        near_0 = column_pieces(fc_keep, fc_send) + row_pieces(w_proj[0])
    params = gather_vectors(norm_gain, norm_bias, qv_bias, out_bias, fc_bias)
    later = (w_qkv, w_fc, w_o)
    later, pieces_0, x_far, o, near_0 = pin(later, pieces_0, x_far, o, near_0)
    far_0 = [jnp.concatenate(pieces_0)] if ringed else None
    ring_pass(far_0, 1)
    xs = gather_rows(block_input[0], x_far)
    keep, send, fc_keep, fc_send, o_next = split_columns(sidx, *later, 1)
    fc_near = swap(fc_send, SWAP_CORE)
    later, far_0, xs, params, fc_near, keep, send, o_next = pin(
        later, far_0, xs, params, fc_near, keep, send, o_next
    )
    wide, qkv_bias, fcb = vectors(sidx, *params)
    ring_pass(far_0, 2)
    pieces_1 = far_piece(sidx, later[1], 1) if ringed else ()
    far_0, wide, wq[0][2], o = pin(far_0, wide, wq[0][2], o)
    wo = [[w_o, swap(o, SWAP_X)], None]
    ring_pass(far_0, 3)
    far_0, pieces_1, wq[0] = pin(far_0, pieces_1, wq[0])
    far_1 = [jnp.concatenate(pieces_1)] if ringed else None
    ring_pass(far_0, 4)
    ring_pass(far_1, 1)
    xs, far_0, far_1, wo[0], keep, send, o_next = pin(xs, far_0, far_1, wo[0], keep, send, o_next)
    wq[1] = column_pieces(keep, send)
    wo[1] = [w_o, swap(o_next, SWAP_X)]
    if ringed:
        near_1 = [fc_keep, fc_near, w_proj, swap(w_proj[1], SWAP_X)]
    else:
        near_1 = column_pieces(fc_keep, fc_send) + row_pieces(w_proj[1])

    outs = attn_block_forward(sidx, 0, (xs,), wo[0], wq[0], wide[0], wide[0], qkv_bias[0], drow, dcol)
    ring_pass(far_1, 2)
    outs, far_1, wq[1] = pin(outs, far_1, wq[1])
    ln_a, qkv, att, part, lse = outs
    save_a = [(xs, ln_a, qkv, att, lse)]
    recv = swap(part, SWAP_CORE)
    outs = mlp_block(sidx, 0, wide[0], near_0 + (far_0 or []), ahead=(xs, part, recv), fcb=fcb[0])
    ring_pass(far_1, 3)
    outs, wo[1], cot_far, far_1 = pin(outs, wo[1], swap(output_cotangent[0], SWAP_X), far_1)
    cot = gather_rows(output_cotangent[0], cot_far)
    mid, part, ln_c, act, slope = outs
    save_m = (ln_c, act, slope)
    mids = [mid]
    recv = swap(part, SWAP_CORE)
    outs = attn_block_forward(
        sidx, 1, (mid, part, recv), wo[1], wq[1], wide[1], wide[0], qkv_bias[1], drow, dcol
    )
    ring_pass(far_1, 4)
    outs, near_1, far_1, cot = pin(outs, near_1, far_1, cot)
    x, ln_a, qkv, att, part, lse = outs
    save_a.append((x, ln_a, qkv, att, lse))
    recv = swap(part, SWAP_CORE)
    outs = mlp_block(sidx, 1, wide[1], near_1 + (far_1 or []), ahead=(x, part, recv), back=(cot,), fcb=fcb[1])
    mid, part, own_mid, part_b, *pack, sum_mlp, sum_pre = outs
    mids.append(mid)

    small = [None] * layers

    d = 4 * quarter
    shapes_m = [(quarter, 4 * d), (d, d)]
    shapes_a = [(quarter, 3 * d), (quarter, d)]
    m_part, a_part, both = (quarter, d), (quarter // 2, d), (3 * quarter // 2, d)

    recv = swap(part_b, SWAP_CORE)
    own_m1, other, send = pack
    from_m1 = swap(send, SWAP_CORE)
    got_m1 = along_y(pack_mlp(other, from_m1, 1)) if ringed else None
    outs = attn_block_backward(sidx, 1, cot, mids[1], part_b, recv, wo[1], *save_a[1][2:4], save_a[1][1], wq[1], wide[1], drow, dcol, save_a[1][4])
    outs, got_m1, from_m1 = pin(outs, got_m1, from_m1)
    gm, part_b, own_a1, other_a1, send, sum_attn, gain_c, shift_c, sum_qkv = outs
    small[1] = [sum_qkv, sum_attn, sum_mlp, sum_pre, gain_c, shift_c]
    from_a1 = swap(send, SWAP_CORE)
    recv = swap(part_b, SWAP_CORE)
    if ringed:
        parts_m1 = sum_kernel(
            split_mlp_body, "split_mlp", sidx, (own_m1, from_m1, got_m1), [m_part] * 4, (d, d)
        )
        other_a1 = pack_attn(sidx, other_a1, from_a1, 1)
        recv, parts_m1, other_a1 = pin(recv, parts_m1, other_a1)
        moved = along_z(parts_m1[1:])
        got_a1 = along_y(other_a1)

    outs = mlp_block(sidx, 0, wide[1], near_0 + (far_0 or []), back=(gm, save_a[1][0], part_b, recv, save_m[2], save_m[1], save_m[0]))
    if ringed:
        outs, moved, got_a1 = pin(outs, moved, got_a1)
    g, part_b, own_m0, other_m0, send, sum_mlp, sum_pre, gain_a, shift_a = outs
    small[1] += [gain_a, shift_a]
    recv = swap(part_b, SWAP_CORE)
    from_m0 = swap(send, SWAP_CORE)
    if ringed:
        total_m1, keep_a1, *parts = sum_kernel(
            mlp_total_attn_split_body,
            "total_mlp_split_attn",
            sidx,
            (parts_m1[0], *moved, own_a1, from_a1, got_a1),
            [m_part, a_part] + [both] * 3,
            (2 * quarter, d),
        )
        other_m0 = pack_mlp(other_m0, from_m0, 1)
        recv, parts, other_m0 = pin(recv, parts, other_m0)
        moved_1 = along_z(parts)
        got_m0 = along_y(other_m0)

    outs = attn_block_backward(sidx, 0, g, mids[0], part_b, recv, wo[0], *save_a[0][2:4], save_a[0][1], wq[0], wide[0], drow, dcol, save_a[0][4])
    if ringed:
        outs, moved_1, got_m0 = pin(outs, moved_1, got_m0)
    gm, part_b, own_a0, other_a0, send, sum_attn, gain_c, shift_c, sum_qkv = outs
    small[0] = [sum_qkv, sum_attn, sum_mlp, sum_pre, gain_c, shift_c]
    recv_b = swap(part_b, SWAP_CORE)
    from_a0 = swap(send, SWAP_CORE)
    at = s * block_input.shape[1]
    own = lambda a: lax.dynamic_slice_in_dim(a, at, block_input.shape[1]).astype(f32)

    def rest():
        grad_input, gain_a, shift_a = input_backward(sidx, gm, xs, part_b, recv_b, wide[0])
        small[0].extend([gain_a, shift_a])
        vecs = pack_small(sidx, small, quarter)
        result = own_mid + branch_scale * (own(part) + own(swap(part, SWAP_CORE)) + wide[layers - 1][OUT_M])
        return grad_input, result, vecs

    fin_m = functools.partial(finish_mlp_body, 0)
    fin_a = functools.partial(finish_attn_body, 0)
    if ringed:
        total_a1, keep_m0, *parts = sum_kernel(
            attn_total_mlp_split_body,
            "total_attn_split_mlp",
            sidx,
            (keep_a1, *moved_1, own_m0, from_m0, got_m0),
            [a_part, m_part] + [both] * 3,
            (d, d),
        )
        other_a0 = pack_attn(sidx, other_a0, from_a0, 1)
        by_y = jnp.concatenate([other_a0, total_m1] + [a[:quarter] for a in moved_1])
        parts, by_y, recv_b = pin(parts, by_y, recv_b)
        moved_2 = along_z(parts)
        got_y = along_y(by_y)
        grad_input, result, vecs = rest()
        vecs = vecs + pair_row(vecs, 1)
        moved_2, got_y, vecs, result = pin(moved_2, got_y, vecs, result)
        total_m0 = total_low(keep_m0, [a[:quarter] for a in moved_2])
        moved_m0 = along_z([total_m0] * 3)
        near_a1 = jnp.concatenate([total_a1] + [a[quarter:] for a in moved_2])
        far_a1 = along_y(near_a1)
        keep_a0, *parts = sum_kernel(
            split_attn_body, "split_attn", sidx, (own_a0, from_a0, got_y), [a_part] * 4, (2 * quarter, d)
        )
        outs_m = finish(
            functools.partial(finish_mlp_body, 2 * quarter), "unpack_mlp", sidx, 1, layers, (by_y, got_y), None, shapes_m
        )
        vecs = vecs + pair_row(vecs, 2)
        moved_m0, far_a1, parts, vecs, outs_m = pin(moved_m0, far_a1, parts, vecs, outs_m)
        near_m0 = jnp.concatenate([total_m0] + moved_m0)
        far_m0 = along_y(near_m0)
        moved_a0 = along_z(parts)
        vecs = vecs + pair_row(vecs, 4)
        outs_a = finish(fin_a, "unpack_attn", sidx, 1, layers, (near_a1, far_a1), None, shapes_a)
        moved_a0, vecs, outs_a = pin(moved_a0, vecs, outs_a)
        total_a0 = total_low(keep_a0, moved_a0)
        moved_a0 = along_z([total_a0] * 3)
        small_out = spread_small(sidx, vecs, quarter)
        moved_a0, far_m0, small_out = pin(moved_a0, far_m0, small_out)
        near_a0 = jnp.concatenate([total_a0] + moved_a0)
        far_a0 = along_y(near_a0)
        pair_m0, pair_a0 = (near_m0, far_m0), (near_a0, far_a0)
    else:
        grad_input, result, vecs = rest()
        sums = []
        for own_m, other, recv in ((own_m1, other, from_m1), (own_m0, other_m0, from_m0)):
            sums += [pack_mlp(own_m, recv, 0), pack_mlp(other, recv, 1)]
        for own_a, other, recv in ((own_a1, other_a1, from_a1), (own_a0, other_a0, from_a0)):
            sums += [pack_attn(sidx, own_a, recv, 0), pack_attn(sidx, other, recv, 1)]
        sums = lax.psum(sums, "rows")
        outs_m = finish(fin_m, "unpack_mlp", sidx, 1, layers, sums[0:2], None, shapes_m)
        outs_a = finish(fin_a, "unpack_attn", sidx, 1, layers, sums[4:6], None, shapes_a)
        pair_m0, pair_a0 = sums[2:4], sums[6:8]
        small_out = spread_small(sidx, lax.psum(vecs, "rows"), quarter)
    out_gain, out_shift, out_qv, out_out, out_fcb = small_out
    out_fc, out_proj = finish(fin_m, "unpack_mlp", sidx, 0, layers, pair_m0, outs_m, shapes_m)
    out_qkv, out_o = finish(fin_a, "unpack_attn", sidx, 0, layers, pair_a0, outs_a, shapes_a)
    return (
        result[None],
        grad_input[None],
        out_qkv,
        out_o,
        out_fc,
        out_proj,
        out_gain,
        out_shift,
        out_qv,
        out_out,
        out_fcb,
    )


def solution(mesh):
    in_specs = (
        P("rows", "seq", None),
        P("rows", "seq", None),
        P("rows", None),
        P(None, "seq", None),
        P(None, "seq", None),
        P(None, "seq", None),
        P(None, "seq", None),
        P(None, None, "seq"),
        P(None, None, "seq"),
        P(None, None, "seq"),
        P(None, None, "seq"),
        P(None, "seq"),
    )
    out_specs = (
        P("rows", "seq", None),
        P("rows", "seq", None),
        P(None, "seq", None),
        P(None, "seq", None),
        P(None, "seq", None),
        P(None, "seq", None),
        P(None, None, "seq"),
        P(None, None, "seq"),
        P(None, None, "seq"),
        P(None, None, "seq"),
        P(None, "seq"),
    )
    return jax.shard_map(
        on_device, mesh=mesh, in_specs=in_specs, out_specs=out_specs, check_vma=False
    )
```

```python
import functools
import math

import jax
import jax.numpy as jnp
from jax import lax
from jax.experimental import pallas as pl
from jax.experimental.pallas import tpu as pltpu
from jax.sharding import PartitionSpec as P

HD = 64
branch_scale = 48.0 ** (-0.5)
norm_eps = 1e-05
masked_score = -1e30
log2_e = math.log2(math.e)
MIB = 1 << 20
VMEM = 62
BLK = 256

f32 = jnp.float32
bf16 = jnp.bfloat16
STREAM = bf16

SWAP_CORE = [(s, s ^ 1) for s in range(4)]
SWAP_X = [(s, s ^ 2) for s in range(4)]
SWAP_BOTH = [(s, s ^ 3) for s in range(4)]


def dot_nn(a, b):
    return lax.dot_general(a, b, (((1,), (0,)), ((), ())), preferred_element_type=f32)


def dot_nt(a, b):
    return lax.dot_general(a, b, (((1,), (1,)), ((), ())), preferred_element_type=f32)


def dot_tn(a, b):
    return lax.dot_general(a, b, (((0,), (0,)), ((), ())), preferred_element_type=f32)


def call(body, name, sidx, grid, ins, outs, scratch, flops, vmem, exps=0):
    arrays = [a for a, _, _ in ins]
    in_specs = [
        pl.BlockSpec(memory_space=pl.ANY) if b is None else pl.BlockSpec(b, m) for _, b, m in ins
    ]
    out_specs = [
        pl.BlockSpec(memory_space=pl.ANY) if b is None else pl.BlockSpec(b, m) for _, b, m in outs
    ]
    out_shape = [s for s, _, _ in outs]
    nbytes = sum(a.size * a.dtype.itemsize for a in arrays)
    nbytes += sum(math.prod(s.shape) * s.dtype.itemsize for s in out_shape)
    return pl.pallas_call(
        body,
        name=name,
        grid_spec=pltpu.PrefetchScalarGridSpec(
            num_scalar_prefetch=1,
            grid=grid,
            in_specs=in_specs,
            out_specs=out_specs,
            scratch_shapes=scratch,
        ),
        out_shape=out_shape,
        compiler_params=pltpu.CompilerParams(
            dimension_semantics=("arbitrary",) * len(grid), vmem_limit_bytes=vmem * MIB
        ),
        cost_estimate=pl.CostEstimate(
            flops=int(flops), bytes_accessed=int(nbytes), transcendentals=int(exps)
        ),
    )(sidx, *arrays)


RING = [0, 2, 4, 6, 7, 5, 3, 1]
RING_NEXT = [(RING[i], RING[(i + 1) % 8]) for i in range(8)]
RING_PREV = [(b, a) for a, b in RING_NEXT]
RING_STEPS = [0, -1, 1, -2, 2, -3, 3, -4]


def ring_place():
    row = lax.axis_index("rows").astype(jnp.int32)
    return jnp.where(row % 2 == 0, row // 2, 7 - row // 2)


def place_index():
    s = lax.axis_index("seq").astype(jnp.int32)
    zero = jnp.int32(0)
    row = lax.axis_index("rows").astype(jnp.int32) if lax.axis_size("rows") == 8 else zero
    place = ring_place() if lax.axis_size("rows") == 8 else zero
    return jnp.stack([s, s // 2, s % 2, place, row % 2, row // 2])


def sds(shape, dtype):
    return jax.ShapeDtypeStruct(shape, dtype)


def whole(block):
    zeros = (0,) * len(block)
    return lambda i, m: zeros


def row_tile(i, m):
    return (i, 0)


def stack_tile(i, m):
    return (i ^ m[0], 0, 0)


def normed(x):
    centre = x - jnp.mean(x, axis=-1, keepdims=True)
    spread = jnp.mean(centre * centre, axis=-1, keepdims=True)
    rstd = lax.rsqrt(spread + norm_eps)
    return centre * rstd, rstd


def norm_back(x, grad, gain):
    unit, rstd = normed(x)
    inner = grad * gain
    mean_inner = jnp.mean(inner, axis=-1, keepdims=True)
    mean_prod = jnp.mean(inner * unit, axis=-1, keepdims=True)
    return rstd * (inner - mean_inner - unit * mean_prod), unit


GAIN_A, GAIN_C, SHIFT_A, SHIFT_C, OUT_A, OUT_M = range(6)


def row_of(ref, k):
    return ref[k : k + 1, :]


def lane_half(shape):
    return lax.broadcasted_iota(jnp.int32, shape, 1) // HD


def block_start(i):
    return BLK * (i * (i + 1) // 2)


class Mover:
    def __init__(self, sems):
        self.sems = sems
        self.used = 0

    def make(self, src, dst):
        cp = pltpu.make_async_copy(src, dst, self.sems.at[self.used])
        self.used += 1
        return cp

    def go(self, src, dst):
        cp = self.make(src, dst)
        cp.start()
        return cp


def wait_all(copies):
    for cp in copies:
        cp.wait()


def tile_of(i):
    return pl.ds(i * BLK, BLK)


def pieces_in(mover, refs, dst, first, rows, at=0):
    out = []
    width = dst.shape[1]
    for j, ref in enumerate(refs):
        where = pl.multiple_of((first ^ j) * rows, 16)
        src = ref if ref.shape[1] == width else ref.at[:, pl.ds(at, width)]
        out.append(mover.go(src, dst.at[pl.ds(where, rows)]))
    return out


def add_up(ref, value, start):
    here = jnp.sum(value, axis=0, keepdims=True)
    if start:
        ref[...] = here
    else:
        ref[...] += here


def back_pair(pair, pairs, tokens, qkv, att, datt, lse, bias, starts, dqkv, dq_acc):
    blocks = tokens // BLK
    half = lane_half((BLK, 2 * HD))
    score_scale = HD ** (-0.5)
    scale = score_scale * log2_e
    pick_row = lax.broadcasted_iota(jnp.int32, (8, 2 * HD), 0)
    pick = jnp.where(lane_half((8, 2 * HD)) == pick_row, 1.0, 0.0)
    prod = datt[pair].astype(f32) * att[pair].astype(f32)
    delta = lax.dot_general(
        pick, prod, (((1,), (1,)), ((), ())), precision=lax.Precision.HIGHEST, preferred_element_type=f32
    )
    for j in range(blocks):
        first = j * BLK
        span = slice(first, first + BLK)
        rest = pl.ds(first, tokens - first)
        kj = qkv[pair + pairs, span, :]
        vj = qkv[pair + 2 * pairs, span, :]
        qq = qkv[pair, rest, :]
        dd = datt[pair, rest, :]
        width = tokens - first
        zero = jnp.zeros_like(kj)
        dks, dvs, dss, khs = [], [], [], []
        for h in range(2):
            kh = jnp.where(half == h, kj, zero)
            vh = jnp.where(half == h, vj, zero)
            t = dot_nt(kh, qq) * scale + bias[:, starts[j] : starts[j] + width]
            p = jnp.exp2(t - lse[pair, h : h + 1, first:])
            dp = dot_nt(vh, dd)
            ds = (p * (dp - delta[h : h + 1, first:])).astype(bf16)
            dvs.append(dot_nn(p.astype(bf16), dd))
            dks.append(dot_nn(ds, qq))
            dss.append(ds)
            khs.append(kh)
        dk = jnp.where(half == 0, dks[0], dks[1]) * score_scale
        dv = jnp.where(half == 0, dvs[0], dvs[1])
        dqkv[pair + pairs, span, :] = dk.astype(bf16)
        dqkv[pair + 2 * pairs, span, :] = dv.astype(bf16)
        dq = dot_tn(jnp.concatenate(dss, axis=0), jnp.concatenate(khs, axis=0))
        if j == 0:
            dq_acc[...] = dq
        else:
            dq_acc[first:, :] += dq
    dqkv[pair] = (dq_acc[...] * score_scale).astype(bf16)


def forward_pair(pair, pairs, blocks, qkv, bias, att, lse):
    half = lane_half((BLK, 2 * HD))
    scale = HD ** (-0.5) * log2_e
    for i in range(blocks):
        width = BLK * (i + 1)
        span = slice(i * BLK, (i + 1) * BLK)
        qb = qkv[pair, span, :]
        kk = qkv[pair + pairs, 0:width, :]
        vv = qkv[pair + 2 * pairs, 0:width, :]
        mixed, logs = [], []
        for h in range(2):
            qh = jnp.where(half == h, qb, jnp.zeros_like(qb))
            t = dot_nt(qh, kk) * scale + bias[:, block_start(i) : block_start(i) + width]
            top = jnp.max(t, axis=-1, keepdims=True)
            p = jnp.exp2(t - top)
            total = jnp.sum(p, axis=-1, keepdims=True)
            o = dot_nn(p.astype(bf16), vv)
            mixed.append(o / total)
            logs.append(jnp.broadcast_to(top + jnp.log2(total), (BLK, 2 * HD)))
        att[pair, span, :] = jnp.where(half == 0, mixed[0], mixed[1]).astype(bf16)
        turned = jnp.transpose(jnp.where(half == 0, logs[0], logs[1]))
        lse[pair, 0:1, span] = turned[0:1, :]
        lse[pair, 1:2, span] = turned[HD : HD + 1, :]


def attn_block_body(l, first, parts_w, m, *refs):
    count = 1 if first else 3
    sources = refs[:count]
    wo0, wo1 = refs[count : count + 2]
    weights = refs[count + 2 : count + 2 + parts_w]
    refs = refs[count + 2 + parts_w :]
    vec, prev, bias_row, drow, dcol = refs[:5]
    refs = refs[5:]
    if not first:
        x_out, refs = refs[0], refs[1:]
    ln_out, qkv_out, att_out, part_out, lse = refs[:5]
    bufs = refs[5 : 5 + count]
    (wo, w, lns, qkv, att, parts, bias, sems) = refs[5 + count :]
    tokens, d = lns.shape
    blocks = tokens // BLK
    pairs = att.shape[0]
    half = d // 2
    q = half // 2
    move = Mover(sems)
    c_w = attn_weights_in(move, m, weights, w, q)
    c_tiles = []
    for t in range(blocks):
        for ref, dst in zip(sources, bufs):
            src = ref.at[t ^ m[0]] if len(ref.shape) == 3 else ref.at[tile_of(t)]
            c_tiles.append(move.go(src, dst.at[tile_of(t)]))
    c_wo = pieces_in(move, (wo0.at[l], wo1), wo, m[1], q, w.shape[1])
    for i in range(blocks):
        width = BLK * (i + 1)
        begin = i * BLK
        qpos = begin + lax.broadcasted_iota(jnp.int32, (BLK, width), 0)
        kpos = lax.broadcasted_iota(jnp.int32, (BLK, width), 1)
        same = dcol[begin : begin + BLK, :] == drow[:, :width]
        allowed = (kpos <= qpos) & same
        bias[:, block_start(i) : block_start(i) + width] = jnp.where(allowed, 0.0, masked_score)
    wait_all(c_w)
    wait_all(c_tiles)
    c_out = []
    mine = pl.ds(pl.multiple_of(m[1] * half, 128), half)
    for t in range(blocks):
        span = tile_of(t)
        if first:
            x = bufs[0][span, :].astype(f32)
        else:
            part = bufs[1][span, :].astype(f32) + bufs[2][span, :].astype(f32) + row_of(prev, OUT_M)
            x = bufs[0][span, :].astype(f32) + branch_scale * part
            bufs[0][span, :] = x.astype(STREAM)
            c_out.append(move.go(bufs[0].at[span], x_out.at[span]))
        unit, _ = normed(x)
        ln = (unit * row_of(vec, GAIN_A) + row_of(vec, SHIFT_A)).astype(bf16)
        lns[span, :] = ln
        c_out.append(move.go(lns.at[span, mine], ln_out.at[span]))
        row = (dot_nn(ln, w[...]) + bias_row[...]).astype(bf16)
        for k in range(3 * pairs):
            cols = slice(k * 2 * HD, (k + 1) * 2 * HD)
            qkv[k, span, :] = row[:, cols]
    for k in range(3 * pairs):
        c_out.append(move.go(qkv.at[k], qkv_out.at[k]))

    @pl.loop(0, pairs)
    def _(pair):
        forward_pair(pair, pairs, blocks, qkv, bias, att, lse)

    for k in range(pairs):
        c_out.append(move.go(att.at[k], att_out.at[k]))
    wait_all(c_wo)
    for t in range(blocks):
        span = tile_of(t)
        row = jnp.concatenate([att[k, span, :] for k in range(pairs)], axis=1)
        parts[span, :] = dot_nn(row, wo[...]).astype(bf16)
        c_out.append(move.go(parts.at[span], part_out.at[span]))
    wait_all(c_out)


def attn_block_forward(sidx, l, source, wo_pieces, pieces, vec, prev, bias, drow, dcol):
    first = len(source) == 1
    q, cols = pieces[0].shape
    d = 4 * q
    tokens = drow.shape[1]
    width = cols // 3
    pairs = width // (2 * HD)
    ins = [(a, None, None) for a in (*source, *wo_pieces, *pieces)]
    ins += [(a, a.shape, whole(a.shape)) for a in (vec, prev, bias, drow, dcol)]
    outs = [] if first else [(sds((tokens, d), STREAM), None, None)]
    outs += [
        (sds((tokens, d // 2), bf16), None, None),
        (sds((3 * pairs, tokens, 2 * HD), bf16), None, None),
        (sds((pairs, tokens, 2 * HD), bf16), None, None),
        (sds((tokens, d), bf16), None, None),
        (sds((pairs, 8, tokens), f32), (pairs, 8, tokens), whole((0, 0, 0))),
    ]
    blocks = tokens // BLK
    scratch = [pltpu.VMEM((tokens, d), a.dtype) for a in source]
    scratch += [
        pltpu.VMEM((width, d), bf16),
        pltpu.VMEM((d, cols), bf16),
        pltpu.VMEM((tokens, d), bf16),
        pltpu.VMEM((3 * pairs, tokens, 2 * HD), bf16),
        pltpu.VMEM((pairs, tokens, 2 * HD), bf16),
        pltpu.VMEM((tokens, d), bf16),
        pltpu.VMEM((BLK, block_start(blocks)), f32),
        pltpu.SemaphoreType.DMA((64,)),
    ]
    return call(
        functools.partial(attn_block_body, l, first, len(pieces)),
        "attention_block",
        sidx,
        (1,),
        ins,
        outs,
        scratch,
        4 * tokens * tokens * width + 2 * tokens * d * (cols + width),
        VMEM,
        exps=tokens * tokens * pairs,
    )


def far_in(move, m, refs, dst, q, lanes):
    out = []
    part = q // 4
    for ref, t in zip(refs, RING_STEPS):
        chunk = (m[3] + t + len(refs)) % len(refs)
        at = pl.multiple_of((m[0] ^ (2 + chunk // 4)) * q + (chunk % 4) * part, 16)
        out.append(move.go(ref.at[:, lanes], dst.at[pl.ds(at, part)]))
    return out


def attn_weights_in(move, m, refs, w, q):
    out = pieces_in(move, refs[:4] if len(refs) == 4 else refs[:2], w, m[0], q)
    if len(refs) > 4:
        out += far_in(move, m, refs[2:], w, q, pl.ds(0, w.shape[1]))
    return out


def mlp_weights_in(move, l, m, refs, wf, wp):
    if len(refs) == 6:
        first = pieces_in(move, refs[:4], wf, m[0], refs[0].shape[0])
        return first, pieces_in(move, refs[4:], wp, m[1], refs[4].shape[0])
    keep, near, own = refs[0], refs[1], refs[2].at[l]
    q, hidden = keep.shape
    deep = own.shape[0]
    half = deep // 2
    far = refs[-8:]
    base = far[0].shape[1] - hidden if l == 0 else 0
    first = pieces_in(move, (keep, near), wf, m[0], q)
    first += far_in(move, m, far, wf, q, pl.ds(base, hidden))
    second = pieces_in(move, (own,), wp, m[1], deep)
    there = (1 - m[1]) * deep
    at = pl.multiple_of(there, 16)
    second.append(move.go(refs[3], wp.at[pl.ds(at, refs[3].shape[0])]))
    if l:
        part = q // 4
        for ref, t in zip(far, RING_STEPS):
            chunk = (m[3] + t + 8) % 8
            at = pl.multiple_of(there + half + chunk * part, 16)
            src = ref.at[:, pl.ds(hidden, own.shape[1])]
            second.append(move.go(src, wp.at[pl.ds(at, part)]))
    return first, second


def gelu_and_slope(pre):
    root = math.sqrt(2.0 / math.pi)
    sq = pre * pre
    gate = 0.5 * jnp.tanh(pre * (root + root * 0.044715 * sq)) + 0.5
    rise = pre * (2.0 * root + 6.0 * root * 0.044715 * sq)
    return pre * gate, gate + gate * ((1.0 - gate) * rise)


def mlp_block_body(l, ahead, back, count, m, *refs):
    take = lambda k: (refs[:k], refs[k:])
    vec = prev = fcb = None
    sources, refs = take(3 if ahead else 0)
    (cot,), refs = take(1) if ahead and back else ((None,), refs)
    grads, refs = take(4 if back and not ahead else 0)
    (slope_in, act_in, ln_in), refs = take(3) if back and not ahead else ((None,) * 3, refs)
    weights, refs = take(count)
    if ahead:
        (vec, fcb), refs = take(2)
    else:
        (vec,), refs = take(1)
    if ahead:
        (mid_out, part_out), refs = take(2)
        if back:
            (own_out,), refs = take(1)
        else:
            (ln_out, act_out, slope_out), refs = take(3)
    if back:
        if not ahead:
            (g_out,), refs = take(1)
        (back_out, mine, other, send_mine, send_other, sum_mlp, sum_pre), refs = take(7)
        if not ahead:
            (sum_gain, sum_shift), refs = take(2)
    b0, b1, b2, b3, wf, wp, lns, act, slope, dmlp, sems = refs
    tokens, d = b1.shape
    blocks = tokens // BLK
    hidden = wf.shape[1]
    q = d // 4
    move = Mover(sems)
    c_tiles = []
    if ahead:
        loads = list(zip(sources, (b0, b1, b2))) + ([(cot, b3)] if back else [])
    else:
        loads = list(zip(grads, (b0, b1, b2, b3)))
    c_wp = []
    if ahead:
        c_wf, c_wp = mlp_weights_in(move, l, m, weights, wf, wp)
    for t in range(blocks):
        for ref, dst in loads:
            src = ref.at[t ^ m[0]] if len(ref.shape) == 3 else ref.at[tile_of(t)]
            c_tiles.append(move.go(src, dst.at[tile_of(t)]))
    if not ahead:
        c_wf, c_wp = mlp_weights_in(move, l, m, weights, wf, wp)
        c_slope = [move.go(slope_in.at[tile_of(t)], slope.at[tile_of(t)]) for t in range(blocks)]
        c_late = [move.go(act_in, act.at[:, pl.ds(0, act_in.shape[1])]), move.go(ln_in, lns.at[:, pl.ds(0, d // 2)])]
    c_out = []
    n = len(loads)
    wide = hidden // 2
    for t in range(blocks):
        wait_all(c_tiles[n * t : n * t + n])
        span = tile_of(t)
        if ahead:
            part = b1[span, :].astype(f32) + b2[span, :].astype(f32) + row_of(vec, OUT_A)
            mid = b0[span, :].astype(f32) + branch_scale * part
            b0[span, :] = mid.astype(b0.dtype)
            c_out.append(move.go(b0.at[span], mid_out.at[span]))
            if back:

                @pl.when(m[0] == t)
                def _():
                    own_out[...] = mid

            unit, _ = normed(mid)
            ln = (unit * row_of(vec, GAIN_C) + row_of(vec, SHIFT_C)).astype(bf16)
            lns[span, :] = ln
            if t == 0:
                wait_all(c_wf)
            value, rise = gelu_and_slope(dot_nn(ln, wf[...]) + fcb[...])
            low = value.astype(bf16)
            act[span, :] = low
            if not back:
                slope[span, :] = rise.astype(bf16)
                cols = pl.ds(pl.multiple_of(m[1] * (d // 2), 128), d // 2)
                c_out.append(move.go(lns.at[span, cols], ln_out.at[span]))
                cols = pl.ds(pl.multiple_of(m[1] * wide, 128), wide)
                c_out.append(move.go(act.at[span, cols], act_out.at[span]))
                c_out.append(move.go(slope.at[span], slope_out.at[span]))
            if t == 0:
                wait_all(c_wp)
            b1[span, :] = dot_nn(low, wp[...]).astype(bf16)
            c_out.append(move.go(b1.at[span], part_out.at[span]))
        if back:
            if ahead:
                g = b3[span, :].astype(f32)
            else:
                if t == 0:
                    wait_all(c_wp)
                wait_all(c_slope[t : t + 1])
                rise = slope[span, :].astype(f32)
                grad = b2[span, :].astype(f32) + b3[span, :].astype(f32)
                part, unit = norm_back(b1[span, :].astype(f32), grad, row_of(vec, GAIN_A))
                add_up(sum_gain, grad * unit, t == 0)
                add_up(sum_shift, grad, t == 0)
                g = b0[span, :].astype(f32) + part
                b0[span, :] = g.astype(b0.dtype)
                c_out.append(move.go(b0.at[span], g_out.at[span]))
            low = (branch_scale * g).astype(bf16)
            dmlp[span, :] = low
            add_up(sum_mlp, low.astype(f32), t == 0)
            dpre = (dot_nt(low, wp[...]) * rise).astype(bf16)
            slope[span, :] = dpre
            add_up(sum_pre, dpre.astype(f32), t == 0)
            if t == 0 and not ahead:
                wait_all(c_wf)
            b2[span, :] = dot_nt(dpre, wf[...]).astype(bf16)
            c_out.append(move.go(b2.at[span], back_out.at[span]))
    if back:
        y = m[4]
        if not ahead:
            wait_all(c_late)
            turned = jnp.transpose(act[:, 0:wide])
        else:
            turned = jnp.transpose(jnp.where(m[1] == 0, act[:, 0:wide], act[:, wide:]))
        grad = dot_nn(turned, dmlp[...]).astype(bf16)
        h = grad.shape[0] // 2
        mine[0:h, :] = jnp.where(y == 0, grad[:h], grad[h:])
        other[0:h, :] = jnp.where(y == 0, grad[h:], grad[:h])
        half = d // 2
        if not ahead:
            turned = jnp.transpose(lns[:, 0:half])
        else:
            turned = jnp.transpose(jnp.where(m[1] == 0, lns[:, 0:half], lns[:, half:]))
        sides = [dot_nn(turned, slope[:, i * d : (i + 1) * d]).astype(bf16) for i in range(2)]
        for here, there, i in ((mine, send_mine, 0), (other, send_other, 1)):
            side = jnp.where(y == i, sides[0], sides[1])
            here[h : h + q, :] = jnp.where(m[2] == 0, side[:q], side[q:])
            there[...] = jnp.where(m[2] == 0, side[q:], side[:q])
    wait_all(c_out)


def mlp_block(sidx, l, vec, weights, ahead=None, back=None, fcb=None):
    d = vec.shape[1]
    if ahead is not None:
        tokens = ahead[1].shape[0]
        hidden = fcb.shape[1]
        sources = list(ahead) + ([back[0]] if back else [])
        types = [STREAM if ahead[0].ndim == 2 else ahead[0].dtype, bf16, bf16, bf16]
        vectors_in = [vec, fcb]
    else:
        tokens, hidden = back[4].shape
        sources = list(back)
        types = [back[0].dtype, back[1].dtype, bf16, bf16]
        vectors_in = [vec]
    q = d // 4
    ins = [(a, None, None) for a in sources + list(weights)]
    ins += [(a, a.shape, whole(a.shape)) for a in vectors_in]
    stay = lambda shape, dtype: (sds(shape, dtype), shape, whole(shape))
    away = lambda shape, dtype: (sds(shape, dtype), None, None)
    outs = []
    if ahead is not None:
        outs += [away((tokens, d), STREAM), away((tokens, d), bf16)]
        if back:
            outs += [stay((BLK, d), f32)]
        else:
            outs += [
                away((tokens, d // 2), bf16),
                away((tokens, hidden // 2), bf16),
                away((tokens, hidden), bf16),
            ]
    if back:
        if ahead is None:
            outs += [away((tokens, d), back[0].dtype)]
        outs += [away((tokens, d), bf16)]
        outs += [stay((3 * q, d), bf16)] * 2 + [stay((q, d), bf16)] * 2
        outs += [stay((1, d), f32), stay((1, hidden), f32)]
        if ahead is None:
            outs += [stay((1, d), f32)] * 2
    scratch = [pltpu.VMEM((tokens, d), t) for t in types]
    scratch += [
        pltpu.VMEM((d, hidden), bf16),
        pltpu.VMEM((hidden, d), bf16),
        pltpu.VMEM((tokens, d), bf16),
        pltpu.VMEM((tokens, hidden), bf16),
        pltpu.VMEM((tokens, hidden), bf16),
        pltpu.VMEM((tokens, d), bf16),
        pltpu.SemaphoreType.DMA((96,)),
    ]
    return call(
        functools.partial(mlp_block_body, l, ahead is not None, bool(back), len(weights)),
        "mlp_block" + ("_forward" if ahead is not None else "") + ("_backward" if back else ""),
        sidx,
        (1,),
        ins,
        outs,
        scratch,
        (4 * bool(ahead is not None) + 8 * bool(back)) * tokens * d * hidden,
        VMEM,
        exps=tokens * hidden,
    )


def attn_block_back_body(l, parts_w, m, *refs):
    (g_in, mid_in, p_in, r_in, wo0, wo1, qkv_in, att_in, ln_in) = refs[:9]
    weights = refs[9 : 9 + parts_w]
    refs = refs[:9] + refs[9 + parts_w :]
    (vec, drow, dcol, lse) = refs[9:13]
    refs = refs[:9] + (None,) * 4 + refs[9:]
    (gm_out, part_out, mine, other, to_core) = refs[17:22]
    (sum_attn, sum_gain, sum_shift, sum_qkv) = refs[22:26]
    (gs, mids, ps, rs, wo, qkv, att, lns, w, dattn, datt, dqkv, bias, dq_acc, sems) = refs[26:]
    tokens, d = mids.shape
    blocks = tokens // BLK
    pairs = att.shape[0]
    q = d // 4
    move = Mover(sems)
    c_wo = pieces_in(move, (wo0.at[l], wo1), wo, m[1], q, w.shape[1])
    c_tiles = []
    loads = [(g_in, gs), (mid_in, mids), (p_in, ps), (r_in, rs)]
    for t in range(blocks):
        for ref, dst in loads:
            src = ref.at[t ^ m[0]] if len(ref.shape) == 3 else ref.at[tile_of(t)]
            c_tiles.append(move.go(src, dst.at[tile_of(t)]))
    c_qkv = [move.go(qkv_in, qkv), move.go(att_in, att)]
    c_w = attn_weights_in(move, m, weights, w, q)
    half = d // 2
    c_ln = [move.go(ln_in, lns)]

    starts = [sum(tokens - BLK * a for a in range(j)) for j in range(blocks)]
    for j in range(blocks):
        width = tokens - j * BLK
        first = j * BLK
        kpos = lax.broadcasted_iota(jnp.int32, (BLK, width), 0)
        qpos = lax.broadcasted_iota(jnp.int32, (BLK, width), 1)
        same = dcol[first : first + BLK, :] == drow[:, first:]
        allowed = (kpos <= qpos) & same
        bias[:, starts[j] : starts[j] + width] = jnp.where(allowed, 0.0, masked_score)

    wait_all(c_wo)
    c_out = []
    for t in range(blocks):
        wait_all(c_tiles[4 * t : 4 * t + 4])
        span = tile_of(t)
        grad = ps[span, :].astype(f32) + rs[span, :].astype(f32)
        part, unit = norm_back(mids[span, :].astype(f32), grad, row_of(vec, GAIN_C))
        add_up(sum_gain, grad * unit, t == 0)
        add_up(sum_shift, grad, t == 0)
        gm = gs[span, :].astype(f32) + part
        gs[span, :] = gm.astype(gs.dtype)
        c_out.append(move.go(gs.at[span], gm_out.at[span]))
        low = (branch_scale * gm).astype(bf16)
        dattn[span, :] = low
        add_up(sum_attn, low.astype(f32), t == 0)
        heads = dot_nt(low, wo[...]).astype(bf16)
        for k in range(pairs):
            datt[k, span, :] = heads[:, k * 2 * HD : (k + 1) * 2 * HD]

    wait_all(c_qkv)

    @pl.loop(0, pairs)
    def _(pair):
        back_pair(pair, pairs, tokens, qkv, att, datt, lse, bias, starts, dqkv, dq_acc)

    wait_all(c_w)
    for t in range(blocks):
        span = tile_of(t)
        row = jnp.concatenate([dqkv[k, span, :] for k in range(3 * pairs)], axis=1)
        ps[span, :] = dot_nt(row, w[...]).astype(bf16)
        c_out.append(move.go(ps.at[span], part_out.at[span]))
        add_up(sum_qkv, row.astype(f32), t == 0)

    wait_all(c_ln)
    quart = q // 2
    y = m[4]
    turned = jnp.concatenate([jnp.transpose(att[k]) for k in range(pairs)], axis=0)
    left = jnp.where(m[1] == 0, turned[:q], turned[q : 2 * q])
    g_o = dot_nn(left, dattn[...]).astype(bf16)
    for i in range(2):
        cols = slice(i * half, (i + 1) * half)
        a, b = g_o[:quart, cols], g_o[quart:, cols]
        mine[i * quart : (i + 1) * quart, :] = jnp.where(y == 0, a, b)
        other[i * quart : (i + 1) * quart, :] = jnp.where(y == 0, b, a)
    turned = jnp.transpose(lns[...])
    for p in range(3):
        right = jnp.concatenate([dqkv[p * pairs + k] for k in range(pairs)], axis=1)
        grad = dot_nn(turned, right).astype(bf16)
        keep = jnp.where(m[2] == 0, grad[:q], grad[q:])
        send = jnp.where(m[2] == 0, grad[q:], grad[:q])
        at = (2 + p) * quart
        mine[at : at + quart, :] = jnp.where(y == 0, keep[:quart], keep[quart:])
        other[at : at + quart, :] = jnp.where(y == 0, keep[quart:], keep[:quart])
        at = p * quart
        to_core[at : at + quart, :] = jnp.where(y == 0, send[:quart], send[quart:])
        at += 3 * quart
        to_core[at : at + quart, :] = jnp.where(y == 0, send[quart:], send[:quart])
    wait_all(c_out)


def attn_block_backward(sidx, l, g, mid, part, recv, wo_pieces, qkv, att, ln_a, pieces, vec, drow, dcol, lse):
    tokens, d = mid.shape
    q, cols = pieces[0].shape
    width = cols // 3
    pairs = width // (2 * HD)
    ins = [(a, None, None) for a in (g, mid, part, recv, *wo_pieces, qkv, att, ln_a, *pieces)]
    ins += [(a, a.shape, whole(a.shape)) for a in (vec, drow, dcol, lse)]
    stay = lambda shape, dtype: (sds(shape, dtype), shape, whole(shape))
    outs = [
        (sds((tokens, d), STREAM), None, None),
        (sds((tokens, d), bf16), None, None),
        stay((5 * q // 2, width), bf16),
        stay((5 * q // 2, width), bf16),
        stay((3 * q, width), bf16),
        stay((1, d), f32),
        stay((1, d), f32),
        stay((1, d), f32),
        stay((1, cols), f32),
    ]
    blocks = tokens // BLK
    wide = (tokens, 2 * HD)
    scratch = [
        pltpu.VMEM((tokens, d), g.dtype),
        pltpu.VMEM((tokens, d), mid.dtype),
        pltpu.VMEM((tokens, d), bf16),
        pltpu.VMEM((tokens, d), bf16),
        pltpu.VMEM((width, d), bf16),
        pltpu.VMEM((3 * pairs,) + wide, bf16),
        pltpu.VMEM((pairs,) + wide, bf16),
        pltpu.VMEM((tokens, d // 2), bf16),
        pltpu.VMEM((d, cols), bf16),
        pltpu.VMEM((tokens, d), bf16),
        pltpu.VMEM((pairs,) + wide, bf16),
        pltpu.VMEM((3 * pairs,) + wide, bf16),
        pltpu.VMEM((BLK, block_start(blocks)), f32),
        pltpu.VMEM(wide, f32),
        pltpu.SemaphoreType.DMA((64,)),
    ]
    return call(
        functools.partial(attn_block_back_body, l, len(pieces)),
        "attention_block_backward",
        sidx,
        (1,),
        ins,
        outs,
        scratch,
        10 * tokens * tokens * width,
        VMEM,
        exps=tokens * tokens * pairs,
    )


def add_rows(ref, value, start):
    @pl.when(start)
    def _():
        ref[...] = jnp.zeros_like(ref)

    ref[...] += jnp.sum(value, axis=0, keepdims=True)


def input_back_body(m, gm_ref, x_ref, p_ref, r_ref, vec, out_ref, sum_gain, sum_shift):
    tile = pl.program_id(0)
    grad = p_ref[...].astype(f32) + r_ref[...].astype(f32)
    part, unit = norm_back(x_ref[0].astype(f32), grad, row_of(vec, GAIN_A))
    add_rows(sum_gain, grad * unit, tile == 0)
    add_rows(sum_shift, grad, tile == 0)

    @pl.when(tile == m[0])
    def _():
        out_ref[...] = gm_ref[...].astype(f32) + part


def input_backward(sidx, gm, x, part, recv, vec):
    tokens, depth = gm.shape
    tile = (BLK, depth)
    ins = [(gm, tile, row_tile), (x, (1, BLK, depth), stack_tile)]
    ins += [(a, tile, row_tile) for a in (part, recv)]
    ins.append((vec, vec.shape, whole(vec.shape)))
    outs = [(sds((BLK, depth), f32), tile, whole((0, 0)))]
    outs += [(sds((1, depth), f32), (1, depth), whole((0, 0)))] * 2
    return call(input_back_body, "input_backward", sidx, (tokens // BLK,), ins, outs, [], tokens * depth, VMEM)


def swap(a, perm):
    return lax.ppermute(a, "seq", perm)


def split_body(m, qkv_ref, fc_ref, o_ref, qkv_keep, qkv_send, fc_keep, fc_send, o_out):
    core = m[2]
    o_out[...] = o_ref[0]
    q = qkv_ref.shape[1]
    pair = 2 * q
    for p in range(3):
        own, other = [], []
        for xside in range(2):
            col = (2 * p + xside) * pair
            both = qkv_ref[0, :, col : col + pair]
            own.append(jnp.where(core == 0, both[:, :q], both[:, q:]))
            other.append(jnp.where(core == 0, both[:, q:], both[:, :q]))
        qkv_keep[:, p * pair : (p + 1) * pair] = jnp.concatenate(own, axis=1)
        qkv_send[:, p * pair : (p + 1) * pair] = jnp.concatenate(other, axis=1)
    d = fc_ref.shape[2] // 4
    for xside in range(2):
        one = fc_ref[0, :, 2 * xside * d : (2 * xside + 1) * d]
        two = fc_ref[0, :, (2 * xside + 1) * d : (2 * xside + 2) * d]
        fc_keep[:, xside * d : (xside + 1) * d] = jnp.where(core == 0, one, two)
        fc_send[:, xside * d : (xside + 1) * d] = jnp.where(core == 0, two, one)


def split_columns(sidx, w_qkv, w_fc, w_o, l):
    _, rows, cols = w_qkv.shape
    hidden = w_fc.shape[2]
    at = lambda i, m: (l, 0, 0)
    depth = w_o.shape[2]
    ins = [(w_qkv, (1, rows, cols), at), (w_fc, (1, rows, hidden), at), (w_o, (1, rows, depth), at)]
    outs = []
    for width in (cols // 2, cols // 2, hidden // 2, hidden // 2, depth):
        outs.append((sds((rows, width), bf16), (rows, width), whole((0, 0))))
    return call(split_body, "split_columns", sidx, (1,), ins, outs, [], rows * cols, VMEM)


def column_pieces(keep, send):
    return [keep, swap(send, SWAP_CORE), swap(keep, SWAP_X), swap(send, SWAP_BOTH)]


def row_pieces(w):
    return [w, swap(w, SWAP_X)]


def half_columns(w, core):
    q = w.shape[1] // 12
    out = []
    for k in range(6):
        both = w[:, 2 * k * q : (2 * k + 2) * q]
        out.append(jnp.where(core == 0, both[:, :q], both[:, q:]))
    return jnp.concatenate(out, axis=1)


def far_piece_body(l, m, w_fc, w_more, out, *refs):
    rows_in, sems = refs[-2:]
    part = out.shape[0]
    hidden = w_fc.shape[2]
    d = hidden // 4
    move = Mover(sems)
    rows = pl.ds(pl.multiple_of((m[3] % 4) * part, 16), part)
    core = m[2] ^ (m[3] // 4)
    base = 0 if l else out.shape[1] - 2 * d
    copies = []
    for xside in range(2):
        here = pl.ds(pl.multiple_of((2 * xside + core) * d, 128), d)
        copies.append(move.go(w_fc.at[l, rows, here], out.at[:, pl.ds(base + xside * d, d)]))
    if l == 0:
        move.go(w_more.at[l, rows], rows_in).wait()
        out[:, :base] = half_columns(rows_in[...], core)
    else:
        rows = pl.ds(pl.multiple_of(8 * part + m[3] * part, 16), part)
        copies.append(move.go(w_more.at[l, rows], refs[0]))
    wait_all(copies)


def far_piece(sidx, l, w_fc, w_more):
    _, q, hidden = w_fc.shape
    d, part = hidden // 4, q // 4
    widths = [hidden // 2 + w_more.shape[2] // 2] if l == 0 else [hidden // 2, d]
    ins = [(a, None, None) for a in (w_fc, w_more)]
    outs = [(sds((part, w), bf16), (part, w), whole((0, 0))) for w in widths]
    scratch = [pltpu.VMEM((part, w_more.shape[2]), bf16), pltpu.SemaphoreType.DMA((4,))]
    return call(
        functools.partial(far_piece_body, l), "far_piece", sidx, (1,), ins, outs, scratch, 0, VMEM
    )


def cross(a):
    pairs = []
    for r in range(8):
        turn = 2 if RING.index(r) < 4 else 3
        pairs += [(4 * r + s, 4 * r + (s ^ turn)) for s in range(4)]
    return lax.ppermute(a, ("rows", "seq"), pairs)


def ring_pass(held, t):
    if held is None:
        return []
    on = lax.ppermute(held[max(0, len(held) - 2)], "rows", RING_NEXT)
    if t == 4:
        new = [on]
    else:
        new = [on, lax.ppermute(held[-1], "rows", RING_PREV)]
    held += new
    return new


def gather_rows(a, far):
    return jnp.stack([a, swap(a, SWAP_CORE), far, swap(far, SWAP_CORE)])


SWAP_Y = [(r, r ^ 1) for r in range(8)]
SWAP_Z = [None] + [[(r, r ^ (2 * d)) for r in range(8)] for d in range(1, 4)]


def join_attn(own, recv, at):
    n = own.shape[0] // 5
    bit = lambda k: own[k * n : (k + 1) * n, :]
    got = lambda k: recv[at + k * n : at + (k + 1) * n, :]
    pairs = [(bit(0), bit(1)), (bit(2), bit(3)), (bit(4), got(0)), (got(1), got(2))]
    return [jnp.concatenate(p, axis=1) for p in pairs]


def pack_attn_body(which, m, own, recv, out):
    n = out.shape[0] // 4
    for k, rows in enumerate(join_attn(own, recv, which * 3 * n)):
        out[k * n : (k + 1) * n, :] = rows


def pack_attn(sidx, own, recv, which):
    shape = (4 * (own.shape[0] // 5), 2 * own.shape[1])
    ins = [(a, a.shape, whole(a.shape)) for a in (own, recv)]
    outs = [(sds(shape, bf16), shape, whole(shape))]
    return call(
        functools.partial(pack_attn_body, which), "pack_attn", sidx, (1,), ins, outs, [], 0, 16
    )[0]


def add_low(a, b):
    return (a.astype(f32) + b.astype(f32)).astype(bf16)


def total_low(first, rest):
    return (first.astype(f32) + sum(r.astype(f32) for r in rest)).astype(bf16)


def fill_mlp(full, own, recv, got, got_recv):
    cut = own.shape[0]
    full[0:cut, :] = add_low(own[...], got[...])
    full[cut:, :] = add_low(recv[...], got_recv[...])


def fill_attn(full, own, recv, got):
    n = full.shape[0] // 4
    for k, rows in enumerate(join_attn(own, recv, 0)):
        full[k * n : (k + 1) * n, :] = add_low(rows, got[k * n : (k + 1) * n, :])


def quarter_at(full, m, d):
    n = full.shape[0] // 4
    return full[pl.ds(pl.multiple_of((m[5] ^ d) * n, 16), n), :]


def split_mlp_body(m, own, recv, got, got_recv, *refs):
    outs, full = refs[:-1], refs[-1]
    fill_mlp(full, own, recv, got, got_recv)
    for d, out in enumerate(outs):
        out[...] = quarter_at(full, m, d)


def split_attn_body(m, own, recv, got, *refs):
    outs, full = refs[:-1], refs[-1]
    fill_attn(full, own, recv, got)
    for d, out in enumerate(outs):
        out[...] = quarter_at(full, m, d)


def mlp_total_attn_split_body(m, first, g1, g2, g3, own, recv, got, total, keep, s1, s2, s3, full):
    acc = total_low(first[...], [g1[...], g2[...], g3[...]])
    total[...] = acc
    n = acc.shape[0]
    fill_attn(full, own, recv, got)
    keep[...] = quarter_at(full, m, 0)
    for d, out in enumerate((s1, s2, s3)):
        out[0:n, :] = acc
        out[n:, :] = quarter_at(full, m, d + 1)


def phase_load_body(m, first, g1, g2, g3, low, own, recv, got, got_recv, other, from_a, total, keep, s1, s2, s3, by_y, full):
    n, k = low.shape[0], first.shape[0]
    acc = total_low(first[...], [g[n:, :] for g in (g1, g2, g3)])
    total[...] = acc
    fill_mlp(full, own, recv, got, got_recv)
    keep[...] = quarter_at(full, m, 0)
    for d, out in enumerate((s1, s2, s3)):
        out[0:n, :] = quarter_at(full, m, d + 1)
        out[n:, :] = acc
    at = 0
    for rows in join_attn(other, from_a, 3 * k):
        by_y[at : at + k, :] = rows
        at += k
    for rows in (low[...], g1[0:n, :], g2[0:n, :], g3[0:n, :]):
        by_y[at : at + n, :] = rows
        at += n


def mlp_total_body(m, first, low, g1, g2, g3, total, near):
    n = first.shape[0]
    total[...] = total_low(first[...], [g[0:n, :] for g in (g1, g2, g3)])
    k = low.shape[0]
    near[0:k, :] = low[...]
    for i, g in enumerate((g1, g2, g3)):
        near[(i + 1) * k : (i + 2) * k, :] = g[n:, :]


def sum_kernel(body, name, sidx, arrays, shapes, scratch=None):
    ins = [(a, a.shape, whole(a.shape)) for a in arrays]
    outs = [(sds(sh, bf16), sh, whole(sh)) for sh in shapes]
    extra = [] if scratch is None else [pltpu.VMEM(scratch, bf16)]
    return call(body, name, sidx, (1,), ins, outs, extra, 0, VMEM)


def along_y(a):
    return lax.ppermute(a, "rows", SWAP_Y)


def along_z(arrays):
    return [lax.ppermute(a, "rows", SWAP_Z[d + 1]) for d, a in enumerate(arrays)]


def pick_quarter(m, refs, k, at, n):
    if len(refs) == 1:
        return refs[0][pl.ds(pl.multiple_of(at + (k ^ m[5]) * n, 16), n), :].astype(f32)
    d = k ^ m[5]
    low = jnp.where(d % 2 == 0, refs[0][...], refs[1][...])
    high = jnp.where(d % 2 == 0, refs[2][...], refs[3][...])
    return jnp.where(d < 2, low, high).astype(f32)


def halves(m, near, far, at, n):
    def quarter(k):
        a, b = pick_quarter(m, near, k, at, n), pick_quarter(m, far, k, at, n)
        return jnp.where(m[4] == 0, a, b), jnp.where(m[4] == 0, b, a)

    return [quarter(k) for k in range(4)]


def finish_mlp_body(at, count, m, *refs):
    near, far = refs[:count], refs[count : 2 * count]
    out_fc, out_proj = refs[-2:]
    q, d = out_fc.shape[1], out_proj.shape[2]
    parts = halves(m, near, far, at, q)
    for h in range(2):
        for k in range(2):
            row = (2 * h + k) * q
            out_proj[0, row : row + q, :] = parts[k][h]
        for c in range(2):
            col = (2 * h + c) * d
            out_fc[0, :, col : col + d] = jnp.where(m[2] == c, parts[2][h], parts[3][h])


def finish_attn_body(at, count, m, *refs):
    near, far = refs[:count], refs[count : 2 * count]
    out_qkv, out_o = refs[-2:]
    q, d = out_o.shape[1:]
    n, width = q // 2, d // 2
    parts = halves(m, near, far, at, n)
    for h in range(2):
        span = slice(h * n, (h + 1) * n)
        out_o[0, span, :] = parts[0][h]
        bits = [b for k in range(1, 4) for b in (parts[k][h][:, :width], parts[k][h][:, width:])]
        for p in range(3):
            keep, recv = bits[p], bits[3 + p]
            for xside in range(2):
                a = keep[:, xside * q : (xside + 1) * q]
                b = recv[:, xside * q : (xside + 1) * q]
                col = (2 * p + xside) * width
                out_qkv[0, span, col : col + width] = jnp.concatenate(
                    [jnp.where(m[2] == 0, a, b), jnp.where(m[2] == 0, b, a)], axis=1
                )


def finish(body, name, sidx, l, layers, held, before, shapes, at=0):
    near, far = ([a] if not isinstance(a, (list, tuple)) else list(a) for a in held)
    body = functools.partial(body, at, len(near))
    held = near + far
    args = list(held)
    in_specs = [pl.BlockSpec(a.shape, lambda i, m: (0, 0)) for a in held]
    aliases = {}
    if before is not None:
        aliases = {1 + len(args) + k: k for k in range(len(before))}
        args += list(before)
        in_specs += [pl.BlockSpec(memory_space=pl.ANY)] * len(before)
    size = sum(math.prod(sh) for sh in shapes)
    return pl.pallas_call(
        body,
        name=name,
        grid_spec=pltpu.PrefetchScalarGridSpec(
            num_scalar_prefetch=1,
            grid=(1,),
            in_specs=in_specs,
            out_specs=[pl.BlockSpec((1,) + sh, lambda i, m: (l, 0, 0)) for sh in shapes],
        ),
        out_shape=[sds((layers,) + sh, f32) for sh in shapes],
        input_output_aliases=aliases,
        compiler_params=pltpu.CompilerParams(vmem_limit_bytes=32 * MIB),
        cost_estimate=pl.CostEstimate(flops=size, bytes_accessed=6 * size, transcendentals=0),
    )(sidx, *args)


def pair_row(a, step):
    n = lax.axis_size("rows")
    return lax.ppermute(a, "rows", [(r, r ^ step) for r in range(n)])


def vectors_body(m, near, far, wide, qkv_bias, fcb):
    layers = near.shape[1]
    q = near.shape[3]
    for l in range(layers):
        full = []
        for k in range(4):
            core = (k % 2) ^ m[2]
            full.append(jnp.where(m[1] == k // 2, near[core, l], far[core, l]).astype(f32))
        every = jnp.concatenate(full, axis=1)
        wide[l, 0:4, :] = every[0:4]
        wide[l, 4:6, :] = every[6:8]
        wide[l, 6:8, :] = jnp.zeros((2, 4 * q), f32)
        here = [jnp.where(m[2] == 0, full[2 * xside], full[2 * xside + 1]) for xside in range(2)]
        pick = lambda r: [a[r : r + 1] for a in here]
        none = jnp.zeros((1, 2 * q), f32)
        qkv_bias[l] = jnp.concatenate(pick(4) + [none] + pick(5), axis=1)
        rest = [a[r : r + 1] for a in here for r in range(8, a.shape[0])]
        fcb[l] = jnp.concatenate(rest, axis=1)


def pack_small_body(q, m, *refs):
    out = refs[-1]
    count = len(refs[:-1]) // out.shape[0]
    for l in range(out.shape[0]):
        sum_qkv, attn, mlp, pre, gain_c, shift_c, gain_a, shift_a = refs[l * count : (l + 1) * count]

        def mine(ref):
            bits = [ref[:, k * q : (k + 1) * q] for k in range(4)]
            return jnp.where(
                m[1] == 0, jnp.where(m[2] == 0, bits[0], bits[1]), jnp.where(m[2] == 0, bits[2], bits[3])
            )

        side = lambda ref, at, n: jnp.where(m[1] == 0, ref[:, at : at + n], ref[:, at + n : at + 2 * n])
        row = [mine(gain_a), mine(gain_c), mine(shift_a), mine(shift_c)]
        row += [side(sum_qkv, 0, q), side(sum_qkv, 4 * q, q), mine(attn), mine(mlp), side(pre, 0, 4 * q)]
        out[l : l + 1, :] = jnp.concatenate(row, axis=1)


def pack_small(sidx, small, q):
    arrays = [a for row in small for a in row]
    ins = [(a, a.shape, whole(a.shape)) for a in arrays]
    shape = (len(small), 12 * q)
    outs = [(sds(shape, f32), shape, whole(shape))]
    return call(functools.partial(pack_small_body, q), "pack_small", sidx, (1,), ins, outs, [], 0, 16)[0]


def spread_small_body(q, m, all_ref, gain, shift, qv, outb, fcb):
    for l in range(all_ref.shape[0]):
        for k, ref in enumerate((gain, shift, qv, outb)):
            for i in range(2):
                at = (2 * k + i) * q
                ref[l, i : i + 1, :] = all_ref[l : l + 1, at : at + q]
    fcb[...] = all_ref[:, 8 * q :]


def spread_small(sidx, sums, q):
    layers = sums.shape[0]
    ins = [(sums, sums.shape, whole(sums.shape))]
    shapes = [(layers, 2, q)] * 4 + [(layers, 4 * q)]
    outs = [(sds(sh, f32), sh, whole(sh)) for sh in shapes]
    return call(functools.partial(spread_small_body, q), "spread_small", sidx, (1,), ins, outs, [], 0, 16)


def gather_vectors(norm_gain, norm_bias, qv_bias, out_bias, fc_bias):
    layers, _, q = norm_gain.shape
    mine = jnp.concatenate(
        [norm_gain, norm_bias, qv_bias, out_bias, fc_bias.reshape(layers, -1, q)], axis=1
    )
    return jnp.stack([mine, swap(mine, SWAP_CORE)])


def vectors(sidx, near, far):
    _, layers, rows, q = near.shape
    ins = [(a, a.shape, whole(a.shape)) for a in (near, far)]
    hidden = 2 * (rows - 8) * q
    outs = []
    for shape in ((layers, 8, 4 * q), (layers, 1, 6 * q), (layers, 1, hidden)):
        outs.append((sds(shape, f32), shape, whole(shape)))
    return call(vectors_body, "vectors", sidx, (1,), ins, outs, [], near.size, 16)


def on_device(
    block_input,
    output_cotangent,
    doc_ids,
    w_qkv,
    w_o,
    w_fc,
    w_proj,
    norm_gain,
    norm_bias,
    qv_bias,
    out_bias,
    fc_bias,
):
    sidx = place_index()
    s, xi, core = sidx[0], sidx[1], sidx[2]
    layers = w_qkv.shape[0]
    quarter = w_qkv.shape[1]
    tokens = doc_ids.shape[1]
    drow = doc_ids
    dcol = doc_ids.reshape(tokens, 1)

    def pin(outs, *groups):
        flat, tree = jax.tree.flatten((outs, groups))
        outs, groups = jax.tree.unflatten(tree, lax.optimization_barrier(flat))
        return (outs,) + tuple(groups)

    ringed = lax.axis_size("rows") == 8
    args = (w_qkv, w_fc, w_o, w_proj)
    piece = None
    if ringed:
        piece = far_piece(sidx, 0, w_fc, w_qkv)
        args, piece = pin(args, piece)
        piece = cross(piece[0])
    keep, send, fc_keep, fc_send, o = split_columns(sidx, *args[:3], 0)
    params = gather_vectors(norm_gain, norm_bias, qv_bias, out_bias, fc_bias)
    args, piece, keep, send, fc_keep, fc_send, o, params = pin(
        args, piece, keep, send, fc_keep, fc_send, o, params
    )
    x_far = swap(block_input[0], SWAP_X)
    params = (params, swap(params, SWAP_X))
    far_0 = [piece] if ringed else None
    ring_pass(far_0, 1)
    wo = [[w_o, swap(o, SWAP_X)], None]
    halves_0 = halves_1 = None
    if ringed:
        wq = [[keep, swap(send, SWAP_CORE)], None]
        near_0 = [fc_keep, swap(fc_send, SWAP_CORE), w_proj]
        halves_0 = args[3][0]
        halves_1 = args[3][1, : 2 * quarter]
    else:
        wq = [column_pieces(keep, send), None]
        near_0 = column_pieces(fc_keep, fc_send) + row_pieces(w_proj[0])
    keep, send, fc_keep, fc_send, o_next = split_columns(sidx, *args[:3], 1)
    far_0, x_far, params, keep, send, o_next, fc_send, args, wq[0], near_0, halves_0, halves_1 = pin(
        far_0, x_far, params, keep, send, o_next, fc_send, args, wq[0], near_0, halves_0, halves_1
    )
    xs = gather_rows(block_input[0], x_far)
    ring_pass(far_0, 2)
    fc_near = swap(fc_send, SWAP_CORE)
    piece = far_piece(sidx, 1, args[1], args[3]) if ringed else None
    far_0, xs, piece, fc_near, wo[0] = pin(far_0, xs, piece, fc_near, wo[0])
    if ringed:
        piece = [cross(piece[0]), swap(piece[1], SWAP_X)]
    wide, qkv_bias, fcb = vectors(sidx, *params)
    ring_pass(far_0, 3)
    far_0, piece, wide, halves_0, keep, send, o_next = pin(far_0, piece, wide, halves_0, keep, send, o_next)
    far_1 = [jnp.concatenate(piece, axis=1)] if ringed else None
    ring_pass(far_0, 4)
    ring_pass(far_1, 1)
    xs, far_0, far_1, o_next, keep, send = pin(xs, far_0, far_1, o_next, keep, send)
    if ringed:
        both = swap(jnp.concatenate([keep, o_next], axis=1), SWAP_X)
        wq[1] = [keep, swap(send, SWAP_CORE), both, swap(send, SWAP_BOTH)]
        wo[1] = [w_o, both]
        wq[0] += far_0
        near_0 += [swap(halves_0, SWAP_X)]
        near_1 = [fc_keep, fc_near, w_proj, halves_1]
    else:
        near_1 = column_pieces(fc_keep, fc_send) + row_pieces(w_proj[1])
        wq[1] = column_pieces(keep, send)
        wo[1] = [w_o, swap(o_next, SWAP_X)]

    outs = attn_block_forward(sidx, 0, (xs,), wo[0], wq[0], wide[0], wide[0], qkv_bias[0], drow, dcol)
    ring_pass(far_1, 2)
    outs, far_1, near_0, wq[1][3] = pin(outs, far_1, near_0, wq[1][3])
    ln_a, qkv, att, part, lse = outs
    save_a = [(xs, ln_a, qkv, att, lse)]
    recv = swap(part, SWAP_CORE)
    outs = mlp_block(sidx, 0, wide[0], near_0 + (far_0 or []), ahead=(xs, part, recv), fcb=fcb[0])
    ring_pass(far_1, 3)
    outs, wq[1], far_1 = pin(outs, wq[1], far_1)
    wo[1] = [w_o, wq[1][2] if ringed else wo[1][1]]
    cot_far = swap(output_cotangent[0], SWAP_X)
    if ringed:
        near_1[3] = swap(near_1[3], SWAP_X)
    mid, part, ln_c, act, slope = outs
    save_m = (ln_c, act, slope)
    mids = [mid]
    recv = swap(part, SWAP_CORE)
    outs = attn_block_forward(
        sidx, 1, (mid, part, recv), wo[1], wq[1], wide[1], wide[0], qkv_bias[1], drow, dcol
    )
    ring_pass(far_1, 4)
    outs, near_1, far_1, cot_far = pin(outs, near_1, far_1, cot_far)
    cot = gather_rows(output_cotangent[0], cot_far)
    x, ln_a, qkv, att, part, lse = outs
    save_a.append((x, ln_a, qkv, att, lse))
    recv = swap(part, SWAP_CORE)
    outs = mlp_block(sidx, 1, wide[1], near_1 + (far_1 or []), ahead=(x, part, recv), back=(cot,), fcb=fcb[1])
    mid, part, own_mid, part_b, *pack, sum_mlp, sum_pre = outs
    mids.append(mid)

    small = [None] * layers

    d = 4 * quarter
    shapes_m = [(quarter, 4 * d), (d, d)]
    shapes_a = [(quarter, 3 * d), (quarter, d)]
    m_part, a_part, both = (quarter, d), (quarter // 2, d), (3 * quarter // 2, d)

    recv = swap(part_b, SWAP_CORE)
    own_m1, other_m1, *send = pack
    from_m1 = [swap(a, SWAP_CORE) for a in send]
    got_m1 = [along_y(other_m1), along_y(from_m1[1])] if ringed else None
    outs = attn_block_backward(sidx, 1, cot, mids[1], part_b, recv, wo[1], *save_a[1][2:4], save_a[1][1], wq[1], wide[1], drow, dcol, save_a[1][4])
    outs, got_m1, from_m1 = pin(outs, got_m1, from_m1)
    gm, part_b, own_a1, other_a1, send, sum_attn, gain_c, shift_c, sum_qkv = outs
    small[1] = [sum_qkv, sum_attn, sum_mlp, sum_pre, gain_c, shift_c]
    from_a1 = swap(send, SWAP_CORE)
    recv = swap(part_b, SWAP_CORE)
    if ringed:
        parts_m1 = sum_kernel(
            split_mlp_body, "split_mlp", sidx, (own_m1, from_m1[0], *got_m1), [m_part] * 4, (d, d)
        )
        other_a1 = pack_attn(sidx, other_a1, from_a1, 1)
        recv, parts_m1, other_a1 = pin(recv, parts_m1, other_a1)
        moved = along_z(parts_m1[1:])
        got_a1 = along_y(other_a1)

    outs = mlp_block(sidx, 0, wide[1], near_0 + (far_0 or []), back=(gm, save_a[1][0], part_b, recv, save_m[2], save_m[1], save_m[0]))
    if ringed:
        outs, moved, got_a1 = pin(outs, moved, got_a1)
    g, part_b, own_m0, other_m0, *send, sum_mlp, sum_pre, gain_a, shift_a = outs
    small[1] += [gain_a, shift_a]
    recv = swap(part_b, SWAP_CORE)
    from_m0 = [swap(a, SWAP_CORE) for a in send]
    if ringed:
        total_m1, keep_a1, *parts = sum_kernel(
            mlp_total_attn_split_body,
            "total_mlp_split_attn",
            sidx,
            (parts_m1[0], *moved, own_a1, from_a1, got_a1),
            [m_part, a_part] + [both] * 3,
            (2 * quarter, d),
        )
        recv, parts, other_m0, from_m0 = pin(recv, parts, other_m0, from_m0)
        moved_1 = along_z(parts)
        got_m0 = [along_y(other_m0), along_y(from_m0[1])]

    outs = attn_block_backward(sidx, 0, g, mids[0], part_b, recv, wo[0], *save_a[0][2:4], save_a[0][1], wq[0], wide[0], drow, dcol, save_a[0][4])
    if ringed:
        outs, moved_1, got_m0 = pin(outs, moved_1, got_m0)
    gm, part_b, own_a0, other_a0, send, sum_attn, gain_c, shift_c, sum_qkv = outs
    small[0] = [sum_qkv, sum_attn, sum_mlp, sum_pre, gain_c, shift_c]
    recv_b = swap(part_b, SWAP_CORE)
    from_a0 = swap(send, SWAP_CORE)
    at = s * block_input.shape[1]
    own = lambda a: lax.dynamic_slice_in_dim(a, at, block_input.shape[1]).astype(f32)

    def rest():
        grad_input, gain_a, shift_a = input_backward(sidx, gm, xs, part_b, recv_b, wide[0])
        small[0].extend([gain_a, shift_a])
        vecs = pack_small(sidx, small, quarter)
        result = own_mid + branch_scale * (own(part) + own(swap(part, SWAP_CORE)) + wide[layers - 1][OUT_M])
        return grad_input, result, vecs

    if ringed:
        total_a1, keep_m0, *parts, by_y = sum_kernel(
            phase_load_body,
            "phase_load",
            sidx,
            (keep_a1, *moved_1, total_m1, own_m0, from_m0[0], *got_m0, other_a0, from_a0),
            [a_part, m_part] + [both] * 3 + [(6 * quarter, d)],
            (d, d),
        )
        parts, by_y, recv_b = pin(parts, by_y, recv_b)
        moved_2 = along_z(parts)
        got_y = along_y(by_y)
        grad_input, result, vecs = rest()
        vecs = vecs + pair_row(vecs, 1)
        moved_2, got_y, vecs, result = pin(moved_2, got_y, vecs, result)
        total_m0, near_a1 = sum_kernel(
            mlp_total_body, "total_mlp", sidx, (keep_m0, total_a1, *moved_2), [m_part, (2 * quarter, d)]
        )
        near_m0 = [total_m0] + along_z([total_m0] * 3)
        far_a1 = along_y(near_a1)
        far_m0 = [along_y(total_m0)]
        keep_a0, *parts = sum_kernel(
            split_attn_body, "split_attn", sidx, (own_a0, from_a0, got_y), [a_part] * 4, (2 * quarter, d)
        )
        outs_m = finish(
            finish_mlp_body, "unpack_mlp", sidx, 1, layers, (by_y, got_y), None, shapes_m, 2 * quarter
        )
        vecs = vecs + pair_row(vecs, 2)
        near_m0, far_a1, far_m0, parts, vecs, outs_m = pin(near_m0, far_a1, far_m0, parts, vecs, outs_m)
        moved_a0 = along_z(parts)
        far_m0 += [along_y(a) for a in near_m0[1:]]
        vecs = vecs + pair_row(vecs, 4)
        outs_a = finish(finish_attn_body, "unpack_attn", sidx, 1, layers, (near_a1, far_a1), None, shapes_a)
        moved_a0, vecs, outs_a = pin(moved_a0, vecs, outs_a)
        total_a0 = total_low(keep_a0, moved_a0)
        near_a0 = [total_a0] + along_z([total_a0] * 3)
        small_out = spread_small(sidx, vecs, quarter)
        near_a0, far_m0, small_out = pin(near_a0, far_m0, small_out)
        near_a0 = jnp.concatenate(near_a0)
        far_a0 = along_y(near_a0)
        pair_m0, pair_a0 = (near_m0, far_m0), (near_a0, far_a0)
    else:
        grad_input, result, vecs = rest()
        sums = []
        for mine, other, recv in ((own_m1, other_m1, from_m1), (own_m0, other_m0, from_m0)):
            sums += [jnp.concatenate([mine, recv[0]]), jnp.concatenate([other, recv[1]])]
        for mine, other, recv in ((own_a1, other_a1, from_a1), (own_a0, other_a0, from_a0)):
            sums += [pack_attn(sidx, mine, recv, 0), pack_attn(sidx, other, recv, 1)]
        sums = lax.psum(sums, "rows")
        outs_m = finish(finish_mlp_body, "unpack_mlp", sidx, 1, layers, sums[0:2], None, shapes_m)
        outs_a = finish(finish_attn_body, "unpack_attn", sidx, 1, layers, sums[4:6], None, shapes_a)
        pair_m0, pair_a0 = sums[2:4], sums[6:8]
        small_out = spread_small(sidx, lax.psum(vecs, "rows"), quarter)
    out_gain, out_shift, out_qv, out_out, out_fcb = small_out
    out_fc, out_proj = finish(finish_mlp_body, "unpack_mlp", sidx, 0, layers, pair_m0, outs_m, shapes_m)
    out_qkv, out_o = finish(finish_attn_body, "unpack_attn", sidx, 0, layers, pair_a0, outs_a, shapes_a)
    return (
        result[None],
        grad_input[None],
        out_qkv,
        out_o,
        out_fc,
        out_proj,
        out_gain,
        out_shift,
        out_qv,
        out_out,
        out_fcb,
    )


def solution(mesh):
    in_specs = (
        P("rows", "seq", None),
        P("rows", "seq", None),
        P("rows", None),
        P(None, "seq", None),
        P(None, "seq", None),
        P(None, "seq", None),
        P(None, "seq", None),
        P(None, None, "seq"),
        P(None, None, "seq"),
        P(None, None, "seq"),
        P(None, None, "seq"),
        P(None, "seq"),
    )
    out_specs = (
        P("rows", "seq", None),
        P("rows", "seq", None),
        P(None, "seq", None),
        P(None, "seq", None),
        P(None, "seq", None),
        P(None, "seq", None),
        P(None, None, "seq"),
        P(None, None, "seq"),
        P(None, None, "seq"),
        P(None, None, "seq"),
        P(None, "seq"),
    )
    return jax.shard_map(
        on_device, mesh=mesh, in_specs=in_specs, out_specs=out_specs, check_vma=False
    )
```

```python
import functools
import math

import jax
import jax.numpy as jnp
from jax import lax
from jax.experimental import pallas as pl
from jax.experimental.pallas import tpu as pltpu
from jax.sharding import PartitionSpec as P

HD = 64
branch_scale = 48.0 ** (-0.5)
norm_eps = 1e-05
masked_score = -1e30
log2_e = math.log2(math.e)
MIB = 1 << 20
VMEM = 62
BLK = 256

f32 = jnp.float32
bf16 = jnp.bfloat16
STREAM = bf16

SWAP_CORE = [(s, s ^ 1) for s in range(4)]
SWAP_X = [(s, s ^ 2) for s in range(4)]
SWAP_BOTH = [(s, s ^ 3) for s in range(4)]


def dot_nn(a, b):
    return lax.dot_general(a, b, (((1,), (0,)), ((), ())), preferred_element_type=f32)


def dot_nt(a, b):
    return lax.dot_general(a, b, (((1,), (1,)), ((), ())), preferred_element_type=f32)


def dot_tn(a, b):
    return lax.dot_general(a, b, (((0,), (0,)), ((), ())), preferred_element_type=f32)


def call(body, name, sidx, grid, ins, outs, scratch, flops, vmem, exps=0):
    arrays = [a for a, _, _ in ins]
    in_specs = [
        pl.BlockSpec(memory_space=pl.ANY) if b is None else pl.BlockSpec(b, m) for _, b, m in ins
    ]
    out_specs = [
        pl.BlockSpec(memory_space=pl.ANY) if b is None else pl.BlockSpec(b, m) for _, b, m in outs
    ]
    out_shape = [s for s, _, _ in outs]
    nbytes = sum(a.size * a.dtype.itemsize for a in arrays)
    nbytes += sum(math.prod(s.shape) * s.dtype.itemsize for s in out_shape)
    return pl.pallas_call(
        body,
        name=name,
        grid_spec=pltpu.PrefetchScalarGridSpec(
            num_scalar_prefetch=1,
            grid=grid,
            in_specs=in_specs,
            out_specs=out_specs,
            scratch_shapes=scratch,
        ),
        out_shape=out_shape,
        compiler_params=pltpu.CompilerParams(
            dimension_semantics=("arbitrary",) * len(grid), vmem_limit_bytes=vmem * MIB
        ),
        cost_estimate=pl.CostEstimate(
            flops=int(flops), bytes_accessed=int(nbytes), transcendentals=int(exps)
        ),
    )(sidx, *arrays)


RING = [0, 2, 4, 6, 7, 5, 3, 1]
RING_NEXT = [(RING[i], RING[(i + 1) % 8]) for i in range(8)]
RING_PREV = [(b, a) for a, b in RING_NEXT]
RING_STEPS = [0, -1, 1, -2, 2, -3, 3, -4]


def ring_place():
    row = lax.axis_index("rows").astype(jnp.int32)
    return jnp.where(row % 2 == 0, row // 2, 7 - row // 2)


def place_index():
    s = lax.axis_index("seq").astype(jnp.int32)
    zero = jnp.int32(0)
    row = lax.axis_index("rows").astype(jnp.int32) if lax.axis_size("rows") == 8 else zero
    place = ring_place() if lax.axis_size("rows") == 8 else zero
    return jnp.stack([s, s // 2, s % 2, place, row % 2, row // 2])


def sds(shape, dtype):
    return jax.ShapeDtypeStruct(shape, dtype)


def whole(block):
    zeros = (0,) * len(block)
    return lambda i, m: zeros


def row_tile(i, m):
    return (i, 0)


def stack_tile(i, m):
    return (i ^ m[0], 0, 0)


def normed(x):
    centre = x - jnp.mean(x, axis=-1, keepdims=True)
    spread = jnp.mean(centre * centre, axis=-1, keepdims=True)
    rstd = lax.rsqrt(spread + norm_eps)
    return centre * rstd, rstd


def norm_back(x, grad, gain):
    unit, rstd = normed(x)
    inner = grad * gain
    mean_inner = jnp.mean(inner, axis=-1, keepdims=True)
    mean_prod = jnp.mean(inner * unit, axis=-1, keepdims=True)
    return rstd * (inner - mean_inner - unit * mean_prod), unit


GAIN_A, GAIN_C, SHIFT_A, SHIFT_C, OUT_A, OUT_M = range(6)


def row_of(ref, k):
    return ref[k : k + 1, :]


def lane_half(shape):
    return lax.broadcasted_iota(jnp.int32, shape, 1) // HD


def block_start(i):
    return BLK * (i * (i + 1) // 2)


class Mover:
    def __init__(self, sems):
        self.sems = sems
        self.used = 0

    def make(self, src, dst):
        cp = pltpu.make_async_copy(src, dst, self.sems.at[self.used])
        self.used += 1
        return cp

    def go(self, src, dst):
        cp = self.make(src, dst)
        cp.start()
        return cp


def wait_all(copies):
    for cp in copies:
        cp.wait()


def tile_of(i):
    return pl.ds(i * BLK, BLK)


def pieces_in(mover, refs, dst, first, rows, at=0):
    out = []
    width = dst.shape[1]
    for j, ref in enumerate(refs):
        where = pl.multiple_of((first ^ j) * rows, 16)
        src = ref if ref.shape[1] == width else ref.at[:, pl.ds(at, width)]
        out.append(mover.go(src, dst.at[pl.ds(where, rows)]))
    return out


def add_up(ref, value, start):
    here = jnp.sum(value, axis=0, keepdims=True)
    if start:
        ref[...] = here
    else:
        ref[...] += here


def back_pair(pair, pairs, tokens, qkv, att, datt, lse, bias, starts, dqkv, dq_acc):
    blocks = tokens // BLK
    half = lane_half((BLK, 2 * HD))
    score_scale = HD ** (-0.5)
    scale = score_scale * log2_e
    pick_row = lax.broadcasted_iota(jnp.int32, (8, 2 * HD), 0)
    pick = jnp.where(lane_half((8, 2 * HD)) == pick_row, 1.0, 0.0)
    prod = datt[pair].astype(f32) * att[pair].astype(f32)
    delta = lax.dot_general(
        pick, prod, (((1,), (1,)), ((), ())), precision=lax.Precision.HIGHEST, preferred_element_type=f32
    )
    for j in range(blocks):
        first = j * BLK
        span = slice(first, first + BLK)
        rest = pl.ds(first, tokens - first)
        kj = qkv[pair + pairs, span, :]
        vj = qkv[pair + 2 * pairs, span, :]
        qq = qkv[pair, rest, :]
        dd = datt[pair, rest, :]
        width = tokens - first
        zero = jnp.zeros_like(kj)
        dks, dvs, dss, khs = [], [], [], []
        for h in range(2):
            kh = jnp.where(half == h, kj, zero)
            vh = jnp.where(half == h, vj, zero)
            t = dot_nt(kh, qq) * scale + bias[:, starts[j] : starts[j] + width]
            p = jnp.exp2(t - lse[pair, h : h + 1, first:])
            dp = dot_nt(vh, dd)
            ds = (p * (dp - delta[h : h + 1, first:])).astype(bf16)
            dvs.append(dot_nn(p.astype(bf16), dd))
            dks.append(dot_nn(ds, qq))
            dss.append(ds)
            khs.append(kh)
        dk = jnp.where(half == 0, dks[0], dks[1]) * score_scale
        dv = jnp.where(half == 0, dvs[0], dvs[1])
        dqkv[pair + pairs, span, :] = dk.astype(bf16)
        dqkv[pair + 2 * pairs, span, :] = dv.astype(bf16)
        dq = dot_tn(jnp.concatenate(dss, axis=0), jnp.concatenate(khs, axis=0))
        if j == 0:
            dq_acc[...] = dq
        else:
            dq_acc[first:, :] += dq
    dqkv[pair] = (dq_acc[...] * score_scale).astype(bf16)


def forward_pair(pair, pairs, blocks, qkv, bias, att, lse):
    half = lane_half((BLK, 2 * HD))
    scale = HD ** (-0.5) * log2_e
    for i in range(blocks):
        width = BLK * (i + 1)
        span = slice(i * BLK, (i + 1) * BLK)
        qb = qkv[pair, span, :]
        kk = qkv[pair + pairs, 0:width, :]
        vv = qkv[pair + 2 * pairs, 0:width, :]
        mixed, logs = [], []
        for h in range(2):
            qh = jnp.where(half == h, qb, jnp.zeros_like(qb))
            t = dot_nt(qh, kk) * scale + bias[:, block_start(i) : block_start(i) + width]
            top = jnp.max(t, axis=-1, keepdims=True)
            p = jnp.exp2(t - top)
            total = jnp.sum(p, axis=-1, keepdims=True)
            o = dot_nn(p.astype(bf16), vv)
            mixed.append(o / total)
            logs.append(jnp.broadcast_to(top + jnp.log2(total), (BLK, 2 * HD)))
        att[pair, span, :] = jnp.where(half == 0, mixed[0], mixed[1]).astype(bf16)
        turned = jnp.transpose(jnp.where(half == 0, logs[0], logs[1]))
        lse[pair, 0:1, span] = turned[0:1, :]
        lse[pair, 1:2, span] = turned[HD : HD + 1, :]


def attn_block_body(l, first, parts_w, m, *refs):
    count = 1 if first else 3
    sources = refs[:count]
    wo0, wo1 = refs[count : count + 2]
    weights = refs[count + 2 : count + 2 + parts_w]
    refs = refs[count + 2 + parts_w :]
    vec, prev, bias_row, drow, dcol = refs[:5]
    refs = refs[5:]
    if not first:
        x_out, refs = refs[0], refs[1:]
    ln_out, qkv_out, att_out, part_out, lse = refs[:5]
    bufs = refs[5 : 5 + count]
    (wo, w, lns, qkv, att, parts, bias, sems) = refs[5 + count :]
    tokens, d = lns.shape
    blocks = tokens // BLK
    pairs = att.shape[0]
    half = d // 2
    q = half // 2
    move = Mover(sems)
    c_w = attn_weights_in(move, m, weights, w, q)
    c_tiles = []
    for t in range(blocks):
        for ref, dst in zip(sources, bufs):
            src = ref.at[t ^ m[0]] if len(ref.shape) == 3 else ref.at[tile_of(t)]
            c_tiles.append(move.go(src, dst.at[tile_of(t)]))
    c_wo = pieces_in(move, (wo0.at[l], wo1), wo, m[1], q, w.shape[1])
    for i in range(blocks):
        width = BLK * (i + 1)
        begin = i * BLK
        qpos = begin + lax.broadcasted_iota(jnp.int32, (BLK, width), 0)
        kpos = lax.broadcasted_iota(jnp.int32, (BLK, width), 1)
        same = dcol[begin : begin + BLK, :] == drow[:, :width]
        allowed = (kpos <= qpos) & same
        bias[:, block_start(i) : block_start(i) + width] = jnp.where(allowed, 0.0, masked_score)
    wait_all(c_w)
    wait_all(c_tiles)
    c_out = []
    mine = pl.ds(pl.multiple_of(m[1] * half, 128), half)
    for t in range(blocks):
        span = tile_of(t)
        if first:
            x = bufs[0][span, :].astype(f32)
        else:
            part = bufs[1][span, :].astype(f32) + bufs[2][span, :].astype(f32) + row_of(prev, OUT_M)
            x = bufs[0][span, :].astype(f32) + branch_scale * part
            bufs[0][span, :] = x.astype(STREAM)
            c_out.append(move.go(bufs[0].at[span], x_out.at[span]))
        unit, _ = normed(x)
        ln = (unit * row_of(vec, GAIN_A) + row_of(vec, SHIFT_A)).astype(bf16)
        lns[span, :] = ln
        c_out.append(move.go(lns.at[span, mine], ln_out.at[span]))
        row = (dot_nn(ln, w[...]) + bias_row[...]).astype(bf16)
        for k in range(3 * pairs):
            cols = slice(k * 2 * HD, (k + 1) * 2 * HD)
            qkv[k, span, :] = row[:, cols]
    for k in range(3 * pairs):
        c_out.append(move.go(qkv.at[k], qkv_out.at[k]))

    @pl.loop(0, pairs)
    def _(pair):
        forward_pair(pair, pairs, blocks, qkv, bias, att, lse)

    for k in range(pairs):
        c_out.append(move.go(att.at[k], att_out.at[k]))
    wait_all(c_wo)
    for t in range(blocks):
        span = tile_of(t)
        row = jnp.concatenate([att[k, span, :] for k in range(pairs)], axis=1)
        parts[span, :] = dot_nn(row, wo[...]).astype(bf16)
        c_out.append(move.go(parts.at[span], part_out.at[span]))
    wait_all(c_out)


def attn_block_forward(sidx, l, source, wo_pieces, pieces, vec, prev, bias, drow, dcol):
    first = len(source) == 1
    q, cols = pieces[0].shape
    d = 4 * q
    tokens = drow.shape[1]
    width = cols // 3
    pairs = width // (2 * HD)
    ins = [(a, None, None) for a in (*source, *wo_pieces, *pieces)]
    ins += [(a, a.shape, whole(a.shape)) for a in (vec, prev, bias, drow, dcol)]
    outs = [] if first else [(sds((tokens, d), STREAM), None, None)]
    outs += [
        (sds((tokens, d // 2), bf16), None, None),
        (sds((3 * pairs, tokens, 2 * HD), bf16), None, None),
        (sds((pairs, tokens, 2 * HD), bf16), None, None),
        (sds((tokens, d), bf16), None, None),
        (sds((pairs, 8, tokens), f32), (pairs, 8, tokens), whole((0, 0, 0))),
    ]
    blocks = tokens // BLK
    scratch = [pltpu.VMEM((tokens, d), a.dtype) for a in source]
    scratch += [
        pltpu.VMEM((width, d), bf16),
        pltpu.VMEM((d, cols), bf16),
        pltpu.VMEM((tokens, d), bf16),
        pltpu.VMEM((3 * pairs, tokens, 2 * HD), bf16),
        pltpu.VMEM((pairs, tokens, 2 * HD), bf16),
        pltpu.VMEM((tokens, d), bf16),
        pltpu.VMEM((BLK, block_start(blocks)), f32),
        pltpu.SemaphoreType.DMA((64,)),
    ]
    return call(
        functools.partial(attn_block_body, l, first, len(pieces)),
        "attention_block",
        sidx,
        (1,),
        ins,
        outs,
        scratch,
        4 * tokens * tokens * width + 2 * tokens * d * (cols + width),
        VMEM,
        exps=tokens * tokens * pairs,
    )


def far_in(move, m, refs, dst, q, lanes):
    out = []
    part = q // 4
    for ref, t in zip(refs, RING_STEPS):
        chunk = (m[3] + t + len(refs)) % len(refs)
        at = pl.multiple_of((m[0] ^ (2 + chunk // 4)) * q + (chunk % 4) * part, 16)
        out.append(move.go(ref.at[:, lanes], dst.at[pl.ds(at, part)]))
    return out


def attn_weights_in(move, m, refs, w, q):
    out = pieces_in(move, refs[:4] if len(refs) == 4 else refs[:2], w, m[0], q)
    if len(refs) > 4:
        out += far_in(move, m, refs[2:], w, q, pl.ds(0, w.shape[1]))
    return out


def mlp_weights_in(move, l, m, refs, wf, wp):
    if len(refs) == 6:
        first = pieces_in(move, refs[:4], wf, m[0], refs[0].shape[0])
        return first, pieces_in(move, refs[4:], wp, m[1], refs[4].shape[0])
    keep, near, own = refs[0], refs[1], refs[2].at[l]
    q, hidden = keep.shape
    deep = own.shape[0]
    half = deep // 2
    far = refs[-8:]
    base = far[0].shape[1] - hidden if l == 0 else 0
    first = pieces_in(move, (keep, near), wf, m[0], q)
    first += far_in(move, m, far, wf, q, pl.ds(base, hidden))
    second = pieces_in(move, (own,), wp, m[1], deep)
    there = (1 - m[1]) * deep
    at = pl.multiple_of(there, 16)
    second.append(move.go(refs[3], wp.at[pl.ds(at, refs[3].shape[0])]))
    if l:
        part = q // 4
        for ref, t in zip(far, RING_STEPS):
            chunk = (m[3] + t + 8) % 8
            at = pl.multiple_of(there + half + chunk * part, 16)
            src = ref.at[:, pl.ds(hidden, own.shape[1])]
            second.append(move.go(src, wp.at[pl.ds(at, part)]))
    return first, second


def gelu_and_slope(pre):
    root = math.sqrt(2.0 / math.pi)
    sq = pre * pre
    gate = 0.5 * jnp.tanh(pre * (root + root * 0.044715 * sq)) + 0.5
    rise = pre * (2.0 * root + 6.0 * root * 0.044715 * sq)
    return pre * gate, gate + gate * ((1.0 - gate) * rise)


def mlp_block_body(l, ahead, back, count, m, *refs):
    take = lambda k: (refs[:k], refs[k:])
    vec = prev = fcb = None
    sources, refs = take(3 if ahead else 0)
    (cot,), refs = take(1) if ahead and back else ((None,), refs)
    grads, refs = take(4 if back and not ahead else 0)
    (slope_in, act_in, ln_in), refs = take(3) if back and not ahead else ((None,) * 3, refs)
    weights, refs = take(count)
    if ahead:
        (vec, fcb), refs = take(2)
    else:
        (vec,), refs = take(1)
    if ahead:
        (mid_out, part_out), refs = take(2)
        if back:
            (own_out,), refs = take(1)
        else:
            (ln_out, act_out, slope_out), refs = take(3)
    if back:
        if not ahead:
            (g_out,), refs = take(1)
        (back_out, mine, other, send_mine, send_other, sum_mlp, sum_pre), refs = take(7)
        if not ahead:
            (sum_gain, sum_shift), refs = take(2)
    b0, b1, b2, b3, wf, wp, lns, act, slope, dmlp, sems = refs
    tokens, d = b1.shape
    blocks = tokens // BLK
    hidden = wf.shape[1]
    q = d // 4
    move = Mover(sems)
    c_tiles = []
    if ahead:
        loads = list(zip(sources, (b0, b1, b2))) + ([(cot, b3)] if back else [])
    else:
        loads = list(zip(grads, (b0, b1, b2, b3)))
    c_wp = []
    if ahead:
        c_wf, c_wp = mlp_weights_in(move, l, m, weights, wf, wp)
    for t in range(blocks):
        for ref, dst in loads:
            src = ref.at[t ^ m[0]] if len(ref.shape) == 3 else ref.at[tile_of(t)]
            c_tiles.append(move.go(src, dst.at[tile_of(t)]))
    if not ahead:
        c_wf, c_wp = mlp_weights_in(move, l, m, weights, wf, wp)
        c_slope = [move.go(slope_in.at[tile_of(t)], slope.at[tile_of(t)]) for t in range(blocks)]
        c_late = [move.go(act_in, act.at[:, pl.ds(0, act_in.shape[1])]), move.go(ln_in, lns.at[:, pl.ds(0, d // 2)])]
    c_out = []
    n = len(loads)
    wide = hidden // 2
    if not back:
        wait_all(c_tiles + c_wf + c_wp)
    for t in range(blocks):
        if back:
            wait_all(c_tiles[n * t : n * t + n])
        span = tile_of(t)
        if ahead:
            part = b1[span, :].astype(f32) + b2[span, :].astype(f32) + row_of(vec, OUT_A)
            mid = b0[span, :].astype(f32) + branch_scale * part
            b0[span, :] = mid.astype(b0.dtype)
            c_out.append(move.go(b0.at[span], mid_out.at[span]))
            if back:

                @pl.when(m[0] == t)
                def _():
                    own_out[...] = mid

            unit, _ = normed(mid)
            ln = (unit * row_of(vec, GAIN_C) + row_of(vec, SHIFT_C)).astype(bf16)
            lns[span, :] = ln
            if t == 0 and back:
                wait_all(c_wf)
            value, rise = gelu_and_slope(dot_nn(ln, wf[...]) + fcb[...])
            low = value.astype(bf16)
            act[span, :] = low
            if not back:
                slope[span, :] = rise.astype(bf16)
                cols = pl.ds(pl.multiple_of(m[1] * (d // 2), 128), d // 2)
                c_out.append(move.go(lns.at[span, cols], ln_out.at[span]))
                cols = pl.ds(pl.multiple_of(m[1] * wide, 128), wide)
                c_out.append(move.go(act.at[span, cols], act_out.at[span]))
                c_out.append(move.go(slope.at[span], slope_out.at[span]))
            if t == 0 and back:
                wait_all(c_wp)
            b1[span, :] = dot_nn(low, wp[...]).astype(bf16)
            c_out.append(move.go(b1.at[span], part_out.at[span]))
        if back:
            if ahead:
                g = b3[span, :].astype(f32)
            else:
                if t == 0:
                    wait_all(c_wp)
                wait_all(c_slope[t : t + 1])
                rise = slope[span, :].astype(f32)
                grad = b2[span, :].astype(f32) + b3[span, :].astype(f32)
                part, unit = norm_back(b1[span, :].astype(f32), grad, row_of(vec, GAIN_A))
                add_up(sum_gain, grad * unit, t == 0)
                add_up(sum_shift, grad, t == 0)
                g = b0[span, :].astype(f32) + part
                b0[span, :] = g.astype(b0.dtype)
                c_out.append(move.go(b0.at[span], g_out.at[span]))
            low = (branch_scale * g).astype(bf16)
            dmlp[span, :] = low
            add_up(sum_mlp, low.astype(f32), t == 0)
            dpre = (dot_nt(low, wp[...]) * rise).astype(bf16)
            slope[span, :] = dpre
            add_up(sum_pre, dpre.astype(f32), t == 0)
            if t == 0 and not ahead:
                wait_all(c_wf)
            b2[span, :] = dot_nt(dpre, wf[...]).astype(bf16)
            c_out.append(move.go(b2.at[span], back_out.at[span]))
    if back:
        y = m[4]
        if not ahead:
            wait_all(c_late)
            turned = jnp.transpose(act[:, 0:wide])
        else:
            turned = jnp.transpose(jnp.where(m[1] == 0, act[:, 0:wide], act[:, wide:]))
        grad = dot_nn(turned, dmlp[...]).astype(bf16)
        h = grad.shape[0] // 2
        mine[0:h, :] = jnp.where(y == 0, grad[:h], grad[h:])
        other[0:h, :] = jnp.where(y == 0, grad[h:], grad[:h])
        half = d // 2
        if not ahead:
            turned = jnp.transpose(lns[:, 0:half])
        else:
            turned = jnp.transpose(jnp.where(m[1] == 0, lns[:, 0:half], lns[:, half:]))
        sides = [dot_nn(turned, slope[:, i * d : (i + 1) * d]).astype(bf16) for i in range(2)]
        for here, there, i in ((mine, send_mine, 0), (other, send_other, 1)):
            side = jnp.where(y == i, sides[0], sides[1])
            here[h : h + q, :] = jnp.where(m[2] == 0, side[:q], side[q:])
            there[...] = jnp.where(m[2] == 0, side[q:], side[:q])
    wait_all(c_out)


def mlp_block(sidx, l, vec, weights, ahead=None, back=None, fcb=None):
    d = vec.shape[1]
    if ahead is not None:
        tokens = ahead[1].shape[0]
        hidden = fcb.shape[1]
        sources = list(ahead) + ([back[0]] if back else [])
        types = [STREAM if ahead[0].ndim == 2 else ahead[0].dtype, bf16, bf16, bf16]
        vectors_in = [vec, fcb]
    else:
        tokens, hidden = back[4].shape
        sources = list(back)
        types = [back[0].dtype, back[1].dtype, bf16, bf16]
        vectors_in = [vec]
    q = d // 4
    ins = [(a, None, None) for a in sources + list(weights)]
    ins += [(a, a.shape, whole(a.shape)) for a in vectors_in]
    stay = lambda shape, dtype: (sds(shape, dtype), shape, whole(shape))
    away = lambda shape, dtype: (sds(shape, dtype), None, None)
    outs = []
    if ahead is not None:
        outs += [away((tokens, d), STREAM), away((tokens, d), bf16)]
        if back:
            outs += [stay((BLK, d), f32)]
        else:
            outs += [
                away((tokens, d // 2), bf16),
                away((tokens, hidden // 2), bf16),
                away((tokens, hidden), bf16),
            ]
    if back:
        if ahead is None:
            outs += [away((tokens, d), back[0].dtype)]
        outs += [away((tokens, d), bf16)]
        outs += [stay((3 * q, d), bf16)] * 2 + [stay((q, d), bf16)] * 2
        outs += [stay((1, d), f32), stay((1, hidden), f32)]
        if ahead is None:
            outs += [stay((1, d), f32)] * 2
    scratch = [pltpu.VMEM((tokens, d), t) for t in types]
    scratch += [
        pltpu.VMEM((d, hidden), bf16),
        pltpu.VMEM((hidden, d), bf16),
        pltpu.VMEM((tokens, d), bf16),
        pltpu.VMEM((tokens, hidden), bf16),
        pltpu.VMEM((tokens, hidden), bf16),
        pltpu.VMEM((tokens, d), bf16),
        pltpu.SemaphoreType.DMA((96,)),
    ]
    return call(
        functools.partial(mlp_block_body, l, ahead is not None, bool(back), len(weights)),
        "mlp_block" + ("_forward" if ahead is not None else "") + ("_backward" if back else ""),
        sidx,
        (1,),
        ins,
        outs,
        scratch,
        (4 * bool(ahead is not None) + 8 * bool(back)) * tokens * d * hidden,
        VMEM,
        exps=tokens * hidden,
    )


def attn_block_back_body(l, parts_w, m, *refs):
    (g_in, mid_in, p_in, r_in, wo0, wo1, qkv_in, att_in, ln_in) = refs[:9]
    weights = refs[9 : 9 + parts_w]
    refs = refs[:9] + refs[9 + parts_w :]
    (vec, drow, dcol, lse) = refs[9:13]
    refs = refs[:9] + (None,) * 4 + refs[9:]
    (gm_out, part_out, mine, other, to_core) = refs[17:22]
    (sum_attn, sum_gain, sum_shift, sum_qkv) = refs[22:26]
    (gs, mids, ps, rs, wo, qkv, att, lns, w, dattn, datt, dqkv, bias, dq_acc, sems) = refs[26:]
    tokens, d = mids.shape
    blocks = tokens // BLK
    pairs = att.shape[0]
    q = d // 4
    move = Mover(sems)
    c_wo = pieces_in(move, (wo0.at[l], wo1), wo, m[1], q, w.shape[1])
    c_tiles = []
    loads = [(g_in, gs), (mid_in, mids), (p_in, ps), (r_in, rs)]
    for t in range(blocks):
        for ref, dst in loads:
            src = ref.at[t ^ m[0]] if len(ref.shape) == 3 else ref.at[tile_of(t)]
            c_tiles.append(move.go(src, dst.at[tile_of(t)]))
    c_qkv = [move.go(qkv_in, qkv), move.go(att_in, att)]
    c_w = attn_weights_in(move, m, weights, w, q)
    half = d // 2
    c_ln = [move.go(ln_in, lns)]

    starts = [sum(tokens - BLK * a for a in range(j)) for j in range(blocks)]
    for j in range(blocks):
        width = tokens - j * BLK
        first = j * BLK
        kpos = lax.broadcasted_iota(jnp.int32, (BLK, width), 0)
        qpos = lax.broadcasted_iota(jnp.int32, (BLK, width), 1)
        same = dcol[first : first + BLK, :] == drow[:, first:]
        allowed = (kpos <= qpos) & same
        bias[:, starts[j] : starts[j] + width] = jnp.where(allowed, 0.0, masked_score)

    wait_all(c_wo)
    c_out = []
    for t in range(blocks):
        wait_all(c_tiles[4 * t : 4 * t + 4])
        span = tile_of(t)
        grad = ps[span, :].astype(f32) + rs[span, :].astype(f32)
        part, unit = norm_back(mids[span, :].astype(f32), grad, row_of(vec, GAIN_C))
        add_up(sum_gain, grad * unit, t == 0)
        add_up(sum_shift, grad, t == 0)
        gm = gs[span, :].astype(f32) + part
        gs[span, :] = gm.astype(gs.dtype)
        c_out.append(move.go(gs.at[span], gm_out.at[span]))
        low = (branch_scale * gm).astype(bf16)
        dattn[span, :] = low
        add_up(sum_attn, low.astype(f32), t == 0)
        heads = dot_nt(low, wo[...]).astype(bf16)
        for k in range(pairs):
            datt[k, span, :] = heads[:, k * 2 * HD : (k + 1) * 2 * HD]

    wait_all(c_qkv)

    @pl.loop(0, pairs)
    def _(pair):
        back_pair(pair, pairs, tokens, qkv, att, datt, lse, bias, starts, dqkv, dq_acc)

    wait_all(c_w)
    for t in range(blocks):
        span = tile_of(t)
        row = jnp.concatenate([dqkv[k, span, :] for k in range(3 * pairs)], axis=1)
        ps[span, :] = dot_nt(row, w[...]).astype(bf16)
        c_out.append(move.go(ps.at[span], part_out.at[span]))
        add_up(sum_qkv, row.astype(f32), t == 0)

    wait_all(c_ln)
    quart = q // 2
    y = m[4]
    turned = jnp.concatenate([jnp.transpose(att[k]) for k in range(pairs)], axis=0)
    left = jnp.where(m[1] == 0, turned[:q], turned[q : 2 * q])
    g_o = dot_nn(left, dattn[...]).astype(bf16)
    for i in range(2):
        cols = slice(i * half, (i + 1) * half)
        a, b = g_o[:quart, cols], g_o[quart:, cols]
        mine[i * quart : (i + 1) * quart, :] = jnp.where(y == 0, a, b)
        other[i * quart : (i + 1) * quart, :] = jnp.where(y == 0, b, a)
    turned = jnp.transpose(lns[...])
    for p in range(3):
        right = jnp.concatenate([dqkv[p * pairs + k] for k in range(pairs)], axis=1)
        grad = dot_nn(turned, right).astype(bf16)
        keep = jnp.where(m[2] == 0, grad[:q], grad[q:])
        send = jnp.where(m[2] == 0, grad[q:], grad[:q])
        at = (2 + p) * quart
        mine[at : at + quart, :] = jnp.where(y == 0, keep[:quart], keep[quart:])
        other[at : at + quart, :] = jnp.where(y == 0, keep[quart:], keep[:quart])
        at = p * quart
        to_core[at : at + quart, :] = jnp.where(y == 0, send[:quart], send[quart:])
        at += 3 * quart
        to_core[at : at + quart, :] = jnp.where(y == 0, send[quart:], send[:quart])
    wait_all(c_out)


def attn_block_backward(sidx, l, g, mid, part, recv, wo_pieces, qkv, att, ln_a, pieces, vec, drow, dcol, lse):
    tokens, d = mid.shape
    q, cols = pieces[0].shape
    width = cols // 3
    pairs = width // (2 * HD)
    ins = [(a, None, None) for a in (g, mid, part, recv, *wo_pieces, qkv, att, ln_a, *pieces)]
    ins += [(a, a.shape, whole(a.shape)) for a in (vec, drow, dcol, lse)]
    stay = lambda shape, dtype: (sds(shape, dtype), shape, whole(shape))
    outs = [
        (sds((tokens, d), STREAM), None, None),
        (sds((tokens, d), bf16), None, None),
        stay((5 * q // 2, width), bf16),
        stay((5 * q // 2, width), bf16),
        stay((3 * q, width), bf16),
        stay((1, d), f32),
        stay((1, d), f32),
        stay((1, d), f32),
        stay((1, cols), f32),
    ]
    blocks = tokens // BLK
    wide = (tokens, 2 * HD)
    scratch = [
        pltpu.VMEM((tokens, d), g.dtype),
        pltpu.VMEM((tokens, d), mid.dtype),
        pltpu.VMEM((tokens, d), bf16),
        pltpu.VMEM((tokens, d), bf16),
        pltpu.VMEM((width, d), bf16),
        pltpu.VMEM((3 * pairs,) + wide, bf16),
        pltpu.VMEM((pairs,) + wide, bf16),
        pltpu.VMEM((tokens, d // 2), bf16),
        pltpu.VMEM((d, cols), bf16),
        pltpu.VMEM((tokens, d), bf16),
        pltpu.VMEM((pairs,) + wide, bf16),
        pltpu.VMEM((3 * pairs,) + wide, bf16),
        pltpu.VMEM((BLK, block_start(blocks)), f32),
        pltpu.VMEM(wide, f32),
        pltpu.SemaphoreType.DMA((64,)),
    ]
    return call(
        functools.partial(attn_block_back_body, l, len(pieces)),
        "attention_block_backward",
        sidx,
        (1,),
        ins,
        outs,
        scratch,
        10 * tokens * tokens * width,
        VMEM,
        exps=tokens * tokens * pairs,
    )


def add_rows(ref, value, start):
    @pl.when(start)
    def _():
        ref[...] = jnp.zeros_like(ref)

    ref[...] += jnp.sum(value, axis=0, keepdims=True)


def input_back_body(m, gm_ref, x_ref, p_ref, r_ref, vec, out_ref, sum_gain, sum_shift):
    tile = pl.program_id(0)
    grad = p_ref[...].astype(f32) + r_ref[...].astype(f32)
    part, unit = norm_back(x_ref[0].astype(f32), grad, row_of(vec, GAIN_A))
    add_rows(sum_gain, grad * unit, tile == 0)
    add_rows(sum_shift, grad, tile == 0)

    @pl.when(tile == m[0])
    def _():
        out_ref[...] = gm_ref[...].astype(f32) + part


def input_backward(sidx, gm, x, part, recv, vec):
    tokens, depth = gm.shape
    tile = (BLK, depth)
    ins = [(gm, tile, row_tile), (x, (1, BLK, depth), stack_tile)]
    ins += [(a, tile, row_tile) for a in (part, recv)]
    ins.append((vec, vec.shape, whole(vec.shape)))
    outs = [(sds((BLK, depth), f32), tile, whole((0, 0)))]
    outs += [(sds((1, depth), f32), (1, depth), whole((0, 0)))] * 2
    return call(input_back_body, "input_backward", sidx, (tokens // BLK,), ins, outs, [], tokens * depth, VMEM)


def swap(a, perm):
    return lax.ppermute(a, "seq", perm)


def split_body(m, qkv_ref, fc_ref, o_ref, qkv_keep, qkv_send, fc_keep, fc_send, o_out):
    core = m[2]
    o_out[...] = o_ref[0]
    q = qkv_ref.shape[1]
    pair = 2 * q
    for p in range(3):
        own, other = [], []
        for xside in range(2):
            col = (2 * p + xside) * pair
            both = qkv_ref[0, :, col : col + pair]
            own.append(jnp.where(core == 0, both[:, :q], both[:, q:]))
            other.append(jnp.where(core == 0, both[:, q:], both[:, :q]))
        qkv_keep[:, p * pair : (p + 1) * pair] = jnp.concatenate(own, axis=1)
        qkv_send[:, p * pair : (p + 1) * pair] = jnp.concatenate(other, axis=1)
    d = fc_ref.shape[2] // 4
    for xside in range(2):
        one = fc_ref[0, :, 2 * xside * d : (2 * xside + 1) * d]
        two = fc_ref[0, :, (2 * xside + 1) * d : (2 * xside + 2) * d]
        fc_keep[:, xside * d : (xside + 1) * d] = jnp.where(core == 0, one, two)
        fc_send[:, xside * d : (xside + 1) * d] = jnp.where(core == 0, two, one)


def split_columns(sidx, w_qkv, w_fc, w_o, l):
    _, rows, cols = w_qkv.shape
    hidden = w_fc.shape[2]
    at = lambda i, m: (l, 0, 0)
    depth = w_o.shape[2]
    ins = [(w_qkv, (1, rows, cols), at), (w_fc, (1, rows, hidden), at), (w_o, (1, rows, depth), at)]
    outs = []
    for width in (cols // 2, cols // 2, hidden // 2, hidden // 2, depth):
        outs.append((sds((rows, width), bf16), (rows, width), whole((0, 0))))
    return call(split_body, "split_columns", sidx, (1,), ins, outs, [], rows * cols, VMEM)


def column_pieces(keep, send):
    return [keep, swap(send, SWAP_CORE), swap(keep, SWAP_X), swap(send, SWAP_BOTH)]


def row_pieces(w):
    return [w, swap(w, SWAP_X)]


def half_columns(w, core):
    q = w.shape[1] // 12
    out = []
    for k in range(6):
        both = w[:, 2 * k * q : (2 * k + 2) * q]
        out.append(jnp.where(core == 0, both[:, :q], both[:, q:]))
    return jnp.concatenate(out, axis=1)


def far_piece_body(l, m, w_fc, w_more, out, *refs):
    rows_in, sems = refs[-2:]
    part = out.shape[0]
    hidden = w_fc.shape[2]
    d = hidden // 4
    move = Mover(sems)
    rows = pl.ds(pl.multiple_of((m[3] % 4) * part, 16), part)
    core = m[2] ^ (m[3] // 4)
    base = 0 if l else out.shape[1] - 2 * d
    copies = []
    for xside in range(2):
        here = pl.ds(pl.multiple_of((2 * xside + core) * d, 128), d)
        copies.append(move.go(w_fc.at[l, rows, here], out.at[:, pl.ds(base + xside * d, d)]))
    if l == 0:
        move.go(w_more.at[l, rows], rows_in).wait()
        out[:, :base] = half_columns(rows_in[...], core)
    else:
        rows = pl.ds(pl.multiple_of(8 * part + m[3] * part, 16), part)
        copies.append(move.go(w_more.at[l, rows], refs[0]))
    wait_all(copies)


def far_piece(sidx, l, w_fc, w_more):
    _, q, hidden = w_fc.shape
    d, part = hidden // 4, q // 4
    widths = [hidden // 2 + w_more.shape[2] // 2] if l == 0 else [hidden // 2, d]
    ins = [(a, None, None) for a in (w_fc, w_more)]
    outs = [(sds((part, w), bf16), (part, w), whole((0, 0))) for w in widths]
    scratch = [pltpu.VMEM((part, w_more.shape[2]), bf16), pltpu.SemaphoreType.DMA((4,))]
    return call(
        functools.partial(far_piece_body, l), "far_piece", sidx, (1,), ins, outs, scratch, 0, VMEM
    )


def cross(a):
    pairs = []
    for r in range(8):
        turn = 2 if RING.index(r) < 4 else 3
        pairs += [(4 * r + s, 4 * r + (s ^ turn)) for s in range(4)]
    return lax.ppermute(a, ("rows", "seq"), pairs)


def ring_pass(held, t):
    if held is None:
        return []
    on = lax.ppermute(held[max(0, len(held) - 2)], "rows", RING_NEXT)
    if t == 4:
        new = [on]
    else:
        new = [on, lax.ppermute(held[-1], "rows", RING_PREV)]
    held += new
    return new


def gather_rows(a, far):
    return jnp.stack([a, swap(a, SWAP_CORE), far, swap(far, SWAP_CORE)])


SWAP_Y = [(r, r ^ 1) for r in range(8)]
SWAP_Z = [None] + [[(r, r ^ (2 * d)) for r in range(8)] for d in range(1, 4)]


def join_attn(own, recv, at):
    n = own.shape[0] // 5
    bit = lambda k: own[k * n : (k + 1) * n, :]
    got = lambda k: recv[at + k * n : at + (k + 1) * n, :]
    pairs = [(bit(0), bit(1)), (bit(2), bit(3)), (bit(4), got(0)), (got(1), got(2))]
    return [jnp.concatenate(p, axis=1) for p in pairs]


def pack_attn_body(which, m, own, recv, out):
    n = out.shape[0] // 4
    for k, rows in enumerate(join_attn(own, recv, which * 3 * n)):
        out[k * n : (k + 1) * n, :] = rows


def pack_attn(sidx, own, recv, which):
    shape = (4 * (own.shape[0] // 5), 2 * own.shape[1])
    ins = [(a, a.shape, whole(a.shape)) for a in (own, recv)]
    outs = [(sds(shape, bf16), shape, whole(shape))]
    return call(
        functools.partial(pack_attn_body, which), "pack_attn", sidx, (1,), ins, outs, [], 0, 16
    )[0]


def add_low(a, b):
    return (a.astype(f32) + b.astype(f32)).astype(bf16)


def total_low(first, rest):
    return (first.astype(f32) + sum(r.astype(f32) for r in rest)).astype(bf16)


def fill_mlp(full, own, recv, got, got_recv):
    cut = own.shape[0]
    full[0:cut, :] = add_low(own[...], got[...])
    full[cut:, :] = add_low(recv[...], got_recv[...])


def fill_attn(full, own, recv, got):
    n = full.shape[0] // 4
    for k, rows in enumerate(join_attn(own, recv, 0)):
        full[k * n : (k + 1) * n, :] = add_low(rows, got[k * n : (k + 1) * n, :])


def quarter_at(full, m, d):
    n = full.shape[0] // 4
    return full[pl.ds(pl.multiple_of((m[5] ^ d) * n, 16), n), :]


def split_mlp_body(m, own, recv, got, got_recv, *refs):
    outs, full = refs[:-1], refs[-1]
    fill_mlp(full, own, recv, got, got_recv)
    for d, out in enumerate(outs):
        out[...] = quarter_at(full, m, d)


def split_attn_body(m, own, recv, got, *refs):
    outs, full = refs[:-1], refs[-1]
    fill_attn(full, own, recv, got)
    for d, out in enumerate(outs):
        out[...] = quarter_at(full, m, d)


def mlp_total_attn_split_body(m, first, g1, g2, g3, own, recv, got, total, keep, s1, s2, s3, full):
    acc = total_low(first[...], [g1[...], g2[...], g3[...]])
    total[...] = acc
    n = acc.shape[0]
    fill_attn(full, own, recv, got)
    keep[...] = quarter_at(full, m, 0)
    for d, out in enumerate((s1, s2, s3)):
        out[0:n, :] = acc
        out[n:, :] = quarter_at(full, m, d + 1)


def phase_load_body(m, first, g1, g2, g3, low, own, recv, got, got_recv, other, from_a, total, keep, s1, s2, s3, by_y, full):
    n, k = low.shape[0], first.shape[0]
    acc = total_low(first[...], [g[n:, :] for g in (g1, g2, g3)])
    total[...] = acc
    fill_mlp(full, own, recv, got, got_recv)
    keep[...] = quarter_at(full, m, 0)
    for d, out in enumerate((s1, s2, s3)):
        out[0:n, :] = quarter_at(full, m, d + 1)
        out[n:, :] = acc
    at = 0
    for rows in join_attn(other, from_a, 3 * k):
        by_y[at : at + k, :] = rows
        at += k
    for rows in (low[...], g1[0:n, :], g2[0:n, :], g3[0:n, :]):
        by_y[at : at + n, :] = rows
        at += n


def mlp_total_body(m, first, low, g1, g2, g3, total, near):
    n = first.shape[0]
    total[...] = total_low(first[...], [g[0:n, :] for g in (g1, g2, g3)])
    k = low.shape[0]
    near[0:k, :] = low[...]
    for i, g in enumerate((g1, g2, g3)):
        near[(i + 1) * k : (i + 2) * k, :] = g[n:, :]


def sum_kernel(body, name, sidx, arrays, shapes, scratch=None):
    ins = [(a, a.shape, whole(a.shape)) for a in arrays]
    outs = [(sds(sh, bf16), sh, whole(sh)) for sh in shapes]
    extra = [] if scratch is None else [pltpu.VMEM(scratch, bf16)]
    return call(body, name, sidx, (1,), ins, outs, extra, 0, VMEM)


def along_y(a):
    return lax.ppermute(a, "rows", SWAP_Y)


def along_y_and_core(a):
    pairs = [(4 * r + s, 4 * (r ^ 1) + (s ^ 1)) for r in range(8) for s in range(4)]
    return lax.ppermute(a, ("rows", "seq"), pairs)


def along_z(arrays):
    return [lax.ppermute(a, "rows", SWAP_Z[d + 1]) for d, a in enumerate(arrays)]


def pick_quarter(m, refs, k, at, n):
    if len(refs) == 1:
        return refs[0][pl.ds(pl.multiple_of(at + (k ^ m[5]) * n, 16), n), :].astype(f32)
    d = k ^ m[5]
    low = jnp.where(d % 2 == 0, refs[0][...], refs[1][...])
    high = jnp.where(d % 2 == 0, refs[2][...], refs[3][...])
    return jnp.where(d < 2, low, high).astype(f32)


def halves(m, near, far, at, n):
    def quarter(k):
        a, b = pick_quarter(m, near, k, at, n), pick_quarter(m, far, k, at, n)
        return jnp.where(m[4] == 0, a, b), jnp.where(m[4] == 0, b, a)

    return [quarter(k) for k in range(4)]


def finish_mlp_body(at, count, m, *refs):
    near, far = refs[:count], refs[count : 2 * count]
    out_fc, out_proj = refs[-2:]
    q, d = out_fc.shape[1], out_proj.shape[2]
    parts = halves(m, near, far, at, q)
    for h in range(2):
        for k in range(2):
            row = (2 * h + k) * q
            out_proj[0, row : row + q, :] = parts[k][h]
        for c in range(2):
            col = (2 * h + c) * d
            out_fc[0, :, col : col + d] = jnp.where(m[2] == c, parts[2][h], parts[3][h])


def finish_attn_body(at, count, m, *refs):
    near, far = refs[:count], refs[count : 2 * count]
    out_qkv, out_o = refs[-2:]
    q, d = out_o.shape[1:]
    n, width = q // 2, d // 2
    parts = halves(m, near, far, at, n)
    for h in range(2):
        span = slice(h * n, (h + 1) * n)
        out_o[0, span, :] = parts[0][h]
        bits = [b for k in range(1, 4) for b in (parts[k][h][:, :width], parts[k][h][:, width:])]
        for p in range(3):
            keep, recv = bits[p], bits[3 + p]
            for xside in range(2):
                a = keep[:, xside * q : (xside + 1) * q]
                b = recv[:, xside * q : (xside + 1) * q]
                col = (2 * p + xside) * width
                out_qkv[0, span, col : col + width] = jnp.concatenate(
                    [jnp.where(m[2] == 0, a, b), jnp.where(m[2] == 0, b, a)], axis=1
                )


def finish(body, name, sidx, l, layers, held, before, shapes, at=0):
    near, far = ([a] if not isinstance(a, (list, tuple)) else list(a) for a in held)
    body = functools.partial(body, at, len(near))
    held = near + far
    args = list(held)
    in_specs = [pl.BlockSpec(a.shape, lambda i, m: (0, 0)) for a in held]
    aliases = {}
    if before is not None:
        aliases = {1 + len(args) + k: k for k in range(len(before))}
        args += list(before)
        in_specs += [pl.BlockSpec(memory_space=pl.ANY)] * len(before)
    size = sum(math.prod(sh) for sh in shapes)
    return pl.pallas_call(
        body,
        name=name,
        grid_spec=pltpu.PrefetchScalarGridSpec(
            num_scalar_prefetch=1,
            grid=(1,),
            in_specs=in_specs,
            out_specs=[pl.BlockSpec((1,) + sh, lambda i, m: (l, 0, 0)) for sh in shapes],
        ),
        out_shape=[sds((layers,) + sh, f32) for sh in shapes],
        input_output_aliases=aliases,
        compiler_params=pltpu.CompilerParams(vmem_limit_bytes=32 * MIB),
        cost_estimate=pl.CostEstimate(flops=size, bytes_accessed=6 * size, transcendentals=0),
    )(sidx, *args)


def pair_row(a, step):
    n = lax.axis_size("rows")
    return lax.ppermute(a, "rows", [(r, r ^ step) for r in range(n)])


def vectors_body(m, near, far, wide, qkv_bias, fcb):
    layers = near.shape[1]
    q = near.shape[3]
    for l in range(layers):
        full = []
        for k in range(4):
            core = (k % 2) ^ m[2]
            full.append(jnp.where(m[1] == k // 2, near[core, l], far[core, l]).astype(f32))
        every = jnp.concatenate(full, axis=1)
        wide[l, 0:4, :] = every[0:4]
        wide[l, 4:6, :] = every[6:8]
        wide[l, 6:8, :] = jnp.zeros((2, 4 * q), f32)
        here = [jnp.where(m[2] == 0, full[2 * xside], full[2 * xside + 1]) for xside in range(2)]
        pick = lambda r: [a[r : r + 1] for a in here]
        none = jnp.zeros((1, 2 * q), f32)
        qkv_bias[l] = jnp.concatenate(pick(4) + [none] + pick(5), axis=1)
        rest = [a[r : r + 1] for a in here for r in range(8, a.shape[0])]
        fcb[l] = jnp.concatenate(rest, axis=1)


def pack_small_body(q, m, *refs):
    out = refs[-1]
    count = len(refs[:-1]) // out.shape[0]
    for l in range(out.shape[0]):
        sum_qkv, attn, mlp, pre, gain_c, shift_c, gain_a, shift_a = refs[l * count : (l + 1) * count]

        def mine(ref):
            bits = [ref[:, k * q : (k + 1) * q] for k in range(4)]
            return jnp.where(
                m[1] == 0, jnp.where(m[2] == 0, bits[0], bits[1]), jnp.where(m[2] == 0, bits[2], bits[3])
            )

        side = lambda ref, at, n: jnp.where(m[1] == 0, ref[:, at : at + n], ref[:, at + n : at + 2 * n])
        row = [mine(gain_a), mine(gain_c), mine(shift_a), mine(shift_c)]
        row += [side(sum_qkv, 0, q), side(sum_qkv, 4 * q, q), mine(attn), mine(mlp), side(pre, 0, 4 * q)]
        out[l : l + 1, :] = jnp.concatenate(row, axis=1)


def pack_small(sidx, small, q):
    arrays = [a for row in small for a in row]
    ins = [(a, a.shape, whole(a.shape)) for a in arrays]
    shape = (len(small), 12 * q)
    outs = [(sds(shape, f32), shape, whole(shape))]
    return call(functools.partial(pack_small_body, q), "pack_small", sidx, (1,), ins, outs, [], 0, 16)[0]


def spread_small_body(q, m, all_ref, gain, shift, qv, outb, fcb):
    for l in range(all_ref.shape[0]):
        for k, ref in enumerate((gain, shift, qv, outb)):
            for i in range(2):
                at = (2 * k + i) * q
                ref[l, i : i + 1, :] = all_ref[l : l + 1, at : at + q]
    fcb[...] = all_ref[:, 8 * q :]


def spread_small(sidx, sums, q):
    layers = sums.shape[0]
    ins = [(sums, sums.shape, whole(sums.shape))]
    shapes = [(layers, 2, q)] * 4 + [(layers, 4 * q)]
    outs = [(sds(sh, f32), sh, whole(sh)) for sh in shapes]
    return call(functools.partial(spread_small_body, q), "spread_small", sidx, (1,), ins, outs, [], 0, 16)


def gather_vectors(norm_gain, norm_bias, qv_bias, out_bias, fc_bias):
    layers, _, q = norm_gain.shape
    mine = jnp.concatenate(
        [norm_gain, norm_bias, qv_bias, out_bias, fc_bias.reshape(layers, -1, q)], axis=1
    )
    return jnp.stack([mine, swap(mine, SWAP_CORE)])


def vectors(sidx, near, far):
    _, layers, rows, q = near.shape
    ins = [(a, a.shape, whole(a.shape)) for a in (near, far)]
    hidden = 2 * (rows - 8) * q
    outs = []
    for shape in ((layers, 8, 4 * q), (layers, 1, 6 * q), (layers, 1, hidden)):
        outs.append((sds(shape, f32), shape, whole(shape)))
    return call(vectors_body, "vectors", sidx, (1,), ins, outs, [], near.size, 16)


def on_device(
    block_input,
    output_cotangent,
    doc_ids,
    w_qkv,
    w_o,
    w_fc,
    w_proj,
    norm_gain,
    norm_bias,
    qv_bias,
    out_bias,
    fc_bias,
):
    sidx = place_index()
    s, xi, core = sidx[0], sidx[1], sidx[2]
    layers = w_qkv.shape[0]
    quarter = w_qkv.shape[1]
    tokens = doc_ids.shape[1]
    drow = doc_ids
    dcol = doc_ids.reshape(tokens, 1)

    def pin(outs, *groups):
        flat, tree = jax.tree.flatten((outs, groups))
        outs, groups = jax.tree.unflatten(tree, lax.optimization_barrier(flat))
        return (outs,) + tuple(groups)

    ringed = lax.axis_size("rows") == 8
    args = (w_qkv, w_fc, w_o, w_proj)
    piece = None
    if ringed:
        piece = far_piece(sidx, 0, w_fc, w_qkv)
        args, piece = pin(args, piece)
        piece = cross(piece[0])
    keep, send, fc_keep, fc_send, o = split_columns(sidx, *args[:3], 0)
    params = gather_vectors(norm_gain, norm_bias, qv_bias, out_bias, fc_bias)
    args, piece, keep, send, fc_keep, fc_send, o, params = pin(
        args, piece, keep, send, fc_keep, fc_send, o, params
    )
    x_far = swap(block_input[0], SWAP_X)
    params = (params, swap(params, SWAP_X))
    far_0 = [piece] if ringed else None
    ring_pass(far_0, 1)
    wo = [[w_o, swap(o, SWAP_X)], None]
    halves_0 = halves_1 = None
    if ringed:
        wq = [[keep, swap(send, SWAP_CORE)], None]
        near_0 = [fc_keep, swap(fc_send, SWAP_CORE), w_proj]
        halves_0 = args[3][0]
        halves_1 = args[3][1, : 2 * quarter]
    else:
        wq = [column_pieces(keep, send), None]
        near_0 = column_pieces(fc_keep, fc_send) + row_pieces(w_proj[0])
    keep, send, fc_keep, fc_send, o_next = split_columns(sidx, *args[:3], 1)
    far_0, x_far, params, keep, send, o_next, fc_send, args, wq[0], near_0, halves_0, halves_1 = pin(
        far_0, x_far, params, keep, send, o_next, fc_send, args, wq[0], near_0, halves_0, halves_1
    )
    xs = gather_rows(block_input[0], x_far)
    ring_pass(far_0, 2)
    fc_near = swap(fc_send, SWAP_CORE)
    piece = far_piece(sidx, 1, args[1], args[3]) if ringed else None
    far_0, xs, piece, fc_near, wo[0] = pin(far_0, xs, piece, fc_near, wo[0])
    if ringed:
        piece = [cross(piece[0]), swap(piece[1], SWAP_X)]
    wide, qkv_bias, fcb = vectors(sidx, *params)
    ring_pass(far_0, 3)
    far_0, piece, wide, halves_0, keep, send, o_next = pin(far_0, piece, wide, halves_0, keep, send, o_next)
    far_1 = [jnp.concatenate(piece, axis=1)] if ringed else None
    ring_pass(far_0, 4)
    ring_pass(far_1, 1)
    xs, far_0, far_1, o_next, keep, send = pin(xs, far_0, far_1, o_next, keep, send)
    if ringed:
        both = swap(jnp.concatenate([keep, o_next], axis=1), SWAP_X)
        wq[1] = [keep, swap(send, SWAP_CORE), both, swap(send, SWAP_BOTH)]
        wo[1] = [w_o, both]
        wq[0] += far_0
        near_0 += [swap(halves_0, SWAP_X)]
        near_1 = [fc_keep, fc_near, w_proj, halves_1]
    else:
        near_1 = column_pieces(fc_keep, fc_send) + row_pieces(w_proj[1])
        wq[1] = column_pieces(keep, send)
        wo[1] = [w_o, swap(o_next, SWAP_X)]

    outs = attn_block_forward(sidx, 0, (xs,), wo[0], wq[0], wide[0], wide[0], qkv_bias[0], drow, dcol)
    ring_pass(far_1, 2)
    outs, far_1, near_0, wq[1][3] = pin(outs, far_1, near_0, wq[1][3])
    ln_a, qkv, att, part, lse = outs
    save_a = [(xs, ln_a, qkv, att, lse)]
    recv = swap(part, SWAP_CORE)
    outs = mlp_block(sidx, 0, wide[0], near_0 + (far_0 or []), ahead=(xs, part, recv), fcb=fcb[0])
    ring_pass(far_1, 3)
    outs, wq[1], far_1 = pin(outs, wq[1], far_1)
    wo[1] = [w_o, wq[1][2] if ringed else wo[1][1]]
    cot_far = swap(output_cotangent[0], SWAP_X)
    if ringed:
        near_1[3] = swap(near_1[3], SWAP_X)
    mid, part, ln_c, act, slope = outs
    save_m = (ln_c, act, slope)
    mids = [mid]
    recv = swap(part, SWAP_CORE)
    outs = attn_block_forward(
        sidx, 1, (mid, part, recv), wo[1], wq[1], wide[1], wide[0], qkv_bias[1], drow, dcol
    )
    ring_pass(far_1, 4)
    outs, near_1, far_1, cot_far = pin(outs, near_1, far_1, cot_far)
    cot = gather_rows(output_cotangent[0], cot_far)
    x, ln_a, qkv, att, part, lse = outs
    save_a.append((x, ln_a, qkv, att, lse))
    recv = swap(part, SWAP_CORE)
    outs = mlp_block(sidx, 1, wide[1], near_1 + (far_1 or []), ahead=(x, part, recv), back=(cot,), fcb=fcb[1])
    mid, part, own_mid, part_b, *pack, sum_mlp, sum_pre = outs
    mids.append(mid)

    small = [None] * layers

    d = 4 * quarter
    shapes_m = [(quarter, 4 * d), (d, d)]
    shapes_a = [(quarter, 3 * d), (quarter, d)]
    m_part, a_part, both = (quarter, d), (quarter // 2, d), (3 * quarter // 2, d)

    recv = swap(part_b, SWAP_CORE)
    own_m1, other_m1, *send = pack
    from_m1 = [swap(a, SWAP_CORE) for a in (send[:1] if ringed else send)]
    got_m1 = [along_y(other_m1), along_y_and_core(send[1])] if ringed else None
    outs = attn_block_backward(sidx, 1, cot, mids[1], part_b, recv, wo[1], *save_a[1][2:4], save_a[1][1], wq[1], wide[1], drow, dcol, save_a[1][4])
    outs, got_m1, from_m1 = pin(outs, got_m1, from_m1)
    gm, part_b, own_a1, other_a1, send, sum_attn, gain_c, shift_c, sum_qkv = outs
    small[1] = [sum_qkv, sum_attn, sum_mlp, sum_pre, gain_c, shift_c]
    from_a1 = swap(send, SWAP_CORE)
    recv = swap(part_b, SWAP_CORE)
    if ringed:
        parts_m1 = sum_kernel(
            split_mlp_body, "split_mlp", sidx, (own_m1, from_m1[0], *got_m1), [m_part] * 4, (d, d)
        )
        other_a1 = pack_attn(sidx, other_a1, from_a1, 1)
        recv, parts_m1, other_a1 = pin(recv, parts_m1, other_a1)
        moved = along_z(parts_m1[1:])
        got_a1 = along_y(other_a1)

    outs = mlp_block(sidx, 0, wide[1], near_0 + (far_0 or []), back=(gm, save_a[1][0], part_b, recv, save_m[2], save_m[1], save_m[0]))
    if ringed:
        outs, moved, got_a1 = pin(outs, moved, got_a1)
    g, part_b, own_m0, other_m0, *send, sum_mlp, sum_pre, gain_a, shift_a = outs
    small[1] += [gain_a, shift_a]
    recv = swap(part_b, SWAP_CORE)
    from_m0 = [swap(a, SWAP_CORE) for a in (send[:1] if ringed else send)]
    if ringed:
        total_m1, keep_a1, *parts = sum_kernel(
            mlp_total_attn_split_body,
            "total_mlp_split_attn",
            sidx,
            (parts_m1[0], *moved, own_a1, from_a1, got_a1),
            [m_part, a_part] + [both] * 3,
            (2 * quarter, d),
        )
        recv, parts, other_m0, from_m0, send = pin(recv, parts, other_m0, from_m0, send)
        moved_1 = along_z(parts)
        got_m0 = [along_y(other_m0), along_y_and_core(send[1])]

    outs = attn_block_backward(sidx, 0, g, mids[0], part_b, recv, wo[0], *save_a[0][2:4], save_a[0][1], wq[0], wide[0], drow, dcol, save_a[0][4])
    if ringed:
        outs, moved_1, got_m0 = pin(outs, moved_1, got_m0)
    gm, part_b, own_a0, other_a0, send, sum_attn, gain_c, shift_c, sum_qkv = outs
    small[0] = [sum_qkv, sum_attn, sum_mlp, sum_pre, gain_c, shift_c]
    recv_b = swap(part_b, SWAP_CORE)
    from_a0 = swap(send, SWAP_CORE)
    at = s * block_input.shape[1]
    own = lambda a: lax.dynamic_slice_in_dim(a, at, block_input.shape[1]).astype(f32)

    def rest():
        grad_input, gain_a, shift_a = input_backward(sidx, gm, xs, part_b, recv_b, wide[0])
        small[0].extend([gain_a, shift_a])
        vecs = pack_small(sidx, small, quarter)
        result = own_mid + branch_scale * (own(part) + own(swap(part, SWAP_CORE)) + wide[layers - 1][OUT_M])
        return grad_input, result, vecs

    if ringed:
        total_a1, keep_m0, *parts, by_y = sum_kernel(
            phase_load_body,
            "phase_load",
            sidx,
            (keep_a1, *moved_1, total_m1, own_m0, from_m0[0], *got_m0, other_a0, from_a0),
            [a_part, m_part] + [both] * 3 + [(6 * quarter, d)],
            (d, d),
        )
        parts, by_y, recv_b = pin(parts, by_y, recv_b)
        moved_2 = along_z(parts)
        got_y = along_y(by_y)
        grad_input, result, vecs = rest()
        vecs = vecs + pair_row(vecs, 1)
        moved_2, got_y, vecs, result = pin(moved_2, got_y, vecs, result)
        total_m0, near_a1 = sum_kernel(
            mlp_total_body, "total_mlp", sidx, (keep_m0, total_a1, *moved_2), [m_part, (2 * quarter, d)]
        )
        near_m0 = [total_m0] + along_z([total_m0] * 3)
        far_a1 = along_y(near_a1)
        far_m0 = [along_y(total_m0)]
        keep_a0, *parts = sum_kernel(
            split_attn_body, "split_attn", sidx, (own_a0, from_a0, got_y), [a_part] * 4, (2 * quarter, d)
        )
        outs_m = finish(
            finish_mlp_body, "unpack_mlp", sidx, 1, layers, (by_y, got_y), None, shapes_m, 2 * quarter
        )
        vecs = vecs + pair_row(vecs, 2)
        near_m0, far_a1, far_m0, parts, vecs, outs_m = pin(near_m0, far_a1, far_m0, parts, vecs, outs_m)
        moved_a0 = along_z(parts)
        far_m0 += [along_y(a) for a in near_m0[1:]]
        vecs = vecs + pair_row(vecs, 4)
        outs_a = finish(finish_attn_body, "unpack_attn", sidx, 1, layers, (near_a1, far_a1), None, shapes_a)
        moved_a0, vecs, outs_a = pin(moved_a0, vecs, outs_a)
        total_a0 = total_low(keep_a0, moved_a0)
        near_a0 = [total_a0] + along_z([total_a0] * 3)
        small_out = spread_small(sidx, vecs, quarter)
        near_a0, far_m0, small_out = pin(near_a0, far_m0, small_out)
        near_a0 = jnp.concatenate(near_a0)
        far_a0 = along_y(near_a0)
        pair_m0, pair_a0 = (near_m0, far_m0), (near_a0, far_a0)
    else:
        grad_input, result, vecs = rest()
        sums = []
        for mine, other, recv in ((own_m1, other_m1, from_m1), (own_m0, other_m0, from_m0)):
            sums += [jnp.concatenate([mine, recv[0]]), jnp.concatenate([other, recv[1]])]
        for mine, other, recv in ((own_a1, other_a1, from_a1), (own_a0, other_a0, from_a0)):
            sums += [pack_attn(sidx, mine, recv, 0), pack_attn(sidx, other, recv, 1)]
        sums = lax.psum(sums, "rows")
        outs_m = finish(finish_mlp_body, "unpack_mlp", sidx, 1, layers, sums[0:2], None, shapes_m)
        outs_a = finish(finish_attn_body, "unpack_attn", sidx, 1, layers, sums[4:6], None, shapes_a)
        pair_m0, pair_a0 = sums[2:4], sums[6:8]
        small_out = spread_small(sidx, lax.psum(vecs, "rows"), quarter)
    out_gain, out_shift, out_qv, out_out, out_fcb = small_out
    out_fc, out_proj = finish(finish_mlp_body, "unpack_mlp", sidx, 0, layers, pair_m0, outs_m, shapes_m)
    out_qkv, out_o = finish(finish_attn_body, "unpack_attn", sidx, 0, layers, pair_a0, outs_a, shapes_a)
    return (
        result[None],
        grad_input[None],
        out_qkv,
        out_o,
        out_fc,
        out_proj,
        out_gain,
        out_shift,
        out_qv,
        out_out,
        out_fcb,
    )


def solution(mesh):
    in_specs = (
        P("rows", "seq", None),
        P("rows", "seq", None),
        P("rows", None),
        P(None, "seq", None),
        P(None, "seq", None),
        P(None, "seq", None),
        P(None, "seq", None),
        P(None, None, "seq"),
        P(None, None, "seq"),
        P(None, None, "seq"),
        P(None, None, "seq"),
        P(None, "seq"),
    )
    out_specs = (
        P("rows", "seq", None),
        P("rows", "seq", None),
        P(None, "seq", None),
        P(None, "seq", None),
        P(None, "seq", None),
        P(None, "seq", None),
        P(None, None, "seq"),
        P(None, None, "seq"),
        P(None, None, "seq"),
        P(None, None, "seq"),
        P(None, "seq"),
    )
    return jax.shard_map(
        on_device, mesh=mesh, in_specs=in_specs, out_specs=out_specs, check_vma=False
    )
```

```python
import functools
import math

import jax
import jax.numpy as jnp
from jax import lax
from jax.experimental import pallas as pl
from jax.experimental.pallas import tpu as pltpu
from jax.sharding import PartitionSpec as P

HD = 64
branch_scale = 48.0 ** (-0.5)
norm_eps = 1e-05
masked_score = -1e30
log2_e = math.log2(math.e)
MIB = 1 << 20
VMEM = 62
BLK = 256

f32 = jnp.float32
bf16 = jnp.bfloat16
STREAM = bf16

SWAP_CORE = [(s, s ^ 1) for s in range(4)]
SWAP_X = [(s, s ^ 2) for s in range(4)]
SWAP_BOTH = [(s, s ^ 3) for s in range(4)]


def dot_nn(a, b):
    return lax.dot_general(a, b, (((1,), (0,)), ((), ())), preferred_element_type=f32)


def dot_nt(a, b):
    return lax.dot_general(a, b, (((1,), (1,)), ((), ())), preferred_element_type=f32)


def dot_tn(a, b):
    return lax.dot_general(a, b, (((0,), (0,)), ((), ())), preferred_element_type=f32)


def call(body, name, sidx, grid, ins, outs, scratch, flops, vmem, exps=0):
    arrays = [a for a, _, _ in ins]
    in_specs = [
        pl.BlockSpec(memory_space=pl.ANY) if b is None else pl.BlockSpec(b, m) for _, b, m in ins
    ]
    out_specs = [
        pl.BlockSpec(memory_space=pl.ANY) if b is None else pl.BlockSpec(b, m) for _, b, m in outs
    ]
    out_shape = [s for s, _, _ in outs]
    nbytes = sum(a.size * a.dtype.itemsize for a in arrays)
    nbytes += sum(math.prod(s.shape) * s.dtype.itemsize for s in out_shape)
    return pl.pallas_call(
        body,
        name=name,
        grid_spec=pltpu.PrefetchScalarGridSpec(
            num_scalar_prefetch=1,
            grid=grid,
            in_specs=in_specs,
            out_specs=out_specs,
            scratch_shapes=scratch,
        ),
        out_shape=out_shape,
        compiler_params=pltpu.CompilerParams(
            dimension_semantics=("arbitrary",) * len(grid), vmem_limit_bytes=vmem * MIB
        ),
        cost_estimate=pl.CostEstimate(
            flops=int(flops), bytes_accessed=int(nbytes), transcendentals=int(exps)
        ),
    )(sidx, *arrays)


RING = [0, 2, 4, 6, 7, 5, 3, 1]
RING_NEXT = [(RING[i], RING[(i + 1) % 8]) for i in range(8)]
RING_PREV = [(b, a) for a, b in RING_NEXT]
RING_STEPS = [0, -1, 1, -2, 2, -3, 3, -4]


def ring_place():
    row = lax.axis_index("rows").astype(jnp.int32)
    return jnp.where(row % 2 == 0, row // 2, 7 - row // 2)


def place_index():
    s = lax.axis_index("seq").astype(jnp.int32)
    zero = jnp.int32(0)
    row = lax.axis_index("rows").astype(jnp.int32) if lax.axis_size("rows") == 8 else zero
    place = ring_place() if lax.axis_size("rows") == 8 else zero
    return jnp.stack([s, s // 2, s % 2, place, row % 2, row // 2])


def sds(shape, dtype):
    return jax.ShapeDtypeStruct(shape, dtype)


def whole(block):
    zeros = (0,) * len(block)
    return lambda i, m: zeros


def row_tile(i, m):
    return (i, 0)


def stack_tile(i, m):
    return (i ^ m[0], 0, 0)


def normed(x):
    centre = x - jnp.mean(x, axis=-1, keepdims=True)
    spread = jnp.mean(centre * centre, axis=-1, keepdims=True)
    rstd = lax.rsqrt(spread + norm_eps)
    return centre * rstd, rstd


def norm_back(x, grad, gain):
    unit, rstd = normed(x)
    inner = grad * gain
    mean_inner = jnp.mean(inner, axis=-1, keepdims=True)
    mean_prod = jnp.mean(inner * unit, axis=-1, keepdims=True)
    return rstd * (inner - mean_inner - unit * mean_prod), unit


GAIN_A, GAIN_C, SHIFT_A, SHIFT_C, OUT_A, OUT_M = range(6)


def row_of(ref, k):
    return ref[k : k + 1, :]


def lane_half(shape):
    return lax.broadcasted_iota(jnp.int32, shape, 1) // HD


def block_start(i):
    return BLK * (i * (i + 1) // 2)


class Mover:
    def __init__(self, sems):
        self.sems = sems
        self.used = 0

    def make(self, src, dst):
        cp = pltpu.make_async_copy(src, dst, self.sems.at[self.used])
        self.used += 1
        return cp

    def go(self, src, dst):
        cp = self.make(src, dst)
        cp.start()
        return cp


def wait_all(copies):
    for cp in copies:
        cp.wait()


def tile_of(i):
    return pl.ds(i * BLK, BLK)


def pieces_in(mover, refs, dst, first, rows, at=0):
    out = []
    width = dst.shape[1]
    for j, ref in enumerate(refs):
        where = pl.multiple_of((first ^ j) * rows, 16)
        src = ref if ref.shape[1] == width else ref.at[:, pl.ds(at, width)]
        out.append(mover.go(src, dst.at[pl.ds(where, rows)]))
    return out


def add_up(ref, value, start):
    here = jnp.sum(value, axis=0, keepdims=True)
    if start:
        ref[...] = here
    else:
        ref[...] += here


def back_pair(pair, pairs, tokens, qkv, att, datt, lse, bias, starts, dqkv, dq_acc):
    blocks = tokens // BLK
    half = lane_half((BLK, 2 * HD))
    score_scale = HD ** (-0.5)
    scale = score_scale * log2_e
    pick_row = lax.broadcasted_iota(jnp.int32, (8, 2 * HD), 0)
    pick = jnp.where(lane_half((8, 2 * HD)) == pick_row, 1.0, 0.0)
    prod = datt[pair].astype(f32) * att[pair].astype(f32)
    delta = lax.dot_general(
        pick, prod, (((1,), (1,)), ((), ())), precision=lax.Precision.HIGHEST, preferred_element_type=f32
    )
    for j in range(blocks):
        first = j * BLK
        span = slice(first, first + BLK)
        rest = pl.ds(first, tokens - first)
        kj = qkv[pair + pairs, span, :]
        vj = qkv[pair + 2 * pairs, span, :]
        qq = qkv[pair, rest, :]
        dd = datt[pair, rest, :]
        width = tokens - first
        zero = jnp.zeros_like(kj)
        dks, dvs, dss, khs = [], [], [], []
        for h in range(2):
            kh = jnp.where(half == h, kj, zero)
            vh = jnp.where(half == h, vj, zero)
            t = dot_nt(kh, qq) * scale + bias[:, starts[j] : starts[j] + width]
            p = jnp.exp2(t - lse[pair, h : h + 1, first:])
            dp = dot_nt(vh, dd)
            ds = (p * (dp - delta[h : h + 1, first:])).astype(bf16)
            dvs.append(dot_nn(p.astype(bf16), dd))
            dks.append(dot_nn(ds, qq))
            dss.append(ds)
            khs.append(kh)
        dk = jnp.where(half == 0, dks[0], dks[1]) * score_scale
        dv = jnp.where(half == 0, dvs[0], dvs[1])
        dqkv[pair + pairs, span, :] = dk.astype(bf16)
        dqkv[pair + 2 * pairs, span, :] = dv.astype(bf16)
        dq = dot_tn(jnp.concatenate(dss, axis=0), jnp.concatenate(khs, axis=0))
        if j == 0:
            dq_acc[...] = dq
        else:
            dq_acc[first:, :] += dq
    dqkv[pair] = (dq_acc[...] * score_scale).astype(bf16)


def forward_pair(pair, pairs, blocks, qkv, bias, att, lse):
    half = lane_half((BLK, 2 * HD))
    scale = HD ** (-0.5) * log2_e
    for i in range(blocks):
        width = BLK * (i + 1)
        span = slice(i * BLK, (i + 1) * BLK)
        qb = qkv[pair, span, :]
        kk = qkv[pair + pairs, 0:width, :]
        vv = qkv[pair + 2 * pairs, 0:width, :]
        mixed, logs = [], []
        for h in range(2):
            qh = jnp.where(half == h, qb, jnp.zeros_like(qb))
            t = dot_nt(qh, kk) * scale + bias[:, block_start(i) : block_start(i) + width]
            top = jnp.max(t, axis=-1, keepdims=True)
            p = jnp.exp2(t - top)
            total = jnp.sum(p, axis=-1, keepdims=True)
            o = dot_nn(p.astype(bf16), vv)
            mixed.append(o / total)
            logs.append(jnp.broadcast_to(top + jnp.log2(total), (BLK, 2 * HD)))
        att[pair, span, :] = jnp.where(half == 0, mixed[0], mixed[1]).astype(bf16)
        turned = jnp.transpose(jnp.where(half == 0, logs[0], logs[1]))
        lse[pair, 0:1, span] = turned[0:1, :]
        lse[pair, 1:2, span] = turned[HD : HD + 1, :]


def attn_block_body(l, first, parts_w, m, *refs):
    count = 1 if first else 3
    sources = refs[:count]
    wo0, wo1 = refs[count : count + 2]
    weights = refs[count + 2 : count + 2 + parts_w]
    refs = refs[count + 2 + parts_w :]
    vec, prev, bias_row, drow, dcol = refs[:5]
    refs = refs[5:]
    if not first:
        x_out, refs = refs[0], refs[1:]
    ln_out, qkv_out, att_out, part_out, lse = refs[:5]
    bufs = refs[5 : 5 + count]
    (wo, w, lns, qkv, att, parts, bias, sems) = refs[5 + count :]
    tokens, d = lns.shape
    blocks = tokens // BLK
    pairs = att.shape[0]
    half = d // 2
    q = half // 2
    move = Mover(sems)
    c_w = attn_weights_in(move, m, weights, w, q)
    c_tiles = []
    for t in range(blocks):
        for ref, dst in zip(sources, bufs):
            src = ref.at[t ^ m[0]] if len(ref.shape) == 3 else ref.at[tile_of(t)]
            c_tiles.append(move.go(src, dst.at[tile_of(t)]))
    c_wo = pieces_in(move, (wo0.at[l], wo1), wo, m[1], q, w.shape[1])
    for i in range(blocks):
        width = BLK * (i + 1)
        begin = i * BLK
        qpos = begin + lax.broadcasted_iota(jnp.int32, (BLK, width), 0)
        kpos = lax.broadcasted_iota(jnp.int32, (BLK, width), 1)
        same = dcol[begin : begin + BLK, :] == drow[:, :width]
        allowed = (kpos <= qpos) & same
        bias[:, block_start(i) : block_start(i) + width] = jnp.where(allowed, 0.0, masked_score)
    wait_all(c_w)
    wait_all(c_tiles)
    c_out = []
    mine = pl.ds(pl.multiple_of(m[1] * half, 128), half)
    for t in range(blocks):
        span = tile_of(t)
        if first:
            x = bufs[0][span, :].astype(f32)
        else:
            part = bufs[1][span, :].astype(f32) + bufs[2][span, :].astype(f32) + row_of(prev, OUT_M)
            x = bufs[0][span, :].astype(f32) + branch_scale * part
            bufs[0][span, :] = x.astype(STREAM)
            c_out.append(move.go(bufs[0].at[span], x_out.at[span]))
        unit, _ = normed(x)
        ln = (unit * row_of(vec, GAIN_A) + row_of(vec, SHIFT_A)).astype(bf16)
        lns[span, :] = ln
        c_out.append(move.go(lns.at[span, mine], ln_out.at[span]))
        row = (dot_nn(ln, w[...]) + bias_row[...]).astype(bf16)
        for k in range(3 * pairs):
            cols = slice(k * 2 * HD, (k + 1) * 2 * HD)
            qkv[k, span, :] = row[:, cols]
    for k in range(3 * pairs):
        c_out.append(move.go(qkv.at[k], qkv_out.at[k]))

    @pl.loop(0, pairs)
    def _(pair):
        forward_pair(pair, pairs, blocks, qkv, bias, att, lse)

    for k in range(pairs):
        c_out.append(move.go(att.at[k], att_out.at[k]))
    wait_all(c_wo)
    for t in range(blocks):
        span = tile_of(t)
        row = jnp.concatenate([att[k, span, :] for k in range(pairs)], axis=1)
        parts[span, :] = dot_nn(row, wo[...]).astype(bf16)
        c_out.append(move.go(parts.at[span], part_out.at[span]))
    wait_all(c_out)


def attn_block_forward(sidx, l, source, wo_pieces, pieces, vec, prev, bias, drow, dcol):
    first = len(source) == 1
    q, cols = pieces[0].shape
    d = 4 * q
    tokens = drow.shape[1]
    width = cols // 3
    pairs = width // (2 * HD)
    ins = [(a, None, None) for a in (*source, *wo_pieces, *pieces)]
    ins += [(a, a.shape, whole(a.shape)) for a in (vec, prev, bias, drow, dcol)]
    outs = [] if first else [(sds((tokens, d), STREAM), None, None)]
    outs += [
        (sds((tokens, d // 2), bf16), None, None),
        (sds((3 * pairs, tokens, 2 * HD), bf16), None, None),
        (sds((pairs, tokens, 2 * HD), bf16), None, None),
        (sds((tokens, d), bf16), None, None),
        (sds((pairs, 8, tokens), f32), (pairs, 8, tokens), whole((0, 0, 0))),
    ]
    blocks = tokens // BLK
    scratch = [pltpu.VMEM((tokens, d), a.dtype) for a in source]
    scratch += [
        pltpu.VMEM((width, d), bf16),
        pltpu.VMEM((d, cols), bf16),
        pltpu.VMEM((tokens, d), bf16),
        pltpu.VMEM((3 * pairs, tokens, 2 * HD), bf16),
        pltpu.VMEM((pairs, tokens, 2 * HD), bf16),
        pltpu.VMEM((tokens, d), bf16),
        pltpu.VMEM((BLK, block_start(blocks)), f32),
        pltpu.SemaphoreType.DMA((64,)),
    ]
    return call(
        functools.partial(attn_block_body, l, first, len(pieces)),
        "attention_block",
        sidx,
        (1,),
        ins,
        outs,
        scratch,
        4 * tokens * tokens * width + 2 * tokens * d * (cols + width),
        VMEM,
        exps=tokens * tokens * pairs,
    )


def far_in(move, m, refs, dst, q, lanes):
    out = []
    part = q // 4
    for ref, t in zip(refs, RING_STEPS):
        chunk = (m[3] + t + len(refs)) % len(refs)
        at = pl.multiple_of((m[0] ^ (2 + chunk // 4)) * q + (chunk % 4) * part, 16)
        out.append(move.go(ref.at[:, lanes], dst.at[pl.ds(at, part)]))
    return out


def attn_weights_in(move, m, refs, w, q):
    out = pieces_in(move, refs[:4] if len(refs) == 4 else refs[:2], w, m[0], q)
    if len(refs) > 4:
        out += far_in(move, m, refs[2:], w, q, pl.ds(0, w.shape[1]))
    return out


def mlp_weights_in(move, l, m, refs, wf, wp):
    if len(refs) == 6:
        first = pieces_in(move, refs[:4], wf, m[0], refs[0].shape[0])
        return first, pieces_in(move, refs[4:], wp, m[1], refs[4].shape[0])
    keep, near, own = refs[0], refs[1], refs[2].at[l]
    q, hidden = keep.shape
    deep = own.shape[0]
    half = deep // 2
    far = refs[-8:]
    base = far[0].shape[1] - hidden if l == 0 else 0
    first = pieces_in(move, (keep, near), wf, m[0], q)
    first += far_in(move, m, far, wf, q, pl.ds(base, hidden))
    second = pieces_in(move, (own,), wp, m[1], deep)
    there = (1 - m[1]) * deep
    at = pl.multiple_of(there, 16)
    second.append(move.go(refs[3], wp.at[pl.ds(at, refs[3].shape[0])]))
    if l:
        part = q // 4
        for ref, t in zip(far, RING_STEPS):
            chunk = (m[3] + t + 8) % 8
            at = pl.multiple_of(there + half + chunk * part, 16)
            src = ref.at[:, pl.ds(hidden, own.shape[1])]
            second.append(move.go(src, wp.at[pl.ds(at, part)]))
    return first, second


def gelu_and_slope(pre):
    root = math.sqrt(2.0 / math.pi)
    sq = pre * pre
    gate = 0.5 * jnp.tanh(pre * (root + root * 0.044715 * sq)) + 0.5
    rise = pre * (2.0 * root + 6.0 * root * 0.044715 * sq)
    return pre * gate, gate + gate * ((1.0 - gate) * rise)


def mlp_block_body(l, ahead, back, count, m, *refs):
    take = lambda k: (refs[:k], refs[k:])
    vec = prev = fcb = None
    sources, refs = take(3 if ahead else 0)
    (cot,), refs = take(1) if ahead and back else ((None,), refs)
    grads, refs = take(4 if back and not ahead else 0)
    (slope_in, act_in, ln_in), refs = take(3) if back and not ahead else ((None,) * 3, refs)
    weights, refs = take(count)
    if ahead:
        (vec, fcb), refs = take(2)
    else:
        (vec,), refs = take(1)
    if ahead:
        (mid_out, part_out), refs = take(2)
        if back:
            (own_out,), refs = take(1)
        else:
            (ln_out, act_out, slope_out), refs = take(3)
    if back:
        if not ahead:
            (g_out,), refs = take(1)
        (back_out, mine, other, send_mine, send_other, sum_mlp, sum_pre), refs = take(7)
        if not ahead:
            (sum_gain, sum_shift), refs = take(2)
    b0, b1, b2, b3, wf, wp, lns, act, slope, dmlp, sems = refs
    tokens, d = b1.shape
    blocks = tokens // BLK
    hidden = wf.shape[1]
    q = d // 4
    move = Mover(sems)
    c_tiles = []
    if ahead:
        loads = list(zip(sources, (b0, b1, b2))) + ([(cot, b3)] if back else [])
    else:
        loads = list(zip(grads, (b0, b1, b2, b3)))
    c_wp = []
    if ahead:
        c_wf, c_wp = mlp_weights_in(move, l, m, weights, wf, wp)
    for t in range(blocks):
        for ref, dst in loads:
            src = ref.at[t ^ m[0]] if len(ref.shape) == 3 else ref.at[tile_of(t)]
            c_tiles.append(move.go(src, dst.at[tile_of(t)]))
    if not ahead:
        c_wf, c_wp = mlp_weights_in(move, l, m, weights, wf, wp)
        c_slope = [move.go(slope_in.at[tile_of(t)], slope.at[tile_of(t)]) for t in range(blocks)]
        c_late = [move.go(act_in, act.at[:, pl.ds(0, act_in.shape[1])]), move.go(ln_in, lns.at[:, pl.ds(0, d // 2)])]
    c_out = []
    n = len(loads)
    wide = hidden // 2
    if not (ahead and back):
        wait_all(c_tiles + c_wf + c_wp)
    if not ahead:
        wait_all(c_slope)
    for t in range(blocks):
        if ahead and back:
            wait_all(c_tiles[n * t : n * t + n])
        span = tile_of(t)
        if ahead:
            part = b1[span, :].astype(f32) + b2[span, :].astype(f32) + row_of(vec, OUT_A)
            mid = b0[span, :].astype(f32) + branch_scale * part
            b0[span, :] = mid.astype(b0.dtype)
            c_out.append(move.go(b0.at[span], mid_out.at[span]))
            if back:

                @pl.when(m[0] == t)
                def _():
                    own_out[...] = mid

            unit, _ = normed(mid)
            ln = (unit * row_of(vec, GAIN_C) + row_of(vec, SHIFT_C)).astype(bf16)
            lns[span, :] = ln
            if t == 0 and back:
                wait_all(c_wf)
            value, rise = gelu_and_slope(dot_nn(ln, wf[...]) + fcb[...])
            low = value.astype(bf16)
            act[span, :] = low
            if not back:
                slope[span, :] = rise.astype(bf16)
                cols = pl.ds(pl.multiple_of(m[1] * (d // 2), 128), d // 2)
                c_out.append(move.go(lns.at[span, cols], ln_out.at[span]))
                cols = pl.ds(pl.multiple_of(m[1] * wide, 128), wide)
                c_out.append(move.go(act.at[span, cols], act_out.at[span]))
                c_out.append(move.go(slope.at[span], slope_out.at[span]))
            if t == 0 and back:
                wait_all(c_wp)
            b1[span, :] = dot_nn(low, wp[...]).astype(bf16)
            c_out.append(move.go(b1.at[span], part_out.at[span]))
        if back:
            if ahead:
                g = b3[span, :].astype(f32)
            else:
                rise = slope[span, :].astype(f32)
                grad = b2[span, :].astype(f32) + b3[span, :].astype(f32)
                part, unit = norm_back(b1[span, :].astype(f32), grad, row_of(vec, GAIN_A))
                add_up(sum_gain, grad * unit, t == 0)
                add_up(sum_shift, grad, t == 0)
                g = b0[span, :].astype(f32) + part
                b0[span, :] = g.astype(b0.dtype)
                c_out.append(move.go(b0.at[span], g_out.at[span]))
            low = (branch_scale * g).astype(bf16)
            dmlp[span, :] = low
            add_up(sum_mlp, low.astype(f32), t == 0)
            dpre = (dot_nt(low, wp[...]) * rise).astype(bf16)
            slope[span, :] = dpre
            add_up(sum_pre, dpre.astype(f32), t == 0)
            b2[span, :] = dot_nt(dpre, wf[...]).astype(bf16)
            c_out.append(move.go(b2.at[span], back_out.at[span]))
    if back:
        y = m[4]
        if not ahead:
            wait_all(c_late)
            turned = jnp.transpose(act[:, 0:wide])
        else:
            turned = jnp.transpose(jnp.where(m[1] == 0, act[:, 0:wide], act[:, wide:]))
        grad = dot_nn(turned, dmlp[...]).astype(bf16)
        h = grad.shape[0] // 2
        mine[0:h, :] = jnp.where(y == 0, grad[:h], grad[h:])
        other[0:h, :] = jnp.where(y == 0, grad[h:], grad[:h])
        half = d // 2
        if not ahead:
            turned = jnp.transpose(lns[:, 0:half])
        else:
            turned = jnp.transpose(jnp.where(m[1] == 0, lns[:, 0:half], lns[:, half:]))
        sides = [dot_nn(turned, slope[:, i * d : (i + 1) * d]).astype(bf16) for i in range(2)]
        for here, there, i in ((mine, send_mine, 0), (other, send_other, 1)):
            side = jnp.where(y == i, sides[0], sides[1])
            here[h : h + q, :] = jnp.where(m[2] == 0, side[:q], side[q:])
            there[...] = jnp.where(m[2] == 0, side[q:], side[:q])
    wait_all(c_out)


def mlp_block(sidx, l, vec, weights, ahead=None, back=None, fcb=None):
    d = vec.shape[1]
    if ahead is not None:
        tokens = ahead[1].shape[0]
        hidden = fcb.shape[1]
        sources = list(ahead) + ([back[0]] if back else [])
        types = [STREAM if ahead[0].ndim == 2 else ahead[0].dtype, bf16, bf16, bf16]
        vectors_in = [vec, fcb]
    else:
        tokens, hidden = back[4].shape
        sources = list(back)
        types = [back[0].dtype, back[1].dtype, bf16, bf16]
        vectors_in = [vec]
    q = d // 4
    ins = [(a, None, None) for a in sources + list(weights)]
    ins += [(a, a.shape, whole(a.shape)) for a in vectors_in]
    stay = lambda shape, dtype: (sds(shape, dtype), shape, whole(shape))
    away = lambda shape, dtype: (sds(shape, dtype), None, None)
    outs = []
    if ahead is not None:
        outs += [away((tokens, d), STREAM), away((tokens, d), bf16)]
        if back:
            outs += [stay((BLK, d), f32)]
        else:
            outs += [
                away((tokens, d // 2), bf16),
                away((tokens, hidden // 2), bf16),
                away((tokens, hidden), bf16),
            ]
    if back:
        if ahead is None:
            outs += [away((tokens, d), back[0].dtype)]
        outs += [away((tokens, d), bf16)]
        outs += [stay((3 * q, d), bf16)] * 2 + [stay((q, d), bf16)] * 2
        outs += [stay((1, d), f32), stay((1, hidden), f32)]
        if ahead is None:
            outs += [stay((1, d), f32)] * 2
    scratch = [pltpu.VMEM((tokens, d), t) for t in types]
    scratch += [
        pltpu.VMEM((d, hidden), bf16),
        pltpu.VMEM((hidden, d), bf16),
        pltpu.VMEM((tokens, d), bf16),
        pltpu.VMEM((tokens, hidden), bf16),
        pltpu.VMEM((tokens, hidden), bf16),
        pltpu.VMEM((tokens, d), bf16),
        pltpu.SemaphoreType.DMA((96,)),
    ]
    return call(
        functools.partial(mlp_block_body, l, ahead is not None, bool(back), len(weights)),
        "mlp_block" + ("_forward" if ahead is not None else "") + ("_backward" if back else ""),
        sidx,
        (1,),
        ins,
        outs,
        scratch,
        (4 * bool(ahead is not None) + 8 * bool(back)) * tokens * d * hidden,
        VMEM,
        exps=tokens * hidden,
    )


def attn_block_back_body(l, parts_w, m, *refs):
    (g_in, mid_in, p_in, r_in, wo0, wo1, qkv_in, att_in, ln_in) = refs[:9]
    weights = refs[9 : 9 + parts_w]
    refs = refs[:9] + refs[9 + parts_w :]
    (vec, drow, dcol, lse) = refs[9:13]
    refs = refs[:9] + (None,) * 4 + refs[9:]
    (gm_out, part_out, mine, other, to_core) = refs[17:22]
    (sum_attn, sum_gain, sum_shift, sum_qkv) = refs[22:26]
    (gs, mids, ps, rs, wo, qkv, att, lns, w, dattn, datt, dqkv, bias, dq_acc, sems) = refs[26:]
    tokens, d = mids.shape
    blocks = tokens // BLK
    pairs = att.shape[0]
    q = d // 4
    move = Mover(sems)
    c_wo = pieces_in(move, (wo0.at[l], wo1), wo, m[1], q, w.shape[1])
    c_tiles = []
    loads = [(g_in, gs), (mid_in, mids), (p_in, ps), (r_in, rs)]
    for t in range(blocks):
        for ref, dst in loads:
            src = ref.at[t ^ m[0]] if len(ref.shape) == 3 else ref.at[tile_of(t)]
            c_tiles.append(move.go(src, dst.at[tile_of(t)]))
    c_qkv = [move.go(qkv_in, qkv), move.go(att_in, att)]
    c_w = attn_weights_in(move, m, weights, w, q)
    half = d // 2
    c_ln = [move.go(ln_in, lns)]

    starts = [sum(tokens - BLK * a for a in range(j)) for j in range(blocks)]
    for j in range(blocks):
        width = tokens - j * BLK
        first = j * BLK
        kpos = lax.broadcasted_iota(jnp.int32, (BLK, width), 0)
        qpos = lax.broadcasted_iota(jnp.int32, (BLK, width), 1)
        same = dcol[first : first + BLK, :] == drow[:, first:]
        allowed = (kpos <= qpos) & same
        bias[:, starts[j] : starts[j] + width] = jnp.where(allowed, 0.0, masked_score)

    wait_all(c_wo)
    c_out = []
    for t in range(blocks):
        wait_all(c_tiles[4 * t : 4 * t + 4])
        span = tile_of(t)
        grad = ps[span, :].astype(f32) + rs[span, :].astype(f32)
        part, unit = norm_back(mids[span, :].astype(f32), grad, row_of(vec, GAIN_C))
        add_up(sum_gain, grad * unit, t == 0)
        add_up(sum_shift, grad, t == 0)
        gm = gs[span, :].astype(f32) + part
        gs[span, :] = gm.astype(gs.dtype)
        c_out.append(move.go(gs.at[span], gm_out.at[span]))
        low = (branch_scale * gm).astype(bf16)
        dattn[span, :] = low
        add_up(sum_attn, low.astype(f32), t == 0)
        heads = dot_nt(low, wo[...]).astype(bf16)
        for k in range(pairs):
            datt[k, span, :] = heads[:, k * 2 * HD : (k + 1) * 2 * HD]

    wait_all(c_qkv)

    @pl.loop(0, pairs)
    def _(pair):
        back_pair(pair, pairs, tokens, qkv, att, datt, lse, bias, starts, dqkv, dq_acc)

    wait_all(c_w)
    for t in range(blocks):
        span = tile_of(t)
        row = jnp.concatenate([dqkv[k, span, :] for k in range(3 * pairs)], axis=1)
        ps[span, :] = dot_nt(row, w[...]).astype(bf16)
        c_out.append(move.go(ps.at[span], part_out.at[span]))
        add_up(sum_qkv, row.astype(f32), t == 0)

    wait_all(c_ln)
    quart = q // 2
    y = m[4]
    turned = jnp.concatenate([jnp.transpose(att[k]) for k in range(pairs)], axis=0)
    left = jnp.where(m[1] == 0, turned[:q], turned[q : 2 * q])
    g_o = dot_nn(left, dattn[...]).astype(bf16)
    for i in range(2):
        cols = slice(i * half, (i + 1) * half)
        a, b = g_o[:quart, cols], g_o[quart:, cols]
        mine[i * quart : (i + 1) * quart, :] = jnp.where(y == 0, a, b)
        other[i * quart : (i + 1) * quart, :] = jnp.where(y == 0, b, a)
    turned = jnp.transpose(lns[...])
    for p in range(3):
        right = jnp.concatenate([dqkv[p * pairs + k] for k in range(pairs)], axis=1)
        grad = dot_nn(turned, right).astype(bf16)
        keep = jnp.where(m[2] == 0, grad[:q], grad[q:])
        send = jnp.where(m[2] == 0, grad[q:], grad[:q])
        at = (2 + p) * quart
        mine[at : at + quart, :] = jnp.where(y == 0, keep[:quart], keep[quart:])
        other[at : at + quart, :] = jnp.where(y == 0, keep[quart:], keep[:quart])
        at = p * quart
        to_core[at : at + quart, :] = jnp.where(y == 0, send[:quart], send[quart:])
        at += 3 * quart
        to_core[at : at + quart, :] = jnp.where(y == 0, send[quart:], send[:quart])
    wait_all(c_out)


def attn_block_backward(sidx, l, g, mid, part, recv, wo_pieces, qkv, att, ln_a, pieces, vec, drow, dcol, lse):
    tokens, d = mid.shape
    q, cols = pieces[0].shape
    width = cols // 3
    pairs = width // (2 * HD)
    ins = [(a, None, None) for a in (g, mid, part, recv, *wo_pieces, qkv, att, ln_a, *pieces)]
    ins += [(a, a.shape, whole(a.shape)) for a in (vec, drow, dcol, lse)]
    stay = lambda shape, dtype: (sds(shape, dtype), shape, whole(shape))
    outs = [
        (sds((tokens, d), STREAM), None, None),
        (sds((tokens, d), bf16), None, None),
        stay((5 * q // 2, width), bf16),
        stay((5 * q // 2, width), bf16),
        stay((3 * q, width), bf16),
        stay((1, d), f32),
        stay((1, d), f32),
        stay((1, d), f32),
        stay((1, cols), f32),
    ]
    blocks = tokens // BLK
    wide = (tokens, 2 * HD)
    scratch = [
        pltpu.VMEM((tokens, d), g.dtype),
        pltpu.VMEM((tokens, d), mid.dtype),
        pltpu.VMEM((tokens, d), bf16),
        pltpu.VMEM((tokens, d), bf16),
        pltpu.VMEM((width, d), bf16),
        pltpu.VMEM((3 * pairs,) + wide, bf16),
        pltpu.VMEM((pairs,) + wide, bf16),
        pltpu.VMEM((tokens, d // 2), bf16),
        pltpu.VMEM((d, cols), bf16),
        pltpu.VMEM((tokens, d), bf16),
        pltpu.VMEM((pairs,) + wide, bf16),
        pltpu.VMEM((3 * pairs,) + wide, bf16),
        pltpu.VMEM((BLK, block_start(blocks)), f32),
        pltpu.VMEM(wide, f32),
        pltpu.SemaphoreType.DMA((64,)),
    ]
    return call(
        functools.partial(attn_block_back_body, l, len(pieces)),
        "attention_block_backward",
        sidx,
        (1,),
        ins,
        outs,
        scratch,
        10 * tokens * tokens * width,
        VMEM,
        exps=tokens * tokens * pairs,
    )


def add_rows(ref, value, start):
    @pl.when(start)
    def _():
        ref[...] = jnp.zeros_like(ref)

    ref[...] += jnp.sum(value, axis=0, keepdims=True)


def input_back_body(m, gm_ref, x_ref, p_ref, r_ref, vec, out_ref, sum_gain, sum_shift):
    tile = pl.program_id(0)
    grad = p_ref[...].astype(f32) + r_ref[...].astype(f32)
    part, unit = norm_back(x_ref[0].astype(f32), grad, row_of(vec, GAIN_A))
    add_rows(sum_gain, grad * unit, tile == 0)
    add_rows(sum_shift, grad, tile == 0)

    @pl.when(tile == m[0])
    def _():
        out_ref[...] = gm_ref[...].astype(f32) + part


def input_backward(sidx, gm, x, part, recv, vec):
    tokens, depth = gm.shape
    tile = (BLK, depth)
    ins = [(gm, tile, row_tile), (x, (1, BLK, depth), stack_tile)]
    ins += [(a, tile, row_tile) for a in (part, recv)]
    ins.append((vec, vec.shape, whole(vec.shape)))
    outs = [(sds((BLK, depth), f32), tile, whole((0, 0)))]
    outs += [(sds((1, depth), f32), (1, depth), whole((0, 0)))] * 2
    return call(input_back_body, "input_backward", sidx, (tokens // BLK,), ins, outs, [], tokens * depth, VMEM)


def swap(a, perm):
    return lax.ppermute(a, "seq", perm)


def split_body(m, qkv_ref, fc_ref, o_ref, qkv_keep, qkv_send, fc_keep, fc_send, o_out):
    core = m[2]
    o_out[...] = o_ref[0]
    q = qkv_ref.shape[1]
    pair = 2 * q
    for p in range(3):
        own, other = [], []
        for xside in range(2):
            col = (2 * p + xside) * pair
            both = qkv_ref[0, :, col : col + pair]
            own.append(jnp.where(core == 0, both[:, :q], both[:, q:]))
            other.append(jnp.where(core == 0, both[:, q:], both[:, :q]))
        qkv_keep[:, p * pair : (p + 1) * pair] = jnp.concatenate(own, axis=1)
        qkv_send[:, p * pair : (p + 1) * pair] = jnp.concatenate(other, axis=1)
    d = fc_ref.shape[2] // 4
    for xside in range(2):
        one = fc_ref[0, :, 2 * xside * d : (2 * xside + 1) * d]
        two = fc_ref[0, :, (2 * xside + 1) * d : (2 * xside + 2) * d]
        fc_keep[:, xside * d : (xside + 1) * d] = jnp.where(core == 0, one, two)
        fc_send[:, xside * d : (xside + 1) * d] = jnp.where(core == 0, two, one)


def split_columns(sidx, w_qkv, w_fc, w_o, l):
    _, rows, cols = w_qkv.shape
    hidden = w_fc.shape[2]
    at = lambda i, m: (l, 0, 0)
    depth = w_o.shape[2]
    ins = [(w_qkv, (1, rows, cols), at), (w_fc, (1, rows, hidden), at), (w_o, (1, rows, depth), at)]
    outs = []
    for width in (cols // 2, cols // 2, hidden // 2, hidden // 2, depth):
        outs.append((sds((rows, width), bf16), (rows, width), whole((0, 0))))
    return call(split_body, "split_columns", sidx, (1,), ins, outs, [], rows * cols, VMEM)


def column_pieces(keep, send):
    return [keep, swap(send, SWAP_CORE), swap(keep, SWAP_X), swap(send, SWAP_BOTH)]


def row_pieces(w):
    return [w, swap(w, SWAP_X)]


def half_columns(w, core):
    q = w.shape[1] // 12
    out = []
    for k in range(6):
        both = w[:, 2 * k * q : (2 * k + 2) * q]
        out.append(jnp.where(core == 0, both[:, :q], both[:, q:]))
    return jnp.concatenate(out, axis=1)


def far_piece_body(l, m, w_fc, w_more, out, *refs):
    rows_in, sems = refs[-2:]
    part = out.shape[0]
    hidden = w_fc.shape[2]
    d = hidden // 4
    move = Mover(sems)
    rows = pl.ds(pl.multiple_of((m[3] % 4) * part, 16), part)
    core = m[2] ^ (m[3] // 4)
    base = 0 if l else out.shape[1] - 2 * d
    copies = []
    for xside in range(2):
        here = pl.ds(pl.multiple_of((2 * xside + core) * d, 128), d)
        copies.append(move.go(w_fc.at[l, rows, here], out.at[:, pl.ds(base + xside * d, d)]))
    if l == 0:
        move.go(w_more.at[l, rows], rows_in).wait()
        out[:, :base] = half_columns(rows_in[...], core)
    else:
        rows = pl.ds(pl.multiple_of(8 * part + m[3] * part, 16), part)
        copies.append(move.go(w_more.at[l, rows], refs[0]))
    wait_all(copies)


def far_piece(sidx, l, w_fc, w_more):
    _, q, hidden = w_fc.shape
    d, part = hidden // 4, q // 4
    widths = [hidden // 2 + w_more.shape[2] // 2] if l == 0 else [hidden // 2, d]
    ins = [(a, None, None) for a in (w_fc, w_more)]
    outs = [(sds((part, w), bf16), (part, w), whole((0, 0))) for w in widths]
    scratch = [pltpu.VMEM((part, w_more.shape[2]), bf16), pltpu.SemaphoreType.DMA((4,))]
    return call(
        functools.partial(far_piece_body, l), "far_piece", sidx, (1,), ins, outs, scratch, 0, VMEM
    )


def cross(a):
    pairs = []
    for r in range(8):
        turn = 2 if RING.index(r) < 4 else 3
        pairs += [(4 * r + s, 4 * r + (s ^ turn)) for s in range(4)]
    return lax.ppermute(a, ("rows", "seq"), pairs)


def ring_pass(held, t):
    if held is None:
        return []
    on = lax.ppermute(held[max(0, len(held) - 2)], "rows", RING_NEXT)
    if t == 4:
        new = [on]
    else:
        new = [on, lax.ppermute(held[-1], "rows", RING_PREV)]
    held += new
    return new


def gather_rows(a, far):
    return jnp.stack([a, swap(a, SWAP_CORE), far, swap(far, SWAP_CORE)])


SWAP_Y = [(r, r ^ 1) for r in range(8)]
SWAP_Z = [None] + [[(r, r ^ (2 * d)) for r in range(8)] for d in range(1, 4)]


def join_attn(own, recv, at):
    n = own.shape[0] // 5
    bit = lambda k: own[k * n : (k + 1) * n, :]
    got = lambda k: recv[at + k * n : at + (k + 1) * n, :]
    pairs = [(bit(0), bit(1)), (bit(2), bit(3)), (bit(4), got(0)), (got(1), got(2))]
    return [jnp.concatenate(p, axis=1) for p in pairs]


def pack_attn_body(which, m, own, recv, out):
    n = out.shape[0] // 4
    for k, rows in enumerate(join_attn(own, recv, which * 3 * n)):
        out[k * n : (k + 1) * n, :] = rows


def pack_attn(sidx, own, recv, which):
    shape = (4 * (own.shape[0] // 5), 2 * own.shape[1])
    ins = [(a, a.shape, whole(a.shape)) for a in (own, recv)]
    outs = [(sds(shape, bf16), shape, whole(shape))]
    return call(
        functools.partial(pack_attn_body, which), "pack_attn", sidx, (1,), ins, outs, [], 0, 16
    )[0]


def add_low(a, b):
    return (a.astype(f32) + b.astype(f32)).astype(bf16)


def total_low(first, rest):
    return (first.astype(f32) + sum(r.astype(f32) for r in rest)).astype(bf16)


def fill_mlp(full, own, recv, got, got_recv):
    cut = own.shape[0]
    full[0:cut, :] = add_low(own[...], got[...])
    full[cut:, :] = add_low(recv[...], got_recv[...])


def fill_attn(full, own, recv, got):
    n = full.shape[0] // 4
    for k, rows in enumerate(join_attn(own, recv, 0)):
        full[k * n : (k + 1) * n, :] = add_low(rows, got[k * n : (k + 1) * n, :])


def quarter_at(full, m, d):
    n = full.shape[0] // 4
    return full[pl.ds(pl.multiple_of((m[5] ^ d) * n, 16), n), :]


def split_mlp_body(m, own, recv, got, got_recv, *refs):
    outs, full = refs[:-1], refs[-1]
    fill_mlp(full, own, recv, got, got_recv)
    for d, out in enumerate(outs):
        out[...] = quarter_at(full, m, d)


def split_attn_body(m, own, recv, got, *refs):
    outs, full = refs[:-1], refs[-1]
    fill_attn(full, own, recv, got)
    for d, out in enumerate(outs):
        out[...] = quarter_at(full, m, d)


def mlp_total_attn_split_body(m, first, g1, g2, g3, own, recv, got, total, keep, s1, s2, s3, full):
    acc = total_low(first[...], [g1[...], g2[...], g3[...]])
    total[...] = acc
    n = acc.shape[0]
    fill_attn(full, own, recv, got)
    keep[...] = quarter_at(full, m, 0)
    for d, out in enumerate((s1, s2, s3)):
        out[0:n, :] = acc
        out[n:, :] = quarter_at(full, m, d + 1)


def phase_load_body(m, first, g1, g2, g3, low, own, recv, got, got_recv, other, from_a, total, keep, s1, s2, s3, by_y, full):
    n, k = low.shape[0], first.shape[0]
    acc = total_low(first[...], [g[n:, :] for g in (g1, g2, g3)])
    total[...] = acc
    fill_mlp(full, own, recv, got, got_recv)
    keep[...] = quarter_at(full, m, 0)
    for d, out in enumerate((s1, s2, s3)):
        out[0:n, :] = quarter_at(full, m, d + 1)
        out[n:, :] = acc
    at = 0
    for rows in join_attn(other, from_a, 3 * k):
        by_y[at : at + k, :] = rows
        at += k
    for rows in (low[...], g1[0:n, :], g2[0:n, :], g3[0:n, :]):
        by_y[at : at + n, :] = rows
        at += n


def mlp_total_body(m, first, low, g1, g2, g3, total, near):
    n = first.shape[0]
    total[...] = total_low(first[...], [g[0:n, :] for g in (g1, g2, g3)])
    k = low.shape[0]
    near[0:k, :] = low[...]
    for i, g in enumerate((g1, g2, g3)):
        near[(i + 1) * k : (i + 2) * k, :] = g[n:, :]


def sum_kernel(body, name, sidx, arrays, shapes, scratch=None):
    ins = [(a, a.shape, whole(a.shape)) for a in arrays]
    outs = [(sds(sh, bf16), sh, whole(sh)) for sh in shapes]
    extra = [] if scratch is None else [pltpu.VMEM(scratch, bf16)]
    return call(body, name, sidx, (1,), ins, outs, extra, 0, VMEM)


def along_y(a):
    return lax.ppermute(a, "rows", SWAP_Y)


def along_y_and_core(a):
    pairs = [(4 * r + s, 4 * (r ^ 1) + (s ^ 1)) for r in range(8) for s in range(4)]
    return lax.ppermute(a, ("rows", "seq"), pairs)


def along_z(arrays):
    return [lax.ppermute(a, "rows", SWAP_Z[d + 1]) for d, a in enumerate(arrays)]


def pick_quarter(m, refs, k, at, n):
    if len(refs) == 1:
        return refs[0][pl.ds(pl.multiple_of(at + (k ^ m[5]) * n, 16), n), :].astype(f32)
    d = k ^ m[5]
    low = jnp.where(d % 2 == 0, refs[0][...], refs[1][...])
    high = jnp.where(d % 2 == 0, refs[2][...], refs[3][...])
    return jnp.where(d < 2, low, high).astype(f32)


def halves(m, near, far, at, n):
    def quarter(k):
        a, b = pick_quarter(m, near, k, at, n), pick_quarter(m, far, k, at, n)
        return jnp.where(m[4] == 0, a, b), jnp.where(m[4] == 0, b, a)

    return [quarter(k) for k in range(4)]


def finish_mlp_body(at, count, m, *refs):
    near, far = refs[:count], refs[count : 2 * count]
    out_fc, out_proj = refs[-2:]
    q, d = out_fc.shape[1], out_proj.shape[2]
    parts = halves(m, near, far, at, q)
    for h in range(2):
        for k in range(2):
            row = (2 * h + k) * q
            out_proj[0, row : row + q, :] = parts[k][h]
        for c in range(2):
            col = (2 * h + c) * d
            out_fc[0, :, col : col + d] = jnp.where(m[2] == c, parts[2][h], parts[3][h])


def finish_attn_body(at, count, m, *refs):
    near, far = refs[:count], refs[count : 2 * count]
    out_qkv, out_o = refs[-2:]
    q, d = out_o.shape[1:]
    n, width = q // 2, d // 2
    parts = halves(m, near, far, at, n)
    for h in range(2):
        span = slice(h * n, (h + 1) * n)
        out_o[0, span, :] = parts[0][h]
        bits = [b for k in range(1, 4) for b in (parts[k][h][:, :width], parts[k][h][:, width:])]
        for p in range(3):
            keep, recv = bits[p], bits[3 + p]
            for xside in range(2):
                a = keep[:, xside * q : (xside + 1) * q]
                b = recv[:, xside * q : (xside + 1) * q]
                col = (2 * p + xside) * width
                out_qkv[0, span, col : col + width] = jnp.concatenate(
                    [jnp.where(m[2] == 0, a, b), jnp.where(m[2] == 0, b, a)], axis=1
                )


def finish(body, name, sidx, l, layers, held, before, shapes, at=0):
    near, far = ([a] if not isinstance(a, (list, tuple)) else list(a) for a in held)
    body = functools.partial(body, at, len(near))
    held = near + far
    args = list(held)
    in_specs = [pl.BlockSpec(a.shape, lambda i, m: (0, 0)) for a in held]
    aliases = {}
    if before is not None:
        aliases = {1 + len(args) + k: k for k in range(len(before))}
        args += list(before)
        in_specs += [pl.BlockSpec(memory_space=pl.ANY)] * len(before)
    size = sum(math.prod(sh) for sh in shapes)
    return pl.pallas_call(
        body,
        name=name,
        grid_spec=pltpu.PrefetchScalarGridSpec(
            num_scalar_prefetch=1,
            grid=(1,),
            in_specs=in_specs,
            out_specs=[pl.BlockSpec((1,) + sh, lambda i, m: (l, 0, 0)) for sh in shapes],
        ),
        out_shape=[sds((layers,) + sh, f32) for sh in shapes],
        input_output_aliases=aliases,
        compiler_params=pltpu.CompilerParams(vmem_limit_bytes=32 * MIB),
        cost_estimate=pl.CostEstimate(flops=size, bytes_accessed=6 * size, transcendentals=0),
    )(sidx, *args)


def pair_row(a, step):
    n = lax.axis_size("rows")
    return lax.ppermute(a, "rows", [(r, r ^ step) for r in range(n)])


def vectors_body(m, near, far, wide, qkv_bias, fcb):
    layers = near.shape[1]
    q = near.shape[3]
    for l in range(layers):
        full = []
        for k in range(4):
            core = (k % 2) ^ m[2]
            full.append(jnp.where(m[1] == k // 2, near[core, l], far[core, l]).astype(f32))
        every = jnp.concatenate(full, axis=1)
        wide[l, 0:4, :] = every[0:4]
        wide[l, 4:6, :] = every[6:8]
        wide[l, 6:8, :] = jnp.zeros((2, 4 * q), f32)
        here = [jnp.where(m[2] == 0, full[2 * xside], full[2 * xside + 1]) for xside in range(2)]
        pick = lambda r: [a[r : r + 1] for a in here]
        none = jnp.zeros((1, 2 * q), f32)
        qkv_bias[l] = jnp.concatenate(pick(4) + [none] + pick(5), axis=1)
        rest = [a[r : r + 1] for a in here for r in range(8, a.shape[0])]
        fcb[l] = jnp.concatenate(rest, axis=1)


def pack_small_body(q, m, *refs):
    out = refs[-1]
    count = len(refs[:-1]) // out.shape[0]
    for l in range(out.shape[0]):
        sum_qkv, attn, mlp, pre, gain_c, shift_c, gain_a, shift_a = refs[l * count : (l + 1) * count]

        def mine(ref):
            bits = [ref[:, k * q : (k + 1) * q] for k in range(4)]
            return jnp.where(
                m[1] == 0, jnp.where(m[2] == 0, bits[0], bits[1]), jnp.where(m[2] == 0, bits[2], bits[3])
            )

        side = lambda ref, at, n: jnp.where(m[1] == 0, ref[:, at : at + n], ref[:, at + n : at + 2 * n])
        row = [mine(gain_a), mine(gain_c), mine(shift_a), mine(shift_c)]
        row += [side(sum_qkv, 0, q), side(sum_qkv, 4 * q, q), mine(attn), mine(mlp), side(pre, 0, 4 * q)]
        out[l : l + 1, :] = jnp.concatenate(row, axis=1)


def pack_small(sidx, small, q):
    arrays = [a for row in small for a in row]
    ins = [(a, a.shape, whole(a.shape)) for a in arrays]
    shape = (len(small), 12 * q)
    outs = [(sds(shape, f32), shape, whole(shape))]
    return call(functools.partial(pack_small_body, q), "pack_small", sidx, (1,), ins, outs, [], 0, 16)[0]


def spread_small_body(q, m, all_ref, gain, shift, qv, outb, fcb):
    for l in range(all_ref.shape[0]):
        for k, ref in enumerate((gain, shift, qv, outb)):
            for i in range(2):
                at = (2 * k + i) * q
                ref[l, i : i + 1, :] = all_ref[l : l + 1, at : at + q]
    fcb[...] = all_ref[:, 8 * q :]


def spread_small(sidx, sums, q):
    layers = sums.shape[0]
    ins = [(sums, sums.shape, whole(sums.shape))]
    shapes = [(layers, 2, q)] * 4 + [(layers, 4 * q)]
    outs = [(sds(sh, f32), sh, whole(sh)) for sh in shapes]
    return call(functools.partial(spread_small_body, q), "spread_small", sidx, (1,), ins, outs, [], 0, 16)


def gather_vectors(norm_gain, norm_bias, qv_bias, out_bias, fc_bias):
    layers, _, q = norm_gain.shape
    mine = jnp.concatenate(
        [norm_gain, norm_bias, qv_bias, out_bias, fc_bias.reshape(layers, -1, q)], axis=1
    )
    return jnp.stack([mine, swap(mine, SWAP_CORE)])


def vectors(sidx, near, far):
    _, layers, rows, q = near.shape
    ins = [(a, a.shape, whole(a.shape)) for a in (near, far)]
    hidden = 2 * (rows - 8) * q
    outs = []
    for shape in ((layers, 8, 4 * q), (layers, 1, 6 * q), (layers, 1, hidden)):
        outs.append((sds(shape, f32), shape, whole(shape)))
    return call(vectors_body, "vectors", sidx, (1,), ins, outs, [], near.size, 16)


def on_device(
    block_input,
    output_cotangent,
    doc_ids,
    w_qkv,
    w_o,
    w_fc,
    w_proj,
    norm_gain,
    norm_bias,
    qv_bias,
    out_bias,
    fc_bias,
):
    sidx = place_index()
    s, xi, core = sidx[0], sidx[1], sidx[2]
    layers = w_qkv.shape[0]
    quarter = w_qkv.shape[1]
    tokens = doc_ids.shape[1]
    drow = doc_ids
    dcol = doc_ids.reshape(tokens, 1)

    def pin(outs, *groups):
        flat, tree = jax.tree.flatten((outs, groups))
        outs, groups = jax.tree.unflatten(tree, lax.optimization_barrier(flat))
        return (outs,) + tuple(groups)

    ringed = lax.axis_size("rows") == 8
    args = (w_qkv, w_fc, w_o, w_proj)
    piece = None
    if ringed:
        piece = far_piece(sidx, 0, w_fc, w_qkv)
        args, piece = pin(args, piece)
        piece = cross(piece[0])
    keep, send, fc_keep, fc_send, o = split_columns(sidx, *args[:3], 0)
    params = gather_vectors(norm_gain, norm_bias, qv_bias, out_bias, fc_bias)
    args, piece, keep, send, fc_keep, fc_send, o, params = pin(
        args, piece, keep, send, fc_keep, fc_send, o, params
    )
    x_far = swap(block_input[0], SWAP_X)
    params = (params, swap(params, SWAP_X))
    far_0 = [piece] if ringed else None
    ring_pass(far_0, 1)
    wo = [[w_o, swap(o, SWAP_X)], None]
    halves_0 = halves_1 = None
    if ringed:
        wq = [[keep, swap(send, SWAP_CORE)], None]
        near_0 = [fc_keep, swap(fc_send, SWAP_CORE), w_proj]
        halves_0 = args[3][0]
        halves_1 = args[3][1, : 2 * quarter]
    else:
        wq = [column_pieces(keep, send), None]
        near_0 = column_pieces(fc_keep, fc_send) + row_pieces(w_proj[0])
    keep, send, fc_keep, fc_send, o_next = split_columns(sidx, *args[:3], 1)
    far_0, x_far, params, keep, send, o_next, fc_send, args, wq[0], near_0, halves_0, halves_1 = pin(
        far_0, x_far, params, keep, send, o_next, fc_send, args, wq[0], near_0, halves_0, halves_1
    )
    xs = gather_rows(block_input[0], x_far)
    ring_pass(far_0, 2)
    fc_near = swap(fc_send, SWAP_CORE)
    piece = far_piece(sidx, 1, args[1], args[3]) if ringed else None
    far_0, xs, piece, fc_near, wo[0] = pin(far_0, xs, piece, fc_near, wo[0])
    if ringed:
        piece = [cross(piece[0]), swap(piece[1], SWAP_X)]
    wide, qkv_bias, fcb = vectors(sidx, *params)
    ring_pass(far_0, 3)
    far_0, piece, wide, halves_0, keep, send, o_next = pin(far_0, piece, wide, halves_0, keep, send, o_next)
    far_1 = [jnp.concatenate(piece, axis=1)] if ringed else None
    ring_pass(far_0, 4)
    ring_pass(far_1, 1)
    xs, far_0, far_1, o_next, keep, send = pin(xs, far_0, far_1, o_next, keep, send)
    if ringed:
        both = swap(jnp.concatenate([keep, o_next], axis=1), SWAP_X)
        wq[1] = [keep, swap(send, SWAP_CORE), both, swap(send, SWAP_BOTH)]
        wo[1] = [w_o, both]
        wq[0] += far_0
        near_0 += [swap(halves_0, SWAP_X)]
        near_1 = [fc_keep, fc_near, w_proj, halves_1]
    else:
        near_1 = column_pieces(fc_keep, fc_send) + row_pieces(w_proj[1])
        wq[1] = column_pieces(keep, send)
        wo[1] = [w_o, swap(o_next, SWAP_X)]

    outs = attn_block_forward(sidx, 0, (xs,), wo[0], wq[0], wide[0], wide[0], qkv_bias[0], drow, dcol)
    ring_pass(far_1, 2)
    outs, far_1, near_0, wq[1][3] = pin(outs, far_1, near_0, wq[1][3])
    ln_a, qkv, att, part, lse = outs
    save_a = [(xs, ln_a, qkv, att, lse)]
    recv = swap(part, SWAP_CORE)
    outs = mlp_block(sidx, 0, wide[0], near_0 + (far_0 or []), ahead=(xs, part, recv), fcb=fcb[0])
    ring_pass(far_1, 3)
    outs, wq[1], far_1 = pin(outs, wq[1], far_1)
    wo[1] = [w_o, wq[1][2] if ringed else wo[1][1]]
    cot_far = swap(output_cotangent[0], SWAP_X)
    if ringed:
        near_1[3] = swap(near_1[3], SWAP_X)
    mid, part, ln_c, act, slope = outs
    save_m = (ln_c, act, slope)
    mids = [mid]
    recv = swap(part, SWAP_CORE)
    outs = attn_block_forward(
        sidx, 1, (mid, part, recv), wo[1], wq[1], wide[1], wide[0], qkv_bias[1], drow, dcol
    )
    ring_pass(far_1, 4)
    outs, near_1, far_1, cot_far = pin(outs, near_1, far_1, cot_far)
    cot = gather_rows(output_cotangent[0], cot_far)
    x, ln_a, qkv, att, part, lse = outs
    save_a.append((x, ln_a, qkv, att, lse))
    recv = swap(part, SWAP_CORE)
    outs = mlp_block(sidx, 1, wide[1], near_1 + (far_1 or []), ahead=(x, part, recv), back=(cot,), fcb=fcb[1])
    mid, part, own_mid, part_b, *pack, sum_mlp, sum_pre = outs
    mids.append(mid)

    small = [None] * layers

    d = 4 * quarter
    shapes_m = [(quarter, 4 * d), (d, d)]
    shapes_a = [(quarter, 3 * d), (quarter, d)]
    m_part, a_part, both = (quarter, d), (quarter // 2, d), (3 * quarter // 2, d)

    recv = swap(part_b, SWAP_CORE)
    own_m1, other_m1, *send = pack
    from_m1 = [swap(a, SWAP_CORE) for a in (send[:1] if ringed else send)]
    got_m1 = [along_y(other_m1), along_y_and_core(send[1])] if ringed else None
    outs = attn_block_backward(sidx, 1, cot, mids[1], part_b, recv, wo[1], *save_a[1][2:4], save_a[1][1], wq[1], wide[1], drow, dcol, save_a[1][4])
    outs, got_m1, from_m1 = pin(outs, got_m1, from_m1)
    gm, part_b, own_a1, other_a1, send, sum_attn, gain_c, shift_c, sum_qkv = outs
    small[1] = [sum_qkv, sum_attn, sum_mlp, sum_pre, gain_c, shift_c]
    from_a1 = swap(send, SWAP_CORE)
    recv = swap(part_b, SWAP_CORE)
    if ringed:
        parts_m1 = sum_kernel(
            split_mlp_body, "split_mlp", sidx, (own_m1, from_m1[0], *got_m1), [m_part] * 4, (d, d)
        )
        other_a1 = pack_attn(sidx, other_a1, from_a1, 1)
        recv, parts_m1, other_a1 = pin(recv, parts_m1, other_a1)
        moved = along_z(parts_m1[1:])
        got_a1 = along_y(other_a1)

    outs = mlp_block(sidx, 0, wide[1], near_0 + (far_0 or []), back=(gm, save_a[1][0], part_b, recv, save_m[2], save_m[1], save_m[0]))
    if ringed:
        outs, moved, got_a1 = pin(outs, moved, got_a1)
    g, part_b, own_m0, other_m0, *send, sum_mlp, sum_pre, gain_a, shift_a = outs
    small[1] += [gain_a, shift_a]
    recv = swap(part_b, SWAP_CORE)
    from_m0 = [swap(a, SWAP_CORE) for a in (send[:1] if ringed else send)]
    if ringed:
        total_m1, keep_a1, *parts = sum_kernel(
            mlp_total_attn_split_body,
            "total_mlp_split_attn",
            sidx,
            (parts_m1[0], *moved, own_a1, from_a1, got_a1),
            [m_part, a_part] + [both] * 3,
            (2 * quarter, d),
        )
        recv, parts, other_m0, from_m0, send = pin(recv, parts, other_m0, from_m0, send)
        moved_1 = along_z(parts)
        got_m0 = [along_y(other_m0), along_y_and_core(send[1])]

    outs = attn_block_backward(sidx, 0, g, mids[0], part_b, recv, wo[0], *save_a[0][2:4], save_a[0][1], wq[0], wide[0], drow, dcol, save_a[0][4])
    if ringed:
        outs, moved_1, got_m0 = pin(outs, moved_1, got_m0)
    gm, part_b, own_a0, other_a0, send, sum_attn, gain_c, shift_c, sum_qkv = outs
    small[0] = [sum_qkv, sum_attn, sum_mlp, sum_pre, gain_c, shift_c]
    recv_b = swap(part_b, SWAP_CORE)
    from_a0 = swap(send, SWAP_CORE)
    at = s * block_input.shape[1]
    own = lambda a: lax.dynamic_slice_in_dim(a, at, block_input.shape[1]).astype(f32)

    def rest():
        grad_input, gain_a, shift_a = input_backward(sidx, gm, xs, part_b, recv_b, wide[0])
        small[0].extend([gain_a, shift_a])
        vecs = pack_small(sidx, small, quarter)
        result = own_mid + branch_scale * (own(part) + own(swap(part, SWAP_CORE)) + wide[layers - 1][OUT_M])
        return grad_input, result, vecs

    if ringed:
        total_a1, keep_m0, *parts, by_y = sum_kernel(
            phase_load_body,
            "phase_load",
            sidx,
            (keep_a1, *moved_1, total_m1, own_m0, from_m0[0], *got_m0, other_a0, from_a0),
            [a_part, m_part] + [both] * 3 + [(6 * quarter, d)],
            (d, d),
        )
        parts, by_y, recv_b = pin(parts, by_y, recv_b)
        moved_2 = along_z(parts)
        got_y = along_y(by_y)
        grad_input, result, vecs = rest()
        vecs = vecs + pair_row(vecs, 1)
        moved_2, got_y, vecs, result = pin(moved_2, got_y, vecs, result)
        total_m0, near_a1 = sum_kernel(
            mlp_total_body, "total_mlp", sidx, (keep_m0, total_a1, *moved_2), [m_part, (2 * quarter, d)]
        )
        near_m0 = [total_m0] + along_z([total_m0] * 3)
        far_a1 = along_y(near_a1)
        far_m0 = [along_y(total_m0)]
        keep_a0, *parts = sum_kernel(
            split_attn_body, "split_attn", sidx, (own_a0, from_a0, got_y), [a_part] * 4, (2 * quarter, d)
        )
        outs_m = finish(
            finish_mlp_body, "unpack_mlp", sidx, 1, layers, (by_y, got_y), None, shapes_m, 2 * quarter
        )
        vecs = vecs + pair_row(vecs, 2)
        near_m0, far_a1, far_m0, parts, vecs, outs_m = pin(near_m0, far_a1, far_m0, parts, vecs, outs_m)
        moved_a0 = along_z(parts)
        far_m0 += [along_y(a) for a in near_m0[1:]]
        vecs = vecs + pair_row(vecs, 4)
        outs_a = finish(finish_attn_body, "unpack_attn", sidx, 1, layers, (near_a1, far_a1), None, shapes_a)
        moved_a0, vecs, outs_a = pin(moved_a0, vecs, outs_a)
        total_a0 = total_low(keep_a0, moved_a0)
        near_a0 = [total_a0] + along_z([total_a0] * 3)
        small_out = spread_small(sidx, vecs, quarter)
        near_a0, far_m0, small_out = pin(near_a0, far_m0, small_out)
        near_a0 = jnp.concatenate(near_a0)
        far_a0 = along_y(near_a0)
        pair_m0, pair_a0 = (near_m0, far_m0), (near_a0, far_a0)
    else:
        grad_input, result, vecs = rest()
        sums = []
        for mine, other, recv in ((own_m1, other_m1, from_m1), (own_m0, other_m0, from_m0)):
            sums += [jnp.concatenate([mine, recv[0]]), jnp.concatenate([other, recv[1]])]
        for mine, other, recv in ((own_a1, other_a1, from_a1), (own_a0, other_a0, from_a0)):
            sums += [pack_attn(sidx, mine, recv, 0), pack_attn(sidx, other, recv, 1)]
        sums = lax.psum(sums, "rows")
        outs_m = finish(finish_mlp_body, "unpack_mlp", sidx, 1, layers, sums[0:2], None, shapes_m)
        outs_a = finish(finish_attn_body, "unpack_attn", sidx, 1, layers, sums[4:6], None, shapes_a)
        pair_m0, pair_a0 = sums[2:4], sums[6:8]
        small_out = spread_small(sidx, lax.psum(vecs, "rows"), quarter)
    out_gain, out_shift, out_qv, out_out, out_fcb = small_out
    out_fc, out_proj = finish(finish_mlp_body, "unpack_mlp", sidx, 0, layers, pair_m0, outs_m, shapes_m)
    out_qkv, out_o = finish(finish_attn_body, "unpack_attn", sidx, 0, layers, pair_a0, outs_a, shapes_a)
    return (
        result[None],
        grad_input[None],
        out_qkv,
        out_o,
        out_fc,
        out_proj,
        out_gain,
        out_shift,
        out_qv,
        out_out,
        out_fcb,
    )


def solution(mesh):
    in_specs = (
        P("rows", "seq", None),
        P("rows", "seq", None),
        P("rows", None),
        P(None, "seq", None),
        P(None, "seq", None),
        P(None, "seq", None),
        P(None, "seq", None),
        P(None, None, "seq"),
        P(None, None, "seq"),
        P(None, None, "seq"),
        P(None, None, "seq"),
        P(None, "seq"),
    )
    out_specs = (
        P("rows", "seq", None),
        P("rows", "seq", None),
        P(None, "seq", None),
        P(None, "seq", None),
        P(None, "seq", None),
        P(None, "seq", None),
        P(None, None, "seq"),
        P(None, None, "seq"),
        P(None, None, "seq"),
        P(None, None, "seq"),
        P(None, "seq"),
    )
    return jax.shard_map(
        on_device, mesh=mesh, in_specs=in_specs, out_specs=out_specs, check_vma=False
    )
```
